128 devices in a mesh: ctx: 32 (over z, y_hi, x), fsdp: 4 (over y_lo, core).
Axes of the slice: x: 4, y: 4 (y_hi: 2, y_lo: 2; y = y_hi * 2 + y_lo), z: 4, core: 2. Of those that a mesh axis runs over, the one named last changes fastest.
Arguments:
- tokens: bfloat16 [4, 4096, 960], P('fsdp', 'ctx'), may hold values from -6 to 6
- cotangent: bfloat16 [4, 4096, 960], P('fsdp', 'ctx'), may hold values from -6 to 6
- block_table: int32 [64], replicated, may hold values from 0 to 63, as said below
- attn_gain: bfloat16 [960], P('fsdp'), may hold values from 0.5 to 1.5
- w_query: bfloat16 [960, 960], P('fsdp'), may hold values from -0.1875 to 0.1875
- w_key: bfloat16 [960, 320], P('fsdp'), may hold values from -0.1875 to 0.1875
- w_value: bfloat16 [960, 320], P('fsdp'), may hold values from -0.1875 to 0.1875
- w_out: bfloat16 [960, 960], P('fsdp'), may hold values from -1 to 1
- mlp_gain: bfloat16 [960], P('fsdp'), may hold values from 0.5 to 1.5
- w_gate: bfloat16 [960, 2560], P('fsdp'), may hold values from -0.1875 to 0.1875
- w_up: bfloat16 [960, 2560], P('fsdp'), may hold values from -0.1875 to 0.1875
- w_down: bfloat16 [2560, 960], P('fsdp'), may hold values from -0.125 to 0.125
Outputs:
- layer_out: bfloat16 [4, 4096, 960], P('fsdp', 'ctx')
- grad_tokens: float32 [4, 4096, 960], P('fsdp', 'ctx')
- grad_attn_gain: float32 [960], P('fsdp')
- grad_query: float32 [960, 960], P('fsdp')
- grad_key: float32 [960, 320], P('fsdp')
- grad_value: float32 [960, 320], P('fsdp')
- grad_out: float32 [960, 960], P('fsdp')
- grad_mlp_gain: float32 [960], P('fsdp')
- grad_gate: float32 [960, 2560], P('fsdp')
- grad_up: float32 [960, 2560], P('fsdp')
- grad_down: float32 [2560, 960], P('fsdp')
The draws below stay inside these ranges and needn't reach their ends.
Inputs may be any that keep to these rules, and one draw needn't show every extreme that they name: `block_table`: entries 2c and 2c + 1 are the numbers of the two blocks of 64 positions held by index c of ctx, in the order of its rows; every block number appears once, and the two numbers of one index sum to 63.
All inputs are finite; a program needn't handle non-finite values.
Results may differ from the reference program's by a relative error of at most 0.034.
Values may be sent and summed in bfloat16 or wider, within the bound.
A program may use at most 192 MiB of HBM per device.

```python
import jax
import jax.numpy as jnp
from jax import lax

D = 960
HEADS = 15
KV_HEADS = 5
HEAD = 64
FF = 2560
TOK_DEV = 128
QW = 960
KVW = 320
LEN = 4096
SEQS = 4
BLOCKS = 64


def draw_block_table(key, part):
    key = jax.random.fold_in(key, 7)
    pair_key, flip_key = jax.random.split(key)
    pair_count = BLOCKS // 2
    early_block = jax.random.permutation(pair_key, pair_count).astype(jnp.int32)
    late_block = (BLOCKS - 1 - early_block).astype(jnp.int32)
    flip_bits = jax.random.randint(flip_key, (pair_count,), 0, 2)
    front_block = jnp.where(flip_bits == 1, late_block, early_block)
    second = jnp.where(flip_bits == 1, early_block, late_block)
    return jnp.stack([front_block, second], axis=1).reshape(BLOCKS).astype(jnp.int32)


def levels(stream_key, extent, cuts, low, largest):
    loudness = 1.0
    for axis_at, shards_of in cuts:
        draws = jax.random.uniform(jax.random.fold_in(jax.random.fold_in(stream_key, 6), axis_at), (shards_of,), jnp.float32, low / len(cuts), largest / len(cuts))
        loudness = loudness * jnp.repeat(jnp.exp(draws), extent[axis_at] // shards_of).reshape((-1,) + (1,) * (len(extent) - 1 - axis_at))
    return loudness


def gaussian(own_key, shape, scale, most, cuts=(), kind=jnp.bfloat16):
    values = jax.random.normal(own_key, shape, jnp.float32) * scale
    if len(cuts) > 0:
        values = levels(own_key, shape, cuts, -0.22, 0.18) * values
    return jnp.clip(values, min=-most, max=most).astype(kind)


def setup_inputs(seed: int = 0) -> dict:
    streams_of = jax.random.split(jax.random.key(seed), 13)
    return {
        "tokens": gaussian(streams_of[0], (SEQS, LEN, D), 1.0, 6.0, ((0, 4), (1, 32))),
        "cotangent": gaussian(streams_of[1], (SEQS, LEN, D), 1.0, 6.0, ((0, 4), (1, 32))),
        "block_table": draw_block_table(jax.random.fold_in(streams_of[12], 71), 0),
        "attn_gain": jnp.clip(1.0 + 0.1 * jax.random.normal(streams_of[3], (D,), jnp.float32), 0.5, 1.5).astype(jnp.bfloat16),
        "w_query": gaussian(streams_of[4], (D, QW), D ** -0.5, 0.1875, ((0, 4),)),
        "w_key": gaussian(streams_of[5], (D, KVW), D ** -0.5, 0.1875, ((0, 4),)),
        "w_value": gaussian(streams_of[6], (D, KVW), D ** -0.5, 0.1875, ((0, 4),)),
        "w_out": gaussian(streams_of[7], (QW, D), (QW // 32) ** -0.5, 1.0, ((0, 4),)),
        "mlp_gain": jnp.clip(1.0 + 0.1 * jax.random.normal(streams_of[8], (D,), jnp.float32), 0.5, 1.5).astype(jnp.bfloat16),
        "w_gate": gaussian(streams_of[9], (D, FF), D ** -0.5, 0.1875, ((0, 4),)),
        "w_up": gaussian(streams_of[10], (D, FF), D ** -0.5, 0.1875, ((0, 4),)),
        "w_down": gaussian(streams_of[11], (FF, D), FF ** -0.5, 0.125, ((0, 4),)),
    }


@jax.custom_vjp
def reduced_precision(v):
    return lax.optimization_barrier(v.astype(jnp.bfloat16)).astype(jnp.float32)

@jax.custom_vjp
def reduced_backward(v):
    return v

def low_keep(v):
    return (reduced_precision(v), None)

def low_pass(kept, grad):
    return (grad,)

def back_keep(v):
    return (v, None)

def back_low(kept, grad):
    return (reduced_precision(grad),)
reduced_precision.defvjp(low_keep, low_pass)
reduced_backward.defvjp(back_keep, back_low)
EPSILON = 1e-05
BASE = 10000.0

def matmul(left_operand, right_operand):
    return jnp.einsum('vcx,xh->vch', left_operand, right_operand, precision=lax.Precision.HIGHEST)

def rms_norm(value_matrix, gain):
    inv_rms = lax.rsqrt(lax.optimization_barrier(jnp.mean(value_matrix * value_matrix, axis=-1, keepdims=True)) + EPSILON)
    return value_matrix * inv_rms * gain

def rope_tables(positions, half_dim):
    frequency = BASE ** (-jnp.arange(half_dim, dtype=jnp.float32) / half_dim)
    angles = positions.astype(jnp.float32)[:, None] * frequency[None, :]
    cosine = jnp.concatenate([jnp.cos(angles), jnp.cos(angles)], axis=-1)[:, None, :]
    sine_table = jnp.concatenate([jnp.sin(angles), jnp.sin(angles)], axis=-1)[:, None, :]
    return (cosine, sine_table)

def rotate(value_matrix, cosine, sine_table):
    half_dim = value_matrix.shape[-1] // 2
    turned = jnp.concatenate([-value_matrix[..., half_dim:], value_matrix[..., :half_dim]], axis=-1)
    return value_matrix * cosine + turned * sine_table

def attend(query_matrix, key_matrix, value_matrix, positions):
    length = query_matrix.shape[0]
    score_scale = HEAD ** (-0.5)
    q_rows = min(length, 512)
    count = length // q_rows
    query_blocks = query_matrix.reshape((count, q_rows) + query_matrix.shape[1:])
    pos_blocks = positions.reshape(count, q_rows)

    def one_block(inputs):
        block_of_queries, query_pos = inputs
        logit_scores = reduced_backward(jnp.einsum('kmcu,nmu->mckn', block_of_queries, key_matrix, precision=lax.Precision.HIGHEST) * score_scale)
        allowed = positions[None, :] <= query_pos[:, None]
        logit_scores = jnp.where(allowed[None, None], logit_scores, -1e+30)
        probabilities = jax.nn.softmax(logit_scores, axis=-1)
        return jnp.einsum('cxfz,zcq->fcxq', reduced_precision(probabilities), value_matrix, precision=lax.Precision.HIGHEST)
    outputs = lax.map(jax.checkpoint(one_block), (query_blocks, pos_blocks))
    return outputs.reshape(query_matrix.shape)

def layer_forward(tokens, attn_gain, w_query, w_key, w_value, w_out, mlp_gain, w_gate, w_up, w_down, positions):
    seq_count, length, model_width = tokens.shape
    group = HEADS // KV_HEADS
    normed_a = reduced_precision(rms_norm(tokens, attn_gain))
    query_pre = reduced_backward(matmul(normed_a, w_query))
    key_pre = reduced_backward(matmul(normed_a, w_key))
    value_matrix = reduced_backward(reduced_precision(matmul(normed_a, w_value)))
    cosine, sine_table = rope_tables(positions, HEAD // 2)
    query_matrix = reduced_precision(rotate(query_pre.reshape(seq_count, length, HEADS, HEAD), cosine, sine_table))
    query_matrix = query_matrix.reshape(seq_count, length, KV_HEADS, group, HEAD)
    key_matrix = reduced_precision(rotate(key_pre.reshape(seq_count, length, KV_HEADS, HEAD), cosine, sine_table))
    value_matrix = value_matrix.reshape(seq_count, length, KV_HEADS, HEAD)
    attention_output = jax.vmap(attend, in_axes=(0, 0, 0, None))(query_matrix, key_matrix, value_matrix, positions)
    attention_output = reduced_backward(reduced_precision(attention_output.reshape(seq_count, length, HEADS * HEAD)))
    middle = tokens + reduced_backward(matmul(attention_output, w_out))
    normed_b = reduced_precision(rms_norm(middle, mlp_gain))
    gate_pre = reduced_backward(matmul(normed_b, w_gate))
    up_pre = reduced_backward(matmul(normed_b, w_up))
    hidden = reduced_precision(jax.nn.silu(gate_pre) * up_pre)
    return middle + matmul(hidden, w_down)

def reference(tokens, cotangent, block_table, attn_gain, w_query, w_key, w_value, w_out, mlp_gain, w_gate, w_up, w_down):
    block_rows = TOK_DEV // 2
    offsets = jnp.arange(block_rows, dtype=jnp.int32)
    positions = (block_table.reshape(-1)[:, None].astype(jnp.int32) * block_rows + offsets[None, :]).reshape(LEN)
    floats = tuple((array.astype(jnp.float32) for array in (tokens, attn_gain, w_query, w_key, w_value, w_out, mlp_gain, w_gate, w_up, w_down)))

    def forward(*params):
        return layer_forward(*params, positions)
    output, pullback = jax.vjp(forward, *floats)
    grads = pullback(cotangent.astype(jnp.float32))
    return (output.astype(jnp.bfloat16), grads[0], grads[1], grads[2], grads[3], grads[4], grads[5], grads[6], grads[7], grads[8], grads[9])
```

```python
import functools
import math

import jax
import jax.numpy as jnp
from jax import lax
from jax.experimental import pallas as pl
from jax.experimental.pallas import tpu as pltpu
from jax.sharding import PartitionSpec as P

D = 960
HEADS = 15
KV_HEADS = 5
GROUP = 3
HEAD = 64
FF = 2560
TOK = 128
HALF = 64
CTX = 32
TILES = 33
KEYS = TILES * 128
SCALE = HEAD ** (-0.5)
EPSILON = 1e-05
BASE = 10000.0
LOG2E = math.log2(math.e)
NEG = -1e30
MESH = pl.DeviceIdType.MESH
ANY = pl.BlockSpec(memory_space=pl.ANY)
VM = pl.BlockSpec(memory_space=pltpu.VMEM)
BIG = 56 * 2**20
F32 = jnp.float32
BF16 = jnp.bfloat16


def here():
    ctx = lax.axis_index("ctx")
    shard = lax.axis_index("fsdp")
    return {
        "z": ctx // 8,
        "yh": (ctx // 4) % 2,
        "x": ctx % 4,
        "yl": shard // 2,
        "c": shard % 2,
    }


def device(place, **moved):
    p = {**place, **moved}
    return (p["z"] * 8 + p["yh"] * 4 + p["x"], p["yl"] * 2 + p["c"])


def greet(devices):
    sem = pltpu.get_barrier_semaphore()
    for d in devices:
        pl.semaphore_signal(sem, inc=1, device_id=d, device_id_type=MESH)
    pl.semaphore_wait(sem, len(devices))


class Sems:
    def __init__(self, send, recv):
        self.send, self.recv, self.at = send, recv, 0

    def push(self, src, dst, dev):
        copy = pltpu.make_async_remote_copy(
            src_ref=src,
            dst_ref=dst,
            send_sem=self.send.at[self.at],
            recv_sem=self.recv.at[self.at],
            device_id=dev,
            device_id_type=MESH,
        )
        self.at += 1
        copy.start()
        return copy


def gather_kernel(count, *refs):
    ins, outs = refs[:count], refs[count : 2 * count]
    send, recv, local = refs[2 * count :]
    me = here()
    f = me["yl"] * 2 + me["c"]
    near = device(me, yl=1 - me["yl"])
    far = device(me, yl=1 - me["yl"], yh=1 - me["yh"])
    mate = device(me, c=1 - me["c"])
    across = (1 - me["yl"]) * 2 + me["c"]
    greet((near, far, mate))
    sems = Sems(send, recv)
    parts, kept, own = [], [], []
    for i, (a, b) in enumerate(zip(ins, outs)):
        rows = a.shape[0]
        first = rows // 32 * 16 if i % 2 else (rows + 31) // 32 * 16
        first = max(first, 0)
        spans = [(0, first, near), (first, rows - first, far)]
        for lo, size, dev in spans:
            if size:
                src = a.at[pl.ds(lo, size)]
                dst = b.at[pl.ds(pl.multiple_of(f * rows + lo, 16), size)]
                parts.append((sems.push(src, dst, dev), b, rows, lo, size))
    for i, (a, b) in enumerate(zip(ins, outs)):
        rows = a.shape[0]
        dst = b.at[pl.ds(pl.multiple_of(f * rows, 16), rows)]
        kept.append(sems.push(a, dst, mate))
        copy = pltpu.make_async_copy(a, dst, local.at[i])
        copy.start()
        own.append(copy)
    for copy, b, rows, lo, size in parts:
        copy.wait_recv()
        span = b.at[pl.ds(pl.multiple_of(across * rows + lo, 16), size)]
        kept.append(sems.push(span, span, mate))
    for copy in own:
        copy.wait()
    for copy in kept:
        copy.wait()
    for copy, *_ in parts:
        copy.wait_send()


def gather_weights(arrays, collective_id):
    n = len(arrays)
    copies = 5 * n
    return pl.pallas_call(
        functools.partial(gather_kernel, n),
        out_shape=[jax.ShapeDtypeStruct((4 * a.shape[0], *a.shape[1:]), a.dtype) for a in arrays],
        in_specs=[ANY] * n,
        out_specs=[ANY] * n,
        scratch_shapes=[
            pltpu.SemaphoreType.DMA((copies,)),
            pltpu.SemaphoreType.DMA((copies,)),
            pltpu.SemaphoreType.DMA((n,)),
        ],
        compiler_params=pltpu.CompilerParams(collective_id=collective_id, has_side_effects=True),
        name="gather_weights",
    )(*arrays)


def around(me, axis):
    return [(d, lax.rem(me[axis] + d, 4)) for d in (1, 3, 2)]


def kv_gather_kernel(kv, out, send, recv, local):
    me = here()
    x, yh, z = me["x"], me["yh"], me["z"]
    other = device(me, yh=1 - yh)
    xs = [(at, device(me, x=at)) for _, at in around(me, "x")]
    zs = [(at, device(me, z=at)) for _, at in around(me, "z")]
    greet([other] + [d for _, d in xs] + [d for _, d in zs])
    sems = Sems(send, recv)
    key, value = pl.ds(0, 320), pl.ds(320, 320)
    mine = pltpu.make_async_copy(kv, out.at[z, yh, x], local.at[0])
    mine.start()
    done = []
    step1 = [sems.push(kv.at[p], out.at[z, yh, x, p], other) for p in (key, value)]
    step2 = {(0, 0): [], (0, 1): [], (1, 0): [], (1, 1): []}
    for _, dev in xs:
        step2[0, 0].append(sems.push(kv.at[key], out.at[z, yh, x, key], dev))
    for _, dev in zs:
        step2[1, 0].append(sems.push(kv.at[value], out.at[z, yh, x, value], dev))
    for axis, (devs, p) in enumerate(((xs, key), (zs, value))):
        step1[axis].wait_recv()
        span = out.at[z, 1 - yh, x, p]
        for _, dev in devs:
            step2[axis, 1].append(sems.push(span, span, dev))
    mine.wait()
    step3 = []
    for hop in (0, 1):
        row = yh if hop == 0 else 1 - yh
        for c in step2[0, hop]:
            c.wait_recv()
        span = out.at[z, row, :, key]
        for _, dev in zs:
            step3.append(sems.push(span, span, dev))
        for c in step2[1, hop]:
            c.wait_recv()
        span = out.at[:, row, x, value]
        for _, dev in xs:
            step3.append(sems.push(span, span, dev))
    for c in step3:
        c.wait_recv()
    for c in step1 + sum(step2.values(), []) + step3:
        c.wait_send()


def gather_kv(kv, collective_id):
    return pl.pallas_call(
        kv_gather_kernel,
        out_shape=jax.ShapeDtypeStruct((4, 2, 4, 640, 128), BF16),
        in_specs=[ANY],
        out_specs=ANY,
        scratch_shapes=[
            pltpu.SemaphoreType.DMA((26,)),
            pltpu.SemaphoreType.DMA((26,)),
            pltpu.SemaphoreType.DMA((1,)),
        ],
        compiler_params=pltpu.CompilerParams(collective_id=collective_id, has_side_effects=True),
        name="gather_kv",
    )(kv).reshape(CTX, 640, 128)


def kv_scatter_kernel(part, out, r1a, r1b, s1a, s1b, r2a, r2b, s2, r3, send, recv):
    me = here()
    x, yh, z = me["x"], me["yh"], me["z"]
    other = device(me, yh=1 - yh)
    xs = [(d, at, device(me, x=at)) for d, at in around(me, "x")]
    zs = [(d, at, device(me, z=at)) for d, at in around(me, "z")]
    greet([other] + [d for *_, d in xs] + [d for *_, d in zs])
    sems = Sems(send, recv)
    key, value = pl.ds(0, 320), pl.ds(320, 320)
    rows = (1 - yh, yh)
    first = {}
    for row in (0, 1):
        for d, at, dev in zs:
            first[0, row, d] = sems.push(part.at[at, rows[row], :, key], r1a.at[d - 1, row], dev)
        for d, at, dev in xs:
            first[1, row, d] = sems.push(part.at[:, rows[row], at, value], r1b.at[d - 1, row], dev)
    second = {}
    for row in (0, 1):
        for axis, (r1, s1) in enumerate(((r1a, s1a), (r1b, s1b))):
            for d in (1, 2, 3):
                first[axis, row, d].wait_recv()
            for i in range(4):
                own = part[z, rows[row], i, 0:320] if axis == 0 else part[i, rows[row], x, 320:640]
                total = own.astype(F32)
                for d in (0, 1, 2):
                    total = total + r1[d, row, i].astype(F32)
                s1[row, i] = total.astype(BF16)
            ring, r2 = ((xs, r2a), (zs, r2b))[axis]
            for d, at, dev in ring:
                second[axis, row, d] = sems.push(s1.at[row, at], r2.at[d - 1, row], dev)
    third = []
    for row in (0, 1):
        for axis, (s1, r2) in enumerate(((s1a, r2a), (s1b, r2b))):
            at = x if axis == 0 else z
            for d in (1, 2, 3):
                second[axis, row, d].wait_recv()
            total = s1[row, at].astype(F32)
            for d in (0, 1, 2):
                total = total + r2[d, row].astype(F32)
            if row == 0:
                s2[axis] = total.astype(BF16)
                third.append(sems.push(s2.at[axis], r3.at[axis], other))
            else:
                out[pl.ds(axis * 320, 320), :] = total
    for axis in (0, 1):
        third[axis].wait_recv()
        span = pl.ds(axis * 320, 320)
        out[span, :] = out[span, :] + r3[axis].astype(F32)
    for c in list(first.values()) + list(second.values()) + third:
        c.wait_send()


def scatter_kv(part, collective_id):
    return pl.pallas_call(
        kv_scatter_kernel,
        out_shape=jax.ShapeDtypeStruct((640, 128), F32),
        in_specs=[VM],
        out_specs=VM,
        scratch_shapes=[
            pltpu.VMEM((3, 2, 4, 320, 128), BF16),
            pltpu.VMEM((3, 2, 4, 320, 128), BF16),
            pltpu.VMEM((2, 4, 320, 128), BF16),
            pltpu.VMEM((2, 4, 320, 128), BF16),
            pltpu.VMEM((3, 2, 320, 128), BF16),
            pltpu.VMEM((3, 2, 320, 128), BF16),
            pltpu.VMEM((2, 320, 128), BF16),
            pltpu.VMEM((2, 320, 128), BF16),
            pltpu.SemaphoreType.DMA((26,)),
            pltpu.SemaphoreType.DMA((26,)),
        ],
        compiler_params=pltpu.CompilerParams(
            collective_id=collective_id, has_side_effects=True, vmem_limit_bytes=BIG
        ),
        name="scatter_kv",
    )(part.reshape(4, 2, 4, 640, 128))


def tile_plan(block_table, ctx):
    early = jnp.min(block_table.reshape(CTX, 2), axis=1)
    mine = lax.dynamic_index_in_dim(early, ctx, keepdims=False)
    late_turn = (early >= mine)[:, None]
    offset = jnp.arange(HALF, dtype=jnp.int32)[None, :]
    m = jnp.broadcast_to(late_turn.astype(F32), (CTX, HALF))
    one, zero = jnp.ones_like(m), jnp.zeros_like(m)

    def rows(a, b, last):
        return jnp.concatenate([jnp.concatenate([a, b], axis=1), last], axis=0)

    blank = jnp.zeros((1, 128), F32)
    flags = rows(one, m, blank)
    left = rows(m, 1.0 - m, blank)
    right = rows(1.0 - m, zero, blank)
    t_first = (early[:, None] - (63 - mine)) * HALF + offset
    t_second = jnp.where(late_turn, mine - early[:, None], early[:, None] - mine) * HALF + offset
    t_last = jnp.concatenate([offset, jnp.full((1, HALF), 10**6, jnp.int32)], axis=1)
    limits = rows(t_first.astype(F32), t_second.astype(F32), t_last.astype(F32))
    return flags, left, right, limits


def build_tiles(head, kv_ref, own_ref, left_ref, tiles_ref, base):
    lane = lax.broadcasted_iota(jnp.int32, (HALF, 128), 1)
    start = pl.multiple_of(base + head * HALF, HALF)

    def one(i, _):
        block = kv_ref[i, pl.ds(start, HALF), :].astype(F32)
        top = jnp.where(lane < HALF, block, 0.0)
        low = pltpu.roll(block, HALF, 1) * left_ref[pl.ds(i, 1), :]
        at = pl.multiple_of(i * 128, 128)
        tiles_ref[pl.ds(at, 128), :] = jnp.concatenate([top, low], axis=0).astype(BF16)
        return 0

    lax.fori_loop(0, CTX, one, 0, unroll=4)
    block = own_ref[pl.ds(start, HALF), :].astype(F32)
    top = jnp.where(lane < HALF, 0.0, pltpu.roll(block, HALF, 1))
    tiles_ref[pl.ds(CTX * 128, 128), :] = jnp.concatenate(
        [top, jnp.zeros_like(top)], axis=0
    ).astype(BF16)


def dot_nt(a, b):
    return lax.dot_general(a, b, (((1,), (1,)), ((), ())), preferred_element_type=F32)


def dot_nn(a, b):
    return lax.dot_general(a, b, (((1,), (0,)), ((), ())), preferred_element_type=F32)


ROWS = GROUP * HALF
STEP = 3


def row_offset():
    return lax.rem(lax.broadcasted_iota(jnp.int32, (ROWS, 128), 0), HALF).astype(F32)


def attend_kernel(q_ref, kv_ref, own_ref, flag_ref, left_ref, limit_ref, o_ref, l_ref, kk, vv, s_ref):
    head = pl.program_id(0)
    build_tiles(head, kv_ref, own_ref, left_ref, kk, 0)
    build_tiles(head, kv_ref, own_ref, left_ref, vv, 320)
    q = q_ref[0]
    offset = row_offset()
    low = jnp.full((ROWS, 128), NEG, F32)

    def scores(j, carry):
        top_l, top_e = carry
        at = pl.multiple_of(j * STEP * 128, 128)
        s = dot_nt(q, kk[pl.ds(at, STEP * 128), :]) * (SCALE * LOG2E)
        for t in range(STEP):
            i = j * STEP + t
            tile = s[:, t * 128 : (t + 1) * 128]
            tile = jnp.where(limit_ref[pl.ds(i, 1), :] <= offset, tile, NEG)
            late = flag_ref[pl.ds(i, 1), :] > 0.5
            top_l = jnp.maximum(top_l, jnp.where(late, tile, NEG))
            top_e = jnp.maximum(top_e, jnp.where(late, NEG, tile))
            s_ref[:, pl.ds(pl.multiple_of(at + t * 128, 128), 128)] = tile
        return top_l, top_e

    top_l, top_e = lax.fori_loop(0, TILES // STEP, scores, (low, low))
    max_l = jnp.broadcast_to(jnp.max(top_l, axis=1, keepdims=True), (ROWS, 128))
    max_e = jnp.broadcast_to(jnp.max(top_e, axis=1, keepdims=True), (ROWS, 128))
    zero = jnp.zeros((ROWS, 128), F32)

    def values(j, carry):
        sum_l, sum_e, total = carry
        at = pl.multiple_of(j * STEP * 128, 128)
        probs = []
        for t in range(STEP):
            i = j * STEP + t
            tile = s_ref[:, pl.ds(pl.multiple_of(at + t * 128, 128), 128)]
            late = flag_ref[pl.ds(i, 1), :] > 0.5
            p = jnp.exp2(tile - jnp.where(late, max_l, max_e))
            p_l = jnp.where(late, p, 0.0)
            sum_l = sum_l + p_l
            sum_e = sum_e + (p - p_l)
            probs.append(p.astype(BF16))
        total = total + dot_nn(jnp.concatenate(probs, axis=1), vv[pl.ds(at, STEP * 128), :])
        return sum_l, sum_e, total

    sum_l, sum_e, total = lax.fori_loop(0, TILES // STEP, values, (zero, zero, zero))
    late = lax.broadcasted_iota(jnp.int32, (ROWS, 128), 1) < HALF
    row_sum = jnp.where(
        late, jnp.sum(sum_l, axis=1, keepdims=True), jnp.sum(sum_e, axis=1, keepdims=True)
    )
    o_ref[0] = total / row_sum
    l_ref[0] = jnp.where(late, max_l, max_e) + jnp.log2(row_sum)


def head_spec(*shape):
    return pl.BlockSpec((1, *shape), lambda h: (h, 0, 0))


def whole_spec(*shape):
    return pl.BlockSpec(shape, lambda h: (0,) * len(shape))


def attend(q, kv, own, plan):
    flags, left, _, limits = plan
    return pl.pallas_call(
        attend_kernel,
        grid=(KV_HEADS,),
        out_shape=[jax.ShapeDtypeStruct((KV_HEADS, ROWS, 128), F32)] * 2,
        in_specs=[
            head_spec(ROWS, 128),
            whole_spec(CTX, 640, 128),
            whole_spec(640, 128),
            whole_spec(TILES, 128),
            whole_spec(TILES, 128),
            whole_spec(TILES, 128),
        ],
        out_specs=[head_spec(ROWS, 128)] * 2,
        scratch_shapes=[
            pltpu.VMEM((KEYS, 128), BF16),
            pltpu.VMEM((KEYS, 128), BF16),
            pltpu.VMEM((ROWS, KEYS), F32),
        ],
        compiler_params=pltpu.CompilerParams(vmem_limit_bytes=BIG),
        name="attend",
    )(q, kv, own, flags, left, limits)


def attend_back_kernel(
    q_ref, qt_ref, do_ref, dot_ref, o_ref, l_ref, kv_ref, own_ref, flag_ref, left_ref, right_ref,
    limit_ref, dq_ref, dkv_ref, kk, vv,
):
    head = pl.program_id(0)
    build_tiles(head, kv_ref, own_ref, left_ref, kk, 0)
    build_tiles(head, kv_ref, own_ref, left_ref, vv, 320)
    q, qt, do, dot = q_ref[0], qt_ref[0], do_ref[0], dot_ref[0]
    offset = row_offset()
    lane = lax.broadcasted_iota(jnp.int32, (ROWS, 128), 1)
    product = do.astype(F32) * o_ref[0]
    shape = (ROWS, 128)
    delta_l = jnp.broadcast_to(
        jnp.sum(jnp.where(lane < HALF, product, 0.0), axis=1, keepdims=True), shape
    )
    delta_e = jnp.broadcast_to(
        jnp.sum(jnp.where(lane < HALF, 0.0, product), axis=1, keepdims=True), shape
    )
    log_l = jnp.broadcast_to(l_ref[0][:, 0:1], shape)
    log_e = jnp.broadcast_to(l_ref[0][:, HALF : HALF + 1], shape)
    k_rows = pl.ds(pl.multiple_of(head * HALF, HALF), HALF)
    v_rows = pl.ds(pl.multiple_of(320 + head * HALF, HALF), HALF)
    small = lax.broadcasted_iota(jnp.int32, (HALF, 128), 1)

    def grads(j, total):
        at = pl.multiple_of(j * STEP * 128, 128)
        keys = kk[pl.ds(at, STEP * 128), :]
        s = dot_nt(q, keys) * (SCALE * LOG2E)
        dp = dot_nt(do, vv[pl.ds(at, STEP * 128), :])
        probs, scores = [], []
        for t in range(STEP):
            i = j * STEP + t
            cut = slice(t * 128, (t + 1) * 128)
            late = flag_ref[pl.ds(i, 1), :] > 0.5
            tile = jnp.where(limit_ref[pl.ds(i, 1), :] <= offset, s[:, cut], NEG)
            p = jnp.exp2(tile - jnp.where(late, log_l, log_e))
            probs.append(p.astype(BF16))
            scores.append((p * (dp[:, cut] - jnp.where(late, delta_l, delta_e))).astype(BF16))
        ds = jnp.concatenate(scores, axis=1)
        total = total + dot_nn(ds, keys)
        dk = dot_nn(qt, ds) * SCALE
        dv = dot_nn(dot, jnp.concatenate(probs, axis=1))
        for t in range(STEP):
            i = j * STEP + t
            cut = slice(t * 128, (t + 1) * 128)
            for rows, both in ((k_rows, dk), (v_rows, dv)):
                top, bottom = both[0:HALF, cut], both[HALF:128, cut]

                @pl.when(i < CTX)
                def _():
                    dkv_ref[i, rows, :] = (
                        top * flag_ref[pl.ds(i, 1), :]
                        + pltpu.roll(bottom, HALF, 1) * right_ref[pl.ds(i, 1), :]
                    ).astype(BF16)

                @pl.when(i == CTX)
                def _():
                    mine = lax.axis_index("ctx")
                    before = dkv_ref[mine, rows, :].astype(F32)
                    dkv_ref[mine, rows, :] = (
                        before + jnp.where(small < HALF, bottom, 0.0)
                    ).astype(BF16)

        return total

    total = lax.fori_loop(0, TILES // STEP, grads, jnp.zeros(shape, F32))
    dq_ref[0] = total * SCALE


def attend_back(q, do, o, logs, kv, own, plan):
    flags, left, right, limits = plan
    return pl.pallas_call(
        attend_back_kernel,
        grid=(KV_HEADS,),
        out_shape=[
            jax.ShapeDtypeStruct((KV_HEADS, ROWS, 128), F32),
            jax.ShapeDtypeStruct((CTX, 640, 128), BF16),
        ],
        in_specs=[
            head_spec(ROWS, 128),
            head_spec(128, ROWS),
            head_spec(ROWS, 128),
            head_spec(128, ROWS),
            head_spec(ROWS, 128),
            head_spec(ROWS, 128),
            whole_spec(CTX, 640, 128),
            whole_spec(640, 128),
            whole_spec(TILES, 128),
            whole_spec(TILES, 128),
            whole_spec(TILES, 128),
            whole_spec(TILES, 128),
        ],
        out_specs=[head_spec(ROWS, 128), whole_spec(CTX, 640, 128)],
        scratch_shapes=[pltpu.VMEM((KEYS, 128), BF16), pltpu.VMEM((KEYS, 128), BF16)],
        compiler_params=pltpu.CompilerParams(vmem_limit_bytes=BIG),
        name="attend_back",
    )(
        q, jnp.swapaxes(q, 1, 2), do, jnp.swapaxes(do, 1, 2), o, logs, kv, own,
        flags, left, right, limits,
    )


def to_rows(a):
    a = a.reshape(2, HALF, KV_HEADS, GROUP, HEAD)[::-1]
    return a.transpose(2, 3, 1, 0, 4).reshape(KV_HEADS, ROWS, 128)


def from_rows(a):
    a = a.reshape(KV_HEADS, GROUP, HALF, 2, HEAD).transpose(3, 2, 0, 1, 4)[::-1]
    return a.reshape(TOK, HEADS * HEAD)


def to_wire(a):
    return a.reshape(2, HALF, KV_HEADS, HEAD).transpose(2, 1, 0, 3).reshape(KV_HEADS * HALF, 128)


def reduce_kernel(jobs, used, pa, pb, extra, *refs):
    refs = list(refs)
    sources = []
    for shared_left, _, shared_right, _ in jobs:
        left = [refs.pop(0) for _ in range(1 if shared_left else 2)]
        right = [refs.pop(0) for _ in range(1 if shared_right else 2)]
        sources.append((left[0], left[-1], right[0], right[-1]))
    if extra:
        extra_refs = (refs.pop(0), refs.pop(0))
    out = refs.pop(0)
    buffers = [(refs.pop(0), refs.pop(0)) for _ in jobs]
    if extra:
        extra_buffer = refs.pop(0)
    grads = refs.pop(0)
    parts = [[refs.pop(0) for _ in range(6)] for _ in range(2)]
    send, recv, local = refs

    me = here()
    x, yh, z, yl = me["x"], me["yh"], me["z"], me["yl"]
    mate = device(me, c=1 - me["c"])
    xs = [(d, at, device(me, x=at)) for d, at in around(me, "x")]
    zs = [(d, at, device(me, z=at)) for d, at in around(me, "z")]
    near = device(me, yl=1 - yl)
    far = device(me, yl=1 - yl, yh=1 - yh)
    same = device(me, yh=1 - yh)
    greet([mate, near, far, same] + [d for *_, d in xs] + [d for *_, d in zs])
    sems = Sems(send, recv)

    mine, traded = [], []
    for (lm, lt, rm, rt), (lb, rb) in zip(sources, buffers):
        traded.append(sems.push(lt, lb.at[:, :, pl.ds(128, 128)], mate))
        traded.append(sems.push(rt, rb.at[:, pl.ds(128, 128)], mate))
        for src, dst in ((lm, lb.at[:, :, pl.ds(0, 128)]), (rm, rb.at[:, pl.ds(0, 128)])):
            copy = pltpu.make_async_copy(src, dst, local.at[len(mine)])
            copy.start()
            mine.append(copy)
    if extra:
        traded.append(sems.push(extra_refs[1], extra_buffer.at[1], mate))
        copy = pltpu.make_async_copy(extra_refs[0], extra_buffer.at[0], local.at[len(mine)])
        copy.start()
        mine.append(copy)
    for copy in mine:
        copy.wait()
    for copy in traded:
        copy.wait_recv()

    base = 0
    for (_, m, _, n), (lb, rb) in zip(jobs, buffers):
        width = 256 if n % 256 == 0 else 128
        for s in range(2):
            left = lb[min(s, lb.shape[0] - 1)]

            def block(i, _, left=left, rb=rb, s=s, m=m, width=width, base=base):
                at = pl.multiple_of(i * width, 128)
                right = rb[min(s, rb.shape[0] - 1), :, pl.ds(at, width)]
                result = dot_nn(left, right).astype(BF16)
                for w in range(width // 128):
                    to = pl.multiple_of(base + (i * (width // 128) + w) * m, 16)
                    grads[s, pl.ds(to, m), :] = result[:, w * 128 : (w + 1) * 128]
                return 0

            lax.fori_loop(0, n // width, block, 0)
        base += m * (n // 128)
    if extra:
        for s in range(2):
            both = extra_buffer[0, s].astype(F32) + extra_buffer[1, s].astype(F32)
            grads[s, pl.ds(base, 16), :] = both.astype(BF16)
        base += 16
    if base < used:
        for s in range(2):
            grads[s, pl.ds(base, used - base), :] = jnp.zeros((used - base, 128), BF16)

    plans = (
        (0, pa, xs, zs, x, z, parts[0]),
        (16 * pa, pb, zs, xs, z, x, parts[1]),
    )
    order = (1, 3, 2, 0)
    first, second = {}, {}
    sent = []
    for k in order:
        for n, (lo, size, ring, cross, i_me, j_me, _) in enumerate(plans):
            r1 = parts[n][0]
            j = lax.rem(j_me + k, 4)
            for d, at, dev in ring:
                src = grads.at[:, pl.ds(pl.multiple_of(lo + (at * 4 + j) * size, 16), size)]
                first[n, k, d] = sems.push(src, r1.at[d - 1, k], dev)
    for k in order:
        for n, (lo, size, ring, cross, i_me, j_me, (r1, s1, r2, s2, r3, fin)) in enumerate(plans):
            j = lax.rem(j_me + k, 4)
            for d in (1, 2, 3):
                first[n, k, d].wait_recv()
            for s in range(2):
                own = grads[s, pl.ds(pl.multiple_of(lo + (i_me * 4 + j) * size, 16), size)]
                total = own.astype(F32)
                for d in (0, 1, 2):
                    total = total + r1[d, k, s].astype(F32)
                s1[k, s] = total.astype(BF16)
            if k:
                dev = [dev for d, _, dev in cross if d == k][0]
                second[n, k] = sems.push(s1.at[k], r2.at[k - 1], dev)
    third = {}
    for n, (lo, size, ring, cross, i_me, j_me, (r1, s1, r2, s2, r3, fin)) in enumerate(plans):
        for k in (1, 2, 3):
            second[n, k].wait_recv()
        for s in range(2):
            total = s1[0, s].astype(F32)
            for d in (0, 1, 2):
                total = total + r2[d, s].astype(F32)
            s2[s] = total.astype(BF16)
        slot = r3.at[yl * 2 + yh]
        third[n, 0] = sems.push(s2.at[1 - yl], slot, near)
        third[n, 1] = sems.push(s2.at[1 - yl], slot, far)
        third[n, 2] = sems.push(s2.at[yl], slot, same)
    fourth, fifth = {}, {}
    for n, (lo, size, ring, cross, i_me, j_me, (r1, s1, r2, s2, r3, fin)) in enumerate(plans):
        r3[yl * 2 + yh] = s2[yl]
        for i in (0, 1, 2):
            third[n, i].wait_recv()
        total = r3[0].astype(F32)
        for i in (1, 2, 3):
            total = total + r3[i].astype(F32)
        fin[...] = total.astype(BF16)
        span = out.at[pl.ds(pl.multiple_of(lo + (i_me * 4 + j_me) * size, 16), size)]
        copy = pltpu.make_async_copy(fin, span, local.at[n])
        copy.start()
        fourth[n, "own"] = copy
        for d, _, dev in cross:
            fourth[n, d] = sems.push(fin, span, dev)
        for d, _, dev in ring:
            fifth[n, 0, d] = sems.push(fin, span, dev)
    for back in (3, 1, 2):
        for n, (lo, size, ring, cross, i_me, j_me, _) in enumerate(plans):
            fourth[n, back].wait_recv()
            j = lax.rem(j_me + 4 - back, 4)
            span = out.at[pl.ds(pl.multiple_of(lo + (i_me * 4 + j) * size, 16), size)]
            for d, _, dev in ring:
                fifth[n, back, d] = sems.push(span, span, dev)
    for copy in fifth.values():
        copy.wait_recv()
    for n in (0, 1):
        fourth.pop((n, "own")).wait()
    for group in (traded, first.values(), second.values(), third.values()):
        for copy in group:
            copy.wait_send()
    for group in (fourth.values(), fifth.values()):
        for copy in group:
            copy.wait_send()


def reduce_grads(jobs, extra, collective_id):
    operands, shapes, buffers, rows = [], [], [], 0
    for left, right in jobs:
        shared_left, shared_right = not isinstance(left, tuple), not isinstance(right, tuple)
        lefts = [left] if shared_left else list(left)
        rights = [right] if shared_right else list(right)
        operands += lefts + rights
        m, n = lefts[0].shape[1], rights[0].shape[2]
        shapes.append((shared_left, m, shared_right, n))
        buffers.append(pltpu.VMEM((lefts[0].shape[0], m, 256), BF16))
        buffers.append(pltpu.VMEM((rights[0].shape[0], 256, n), BF16))
        rows += m * (n // 128)
    if extra is not None:
        operands += list(extra)
        buffers.append(pltpu.VMEM((2, 2, 16, 128), BF16))
        rows += 16
    pieces = -(-rows // 256)
    pa, pb = (pieces + 1) // 2 * 16, pieces // 2 * 16
    used = 16 * (pa + pb)
    scratch = buffers + [pltpu.VMEM((2, used, 128), BF16)]
    for size in (pa, pb):
        scratch += [
            pltpu.VMEM((3, 4, 2, size, 128), BF16),
            pltpu.VMEM((4, 2, size, 128), BF16),
            pltpu.VMEM((3, 2, size, 128), BF16),
            pltpu.VMEM((2, size, 128), BF16),
            pltpu.VMEM((4, size, 128), BF16),
            pltpu.VMEM((size, 128), BF16),
        ]
    copies = 2 * len(jobs) + 1 + 24 + 6 + 6 + 6 + 24
    scratch += [
        pltpu.SemaphoreType.DMA((copies,)),
        pltpu.SemaphoreType.DMA((copies,)),
        pltpu.SemaphoreType.DMA((2 * len(jobs) + 1,)),
    ]
    return pl.pallas_call(
        functools.partial(reduce_kernel, tuple(shapes), used, pa, pb, extra is not None),
        out_shape=jax.ShapeDtypeStruct((used, 128), BF16),
        in_specs=[ANY] * len(operands),
        out_specs=ANY,
        scratch_shapes=scratch,
        compiler_params=pltpu.CompilerParams(
            collective_id=collective_id, has_side_effects=True, vmem_limit_bytes=BIG
        ),
        name="reduce_grads",
    )(*operands)


def pick(a, axis, core):
    return lax.dynamic_index_in_dim(a, core, axis, keepdims=False)


def left_shards(a, core):
    t = a.T.reshape(2, 2, 240, TOK)
    return pick(t, 1, core), pick(t, 1, 1 - core)


def right_shards(a, core):
    t = a.reshape(TOK, 2, 2, a.shape[1] // 4).transpose(1, 2, 0, 3)
    return pick(t, 1, core), pick(t, 1, 1 - core)


def pad_lanes(a):
    extra = -a.shape[1] % 128
    return jnp.pad(a, ((0, 0), (0, extra)))


def unblock(flat, m, columns):
    blocks = -(-columns // 128)
    a = flat[: m * blocks].reshape(blocks, m, 128).transpose(1, 0, 2).reshape(m, blocks * 128)
    return a[:, :columns].astype(F32), flat[m * blocks :]


def norm_forward(values, gain):
    inv_rms = lax.rsqrt(jnp.mean(values * values, axis=-1, keepdims=True) + EPSILON)
    return values * inv_rms * gain, inv_rms


def norm_backward(values, inv_rms, gain, grad_normed):
    scaled = grad_normed * gain
    grad_values = inv_rms * scaled - values * inv_rms * inv_rms * inv_rms * jnp.mean(
        scaled * values, axis=-1, keepdims=True
    )
    grad_gain = jnp.sum(grad_normed * values * inv_rms, axis=0)
    return grad_values, grad_gain


def rope_tables(positions, half_dim):
    frequency = BASE ** (-jnp.arange(half_dim, dtype=F32) / half_dim)
    angles = positions.astype(F32)[:, None] * frequency[None, :]
    cosine = jnp.concatenate([jnp.cos(angles), jnp.cos(angles)], axis=-1)[:, None, :]
    sine = jnp.concatenate([jnp.sin(angles), jnp.sin(angles)], axis=-1)[:, None, :]
    return cosine, sine


def rotate(values, cosine, sine):
    half_dim = values.shape[-1] // 2
    turned = jnp.concatenate([-values[..., half_dim:], values[..., :half_dim]], axis=-1)
    return values * cosine + turned * sine


def dot(a, b):
    return jnp.dot(a, b, preferred_element_type=F32)


def swap_rows(a, swap):
    return jnp.where(swap, jnp.concatenate([a[HALF:], a[:HALF]], axis=0), a)


def on_device(
    tokens, cotangent, block_table, attn_gain, w_query, w_key, w_value, w_out, mlp_gain,
    w_gate, w_up, w_down,
):
    ctx = lax.axis_index("ctx")
    core = lax.axis_index("fsdp") % 2
    gains = jnp.pad(jnp.stack([attn_gain, mlp_gain]), ((0, 14), (0, 16)))
    qkv_shard = jnp.concatenate([w_query, w_key, w_value], axis=1)
    gains_all, qkv_w, out_w, gate_w, up_w, down_w = gather_weights(
        (gains, qkv_shard, w_out, w_gate, w_up, w_down), 0
    )
    gains_all = gains_all.reshape(4, 16, 256)[:, :2, :240].astype(F32)
    gain_a = gains_all[:, 0].reshape(D)
    gain_b = gains_all[:, 1].reshape(D)

    own_blocks = lax.dynamic_slice_in_dim(block_table, 2 * ctx, 2)
    swap = own_blocks[0] > own_blocks[1]
    early = jnp.min(own_blocks)
    offsets = jnp.arange(HALF, dtype=jnp.int32)
    positions = jnp.concatenate([early * HALF + offsets, (63 - early) * HALF + offsets])
    cosine, sine = rope_tables(positions, HEAD // 2)
    plan = tile_plan(block_table, ctx)

    resid_in = swap_rows(tokens[0], swap).astype(F32)
    grad_low = swap_rows(cotangent[0], swap)
    normed_a, inv_a = norm_forward(resid_in, gain_a)
    normed_a_low = normed_a.astype(BF16)
    qkv = dot(normed_a_low, qkv_w)
    value_low = qkv[:, 1280:].astype(BF16)
    queries = rotate(qkv[:, :960].reshape(TOK, HEADS, HEAD), cosine, sine).astype(BF16)
    keys = rotate(qkv[:, 960:1280].reshape(TOK, KV_HEADS, HEAD), cosine, sine).astype(BF16)
    q_rows = to_rows(queries)
    own_kv = jnp.concatenate([to_wire(keys), to_wire(value_low)], axis=0)
    kv = gather_kv(own_kv, 1)
    o_rows, logs = attend(q_rows, kv, own_kv, plan)
    attended_low = from_rows(o_rows).astype(BF16)

    middle = resid_in + dot(attended_low, out_w)
    normed_b, inv_b = norm_forward(middle, gain_b)
    normed_b_low = normed_b.astype(BF16)
    gate_pre = dot(normed_b_low, gate_w)
    up_pre = dot(normed_b_low, up_w)
    sigmoid_gate = jax.nn.sigmoid(gate_pre)
    silu_gate = gate_pre * sigmoid_gate
    hidden_low = (silu_gate * up_pre).astype(BF16)
    layer_out = middle + dot(hidden_low, down_w)

    grad_hidden = dot_nt(grad_low, down_w)
    grad_gate_pre = (
        grad_hidden * up_pre * sigmoid_gate * (1.0 + gate_pre * (1.0 - sigmoid_gate))
    ).astype(BF16)
    grad_up_pre = (grad_hidden * silu_gate).astype(BF16)
    grad_norm_b = dot_nt(grad_gate_pre, gate_w) + dot_nt(grad_up_pre, up_w)
    grad_mid_norm, grad_gain_b = norm_backward(middle, inv_b, gain_b, grad_norm_b)
    grad_middle = grad_low.astype(F32) + grad_mid_norm
    grad_branch = grad_middle.astype(BF16)
    do_rows = to_rows(dot_nt(grad_branch, out_w).astype(BF16))

    flat = reduce_grads(
        (
            (
                left_shards(normed_b_low, core),
                jnp.concatenate([grad_gate_pre, grad_up_pre], axis=1)[None],
            ),
            (grad_low.T[None], right_shards(hidden_low, core)),
            (left_shards(attended_low, core), pad_lanes(grad_branch)[None]),
        ),
        None,
        2,
    )
    shard_g, flat = unblock(flat, 240, 2560)
    shard_u, flat = unblock(flat, 240, 2560)
    shard_d, flat = unblock(flat, 960, 640)
    shard_o, _ = unblock(flat, 240, 960)

    dq_rows, dkv = attend_back(q_rows, do_rows, o_rows, logs, kv, own_kv, plan)
    dkv = scatter_kv(dkv, 3)
    dkv = dkv.T
    grad_value_low = dkv[:, 320:].astype(BF16)
    grad_key_pre = rotate(dkv[:, :320].reshape(TOK, KV_HEADS, HEAD), cosine, -sine)
    grad_query_pre = rotate(from_rows(dq_rows).reshape(TOK, HEADS, HEAD), cosine, -sine)
    grad_qkv = jnp.concatenate(
        [
            grad_query_pre.reshape(TOK, 960).astype(BF16),
            grad_key_pre.reshape(TOK, 320).astype(BF16),
            grad_value_low,
        ],
        axis=1,
    )
    grad_norm_a = dot_nt(grad_qkv, qkv_w)
    grad_in_norm, grad_gain_a = norm_backward(resid_in, inv_a, gain_a, grad_norm_a)
    grad_tokens = grad_middle + grad_in_norm

    gain_rows = jnp.stack([grad_gain_a, grad_gain_b]).reshape(2, 4, 240).transpose(1, 0, 2)
    gain_rows = jnp.pad(gain_rows, ((0, 0), (0, 0), (0, 16))).reshape(2, 2, 4, 128).astype(BF16)
    gain_rows = jnp.pad(gain_rows, ((0, 0), (0, 0), (0, 12), (0, 0)))
    flat = reduce_grads(
        ((left_shards(normed_a_low, core), pad_lanes(grad_qkv)[None]),),
        (pick(gain_rows, 1, core), pick(gain_rows, 1, 1 - core)),
        4,
    )
    shard_qkv, flat = unblock(flat, 240, 1600)
    shard_gains = flat[:4].reshape(2, 256)[:, :240].astype(F32)
    return (
        swap_rows(layer_out.astype(BF16), swap)[None],
        swap_rows(grad_tokens, swap)[None],
        shard_gains[0],
        shard_qkv[:, :960],
        shard_qkv[:, 960:1280],
        shard_qkv[:, 1280:],
        shard_o,
        shard_gains[1],
        shard_g,
        shard_u,
        shard_d.T,
    )


def solution(mesh):
    rows, cut = P("fsdp", "ctx", None), P("fsdp", None)
    return jax.shard_map(
        on_device,
        mesh=mesh,
        in_specs=(rows, rows, P(), P("fsdp"), cut, cut, cut, cut, P("fsdp"), cut, cut, cut),
        out_specs=(rows, rows, P("fsdp"), cut, cut, cut, cut, P("fsdp"), cut, cut, cut),
        check_vma=False,
    )
```

```python
import functools
import math

import jax
import jax.numpy as jnp
from jax import lax
from jax.experimental import pallas as pl
from jax.experimental.pallas import tpu as pltpu
from jax.sharding import PartitionSpec as P

D = 960
HEADS = 15
KV_HEADS = 5
GROUP = 3
HEAD = 64
FF = 2560
TOK = 128
HALF = 64
CTX = 32
TILES = 33
KEYS = TILES * 128
SCALE = HEAD ** (-0.5)
EPSILON = 1e-05
BASE = 10000.0
LOG2E = math.log2(math.e)
NEG = -1e30
MESH = pl.DeviceIdType.MESH
ANY = pl.BlockSpec(memory_space=pl.ANY)
VM = pl.BlockSpec(memory_space=pltpu.VMEM)
BIG = 56 * 2**20
F32 = jnp.float32
BF16 = jnp.bfloat16


def here():
    ctx = lax.axis_index("ctx")
    shard = lax.axis_index("fsdp")
    return {
        "z": ctx // 8,
        "yh": (ctx // 4) % 2,
        "x": ctx % 4,
        "yl": shard // 2,
        "c": shard % 2,
    }


def device(place, **moved):
    p = {**place, **moved}
    return (p["z"] * 8 + p["yh"] * 4 + p["x"], p["yl"] * 2 + p["c"])


def greet(devices):
    sem = pltpu.get_barrier_semaphore()
    for d in devices:
        pl.semaphore_signal(sem, inc=1, device_id=d, device_id_type=MESH)
    pl.semaphore_wait(sem, len(devices))


class Sems:
    def __init__(self, send, recv):
        self.send, self.recv, self.at = send, recv, 0

    def push(self, src, dst, dev):
        copy = pltpu.make_async_remote_copy(
            src_ref=src,
            dst_ref=dst,
            send_sem=self.send.at[self.at],
            recv_sem=self.recv.at[self.at],
            device_id=dev,
            device_id_type=MESH,
        )
        self.at += 1
        copy.start()
        return copy


def start_gather(me, sems, local, arrays):
    f = me["yl"] * 2 + me["c"]
    near = device(me, yl=1 - me["yl"])
    far = device(me, yl=1 - me["yl"], yh=1 - me["yh"])
    mate = device(me, c=1 - me["c"])
    parts, kept, own = [], [], []
    for i, (a, b) in enumerate(arrays):
        rows = a.shape[0]
        first = rows // 32 * 16 if i % 2 else (rows + 31) // 32 * 16
        for lo, size, dev in ((0, first, near), (first, rows - first, far)):
            if size:
                src = a.at[pl.ds(lo, size)]
                dst = b.at[pl.ds(pl.multiple_of(f * rows + lo, 16), size)]
                parts.append((sems.push(src, dst, dev), b, rows, lo, size))
    for i, (a, b) in enumerate(arrays):
        rows = a.shape[0]
        dst = b.at[pl.ds(pl.multiple_of(f * rows, 16), rows)]
        kept.append(sems.push(a, dst, mate))
        copy = pltpu.make_async_copy(a, dst, local.at[i])
        copy.start()
        own.append(copy)
    return parts, kept, own


def relay_gather(me, sems, started):
    parts, kept, _ = started
    across = (1 - me["yl"]) * 2 + me["c"]
    mate = device(me, c=1 - me["c"])
    for copy, b, rows, lo, size in parts:
        copy.wait_recv()
        span = b.at[pl.ds(pl.multiple_of(across * rows + lo, 16), size)]
        kept.append(sems.push(span, span, mate))


def end_gather(started):
    parts, kept, own = started
    for copy in own:
        copy.wait()
    for copy in kept:
        copy.wait()
    for copy, *_ in parts:
        copy.wait_send()


def gather_kernel(count, *refs):
    arrays = list(zip(refs[:count], refs[count : 2 * count]))
    send, recv, local = refs[2 * count :]
    me = here()
    flip = 1 - me["yl"]
    greet((device(me, yl=flip), device(me, yl=flip, yh=1 - me["yh"]), device(me, c=1 - me["c"])))
    sems = Sems(send, recv)
    started = start_gather(me, sems, local, arrays)
    relay_gather(me, sems, started)
    end_gather(started)


def gathered(arrays):
    return [jax.ShapeDtypeStruct((4 * a.shape[0], *a.shape[1:]), a.dtype) for a in arrays]


def gather_weights(arrays, collective_id):
    n = len(arrays)
    return pl.pallas_call(
        functools.partial(gather_kernel, n),
        out_shape=gathered(arrays),
        in_specs=[VM] * n,
        out_specs=[ANY] * n,
        scratch_shapes=[
            pltpu.SemaphoreType.DMA((5 * n,)),
            pltpu.SemaphoreType.DMA((5 * n,)),
            pltpu.SemaphoreType.DMA((n,)),
        ],
        compiler_params=pltpu.CompilerParams(
            collective_id=collective_id, has_side_effects=True, vmem_limit_bytes=BIG
        ),
        name="gather_weights",
    )(*arrays)


def around(me, axis):
    return [(d, lax.rem(me[axis] + d, 4)) for d in (1, 3, 2)]


def gather_kv(me, sems, kv, out):
    x, yh, z = me["x"], me["yh"], me["z"]
    other = device(me, yh=1 - yh)
    xs = [device(me, x=at) for _, at in around(me, "x")]
    zs = [device(me, z=at) for _, at in around(me, "z")]
    key, value = pl.ds(0, 320), pl.ds(320, 320)
    step2 = {}
    step2[0, 0] = [sems.push(kv.at[key], out.at[z, yh, x, key], dev) for dev in xs]
    step2[1, 0] = [sems.push(kv.at[value], out.at[z, yh, x, value], dev) for dev in zs]
    step1 = [sems.push(kv.at[p], out.at[z, yh, x, p], other) for p in (key, value)]
    out[z, yh, x] = kv[...]
    step3 = []
    for hop in (0, 1):
        row = yh if hop == 0 else 1 - yh
        for axis, (devs, p) in enumerate(((zs, key), (xs, value))):
            for c in step2[axis, hop]:
                c.wait_recv()
            span = out.at[z, row, :, key] if axis == 0 else out.at[:, row, x, value]
            for dev in devs:
                step3.append(sems.push(span, span, dev))
        if hop == 0:
            for axis, (devs, p) in enumerate(((xs, key), (zs, value))):
                step1[axis].wait_recv()
                span = out.at[z, 1 - yh, x, p]
                step2[axis, 1] = [sems.push(span, span, dev) for dev in devs]
    for c in step3:
        c.wait_recv()
    return step1 + sum(step2.values(), []) + step3


def kv_scatter_kernel(part, out, r1a, r1b, s1a, s1b, r2a, r2b, s2, r3, send, recv):
    me = here()
    x, yh, z = me["x"], me["yh"], me["z"]
    other = device(me, yh=1 - yh)
    xs = [(d, at, device(me, x=at)) for d, at in around(me, "x")]
    zs = [(d, at, device(me, z=at)) for d, at in around(me, "z")]
    greet([other] + [d for *_, d in xs] + [d for *_, d in zs])
    sems = Sems(send, recv)
    key, value = pl.ds(0, 320), pl.ds(320, 320)
    rows = (1 - yh, yh)
    first = {}
    for row in (0, 1):
        for d, at, dev in zs:
            first[0, row, d] = sems.push(part.at[at, rows[row], :, key], r1a.at[d - 1, row], dev)
        for d, at, dev in xs:
            first[1, row, d] = sems.push(part.at[:, rows[row], at, value], r1b.at[d - 1, row], dev)
    second = {}
    for row in (0, 1):
        for axis, (r1, s1) in enumerate(((r1a, s1a), (r1b, s1b))):
            for d in (1, 2, 3):
                first[axis, row, d].wait_recv()
            for i in range(4):
                own = part[z, rows[row], i, 0:320] if axis == 0 else part[i, rows[row], x, 320:640]
                total = own.astype(F32)
                for d in (0, 1, 2):
                    total = total + r1[d, row, i].astype(F32)
                s1[row, i] = total.astype(BF16)
            ring, r2 = ((xs, r2a), (zs, r2b))[axis]
            for d, at, dev in ring:
                second[axis, row, d] = sems.push(s1.at[row, at], r2.at[d - 1, row], dev)
    third = []
    for row in (0, 1):
        for axis, (s1, r2) in enumerate(((s1a, r2a), (s1b, r2b))):
            at = x if axis == 0 else z
            for d in (1, 2, 3):
                second[axis, row, d].wait_recv()
            total = s1[row, at].astype(F32)
            for d in (0, 1, 2):
                total = total + r2[d, row].astype(F32)
            if row == 0:
                s2[axis] = total.astype(BF16)
                third.append(sems.push(s2.at[axis], r3.at[axis], other))
            else:
                out[pl.ds(axis * 320, 320), :] = total
    for axis in (0, 1):
        third[axis].wait_recv()
        span = pl.ds(axis * 320, 320)
        out[span, :] = out[span, :] + r3[axis].astype(F32)
    for c in list(first.values()) + list(second.values()) + third:
        c.wait_send()


def scatter_kv(part, collective_id):
    return pl.pallas_call(
        kv_scatter_kernel,
        out_shape=jax.ShapeDtypeStruct((640, 128), F32),
        in_specs=[VM],
        out_specs=VM,
        scratch_shapes=[
            pltpu.VMEM((3, 2, 4, 320, 128), BF16),
            pltpu.VMEM((3, 2, 4, 320, 128), BF16),
            pltpu.VMEM((2, 4, 320, 128), BF16),
            pltpu.VMEM((2, 4, 320, 128), BF16),
            pltpu.VMEM((3, 2, 320, 128), BF16),
            pltpu.VMEM((3, 2, 320, 128), BF16),
            pltpu.VMEM((2, 320, 128), BF16),
            pltpu.VMEM((2, 320, 128), BF16),
            pltpu.SemaphoreType.DMA((26,)),
            pltpu.SemaphoreType.DMA((26,)),
        ],
        compiler_params=pltpu.CompilerParams(
            collective_id=collective_id, has_side_effects=True, vmem_limit_bytes=BIG
        ),
        name="scatter_kv",
    )(part.reshape(4, 2, 4, 640, 128))


def tile_plan(block_table, ctx):
    early = jnp.min(block_table.reshape(CTX, 2), axis=1)
    mine = lax.dynamic_index_in_dim(early, ctx, keepdims=False)
    late_turn = (early >= mine)[:, None]
    offset = jnp.arange(HALF, dtype=jnp.int32)[None, :]
    m = jnp.broadcast_to(late_turn.astype(F32), (CTX, HALF))
    one, zero = jnp.ones_like(m), jnp.zeros_like(m)

    def rows(a, b, last):
        return jnp.concatenate([jnp.concatenate([a, b], axis=1), last], axis=0)

    blank = jnp.zeros((1, 128), F32)
    flags = rows(one, m, blank)
    left = rows(m, 1.0 - m, blank)
    right = rows(1.0 - m, zero, blank)
    t_first = (early[:, None] - (63 - mine)) * HALF + offset
    t_second = jnp.where(late_turn, mine - early[:, None], early[:, None] - mine) * HALF + offset
    t_last = jnp.concatenate([offset, jnp.full((1, HALF), 10**6, jnp.int32)], axis=1)
    limits = rows(t_first.astype(F32), t_second.astype(F32), t_last.astype(F32))
    return flags, left, right, limits


def build_tiles(head, kv_ref, own_ref, left_ref, tiles_ref, base):
    lane = lax.broadcasted_iota(jnp.int32, (HALF, 128), 1)
    start = pl.multiple_of(base + head * HALF, HALF)

    def one(i, _):
        block = kv_ref[i, pl.ds(start, HALF), :].astype(F32)
        top = jnp.where(lane < HALF, block, 0.0)
        low = pltpu.roll(block, HALF, 1) * left_ref[pl.ds(i, 1), :]
        at = pl.multiple_of(i * 128, 128)
        tiles_ref[pl.ds(at, 128), :] = jnp.concatenate([top, low], axis=0).astype(BF16)
        return 0

    lax.fori_loop(0, CTX, one, 0, unroll=32)
    block = own_ref[pl.ds(start, HALF), :].astype(F32)
    top = jnp.where(lane < HALF, 0.0, pltpu.roll(block, HALF, 1))
    tiles_ref[pl.ds(CTX * 128, 128), :] = jnp.concatenate(
        [top, jnp.zeros_like(top)], axis=0
    ).astype(BF16)


def dot_nt(a, b):
    return lax.dot_general(a, b, (((1,), (1,)), ((), ())), preferred_element_type=F32)


def dot_nn(a, b):
    return lax.dot_general(a, b, (((1,), (0,)), ((), ())), preferred_element_type=F32)


ROWS = GROUP * HALF
STEP = 33


def row_offset():
    return lax.rem(lax.broadcasted_iota(jnp.int32, (ROWS, 128), 0), HALF).astype(F32)


def attend_head(head, q, kv_ref, own_ref, flag_ref, left_ref, limit_ref, kk, vv):
    build_tiles(head, kv_ref, own_ref, left_ref, kk, 0)
    build_tiles(head, kv_ref, own_ref, left_ref, vv, 320)
    offset = row_offset()
    low = jnp.full((ROWS, 128), NEG, F32)
    s = dot_nt(q, kk[...]) * (SCALE * LOG2E)
    tiles = []
    top_l, top_e = low, low
    for i in range(TILES):
        tile = s[:, i * 128 : (i + 1) * 128]
        tile = jnp.where(limit_ref[i : i + 1, :] <= offset, tile, NEG)
        tiles.append(tile)
        late = flag_ref[i : i + 1, :] > 0.5
        top_l = jnp.maximum(top_l, jnp.where(late, tile, NEG))
        top_e = jnp.maximum(top_e, jnp.where(late, NEG, tile))
    max_l = jnp.broadcast_to(jnp.max(top_l, axis=1, keepdims=True), (ROWS, 128))
    max_e = jnp.broadcast_to(jnp.max(top_e, axis=1, keepdims=True), (ROWS, 128))
    sum_l = jnp.zeros((ROWS, 128), F32)
    sum_e = jnp.zeros((ROWS, 128), F32)
    probs = []
    for i in range(TILES):
        late = flag_ref[i : i + 1, :] > 0.5
        p = jnp.exp2(tiles[i] - jnp.where(late, max_l, max_e))
        p_l = jnp.where(late, p, 0.0)
        sum_l = sum_l + p_l
        sum_e = sum_e + (p - p_l)
        probs.append(p.astype(BF16))
    total = dot_nn(jnp.concatenate(probs, axis=1), vv[...])
    late = lax.broadcasted_iota(jnp.int32, (ROWS, 128), 1) < HALF
    row_sum = jnp.where(
        late, jnp.sum(sum_l, axis=1, keepdims=True), jnp.sum(sum_e, axis=1, keepdims=True)
    )
    return total / row_sum, jnp.where(late, max_l, max_e) + jnp.log2(row_sum)


def head_spec(*shape):
    return pl.BlockSpec((1, *shape), lambda h: (h, 0, 0))


def whole_spec(*shape):
    return pl.BlockSpec(shape, lambda h: (0,) * len(shape))


def forward_kernel(count, q_ref, own_ref, flag_ref, left_ref, limit_ref, *refs):
    shards, refs = refs[:count], refs[count:]
    o_ref, l_ref, kv_out, *full = refs[: 3 + count]
    kv, kk, vv, send, recv, local = refs[3 + count :]
    me = here()
    flip = 1 - me["yl"]
    greet(
        [device(me, yl=flip), device(me, yl=flip, yh=1 - me["yh"]), device(me, c=1 - me["c"])]
        + [device(me, yh=1 - me["yh"])]
        + [device(me, x=at) for _, at in around(me, "x")]
        + [device(me, z=at) for _, at in around(me, "z")]
    )
    sems = Sems(send, recv)
    started = start_gather(me, sems, local, list(zip(shards, full)))
    kv_copies = gather_kv(me, sems, own_ref, kv)
    keep = pltpu.make_async_copy(kv, kv_out, local.at[count])
    keep.start()
    flat = kv.reshape(CTX, 640, 128)

    def one(head, _):
        o, logs = attend_head(
            head, q_ref[head], flat, own_ref, flag_ref, left_ref, limit_ref, kk, vv
        )
        o_ref[head] = o
        l_ref[head] = logs
        return 0

    lax.fori_loop(0, 3, one, 0)
    relay_gather(me, sems, started)
    lax.fori_loop(3, KV_HEADS, one, 0)
    end_gather(started)
    for copy in kv_copies:
        copy.wait_send()
    keep.wait()


def forward(q, own, plan, shards, collective_id):
    flags, left, _, limits = plan
    n = len(shards)
    copies = 5 * n + 26
    return pl.pallas_call(
        functools.partial(forward_kernel, n),
        out_shape=[jax.ShapeDtypeStruct((KV_HEADS, ROWS, 128), F32)] * 2
        + [jax.ShapeDtypeStruct((4, 2, 4, 640, 128), BF16)]
        + gathered(shards),
        in_specs=[VM] * (5 + n),
        out_specs=[VM, VM, ANY] + [ANY] * n,
        scratch_shapes=[
            pltpu.VMEM((4, 2, 4, 640, 128), BF16),
            pltpu.VMEM((KEYS, 128), BF16),
            pltpu.VMEM((KEYS, 128), BF16),
            pltpu.SemaphoreType.DMA((copies,)),
            pltpu.SemaphoreType.DMA((copies,)),
            pltpu.SemaphoreType.DMA((n + 1,)),
        ],
        compiler_params=pltpu.CompilerParams(
            collective_id=collective_id, has_side_effects=True, vmem_limit_bytes=BIG
        ),
        name="forward",
    )(q, own, flags, left, limits, *shards)


def attend_back_kernel(
    q_ref, qt_ref, do_ref, dot_ref, o_ref, l_ref, kv_ref, own_ref, flag_ref, left_ref, right_ref,
    limit_ref, dq_ref, dkv_ref, kk, vv,
):
    head = pl.program_id(0)
    build_tiles(head, kv_ref, own_ref, left_ref, kk, 0)
    build_tiles(head, kv_ref, own_ref, left_ref, vv, 320)
    q, qt, do, dot = q_ref[0], qt_ref[0], do_ref[0], dot_ref[0]
    offset = row_offset()
    lane = lax.broadcasted_iota(jnp.int32, (ROWS, 128), 1)
    product = do.astype(F32) * o_ref[0]
    shape = (ROWS, 128)
    delta_l = jnp.broadcast_to(
        jnp.sum(jnp.where(lane < HALF, product, 0.0), axis=1, keepdims=True), shape
    )
    delta_e = jnp.broadcast_to(
        jnp.sum(jnp.where(lane < HALF, 0.0, product), axis=1, keepdims=True), shape
    )
    log_l = jnp.broadcast_to(l_ref[0][:, 0:1], shape)
    log_e = jnp.broadcast_to(l_ref[0][:, HALF : HALF + 1], shape)
    k_rows = pl.ds(pl.multiple_of(head * HALF, HALF), HALF)
    v_rows = pl.ds(pl.multiple_of(320 + head * HALF, HALF), HALF)
    small = lax.broadcasted_iota(jnp.int32, (HALF, 128), 1)

    def grads(j, total):
        at = pl.multiple_of(j * STEP * 128, 128)
        keys = kk[pl.ds(at, STEP * 128), :]
        s = dot_nt(q, keys) * (SCALE * LOG2E)
        dp = dot_nt(do, vv[pl.ds(at, STEP * 128), :])
        probs, scores = [], []
        for t in range(STEP):
            i = j * STEP + t
            cut = slice(t * 128, (t + 1) * 128)
            late = flag_ref[pl.ds(i, 1), :] > 0.5
            tile = jnp.where(limit_ref[pl.ds(i, 1), :] <= offset, s[:, cut], NEG)
            p = jnp.exp2(tile - jnp.where(late, log_l, log_e))
            probs.append(p.astype(BF16))
            scores.append((p * (dp[:, cut] - jnp.where(late, delta_l, delta_e))).astype(BF16))
        ds = jnp.concatenate(scores, axis=1)
        total = total + dot_nn(ds, keys)
        dk = dot_nn(qt, ds) * SCALE
        dv = dot_nn(dot, jnp.concatenate(probs, axis=1))
        for t in range(STEP):
            i = j * STEP + t
            cut = slice(t * 128, (t + 1) * 128)
            for rows, both in ((k_rows, dk), (v_rows, dv)):
                top, bottom = both[0:HALF, cut], both[HALF:128, cut]

                @pl.when(i < CTX)
                def _():
                    dkv_ref[i, rows, :] = (
                        top * flag_ref[pl.ds(i, 1), :]
                        + pltpu.roll(bottom, HALF, 1) * right_ref[pl.ds(i, 1), :]
                    ).astype(BF16)

                @pl.when(i == CTX)
                def _():
                    mine = lax.axis_index("ctx")
                    before = dkv_ref[mine, rows, :].astype(F32)
                    dkv_ref[mine, rows, :] = (
                        before + jnp.where(small < HALF, bottom, 0.0)
                    ).astype(BF16)

        return total

    total = lax.fori_loop(0, TILES // STEP, grads, jnp.zeros(shape, F32))
    dq_ref[0] = total * SCALE


def attend_back(q, do, o, logs, kv, own, plan):
    flags, left, right, limits = plan
    return pl.pallas_call(
        attend_back_kernel,
        grid=(KV_HEADS,),
        out_shape=[
            jax.ShapeDtypeStruct((KV_HEADS, ROWS, 128), F32),
            jax.ShapeDtypeStruct((CTX, 640, 128), BF16),
        ],
        in_specs=[
            head_spec(ROWS, 128),
            head_spec(128, ROWS),
            head_spec(ROWS, 128),
            head_spec(128, ROWS),
            head_spec(ROWS, 128),
            head_spec(ROWS, 128),
            whole_spec(CTX, 640, 128),
            whole_spec(640, 128),
            whole_spec(TILES, 128),
            whole_spec(TILES, 128),
            whole_spec(TILES, 128),
            whole_spec(TILES, 128),
        ],
        out_specs=[head_spec(ROWS, 128), whole_spec(CTX, 640, 128)],
        scratch_shapes=[pltpu.VMEM((KEYS, 128), BF16), pltpu.VMEM((KEYS, 128), BF16)],
        compiler_params=pltpu.CompilerParams(vmem_limit_bytes=BIG),
        name="attend_back",
    )(
        q, jnp.swapaxes(q, 1, 2), do, jnp.swapaxes(do, 1, 2), o, logs, kv, own,
        flags, left, right, limits,
    )


def to_rows(a):
    a = a.reshape(2, HALF, KV_HEADS, GROUP, HEAD)[::-1]
    return a.transpose(2, 3, 1, 0, 4).reshape(KV_HEADS, ROWS, 128)


def from_rows(a):
    a = a.reshape(KV_HEADS, GROUP, HALF, 2, HEAD).transpose(3, 2, 0, 1, 4)[::-1]
    return a.reshape(TOK, HEADS * HEAD)


def to_wire(a):
    return a.reshape(2, HALF, KV_HEADS, HEAD).transpose(2, 1, 0, 3).reshape(KV_HEADS * HALF, 128)


def reduce_kernel(jobs, used, pa, pb, extra, *refs):
    refs = list(refs)
    sources = []
    for shared_left, _, shared_right, _ in jobs:
        left = [refs.pop(0) for _ in range(1 if shared_left else 2)]
        right = [refs.pop(0) for _ in range(1 if shared_right else 2)]
        sources.append((left[0], left[-1], right[0], right[-1]))
    if extra:
        extra_refs = (refs.pop(0), refs.pop(0))
    out = refs.pop(0)
    buffers = [(refs.pop(0), refs.pop(0)) for _ in jobs]
    if extra:
        extra_buffer = refs.pop(0)
    grads = refs.pop(0)
    parts = [[refs.pop(0) for _ in range(6)] for _ in range(2)]
    send, recv, local = refs

    me = here()
    x, yh, z, yl = me["x"], me["yh"], me["z"], me["yl"]
    mate = device(me, c=1 - me["c"])
    xs = [(d, at, device(me, x=at)) for d, at in around(me, "x")]
    zs = [(d, at, device(me, z=at)) for d, at in around(me, "z")]
    near = device(me, yl=1 - yl)
    far = device(me, yl=1 - yl, yh=1 - yh)
    same = device(me, yh=1 - yh)
    greet([mate, near, far, same] + [d for *_, d in xs] + [d for *_, d in zs])
    sems = Sems(send, recv)

    mine, traded = [], []
    for (lm, lt, rm, rt), (lb, rb) in zip(sources, buffers):
        traded.append(sems.push(lt, lb.at[:, :, pl.ds(128, 128)], mate))
        traded.append(sems.push(rt, rb.at[:, pl.ds(128, 128)], mate))
        for src, dst in ((lm, lb.at[:, :, pl.ds(0, 128)]), (rm, rb.at[:, pl.ds(0, 128)])):
            copy = pltpu.make_async_copy(src, dst, local.at[len(mine)])
            copy.start()
            mine.append(copy)
    if extra:
        traded.append(sems.push(extra_refs[1], extra_buffer.at[1], mate))
        copy = pltpu.make_async_copy(extra_refs[0], extra_buffer.at[0], local.at[len(mine)])
        copy.start()
        mine.append(copy)
    for copy in mine:
        copy.wait()
    for copy in traded:
        copy.wait_recv()

    base = 0
    for (_, m, _, n), (lb, rb) in zip(jobs, buffers):
        width = 256 if n % 256 == 0 else 128
        for s in range(2):
            left = lb[min(s, lb.shape[0] - 1)]

            def block(i, _, left=left, rb=rb, s=s, m=m, width=width, base=base):
                at = pl.multiple_of(i * width, 128)
                right = rb[min(s, rb.shape[0] - 1), :, pl.ds(at, width)]
                result = dot_nn(left, right).astype(BF16)
                for w in range(width // 128):
                    to = pl.multiple_of(base + (i * (width // 128) + w) * m, 16)
                    grads[s, pl.ds(to, m), :] = result[:, w * 128 : (w + 1) * 128]
                return 0

            lax.fori_loop(0, n // width, block, 0)
        base += m * (n // 128)
    if extra:
        for s in range(2):
            both = extra_buffer[0, s].astype(F32) + extra_buffer[1, s].astype(F32)
            grads[s, pl.ds(base, 16), :] = both.astype(BF16)
        base += 16
    if base < used:
        for s in range(2):
            grads[s, pl.ds(base, used - base), :] = jnp.zeros((used - base, 128), BF16)

    plans = (
        (0, pa, xs, zs, x, z, parts[0]),
        (16 * pa, pb, zs, xs, z, x, parts[1]),
    )
    order = (1, 3, 2, 0)
    first, second = {}, {}
    sent = []
    for k in order:
        for n, (lo, size, ring, cross, i_me, j_me, _) in enumerate(plans):
            r1 = parts[n][0]
            j = lax.rem(j_me + k, 4)
            for d, at, dev in ring:
                src = grads.at[:, pl.ds(pl.multiple_of(lo + (at * 4 + j) * size, 16), size)]
                first[n, k, d] = sems.push(src, r1.at[d - 1, k], dev)
    for k in order:
        for n, (lo, size, ring, cross, i_me, j_me, (r1, s1, r2, s2, r3, fin)) in enumerate(plans):
            j = lax.rem(j_me + k, 4)
            for d in (1, 2, 3):
                first[n, k, d].wait_recv()
            for s in range(2):
                own = grads[s, pl.ds(pl.multiple_of(lo + (i_me * 4 + j) * size, 16), size)]
                total = own.astype(F32)
                for d in (0, 1, 2):
                    total = total + r1[d, k, s].astype(F32)
                s1[k, s] = total.astype(BF16)
            if k:
                dev = [dev for d, _, dev in cross if d == k][0]
                second[n, k] = sems.push(s1.at[k], r2.at[k - 1], dev)
    third = {}
    for n, (lo, size, ring, cross, i_me, j_me, (r1, s1, r2, s2, r3, fin)) in enumerate(plans):
        for k in (1, 2, 3):
            second[n, k].wait_recv()
        for s in range(2):
            total = s1[0, s].astype(F32)
            for d in (0, 1, 2):
                total = total + r2[d, s].astype(F32)
            s2[s] = total.astype(BF16)
        slot = r3.at[yl * 2 + yh]
        third[n, 0] = sems.push(s2.at[1 - yl], slot, near)
        third[n, 1] = sems.push(s2.at[1 - yl], slot, far)
        third[n, 2] = sems.push(s2.at[yl], slot, same)
    fourth, fifth = {}, {}
    for n, (lo, size, ring, cross, i_me, j_me, (r1, s1, r2, s2, r3, fin)) in enumerate(plans):
        r3[yl * 2 + yh] = s2[yl]
        for i in (0, 1, 2):
            third[n, i].wait_recv()
        total = r3[0].astype(F32)
        for i in (1, 2, 3):
            total = total + r3[i].astype(F32)
        fin[...] = total.astype(BF16)
        span = out.at[pl.ds(pl.multiple_of(lo + (i_me * 4 + j_me) * size, 16), size)]
        copy = pltpu.make_async_copy(fin, span, local.at[n])
        copy.start()
        fourth[n, "own"] = copy
        for d, _, dev in cross:
            fourth[n, d] = sems.push(fin, span, dev)
        for d, _, dev in ring:
            fifth[n, 0, d] = sems.push(fin, span, dev)
    for back in (3, 1, 2):
        for n, (lo, size, ring, cross, i_me, j_me, _) in enumerate(plans):
            fourth[n, back].wait_recv()
            j = lax.rem(j_me + 4 - back, 4)
            span = out.at[pl.ds(pl.multiple_of(lo + (i_me * 4 + j) * size, 16), size)]
            for d, _, dev in ring:
                fifth[n, back, d] = sems.push(span, span, dev)
    for copy in fifth.values():
        copy.wait_recv()
    for n in (0, 1):
        fourth.pop((n, "own")).wait()
    for group in (traded, first.values(), second.values(), third.values()):
        for copy in group:
            copy.wait_send()
    for group in (fourth.values(), fifth.values()):
        for copy in group:
            copy.wait_send()


def reduce_grads(jobs, extra, collective_id):
    operands, shapes, buffers, rows = [], [], [], 0
    for left, right in jobs:
        shared_left, shared_right = not isinstance(left, tuple), not isinstance(right, tuple)
        lefts = [left] if shared_left else list(left)
        rights = [right] if shared_right else list(right)
        operands += lefts + rights
        m, n = lefts[0].shape[1], rights[0].shape[2]
        shapes.append((shared_left, m, shared_right, n))
        buffers.append(pltpu.VMEM((lefts[0].shape[0], m, 256), BF16))
        buffers.append(pltpu.VMEM((rights[0].shape[0], 256, n), BF16))
        rows += m * (n // 128)
    if extra is not None:
        operands += list(extra)
        buffers.append(pltpu.VMEM((2, 2, 16, 128), BF16))
        rows += 16
    pieces = -(-rows // 256)
    pa, pb = (pieces + 1) // 2 * 16, pieces // 2 * 16
    used = 16 * (pa + pb)
    scratch = buffers + [pltpu.VMEM((2, used, 128), BF16)]
    for size in (pa, pb):
        scratch += [
            pltpu.VMEM((3, 4, 2, size, 128), BF16),
            pltpu.VMEM((4, 2, size, 128), BF16),
            pltpu.VMEM((3, 2, size, 128), BF16),
            pltpu.VMEM((2, size, 128), BF16),
            pltpu.VMEM((4, size, 128), BF16),
            pltpu.VMEM((size, 128), BF16),
        ]
    copies = 2 * len(jobs) + 1 + 24 + 6 + 6 + 6 + 24
    scratch += [
        pltpu.SemaphoreType.DMA((copies,)),
        pltpu.SemaphoreType.DMA((copies,)),
        pltpu.SemaphoreType.DMA((2 * len(jobs) + 1,)),
    ]
    return pl.pallas_call(
        functools.partial(reduce_kernel, tuple(shapes), used, pa, pb, extra is not None),
        out_shape=jax.ShapeDtypeStruct((used, 128), BF16),
        in_specs=[ANY] * len(operands),
        out_specs=ANY,
        scratch_shapes=scratch,
        compiler_params=pltpu.CompilerParams(
            collective_id=collective_id, has_side_effects=True, vmem_limit_bytes=BIG
        ),
        name="reduce_grads",
    )(*operands)


def pick(a, axis, core):
    return lax.dynamic_index_in_dim(a, core, axis, keepdims=False)


def left_shards(a, core):
    t = a.T.reshape(2, 2, 240, TOK)
    return pick(t, 1, core), pick(t, 1, 1 - core)


def right_shards(a, core):
    t = a.reshape(TOK, 2, 2, a.shape[1] // 4).transpose(1, 2, 0, 3)
    return pick(t, 1, core), pick(t, 1, 1 - core)


def pad_lanes(a):
    extra = -a.shape[1] % 128
    return jnp.pad(a, ((0, 0), (0, extra)))


def unblock(flat, m, columns):
    blocks = -(-columns // 128)
    a = flat[: m * blocks].reshape(blocks, m, 128).transpose(1, 0, 2).reshape(m, blocks * 128)
    return a[:, :columns].astype(F32), flat[m * blocks :]


def norm_forward(values, gain):
    inv_rms = lax.rsqrt(jnp.mean(values * values, axis=-1, keepdims=True) + EPSILON)
    return values * inv_rms * gain, inv_rms


def norm_backward(values, inv_rms, gain, grad_normed):
    scaled = grad_normed * gain
    grad_values = inv_rms * scaled - values * inv_rms * inv_rms * inv_rms * jnp.mean(
        scaled * values, axis=-1, keepdims=True
    )
    grad_gain = jnp.sum(grad_normed * values * inv_rms, axis=0)
    return grad_values, grad_gain


def rope_tables(positions, half_dim):
    frequency = BASE ** (-jnp.arange(half_dim, dtype=F32) / half_dim)
    angles = positions.astype(F32)[:, None] * frequency[None, :]
    cosine = jnp.concatenate([jnp.cos(angles), jnp.cos(angles)], axis=-1)[:, None, :]
    sine = jnp.concatenate([jnp.sin(angles), jnp.sin(angles)], axis=-1)[:, None, :]
    return cosine, sine


def rotate(values, cosine, sine):
    half_dim = values.shape[-1] // 2
    turned = jnp.concatenate([-values[..., half_dim:], values[..., :half_dim]], axis=-1)
    return values * cosine + turned * sine


def dot(a, b):
    return jnp.dot(a, b, preferred_element_type=F32)


def swap_rows(a, swap):
    return jnp.where(swap, jnp.concatenate([a[HALF:], a[:HALF]], axis=0), a)


def on_device(
    tokens, cotangent, block_table, attn_gain, w_query, w_key, w_value, w_out, mlp_gain,
    w_gate, w_up, w_down,
):
    ctx = lax.axis_index("ctx")
    core = lax.axis_index("fsdp") % 2
    gains = jnp.pad(jnp.stack([attn_gain, mlp_gain]), ((0, 14), (0, 16)))
    qkv_shard = jnp.concatenate([w_query, w_key, w_value], axis=1)
    gains_all, qkv_w = gather_weights((gains, qkv_shard), 0)
    gains_all = gains_all.reshape(4, 16, 256)[:, :2, :240].astype(F32)
    gain_a = gains_all[:, 0].reshape(D)
    gain_b = gains_all[:, 1].reshape(D)

    own_blocks = lax.dynamic_slice_in_dim(block_table, 2 * ctx, 2)
    swap = own_blocks[0] > own_blocks[1]
    early = jnp.min(own_blocks)
    offsets = jnp.arange(HALF, dtype=jnp.int32)
    positions = jnp.concatenate([early * HALF + offsets, (63 - early) * HALF + offsets])
    cosine, sine = rope_tables(positions, HEAD // 2)
    plan = tile_plan(block_table, ctx)

    resid_in = swap_rows(tokens[0], swap).astype(F32)
    grad_low = swap_rows(cotangent[0], swap)
    normed_a, inv_a = norm_forward(resid_in, gain_a)
    normed_a_low = normed_a.astype(BF16)
    qkv = dot(normed_a_low, qkv_w)
    value_low = qkv[:, 1280:].astype(BF16)
    queries = rotate(qkv[:, :960].reshape(TOK, HEADS, HEAD), cosine, sine).astype(BF16)
    keys = rotate(qkv[:, 960:1280].reshape(TOK, KV_HEADS, HEAD), cosine, sine).astype(BF16)
    q_rows = to_rows(queries)
    own_kv = jnp.concatenate([to_wire(keys), to_wire(value_low)], axis=0)
    o_rows, logs, kv, out_w, gate_w, up_w, down_w = forward(
        q_rows, own_kv, plan, (w_out, w_gate, w_up, w_down), 1
    )
    kv = kv.reshape(CTX, 640, 128)
    attended_low = from_rows(o_rows).astype(BF16)

    middle = resid_in + dot(attended_low, out_w)
    normed_b, inv_b = norm_forward(middle, gain_b)
    normed_b_low = normed_b.astype(BF16)
    gate_pre = dot(normed_b_low, gate_w)
    up_pre = dot(normed_b_low, up_w)
    sigmoid_gate = jax.nn.sigmoid(gate_pre)
    silu_gate = gate_pre * sigmoid_gate
    hidden_low = (silu_gate * up_pre).astype(BF16)
    layer_out = middle + dot(hidden_low, down_w)

    grad_hidden = dot_nt(grad_low, down_w)
    grad_gate_pre = (
        grad_hidden * up_pre * sigmoid_gate * (1.0 + gate_pre * (1.0 - sigmoid_gate))
    ).astype(BF16)
    grad_up_pre = (grad_hidden * silu_gate).astype(BF16)
    grad_norm_b = dot_nt(grad_gate_pre, gate_w) + dot_nt(grad_up_pre, up_w)
    grad_mid_norm, grad_gain_b = norm_backward(middle, inv_b, gain_b, grad_norm_b)
    grad_middle = grad_low.astype(F32) + grad_mid_norm
    grad_branch = grad_middle.astype(BF16)
    do_rows = to_rows(dot_nt(grad_branch, out_w).astype(BF16))

    flat = reduce_grads(
        (
            (
                left_shards(normed_b_low, core),
                jnp.concatenate([grad_gate_pre, grad_up_pre], axis=1)[None],
            ),
            (grad_low.T[None], right_shards(hidden_low, core)),
            (left_shards(attended_low, core), pad_lanes(grad_branch)[None]),
        ),
        None,
        2,
    )
    shard_g, flat = unblock(flat, 240, 2560)
    shard_u, flat = unblock(flat, 240, 2560)
    shard_d, flat = unblock(flat, 960, 640)
    shard_o, _ = unblock(flat, 240, 960)

    dq_rows, dkv = attend_back(q_rows, do_rows, o_rows, logs, kv, own_kv, plan)
    dkv = scatter_kv(dkv, 3)
    dkv = dkv.T
    grad_value_low = dkv[:, 320:].astype(BF16)
    grad_key_pre = rotate(dkv[:, :320].reshape(TOK, KV_HEADS, HEAD), cosine, -sine)
    grad_query_pre = rotate(from_rows(dq_rows).reshape(TOK, HEADS, HEAD), cosine, -sine)
    grad_qkv = jnp.concatenate(
        [
            grad_query_pre.reshape(TOK, 960).astype(BF16),
            grad_key_pre.reshape(TOK, 320).astype(BF16),
            grad_value_low,
        ],
        axis=1,
    )
    grad_norm_a = dot_nt(grad_qkv, qkv_w)
    grad_in_norm, grad_gain_a = norm_backward(resid_in, inv_a, gain_a, grad_norm_a)
    grad_tokens = grad_middle + grad_in_norm

    gain_rows = jnp.stack([grad_gain_a, grad_gain_b]).reshape(2, 4, 240).transpose(1, 0, 2)
    gain_rows = jnp.pad(gain_rows, ((0, 0), (0, 0), (0, 16))).reshape(2, 2, 4, 128).astype(BF16)
    gain_rows = jnp.pad(gain_rows, ((0, 0), (0, 0), (0, 12), (0, 0)))
    flat = reduce_grads(
        ((left_shards(normed_a_low, core), pad_lanes(grad_qkv)[None]),),
        (pick(gain_rows, 1, core), pick(gain_rows, 1, 1 - core)),
        4,
    )
    shard_qkv, flat = unblock(flat, 240, 1600)
    shard_gains = flat[:4].reshape(2, 256)[:, :240].astype(F32)
    return (
        swap_rows(layer_out.astype(BF16), swap)[None],
        swap_rows(grad_tokens, swap)[None],
        shard_gains[0],
        shard_qkv[:, :960],
        shard_qkv[:, 960:1280],
        shard_qkv[:, 1280:],
        shard_o,
        shard_gains[1],
        shard_g,
        shard_u,
        shard_d.T,
    )


def solution(mesh):
    rows, cut = P("fsdp", "ctx", None), P("fsdp", None)
    return jax.shard_map(
        on_device,
        mesh=mesh,
        in_specs=(rows, rows, P(), P("fsdp"), cut, cut, cut, cut, P("fsdp"), cut, cut, cut),
        out_specs=(rows, rows, P("fsdp"), cut, cut, cut, cut, P("fsdp"), cut, cut, cut),
        check_vma=False,
    )
```

```python
import functools
import math

import jax
import jax.numpy as jnp
from jax import lax
from jax.experimental import pallas as pl
from jax.experimental.pallas import tpu as pltpu
from jax.sharding import PartitionSpec as P

D = 960
HEADS = 15
KV_HEADS = 5
GROUP = 3
HEAD = 64
FF = 2560
TOK = 128
HALF = 64
CTX = 32
TILES = 33
KEYS = TILES * 128
SCALE = HEAD ** (-0.5)
EPSILON = 1e-05
BASE = 10000.0
LOG2E = math.log2(math.e)
NEG = -1e30
MESH = pl.DeviceIdType.MESH
ANY = pl.BlockSpec(memory_space=pl.ANY)
VM = pl.BlockSpec(memory_space=pltpu.VMEM)
BIG = 56 * 2**20
F32 = jnp.float32
BF16 = jnp.bfloat16


def here():
    ctx = lax.axis_index("ctx")
    shard = lax.axis_index("fsdp")
    return {
        "z": ctx // 8,
        "yh": (ctx // 4) % 2,
        "x": ctx % 4,
        "yl": shard // 2,
        "c": shard % 2,
    }


def device(place, **moved):
    p = {**place, **moved}
    return (p["z"] * 8 + p["yh"] * 4 + p["x"], p["yl"] * 2 + p["c"])


def greet(devices):
    sem = pltpu.get_barrier_semaphore()
    for d in devices:
        pl.semaphore_signal(sem, inc=1, device_id=d, device_id_type=MESH)
    pl.semaphore_wait(sem, len(devices))


class Sems:
    def __init__(self, send, recv):
        self.send, self.recv, self.at = send, recv, 0

    def push(self, src, dst, dev):
        copy = pltpu.make_async_remote_copy(
            src_ref=src,
            dst_ref=dst,
            send_sem=self.send.at[self.at],
            recv_sem=self.recv.at[self.at],
            device_id=dev,
            device_id_type=MESH,
        )
        self.at += 1
        copy.start()
        return copy


def start_gather(me, sems, local, arrays):
    f = me["yl"] * 2 + me["c"]
    near = device(me, yl=1 - me["yl"])
    far = device(me, yl=1 - me["yl"], yh=1 - me["yh"])
    mate = device(me, c=1 - me["c"])
    parts, kept, own = [], [], []
    for i, (a, b) in enumerate(arrays):
        rows = a.shape[0]
        first = rows // 32 * 16 if i % 2 else (rows + 31) // 32 * 16
        for lo, size, dev in ((0, first, near), (first, rows - first, far)):
            if size:
                src = a.at[pl.ds(lo, size)]
                dst = b.at[pl.ds(pl.multiple_of(f * rows + lo, 16), size)]
                parts.append((sems.push(src, dst, dev), b, rows, lo, size))
    for i, (a, b) in enumerate(arrays):
        rows = a.shape[0]
        dst = b.at[pl.ds(pl.multiple_of(f * rows, 16), rows)]
        kept.append(sems.push(a, dst, mate))
        copy = pltpu.make_async_copy(a, dst, local.at[i])
        copy.start()
        own.append(copy)
    return parts, kept, own


def relay_gather(me, sems, started):
    parts, kept, _ = started
    across = (1 - me["yl"]) * 2 + me["c"]
    mate = device(me, c=1 - me["c"])
    for copy, b, rows, lo, size in parts:
        copy.wait_recv()
        span = b.at[pl.ds(pl.multiple_of(across * rows + lo, 16), size)]
        kept.append(sems.push(span, span, mate))


def end_gather(started):
    parts, kept, own = started
    for copy in own:
        copy.wait()
    for copy in kept:
        copy.wait()
    for copy, *_ in parts:
        copy.wait_send()


def gather_kernel(count, *refs):
    arrays = list(zip(refs[:count], refs[count : 2 * count]))
    send, recv, local = refs[2 * count :]
    me = here()
    flip = 1 - me["yl"]
    greet((device(me, yl=flip), device(me, yl=flip, yh=1 - me["yh"]), device(me, c=1 - me["c"])))
    sems = Sems(send, recv)
    started = start_gather(me, sems, local, arrays)
    relay_gather(me, sems, started)
    end_gather(started)


def gathered(arrays):
    return [jax.ShapeDtypeStruct((4 * a.shape[0], *a.shape[1:]), a.dtype) for a in arrays]


def gather_weights(arrays, collective_id):
    n = len(arrays)
    return pl.pallas_call(
        functools.partial(gather_kernel, n),
        out_shape=gathered(arrays),
        in_specs=[VM] * n,
        out_specs=[ANY] * n,
        scratch_shapes=[
            pltpu.SemaphoreType.DMA((5 * n,)),
            pltpu.SemaphoreType.DMA((5 * n,)),
            pltpu.SemaphoreType.DMA((n,)),
        ],
        compiler_params=pltpu.CompilerParams(
            collective_id=collective_id, has_side_effects=True, vmem_limit_bytes=BIG
        ),
        name="gather_weights",
    )(*arrays)


def around(me, axis):
    return [(d, lax.rem(me[axis] + d, 4)) for d in (1, 3, 2)]


def gather_kv(me, sems, kv, out, once_across):
    x, yh, z = me["x"], me["yh"], me["z"]
    other = device(me, yh=1 - yh)
    xs = [device(me, x=at) for _, at in around(me, "x")]
    zs = [device(me, z=at) for _, at in around(me, "z")]
    key, value = pl.ds(0, 320), pl.ds(320, 320)
    step1 = [sems.push(kv.at[p], out.at[z, yh, x, p], other) for p in (key, value)]
    step2 = {}
    step2[0, 0] = [sems.push(kv.at[key], out.at[z, yh, x, key], dev) for dev in xs]
    step2[1, 0] = [sems.push(kv.at[value], out.at[z, yh, x, value], dev) for dev in zs]
    out[z, yh, x] = kv[...]
    step3 = []
    for hop in (0, 1):
        row = yh if hop == 0 else 1 - yh
        for axis, (devs, p) in enumerate(((zs, key), (xs, value))):
            for c in step2[axis, hop]:
                c.wait_recv()
            span = out.at[z, row, :, key] if axis == 0 else out.at[:, row, x, value]
            for dev in devs:
                step3.append(sems.push(span, span, dev))
        if hop == 0:
            for axis, (devs, p) in enumerate(((xs, key), (zs, value))):
                step1[axis].wait_recv()
                span = out.at[z, 1 - yh, x, p]
                step2[axis, 1] = [sems.push(span, span, dev) for dev in devs]
            once_across()
    for c in step3:
        c.wait_recv()
    return step1 + sum(step2.values(), []) + step3


class Scatter:
    COPIES = 26
    SCRATCH = [
        pltpu.VMEM((3, 2, 4, 320, 128), BF16),
        pltpu.VMEM((3, 2, 4, 320, 128), BF16),
        pltpu.VMEM((2, 4, 320, 128), BF16),
        pltpu.VMEM((2, 4, 320, 128), BF16),
        pltpu.VMEM((3, 2, 320, 128), BF16),
        pltpu.VMEM((3, 2, 320, 128), BF16),
        pltpu.VMEM((2, 320, 128), BF16),
        pltpu.VMEM((2, 320, 128), BF16),
    ]

    def __init__(self, me, sems, part, out, scratch):
        self.me, self.sems, self.part, self.out = me, sems, part, out
        r1a, r1b, s1a, s1b, r2a, r2b, self.s2, self.r3 = scratch
        self.r1, self.s1, self.r2 = (r1a, r1b), (s1a, s1b), (r2a, r2b)
        self.xs = [(d, at, device(me, x=at)) for d, at in around(me, "x")]
        self.zs = [(d, at, device(me, z=at)) for d, at in around(me, "z")]
        self.rows = (1 - me["yh"], me["yh"])
        self.first, self.second, self.third = {}, {}, []

    def start(self):
        x, z, part, push = self.me["x"], self.me["z"], self.part, self.sems.push
        key, value = pl.ds(0, 320), pl.ds(320, 320)
        for r, row in enumerate(self.rows):
            for d, at, dev in self.zs:
                src = part.at[at, row, :, key]
                self.first[0, r, d] = push(src, self.r1[0].at[d - 1, r], dev)
            for d, at, dev in self.xs:
                src = part.at[:, row, at, value]
                self.first[1, r, d] = push(src, self.r1[1].at[d - 1, r], dev)

    def middle(self, r):
        x, z, part, row = self.me["x"], self.me["z"], self.part, self.rows[r]
        for axis in (0, 1):
            r1, s1, r2 = self.r1[axis], self.s1[axis], self.r2[axis]
            for d in (1, 2, 3):
                self.first[axis, r, d].wait_recv()
            for i in range(4):
                own = part[z, row, i, 0:320] if axis == 0 else part[i, row, x, 320:640]
                total = own.astype(F32)
                for d in (0, 1, 2):
                    total = total + r1[d, r, i].astype(F32)
                s1[r, i] = total.astype(BF16)
            for d, at, dev in (self.xs, self.zs)[axis]:
                self.second[axis, r, d] = self.sems.push(s1.at[r, at], r2.at[d - 1, r], dev)

    def last(self, r):
        other = device(self.me, yh=1 - self.me["yh"])
        for axis in (0, 1):
            s1, r2 = self.s1[axis], self.r2[axis]
            at = self.me["x"] if axis == 0 else self.me["z"]
            for d in (1, 2, 3):
                self.second[axis, r, d].wait_recv()
            total = s1[r, at].astype(F32)
            for d in (0, 1, 2):
                total = total + r2[d, r].astype(F32)
            if r == 0:
                self.s2[axis] = total.astype(BF16)
                self.third.append(self.sems.push(self.s2.at[axis], self.r3.at[axis], other))
            else:
                self.out[pl.ds(axis * 320, 320), :] = total

    def end(self):
        for axis in (0, 1):
            self.third[axis].wait_recv()
            span = pl.ds(axis * 320, 320)
            self.out[span, :] = self.out[span, :] + self.r3[axis].astype(F32)
        for c in list(self.first.values()) + list(self.second.values()) + self.third:
            c.wait_send()


def tile_plan(block_table, ctx):
    early = jnp.min(block_table.reshape(CTX, 2), axis=1)
    mine = lax.dynamic_index_in_dim(early, ctx, keepdims=False)
    late_turn = (early >= mine)[:, None]
    offset = jnp.arange(HALF, dtype=jnp.int32)[None, :]
    m = jnp.broadcast_to(late_turn.astype(F32), (CTX, HALF))
    one, zero = jnp.ones_like(m), jnp.zeros_like(m)

    def rows(a, b, last):
        return jnp.concatenate([jnp.concatenate([a, b], axis=1), last], axis=0)

    blank = jnp.zeros((1, 128), F32)
    flags = rows(one, m, blank)
    left = rows(m, 1.0 - m, blank)
    right = rows(1.0 - m, zero, blank)
    t_first = (early[:, None] - (63 - mine)) * HALF + offset
    t_second = jnp.where(late_turn, mine - early[:, None], early[:, None] - mine) * HALF + offset
    t_last = jnp.concatenate([offset, jnp.full((1, HALF), 10**6, jnp.int32)], axis=1)
    limits = rows(t_first.astype(F32), t_second.astype(F32), t_last.astype(F32))
    return flags, left, right, limits


def build_tiles(head, kv_ref, own_ref, left_ref, tiles_ref, base):
    lane = lax.broadcasted_iota(jnp.int32, (HALF, 128), 1)
    start = pl.multiple_of(base + head * HALF, HALF)

    def one(i, _):
        block = kv_ref[i, pl.ds(start, HALF), :].astype(F32)
        top = jnp.where(lane < HALF, block, 0.0)
        low = pltpu.roll(block, HALF, 1) * left_ref[pl.ds(i, 1), :]
        at = pl.multiple_of(i * 128, 128)
        tiles_ref[pl.ds(at, 128), :] = jnp.concatenate([top, low], axis=0).astype(BF16)
        return 0

    lax.fori_loop(0, CTX, one, 0, unroll=32)
    block = own_ref[pl.ds(start, HALF), :].astype(F32)
    top = jnp.where(lane < HALF, 0.0, pltpu.roll(block, HALF, 1))
    tiles_ref[pl.ds(CTX * 128, 128), :] = jnp.concatenate(
        [top, jnp.zeros_like(top)], axis=0
    ).astype(BF16)


def dot_nt(a, b):
    return lax.dot_general(a, b, (((1,), (1,)), ((), ())), preferred_element_type=F32)


def dot_nn(a, b):
    return lax.dot_general(a, b, (((1,), (0,)), ((), ())), preferred_element_type=F32)


ROWS = GROUP * HALF
STEP = 33


def row_offset():
    return lax.rem(lax.broadcasted_iota(jnp.int32, (ROWS, 128), 0), HALF).astype(F32)


def attend_head(head, q, kv_ref, own_ref, flag_ref, left_ref, limit_ref, kk, vv):
    build_tiles(head, kv_ref, own_ref, left_ref, kk, 0)
    build_tiles(head, kv_ref, own_ref, left_ref, vv, 320)
    offset = row_offset()
    low = jnp.full((ROWS, 128), NEG, F32)
    s = dot_nt(q, kk[...]) * (SCALE * LOG2E)
    tiles = []
    top_l, top_e = low, low
    for i in range(TILES):
        tile = s[:, i * 128 : (i + 1) * 128]
        tile = jnp.where(limit_ref[i : i + 1, :] <= offset, tile, NEG)
        tiles.append(tile)
        late = flag_ref[i : i + 1, :] > 0.5
        top_l = jnp.maximum(top_l, jnp.where(late, tile, NEG))
        top_e = jnp.maximum(top_e, jnp.where(late, NEG, tile))
    max_l = jnp.broadcast_to(jnp.max(top_l, axis=1, keepdims=True), (ROWS, 128))
    max_e = jnp.broadcast_to(jnp.max(top_e, axis=1, keepdims=True), (ROWS, 128))
    sum_l = jnp.zeros((ROWS, 128), F32)
    sum_e = jnp.zeros((ROWS, 128), F32)
    probs = []
    for i in range(TILES):
        late = flag_ref[i : i + 1, :] > 0.5
        p = jnp.exp2(tiles[i] - jnp.where(late, max_l, max_e))
        p_l = jnp.where(late, p, 0.0)
        sum_l = sum_l + p_l
        sum_e = sum_e + (p - p_l)
        probs.append(p.astype(BF16))
    total = dot_nn(jnp.concatenate(probs, axis=1), vv[...])
    late = lax.broadcasted_iota(jnp.int32, (ROWS, 128), 1) < HALF
    row_sum = jnp.where(
        late, jnp.sum(sum_l, axis=1, keepdims=True), jnp.sum(sum_e, axis=1, keepdims=True)
    )
    return total / row_sum, jnp.where(late, max_l, max_e) + jnp.log2(row_sum)


def head_spec(*shape):
    return pl.BlockSpec((1, *shape), lambda h: (h, 0, 0))


def whole_spec(*shape):
    return pl.BlockSpec(shape, lambda h: (0,) * len(shape))


def forward_kernel(count, q_ref, own_ref, flag_ref, left_ref, limit_ref, *refs):
    shards, refs = refs[:count], refs[count:]
    o_ref, l_ref, kv_out, *full = refs[: 3 + count]
    kv, kk, vv, send, recv, local = refs[3 + count :]
    me = here()
    greet_axes(me)
    sems = Sems(send, recv)
    started = []

    def start_weights():
        started.extend(start_gather(me, sems, local, list(zip(shards, full))))

    kv_copies = gather_kv(me, sems, own_ref, kv, start_weights)
    keep = pltpu.make_async_copy(kv, kv_out, local.at[count])
    keep.start()
    flat = kv.reshape(CTX, 640, 128)

    def one(head, _):
        o, logs = attend_head(
            head, q_ref[head], flat, own_ref, flag_ref, left_ref, limit_ref, kk, vv
        )
        o_ref[head] = o
        l_ref[head] = logs
        return 0

    lax.fori_loop(0, 3, one, 0)
    relay_gather(me, sems, started)
    lax.fori_loop(3, KV_HEADS, one, 0)
    end_gather(started)
    for copy in kv_copies:
        copy.wait_send()
    keep.wait()


def forward(q, own, plan, shards, collective_id):
    flags, left, _, limits = plan
    n = len(shards)
    copies = 5 * n + 26
    return pl.pallas_call(
        functools.partial(forward_kernel, n),
        out_shape=[jax.ShapeDtypeStruct((KV_HEADS, ROWS, 128), F32)] * 2
        + [jax.ShapeDtypeStruct((4, 2, 4, 640, 128), BF16)]
        + gathered(shards),
        in_specs=[VM] * (5 + n),
        out_specs=[VM, VM, ANY] + [ANY] * n,
        scratch_shapes=[
            pltpu.VMEM((4, 2, 4, 640, 128), BF16),
            pltpu.VMEM((KEYS, 128), BF16),
            pltpu.VMEM((KEYS, 128), BF16),
            pltpu.SemaphoreType.DMA((copies,)),
            pltpu.SemaphoreType.DMA((copies,)),
            pltpu.SemaphoreType.DMA((n + 1,)),
        ],
        compiler_params=pltpu.CompilerParams(
            collective_id=collective_id, has_side_effects=True, vmem_limit_bytes=BIG
        ),
        name="forward",
    )(q, own, flags, left, limits, *shards)


def attend_back_head(
    head, q, qt, do, dot, o, logs, kv_ref, own_ref, flag_ref, left_ref, right_ref, limit_ref,
    dkv_ref, kk, vv,
):
    build_tiles(head, kv_ref, own_ref, left_ref, kk, 0)
    build_tiles(head, kv_ref, own_ref, left_ref, vv, 320)
    offset = row_offset()
    lane = lax.broadcasted_iota(jnp.int32, (ROWS, 128), 1)
    product = do.astype(F32) * o
    shape = (ROWS, 128)
    delta_l = jnp.broadcast_to(
        jnp.sum(jnp.where(lane < HALF, product, 0.0), axis=1, keepdims=True), shape
    )
    delta_e = jnp.broadcast_to(
        jnp.sum(jnp.where(lane < HALF, 0.0, product), axis=1, keepdims=True), shape
    )
    log_l = jnp.broadcast_to(logs[:, 0:1], shape)
    log_e = jnp.broadcast_to(logs[:, HALF : HALF + 1], shape)
    k_rows = pl.ds(pl.multiple_of(head * HALF, HALF), HALF)
    v_rows = pl.ds(pl.multiple_of(320 + head * HALF, HALF), HALF)
    small = lax.broadcasted_iota(jnp.int32, (HALF, 128), 1)
    keys = kk[...]
    s = dot_nt(q, keys) * (SCALE * LOG2E)
    dp = dot_nt(do, vv[...])
    probs, scores = [], []
    for i in range(TILES):
        cut = slice(i * 128, (i + 1) * 128)
        late = flag_ref[i : i + 1, :] > 0.5
        tile = jnp.where(limit_ref[i : i + 1, :] <= offset, s[:, cut], NEG)
        p = jnp.exp2(tile - jnp.where(late, log_l, log_e))
        probs.append(p.astype(BF16))
        scores.append((p * (dp[:, cut] - jnp.where(late, delta_l, delta_e))).astype(BF16))
    ds = jnp.concatenate(scores, axis=1)
    dq = dot_nn(ds, keys) * SCALE
    dk = dot_nn(qt, ds) * SCALE
    dv = dot_nn(dot, jnp.concatenate(probs, axis=1))
    mine = lax.axis_index("ctx")
    for rows, both in ((k_rows, dk), (v_rows, dv)):
        for i in range(CTX):
            cut = slice(i * 128, (i + 1) * 128)
            top, bottom = both[0:HALF, cut], both[HALF:128, cut]
            total = (
                top * flag_ref[i : i + 1, :]
                + pltpu.roll(bottom, HALF, 1) * right_ref[i : i + 1, :]
            )
            dkv_ref[i, rows, :] = total.astype(BF16)
        bottom = both[HALF:128, CTX * 128 :]
        before = dkv_ref[mine, rows, :].astype(F32)
        dkv_ref[mine, rows, :] = (before + jnp.where(small < HALF, bottom, 0.0)).astype(BF16)
    return dq


def to_rows(a):
    a = a.reshape(2, HALF, KV_HEADS, GROUP, HEAD)[::-1]
    return a.transpose(2, 3, 1, 0, 4).reshape(KV_HEADS, ROWS, 128)


def from_rows(a):
    a = a.reshape(KV_HEADS, GROUP, HALF, 2, HEAD).transpose(3, 2, 0, 1, 4)[::-1]
    return a.reshape(TOK, HEADS * HEAD)


def to_wire(a):
    return a.reshape(2, HALF, KV_HEADS, HEAD).transpose(2, 1, 0, 3).reshape(KV_HEADS * HALF, 128)


def pop(refs, count):
    taken = refs[:count]
    del refs[:count]
    return taken


class Reduction:
    def __init__(self, jobs, extra):
        self.operands, self.jobs, self.scratch, rows = [], [], [], 0
        for left, right in jobs:
            lefts = list(left) if isinstance(left, tuple) else [left]
            rights = list(right) if isinstance(right, tuple) else [right]
            self.operands += lefts + rights
            m, n = lefts[0].shape[1], rights[0].shape[2]
            self.jobs.append((len(lefts), m, len(rights), n))
            self.scratch.append(pltpu.VMEM((lefts[0].shape[0], m, 256), BF16))
            self.scratch.append(pltpu.VMEM((rights[0].shape[0], 256, n), BF16))
            rows += m * (n // 128)
        self.extra = extra is not None
        if self.extra:
            self.operands += list(extra)
            self.scratch.append(pltpu.VMEM((2, 2, 16, 128), BF16))
            rows += 16
        pieces = -(-rows // 256)
        self.sizes = ((pieces + 1) // 2 * 16, pieces // 2 * 16)
        self.used = 16 * sum(self.sizes)
        self.scratch.append(pltpu.VMEM((2, self.used, 128), BF16))
        for size in self.sizes:
            self.scratch += [
                pltpu.VMEM((3, 4, 2, size, 128), BF16),
                pltpu.VMEM((4, 2, size, 128), BF16),
                pltpu.VMEM((3, 2, size, 128), BF16),
                pltpu.VMEM((2, size, 128), BF16),
                pltpu.VMEM((4, size, 128), BF16),
            ]
        self.locals = 2 * len(jobs) + 1
        self.copies = 2 * len(jobs) + 1 + 24 + 6 + 6
        self.fin_shape = (sum(self.sizes), 128)

    def bind(self, me, sems, local, operands, scratch, fin):
        operands, scratch = list(operands), list(scratch)
        self.me, self.sems, self.local, self.fin = me, sems, local, fin
        self.sources, self.buffers = [], []
        for lefts, _, rights, _ in self.jobs:
            left, right = pop(operands, lefts), pop(operands, rights)
            self.sources.append((left[0], left[-1], right[0], right[-1]))
            self.buffers.append(pop(scratch, 2))
        if self.extra:
            self.extra_refs = operands
            self.extra_buffer = scratch.pop(0)
        self.grads = scratch.pop(0)
        self.parts = [pop(scratch, 5) for _ in self.sizes]
        xs = [(d, at, device(me, x=at)) for d, at in around(me, "x")]
        zs = [(d, at, device(me, z=at)) for d, at in around(me, "z")]
        x, z = me["x"], me["z"]
        self.plans = (
            (0, self.sizes[0], xs, zs, x, z),
            (16 * self.sizes[0], self.sizes[1], zs, xs, z, x),
        )
        self.first, self.second, self.third = {}, {}, {}

    def trade(self):
        mate = device(self.me, c=1 - self.me["c"])
        push = self.sems.push
        self.mine, self.traded = [], []

        def keep(src, dst):
            copy = pltpu.make_async_copy(src, dst, self.local.at[len(self.mine)])
            copy.start()
            self.mine.append(copy)

        here_, there = pl.ds(0, 128), pl.ds(128, 128)
        for (lm, lt, rm, rt), (lb, rb) in zip(self.sources, self.buffers):
            self.traded.append(push(lt, lb.at[:, :, there], mate))
            self.traded.append(push(rt, rb.at[:, there], mate))
            keep(lm, lb.at[:, :, here_])
            keep(rm, rb.at[:, here_])
        if self.extra:
            self.traded.append(push(self.extra_refs[1], self.extra_buffer.at[1], mate))
            keep(self.extra_refs[0], self.extra_buffer.at[0])

    def multiply(self):
        for copy in self.mine:
            copy.wait()
        for copy in self.traded:
            copy.wait_recv()
        base, grads = 0, self.grads
        for (_, m, _, n), (lb, rb) in zip(self.jobs, self.buffers):
            width = 256 if n % 256 == 0 else 128
            for s in range(2):
                left = lb[min(s, lb.shape[0] - 1)]

                def block(i, _, left=left, rb=rb, s=s, m=m, width=width, base=base):
                    at = pl.multiple_of(i * width, 128)
                    right = rb[min(s, rb.shape[0] - 1), :, pl.ds(at, width)]
                    result = dot_nn(left, right).astype(BF16)
                    for w in range(width // 128):
                        to = pl.multiple_of(base + (i * (width // 128) + w) * m, 16)
                        grads[s, pl.ds(to, m), :] = result[:, w * 128 : (w + 1) * 128]
                    return 0

                lax.fori_loop(0, n // width, block, 0)
            base += m * (n // 128)
        if self.extra:
            for s in range(2):
                both = self.extra_buffer[0, s].astype(F32) + self.extra_buffer[1, s].astype(F32)
                grads[s, pl.ds(base, 16), :] = both.astype(BF16)
            base += 16
        if base < self.used:
            for s in range(2):
                grads[s, pl.ds(base, self.used - base), :] = jnp.zeros(
                    (self.used - base, 128), BF16
                )
        for k in (1, 3, 2, 0):
            for n, (lo, size, ring, _, _, j_me) in enumerate(self.plans):
                r1 = self.parts[n][0]
                j = lax.rem(j_me + k, 4)
                for d, at, dev in ring:
                    src = grads.at[:, pl.ds(pl.multiple_of(lo + (at * 4 + j) * size, 16), size)]
                    self.first[n, k, d] = self.sems.push(src, r1.at[d - 1, k], dev)

    def fold_first(self, k):
        for n, (lo, size, _, cross, i_me, j_me) in enumerate(self.plans):
            r1, s1, r2, _, _ = self.parts[n]
            j = lax.rem(j_me + k, 4)
            for d in (1, 2, 3):
                self.first[n, k, d].wait_recv()
            for s in range(2):
                own = self.grads[s, pl.ds(pl.multiple_of(lo + (i_me * 4 + j) * size, 16), size)]
                total = own.astype(F32)
                for d in (0, 1, 2):
                    total = total + r1[d, k, s].astype(F32)
                s1[k, s] = total.astype(BF16)
            if k:
                dev = [dev for d, _, dev in cross if d == k][0]
                self.second[n, k] = self.sems.push(s1.at[k], r2.at[k - 1], dev)

    def fold_second(self):
        me, push = self.me, self.sems.push
        yh, yl = me["yh"], me["yl"]
        for n in (0, 1):
            _, s1, r2, s2, r3 = self.parts[n]
            for k in (1, 2, 3):
                self.second[n, k].wait_recv()
            for s in range(2):
                total = s1[0, s].astype(F32)
                for d in (0, 1, 2):
                    total = total + r2[d, s].astype(F32)
                s2[s] = total.astype(BF16)
            slot = r3.at[yl * 2 + yh]
            self.third[n, 0] = push(s2.at[1 - yl], slot, device(me, yl=1 - yl))
            self.third[n, 1] = push(s2.at[1 - yl], slot, device(me, yl=1 - yl, yh=1 - yh))
            self.third[n, 2] = push(s2.at[yl], slot, device(me, yh=1 - yh))

    def fold_third(self):
        yh, yl = self.me["yh"], self.me["yl"]
        at = 0
        for n, size in enumerate(self.sizes):
            _, _, _, s2, r3 = self.parts[n]
            r3[yl * 2 + yh] = s2[yl]
            for i in (0, 1, 2):
                self.third[n, i].wait_recv()
            total = r3[0].astype(F32)
            for i in (1, 2, 3):
                total = total + r3[i].astype(F32)
            self.fin[pl.ds(at, size), :] = total.astype(BF16)
            at += size

    def end(self):
        for group in (self.traded, self.first.values(), self.second.values(), self.third.values()):
            for copy in group:
                copy.wait_send()


class Spread:
    COPIES = 30

    def __init__(self, me, sems, local, fin, out, sizes):
        self.sems = sems
        xs = [(d, at, device(me, x=at)) for d, at in around(me, "x")]
        zs = [(d, at, device(me, z=at)) for d, at in around(me, "z")]
        x, z = me["x"], me["z"]
        self.plans = ((0, sizes[0], xs, zs, x, z), (16 * sizes[0], sizes[1], zs, xs, z, x))
        self.out, self.kept, self.cross, self.ring = out, [], {}, {}
        at = 0
        for n, (lo, size, ring, cross, _, j_me) in enumerate(self.plans):
            src = fin.at[pl.ds(at, size)]
            span = self.span(n, j_me)
            copy = pltpu.make_async_copy(src, span, local.at[n])
            copy.start()
            self.kept.append(copy)
            for d, _, dev in cross:
                self.cross[n, d] = sems.push(src, span, dev)
            for d, _, dev in ring:
                self.ring[n, 0, d] = sems.push(src, span, dev)
            at += size

    def span(self, n, j):
        lo, size, _, _, i_me, _ = self.plans[n]
        return self.out.at[pl.ds(pl.multiple_of(lo + (i_me * 4 + j) * size, 16), size)]

    def relay(self):
        for back in (3, 1, 2):
            for n, (_, _, ring, _, _, j_me) in enumerate(self.plans):
                self.cross[n, back].wait_recv()
                span = self.span(n, lax.rem(j_me + 4 - back, 4))
                for d, _, dev in ring:
                    self.ring[n, back, d] = self.sems.push(span, span, dev)

    def end(self):
        for copy in self.ring.values():
            copy.wait_recv()
        for copy in self.kept:
            copy.wait()
        for copy in list(self.cross.values()) + list(self.ring.values()):
            copy.wait_send()


def greet_axes(me):
    flip = 1 - me["yl"]
    greet(
        [device(me, yl=flip), device(me, yl=flip, yh=1 - me["yh"]), device(me, c=1 - me["c"])]
        + [device(me, yh=1 - me["yh"])]
        + [device(me, x=at) for _, at in around(me, "x")]
        + [device(me, z=at) for _, at in around(me, "z")]
    )


def backward_kernel(reduction, *refs):
    refs = list(refs)
    q, qt, do, dot, o, logs, kv, own, flag, left, right, limit = pop(refs, 12)
    operands = pop(refs, len(reduction.operands))
    dq_ref, dkv_own, fin = pop(refs, 3)
    dkv, kk, vv = pop(refs, 3)
    scatter_scratch = pop(refs, len(Scatter.SCRATCH))
    reduce_scratch = pop(refs, len(reduction.scratch))
    send, recv, local = refs
    me = here()
    greet_axes(me)
    sems = Sems(send, recv)
    reduction.bind(me, sems, local, operands, reduce_scratch, fin)
    scatter = Scatter(me, sems, dkv, dkv_own, scatter_scratch)
    flat = dkv.reshape(CTX, 640, 128)

    def one(head, _):
        dq_ref[head] = attend_back_head(
            head, q[head], qt[head], do[head], dot[head], o[head], logs[head], kv, own, flag,
            left, right, limit, flat, kk, vv,
        )
        return 0

    reduction.trade()
    reduction.multiply()
    lax.fori_loop(0, KV_HEADS, one, 0)
    scatter.start()
    for k in (1, 3, 2, 0):
        reduction.fold_first(k)
    scatter.middle(0)
    scatter.middle(1)
    reduction.fold_second()
    scatter.last(0)
    scatter.last(1)
    reduction.fold_third()
    scatter.end()
    reduction.end()


def backward(q, do, o, logs, kv, own, plan, reduction, collective_id):
    flags, left, right, limits = plan
    copies = reduction.copies + Scatter.COPIES
    return pl.pallas_call(
        functools.partial(backward_kernel, reduction),
        out_shape=[
            jax.ShapeDtypeStruct((KV_HEADS, ROWS, 128), F32),
            jax.ShapeDtypeStruct((640, 128), F32),
            jax.ShapeDtypeStruct(reduction.fin_shape, BF16),
        ],
        in_specs=[VM] * 12 + [ANY] * len(reduction.operands),
        out_specs=[VM, VM, VM],
        scratch_shapes=[
            pltpu.VMEM((4, 2, 4, 640, 128), BF16),
            pltpu.VMEM((KEYS, 128), BF16),
            pltpu.VMEM((KEYS, 128), BF16),
            *Scatter.SCRATCH,
            *reduction.scratch,
            pltpu.SemaphoreType.DMA((copies,)),
            pltpu.SemaphoreType.DMA((copies,)),
            pltpu.SemaphoreType.DMA((reduction.locals,)),
        ],
        compiler_params=pltpu.CompilerParams(
            collective_id=collective_id, has_side_effects=True, vmem_limit_bytes=BIG
        ),
        name="backward",
    )(
        q, jnp.swapaxes(q, 1, 2), do, jnp.swapaxes(do, 1, 2), o, logs, kv, own,
        flags, left, right, limits, *reduction.operands,
    )


def finish_kernel(reduction, sizes, *refs):
    refs = list(refs)
    done = refs.pop(0)
    operands = pop(refs, len(reduction.operands))
    out_done, out = pop(refs, 2)
    fin = refs.pop(0)
    reduce_scratch = pop(refs, len(reduction.scratch))
    send, recv, local = refs
    me = here()
    greet_axes(me)
    sems = Sems(send, recv)
    reduction.bind(me, sems, local, operands, reduce_scratch, fin)
    reduction.trade()
    spread = Spread(me, sems, local.at[pl.ds(reduction.locals, 2)], done, out_done, sizes)
    reduction.multiply()
    spread.relay()
    for k in (1, 3, 2, 0):
        reduction.fold_first(k)
    reduction.fold_second()
    reduction.fold_third()
    last = Spread(me, sems, local.at[pl.ds(reduction.locals + 2, 2)], fin, out, reduction.sizes)
    last.relay()
    spread.end()
    last.end()
    reduction.end()


def finish(done, sizes, used, reduction, collective_id):
    copies = reduction.copies + 2 * Spread.COPIES
    return pl.pallas_call(
        functools.partial(finish_kernel, reduction, sizes),
        out_shape=[
            jax.ShapeDtypeStruct((used, 128), BF16),
            jax.ShapeDtypeStruct((reduction.used, 128), BF16),
        ],
        in_specs=[VM] + [ANY] * len(reduction.operands),
        out_specs=[ANY, ANY],
        scratch_shapes=[
            pltpu.VMEM(reduction.fin_shape, BF16),
            *reduction.scratch,
            pltpu.SemaphoreType.DMA((copies,)),
            pltpu.SemaphoreType.DMA((copies,)),
            pltpu.SemaphoreType.DMA((reduction.locals + 4,)),
        ],
        compiler_params=pltpu.CompilerParams(
            collective_id=collective_id, has_side_effects=True, vmem_limit_bytes=BIG
        ),
        name="finish",
    )(done, *reduction.operands)


def pick(a, axis, core):
    return lax.dynamic_index_in_dim(a, core, axis, keepdims=False)


def left_shards(a, core):
    t = a.T.reshape(2, 2, 240, TOK)
    return pick(t, 1, core), pick(t, 1, 1 - core)


def right_shards(a, core):
    t = a.reshape(TOK, 2, 2, a.shape[1] // 4).transpose(1, 2, 0, 3)
    return pick(t, 1, core), pick(t, 1, 1 - core)


def pad_lanes(a):
    extra = -a.shape[1] % 128
    return jnp.pad(a, ((0, 0), (0, extra)))


def unblock(flat, m, columns):
    blocks = -(-columns // 128)
    a = flat[: m * blocks].reshape(blocks, m, 128).transpose(1, 0, 2).reshape(m, blocks * 128)
    return a[:, :columns].astype(F32), flat[m * blocks :]


def norm_forward(values, gain):
    inv_rms = lax.rsqrt(jnp.mean(values * values, axis=-1, keepdims=True) + EPSILON)
    return values * inv_rms * gain, inv_rms


def norm_backward(values, inv_rms, gain, grad_normed):
    scaled = grad_normed * gain
    grad_values = inv_rms * scaled - values * inv_rms * inv_rms * inv_rms * jnp.mean(
        scaled * values, axis=-1, keepdims=True
    )
    grad_gain = jnp.sum(grad_normed * values * inv_rms, axis=0)
    return grad_values, grad_gain


def rope_tables(positions, half_dim):
    frequency = BASE ** (-jnp.arange(half_dim, dtype=F32) / half_dim)
    angles = positions.astype(F32)[:, None] * frequency[None, :]
    cosine = jnp.concatenate([jnp.cos(angles), jnp.cos(angles)], axis=-1)[:, None, :]
    sine = jnp.concatenate([jnp.sin(angles), jnp.sin(angles)], axis=-1)[:, None, :]
    return cosine, sine


def rotate(values, cosine, sine):
    half_dim = values.shape[-1] // 2
    turned = jnp.concatenate([-values[..., half_dim:], values[..., :half_dim]], axis=-1)
    return values * cosine + turned * sine


def dot(a, b):
    return jnp.dot(a, b, preferred_element_type=F32)


def swap_rows(a, swap):
    return jnp.where(swap, jnp.concatenate([a[HALF:], a[:HALF]], axis=0), a)


def on_device(
    tokens, cotangent, block_table, attn_gain, w_query, w_key, w_value, w_out, mlp_gain,
    w_gate, w_up, w_down,
):
    ctx = lax.axis_index("ctx")
    core = lax.axis_index("fsdp") % 2
    gains = jnp.pad(jnp.stack([attn_gain, mlp_gain]), ((0, 14), (0, 16)))
    qkv_shard = jnp.concatenate([w_query, w_key, w_value], axis=1)
    gains_all, qkv_w = gather_weights((gains, qkv_shard), 0)
    gains_all = gains_all.reshape(4, 16, 256)[:, :2, :240].astype(F32)
    gain_a = gains_all[:, 0].reshape(D)
    gain_b = gains_all[:, 1].reshape(D)

    own_blocks = lax.dynamic_slice_in_dim(block_table, 2 * ctx, 2)
    swap = own_blocks[0] > own_blocks[1]
    early = jnp.min(own_blocks)
    offsets = jnp.arange(HALF, dtype=jnp.int32)
    positions = jnp.concatenate([early * HALF + offsets, (63 - early) * HALF + offsets])
    cosine, sine = rope_tables(positions, HEAD // 2)
    plan = tile_plan(block_table, ctx)

    resid_in = swap_rows(tokens[0], swap).astype(F32)
    grad_low = swap_rows(cotangent[0], swap)
    normed_a, inv_a = norm_forward(resid_in, gain_a)
    normed_a_low = normed_a.astype(BF16)
    qkv = dot(normed_a_low, qkv_w)
    value_low = qkv[:, 1280:].astype(BF16)
    queries = rotate(qkv[:, :960].reshape(TOK, HEADS, HEAD), cosine, sine).astype(BF16)
    keys = rotate(qkv[:, 960:1280].reshape(TOK, KV_HEADS, HEAD), cosine, sine).astype(BF16)
    q_rows = to_rows(queries)
    own_kv = jnp.concatenate([to_wire(keys), to_wire(value_low)], axis=0)
    o_rows, logs, kv, out_w, gate_w, up_w, down_w = forward(
        q_rows, own_kv, plan, (w_out, w_gate, w_up, w_down), 1
    )
    kv = kv.reshape(CTX, 640, 128)
    attended_low = from_rows(o_rows).astype(BF16)

    middle = resid_in + dot(attended_low, out_w)
    normed_b, inv_b = norm_forward(middle, gain_b)
    normed_b_low = normed_b.astype(BF16)
    gate_pre = dot(normed_b_low, gate_w)
    up_pre = dot(normed_b_low, up_w)
    sigmoid_gate = jax.nn.sigmoid(gate_pre)
    silu_gate = gate_pre * sigmoid_gate
    hidden_low = (silu_gate * up_pre).astype(BF16)
    layer_out = middle + dot(hidden_low, down_w)

    grad_hidden = dot_nt(grad_low, down_w)
    grad_gate_pre = (
        grad_hidden * up_pre * sigmoid_gate * (1.0 + gate_pre * (1.0 - sigmoid_gate))
    ).astype(BF16)
    grad_up_pre = (grad_hidden * silu_gate).astype(BF16)
    grad_norm_b = dot_nt(grad_gate_pre, gate_w) + dot_nt(grad_up_pre, up_w)
    grad_mid_norm, grad_gain_b = norm_backward(middle, inv_b, gain_b, grad_norm_b)
    grad_middle = grad_low.astype(F32) + grad_mid_norm
    grad_branch = grad_middle.astype(BF16)
    do_rows = to_rows(dot_nt(grad_branch, out_w).astype(BF16))

    ready = Reduction(
        (
            (
                left_shards(normed_b_low, core),
                jnp.concatenate([grad_gate_pre, grad_up_pre], axis=1)[None],
            ),
            (grad_low.T[None], right_shards(hidden_low, core)),
            (left_shards(attended_low, core), pad_lanes(grad_branch)[None]),
        ),
        None,
    )
    dq_rows, dkv, done = backward(q_rows, do_rows, o_rows, logs, kv, own_kv, plan, ready, 2)
    dkv = dkv.T
    grad_value_low = dkv[:, 320:].astype(BF16)
    grad_key_pre = rotate(dkv[:, :320].reshape(TOK, KV_HEADS, HEAD), cosine, -sine)
    grad_query_pre = rotate(from_rows(dq_rows).reshape(TOK, HEADS, HEAD), cosine, -sine)
    grad_qkv = jnp.concatenate(
        [
            grad_query_pre.reshape(TOK, 960).astype(BF16),
            grad_key_pre.reshape(TOK, 320).astype(BF16),
            grad_value_low,
        ],
        axis=1,
    )
    grad_norm_a = dot_nt(grad_qkv, qkv_w)
    grad_in_norm, grad_gain_a = norm_backward(resid_in, inv_a, gain_a, grad_norm_a)
    grad_tokens = grad_middle + grad_in_norm

    gain_rows = jnp.stack([grad_gain_a, grad_gain_b]).reshape(2, 4, 240).transpose(1, 0, 2)
    gain_rows = jnp.pad(gain_rows, ((0, 0), (0, 0), (0, 16))).reshape(2, 2, 4, 128).astype(BF16)
    gain_rows = jnp.pad(gain_rows, ((0, 0), (0, 0), (0, 12), (0, 0)))
    late = Reduction(
        ((left_shards(normed_a_low, core), pad_lanes(grad_qkv)[None]),),
        (pick(gain_rows, 1, core), pick(gain_rows, 1, 1 - core)),
    )
    flat_done, flat = finish(done, ready.sizes, ready.used, late, 3)
    shard_g, flat_done = unblock(flat_done, 240, 2560)
    shard_u, flat_done = unblock(flat_done, 240, 2560)
    shard_d, flat_done = unblock(flat_done, 960, 640)
    shard_o, _ = unblock(flat_done, 240, 960)
    shard_qkv, flat = unblock(flat, 240, 1600)
    shard_gains = flat[:4].reshape(2, 256)[:, :240].astype(F32)
    return (
        swap_rows(layer_out.astype(BF16), swap)[None],
        swap_rows(grad_tokens, swap)[None],
        shard_gains[0],
        shard_qkv[:, :960],
        shard_qkv[:, 960:1280],
        shard_qkv[:, 1280:],
        shard_o,
        shard_gains[1],
        shard_g,
        shard_u,
        shard_d.T,
    )


def solution(mesh):
    rows, cut = P("fsdp", "ctx", None), P("fsdp", None)
    return jax.shard_map(
        on_device,
        mesh=mesh,
        in_specs=(rows, rows, P(), P("fsdp"), cut, cut, cut, cut, P("fsdp"), cut, cut, cut),
        out_specs=(rows, rows, P("fsdp"), cut, cut, cut, cut, P("fsdp"), cut, cut, cut),
        check_vma=False,
    )
```

```python
import functools
import math

import jax
import jax.numpy as jnp
from jax import lax
from jax.experimental import pallas as pl
from jax.experimental.pallas import tpu as pltpu
from jax.sharding import PartitionSpec as P

D = 960
HEADS = 15
KV_HEADS = 5
GROUP = 3
HEAD = 64
FF = 2560
TOK = 128
HALF = 64
CTX = 32
TILES = 33
KEYS = TILES * 128
SCALE = HEAD ** (-0.5)
EPSILON = 1e-05
BASE = 10000.0
LOG2E = math.log2(math.e)
NEG = -1e30
MESH = pl.DeviceIdType.MESH
ANY = pl.BlockSpec(memory_space=pl.ANY)
VM = pl.BlockSpec(memory_space=pltpu.VMEM)
BIG = 56 * 2**20
F32 = jnp.float32
BF16 = jnp.bfloat16


def here():
    ctx = lax.axis_index("ctx")
    shard = lax.axis_index("fsdp")
    return {
        "z": ctx // 8,
        "yh": (ctx // 4) % 2,
        "x": ctx % 4,
        "yl": shard // 2,
        "c": shard % 2,
    }


def device(place, **moved):
    p = {**place, **moved}
    return (p["z"] * 8 + p["yh"] * 4 + p["x"], p["yl"] * 2 + p["c"])


def greet(devices):
    sem = pltpu.get_barrier_semaphore()
    for d in devices:
        pl.semaphore_signal(sem, inc=1, device_id=d, device_id_type=MESH)
    pl.semaphore_wait(sem, len(devices))


class Sems:
    def __init__(self, send, recv):
        self.send, self.recv, self.at = send, recv, 0

    def push(self, src, dst, dev):
        copy = pltpu.make_async_remote_copy(
            src_ref=src,
            dst_ref=dst,
            send_sem=self.send.at[self.at],
            recv_sem=self.recv.at[self.at],
            device_id=dev,
            device_id_type=MESH,
        )
        self.at += 1
        copy.start()
        return copy


def start_gather(me, sems, local, arrays):
    f = me["yl"] * 2 + me["c"]
    near = device(me, yl=1 - me["yl"])
    far = device(me, yl=1 - me["yl"], yh=1 - me["yh"])
    mate = device(me, c=1 - me["c"])
    parts, kept, own = [], [], []
    for i, (a, b) in enumerate(arrays):
        rows = a.shape[0]
        first = rows // 32 * 16 if i % 2 else (rows + 31) // 32 * 16
        for lo, size, dev in ((0, first, near), (first, rows - first, far)):
            if size:
                src = a.at[pl.ds(lo, size)]
                dst = b.at[pl.ds(pl.multiple_of(f * rows + lo, 16), size)]
                parts.append((sems.push(src, dst, dev), b, rows, lo, size))
    for i, (a, b) in enumerate(arrays):
        rows = a.shape[0]
        dst = b.at[pl.ds(pl.multiple_of(f * rows, 16), rows)]
        kept.append(sems.push(a, dst, mate))
        copy = pltpu.make_async_copy(a, dst, local.at[i])
        copy.start()
        own.append(copy)
    return parts, kept, own


def relay_gather(me, sems, started):
    parts, kept, _ = started
    across = (1 - me["yl"]) * 2 + me["c"]
    mate = device(me, c=1 - me["c"])
    for copy, b, rows, lo, size in parts:
        copy.wait_recv()
        span = b.at[pl.ds(pl.multiple_of(across * rows + lo, 16), size)]
        kept.append(sems.push(span, span, mate))


def end_gather(started):
    parts, kept, own = started
    for copy in own:
        copy.wait()
    for copy in kept:
        copy.wait()
    for copy, *_ in parts:
        copy.wait_send()


def gather_kernel(count, *refs):
    arrays = list(zip(refs[:count], refs[count : 2 * count]))
    send, recv, local = refs[2 * count :]
    me = here()
    flip = 1 - me["yl"]
    greet((device(me, yl=flip), device(me, yl=flip, yh=1 - me["yh"]), device(me, c=1 - me["c"])))
    sems = Sems(send, recv)
    started = start_gather(me, sems, local, arrays)
    relay_gather(me, sems, started)
    end_gather(started)


def gathered(arrays):
    return [jax.ShapeDtypeStruct((4 * a.shape[0], *a.shape[1:]), a.dtype) for a in arrays]


def gather_weights(arrays, collective_id):
    n = len(arrays)
    return pl.pallas_call(
        functools.partial(gather_kernel, n),
        out_shape=gathered(arrays),
        in_specs=[VM] * n,
        out_specs=[ANY] * n,
        scratch_shapes=[
            pltpu.SemaphoreType.DMA((5 * n,)),
            pltpu.SemaphoreType.DMA((5 * n,)),
            pltpu.SemaphoreType.DMA((n,)),
        ],
        compiler_params=pltpu.CompilerParams(
            collective_id=collective_id, has_side_effects=True, vmem_limit_bytes=BIG
        ),
        name="gather_weights",
    )(*arrays)


def around(me, axis):
    return [(d, lax.rem(me[axis] + d, 4)) for d in (1, 3, 2)]


def gather_kv(me, sems, kv, out, once_across):
    x, yh, z = me["x"], me["yh"], me["z"]
    other = device(me, yh=1 - yh)
    xs = [device(me, x=at) for _, at in around(me, "x")]
    zs = [device(me, z=at) for _, at in around(me, "z")]
    key, value = pl.ds(0, 320), pl.ds(320, 320)
    step1 = [sems.push(kv.at[p], out.at[z, yh, x, p], other) for p in (key, value)]
    step2 = {}
    step2[0, 0] = [sems.push(kv.at[key], out.at[z, yh, x, key], dev) for dev in xs]
    step2[1, 0] = [sems.push(kv.at[value], out.at[z, yh, x, value], dev) for dev in zs]
    out[z, yh, x] = kv[...]
    step3 = []
    for hop in (0, 1):
        row = yh if hop == 0 else 1 - yh
        for axis, (devs, p) in enumerate(((zs, key), (xs, value))):
            for c in step2[axis, hop]:
                c.wait_recv()
            span = out.at[z, row, :, key] if axis == 0 else out.at[:, row, x, value]
            for dev in devs:
                step3.append(sems.push(span, span, dev))
        if hop == 0:
            for axis, (devs, p) in enumerate(((xs, key), (zs, value))):
                step1[axis].wait_recv()
                span = out.at[z, 1 - yh, x, p]
                step2[axis, 1] = [sems.push(span, span, dev) for dev in devs]
            once_across()
    for c in step3:
        c.wait_recv()
    return step1 + sum(step2.values(), []) + step3


class Scatter:
    COPIES = 26
    SCRATCH = [
        pltpu.VMEM((3, 2, 4, 320, 128), BF16),
        pltpu.VMEM((3, 2, 4, 320, 128), BF16),
        pltpu.VMEM((2, 4, 320, 128), BF16),
        pltpu.VMEM((2, 4, 320, 128), BF16),
        pltpu.VMEM((3, 2, 320, 128), BF16),
        pltpu.VMEM((3, 2, 320, 128), BF16),
        pltpu.VMEM((2, 320, 128), BF16),
        pltpu.VMEM((2, 320, 128), BF16),
    ]

    def __init__(self, me, sems, part, out, scratch):
        self.me, self.sems, self.part, self.out = me, sems, part, out
        r1a, r1b, s1a, s1b, r2a, r2b, self.s2, self.r3 = scratch
        self.r1, self.s1, self.r2 = (r1a, r1b), (s1a, s1b), (r2a, r2b)
        self.xs = [(d, at, device(me, x=at)) for d, at in around(me, "x")]
        self.zs = [(d, at, device(me, z=at)) for d, at in around(me, "z")]
        self.rows = (1 - me["yh"], me["yh"])
        self.first, self.second, self.third = {}, {}, []

    def start(self):
        x, z, part, push = self.me["x"], self.me["z"], self.part, self.sems.push
        key, value = pl.ds(0, 320), pl.ds(320, 320)
        for r, row in enumerate(self.rows):
            for d, at, dev in self.zs:
                src = part.at[at, row, :, key]
                self.first[0, r, d] = push(src, self.r1[0].at[d - 1, r], dev)
            for d, at, dev in self.xs:
                src = part.at[:, row, at, value]
                self.first[1, r, d] = push(src, self.r1[1].at[d - 1, r], dev)

    def middle(self, r):
        x, z, part, row = self.me["x"], self.me["z"], self.part, self.rows[r]
        for axis in (0, 1):
            r1, s1, r2 = self.r1[axis], self.s1[axis], self.r2[axis]
            for d in (1, 2, 3):
                self.first[axis, r, d].wait_recv()
            for i in range(4):
                own = part[z, row, i, 0:320] if axis == 0 else part[i, row, x, 320:640]
                total = own.astype(F32)
                for d in (0, 1, 2):
                    total = total + r1[d, r, i].astype(F32)
                s1[r, i] = total.astype(BF16)
            for d, at, dev in (self.xs, self.zs)[axis]:
                self.second[axis, r, d] = self.sems.push(s1.at[r, at], r2.at[d - 1, r], dev)

    def last(self, r):
        other = device(self.me, yh=1 - self.me["yh"])
        for axis in (0, 1):
            s1, r2 = self.s1[axis], self.r2[axis]
            at = self.me["x"] if axis == 0 else self.me["z"]
            for d in (1, 2, 3):
                self.second[axis, r, d].wait_recv()
            total = s1[r, at].astype(F32)
            for d in (0, 1, 2):
                total = total + r2[d, r].astype(F32)
            if r == 0:
                self.s2[axis] = total.astype(BF16)
                self.third.append(self.sems.push(self.s2.at[axis], self.r3.at[axis], other))
            else:
                self.out[pl.ds(axis * 320, 320), :] = total

    def end(self):
        for axis in (0, 1):
            self.third[axis].wait_recv()
            span = pl.ds(axis * 320, 320)
            self.out[span, :] = self.out[span, :] + self.r3[axis].astype(F32)
        for c in list(self.first.values()) + list(self.second.values()) + self.third:
            c.wait_send()


def build_tiles(head, kv_ref, own_ref, left_ref, tiles_ref, base):
    lane = lax.broadcasted_iota(jnp.int32, (HALF, 128), 1)
    start = pl.multiple_of(base + head * HALF, HALF)

    def one(i, _):
        block = kv_ref[i, pl.ds(start, HALF), :].astype(F32)
        top = jnp.where(lane < HALF, block, 0.0)
        low = pltpu.roll(block, HALF, 1) * left_ref[pl.ds(i, 1), :]
        at = pl.multiple_of(i * 128, 128)
        tiles_ref[pl.ds(at, 128), :] = jnp.concatenate([top, low], axis=0).astype(BF16)
        return 0

    lax.fori_loop(0, CTX, one, 0, unroll=32)
    block = own_ref[pl.ds(start, HALF), :].astype(F32)
    top = jnp.where(lane < HALF, 0.0, pltpu.roll(block, HALF, 1))
    tiles_ref[pl.ds(CTX * 128, 128), :] = jnp.concatenate(
        [top, jnp.zeros_like(top)], axis=0
    ).astype(BF16)


def dot_nt(a, b):
    return lax.dot_general(a, b, (((1,), (1,)), ((), ())), preferred_element_type=F32)


def dot_nn(a, b):
    return lax.dot_general(a, b, (((1,), (0,)), ((), ())), preferred_element_type=F32)


ROWS = GROUP * HALF


def row_offset():
    return lax.rem(lax.broadcasted_iota(jnp.int32, (ROWS, 128), 0), HALF).astype(F32)


def attend_head(head, q, kv_ref, own_ref, flag_ref, left_ref, limit_ref, kk, vv):
    build_tiles(head, kv_ref, own_ref, left_ref, kk, 0)
    build_tiles(head, kv_ref, own_ref, left_ref, vv, 320)
    offset = row_offset()
    low = jnp.full((ROWS, 128), NEG, F32)
    s = dot_nt(q, kk[...]) * (SCALE * LOG2E)
    tiles = []
    top_l, top_e = low, low
    for i in range(TILES):
        tile = s[:, i * 128 : (i + 1) * 128]
        tile = jnp.where(limit_ref[i : i + 1, :] <= offset, tile, NEG)
        tiles.append(tile)
        late = flag_ref[i : i + 1, :] > 0.5
        top_l = jnp.maximum(top_l, jnp.where(late, tile, NEG))
        top_e = jnp.maximum(top_e, jnp.where(late, NEG, tile))
    max_l = jnp.broadcast_to(jnp.max(top_l, axis=1, keepdims=True), (ROWS, 128))
    max_e = jnp.broadcast_to(jnp.max(top_e, axis=1, keepdims=True), (ROWS, 128))
    sum_l = jnp.zeros((ROWS, 128), F32)
    sum_e = jnp.zeros((ROWS, 128), F32)
    probs = []
    for i in range(TILES):
        late = flag_ref[i : i + 1, :] > 0.5
        p = jnp.exp2(tiles[i] - jnp.where(late, max_l, max_e))
        p_l = jnp.where(late, p, 0.0)
        sum_l = sum_l + p_l
        sum_e = sum_e + (p - p_l)
        probs.append(p.astype(BF16))
    total = dot_nn(jnp.concatenate(probs, axis=1), vv[...])
    late = lax.broadcasted_iota(jnp.int32, (ROWS, 128), 1) < HALF
    row_sum = jnp.where(
        late, jnp.sum(sum_l, axis=1, keepdims=True), jnp.sum(sum_e, axis=1, keepdims=True)
    )
    return total / row_sum, jnp.where(late, max_l, max_e) + jnp.log2(row_sum)


def forward_kernel(count, q_ref, own_ref, flag_ref, left_ref, limit_ref, *refs):
    shards, refs = refs[:count], refs[count:]
    o_ref, l_ref, kv_out, *full = refs[: 3 + count]
    kv, kk, vv, send, recv, local = refs[3 + count :]
    me = here()
    greet_axes(me)
    sems = Sems(send, recv)
    started = []

    def start_weights():
        started.extend(start_gather(me, sems, local, list(zip(shards, full))))

    kv_copies = gather_kv(me, sems, own_ref, kv, start_weights)
    keep = pltpu.make_async_copy(kv, kv_out, local.at[count])
    keep.start()
    flat = kv.reshape(CTX, 640, 128)

    def one(head, _):
        o, logs = attend_head(
            head, q_ref[head], flat, own_ref, flag_ref, left_ref, limit_ref, kk, vv
        )
        o_ref[head] = o
        l_ref[head] = logs
        return 0

    lax.fori_loop(0, 3, one, 0)
    relay_gather(me, sems, started)
    lax.fori_loop(3, KV_HEADS, one, 0)
    end_gather(started)
    for copy in kv_copies:
        copy.wait_send()
    keep.wait()


def forward(q, own, plan, shards, collective_id):
    flags, left, _, limits = plan
    n = len(shards)
    copies = 5 * n + 26
    return pl.pallas_call(
        functools.partial(forward_kernel, n),
        out_shape=[jax.ShapeDtypeStruct((KV_HEADS, ROWS, 128), F32)] * 2
        + [jax.ShapeDtypeStruct((4, 2, 4, 640, 128), BF16)]
        + gathered(shards),
        in_specs=[VM] * (5 + n),
        out_specs=[VM, VM, ANY] + [ANY] * n,
        scratch_shapes=[
            pltpu.VMEM((4, 2, 4, 640, 128), BF16),
            pltpu.VMEM((KEYS, 128), BF16),
            pltpu.VMEM((KEYS, 128), BF16),
            pltpu.SemaphoreType.DMA((copies,)),
            pltpu.SemaphoreType.DMA((copies,)),
            pltpu.SemaphoreType.DMA((n + 1,)),
        ],
        compiler_params=pltpu.CompilerParams(
            collective_id=collective_id, has_side_effects=True, vmem_limit_bytes=BIG
        ),
        name="forward",
    )(q, own, flags, left, limits, *shards)


def attend_back_head(
    head, q, do, o, logs, kv_ref, own_ref, flag_ref, left_ref, right_ref, limit_ref,
    dkv_ref, kk, vv,
):
    build_tiles(head, kv_ref, own_ref, left_ref, kk, 0)
    build_tiles(head, kv_ref, own_ref, left_ref, vv, 320)
    offset = row_offset()
    lane = lax.broadcasted_iota(jnp.int32, (ROWS, 128), 1)
    product = do.astype(F32) * o
    shape = (ROWS, 128)
    delta_l = jnp.broadcast_to(
        jnp.sum(jnp.where(lane < HALF, product, 0.0), axis=1, keepdims=True), shape
    )
    delta_e = jnp.broadcast_to(
        jnp.sum(jnp.where(lane < HALF, 0.0, product), axis=1, keepdims=True), shape
    )
    log_l = jnp.broadcast_to(logs[:, 0:1], shape)
    log_e = jnp.broadcast_to(logs[:, HALF : HALF + 1], shape)
    k_rows = pl.ds(pl.multiple_of(head * HALF, HALF), HALF)
    v_rows = pl.ds(pl.multiple_of(320 + head * HALF, HALF), HALF)
    small = lax.broadcasted_iota(jnp.int32, (HALF, 128), 1)
    keys = kk[...]
    s = dot_nt(q, keys) * (SCALE * LOG2E)
    dp = dot_nt(do, vv[...])
    probs, scores = [], []
    for i in range(TILES):
        cut = slice(i * 128, (i + 1) * 128)
        late = flag_ref[i : i + 1, :] > 0.5
        tile = jnp.where(limit_ref[i : i + 1, :] <= offset, s[:, cut], NEG)
        p = jnp.exp2(tile - jnp.where(late, log_l, log_e))
        probs.append(p.astype(BF16))
        scores.append((p * (dp[:, cut] - jnp.where(late, delta_l, delta_e))).astype(BF16))
    ds = jnp.concatenate(scores, axis=1)
    dq = dot_nn(ds, keys) * SCALE
    dk = dot_nn(q.astype(F32).T.astype(BF16), ds) * SCALE
    dv = dot_nn(do.astype(F32).T.astype(BF16), jnp.concatenate(probs, axis=1))
    mine = lax.axis_index("ctx")
    for rows, both in ((k_rows, dk), (v_rows, dv)):
        for i in range(CTX):
            cut = slice(i * 128, (i + 1) * 128)
            top, bottom = both[0:HALF, cut], both[HALF:128, cut]
            total = (
                top * flag_ref[i : i + 1, :]
                + pltpu.roll(bottom, HALF, 1) * right_ref[i : i + 1, :]
            )
            dkv_ref[i, rows, :] = total.astype(BF16)
        bottom = both[HALF:128, CTX * 128 :]
        before = dkv_ref[mine, rows, :].astype(F32)
        dkv_ref[mine, rows, :] = (before + jnp.where(small < HALF, bottom, 0.0)).astype(BF16)
    return dq


def pop(refs, count):
    taken = refs[:count]
    del refs[:count]
    return taken


class Reduction:
    def __init__(self, jobs, extra):
        self.operands, self.jobs, self.scratch, rows = [], [], [], 0
        for left, right in jobs:
            self.operands += [left, right]
            m, n = left.shape[-2], right.shape[-1]
            self.jobs.append((left.ndim == 4, m, right.ndim == 4, n))
            self.scratch.append(pltpu.VMEM((left.shape[0], m, 256), BF16))
            self.scratch.append(pltpu.VMEM((right.shape[0], 256, n), BF16))
            rows += m * (n // 128)
        self.extra = extra is not None
        if self.extra:
            self.operands.append(extra)
            self.scratch.append(pltpu.VMEM((2, 2, 16, 128), BF16))
            rows += 16
        pieces = -(-rows // 256)
        self.sizes = ((pieces + 1) // 2 * 16, pieces // 2 * 16)
        self.used = 16 * sum(self.sizes)
        self.scratch.append(pltpu.VMEM((2, self.used, 128), BF16))
        for size in self.sizes:
            self.scratch += [
                pltpu.VMEM((3, 4, 2, size, 128), BF16),
                pltpu.VMEM((4, 2, size, 128), BF16),
                pltpu.VMEM((3, 2, size, 128), BF16),
                pltpu.VMEM((2, size, 128), BF16),
                pltpu.VMEM((4, size, 128), BF16),
            ]
        self.locals = 2 * len(jobs) + 1
        self.copies = 2 * len(jobs) + 1 + 24 + 6 + 6
        self.fin_shape = (sum(self.sizes), 128)

    def bind(self, me, sems, local, operands, scratch, fin):
        operands, scratch = list(operands), list(scratch)
        self.me, self.sems, self.local, self.fin = me, sems, local, fin
        self.sources, self.buffers = [], []
        core = me["c"]
        for cut_left, _, cut_right, _ in self.jobs:
            left, right = pop(operands, 2)
            lefts = (left.at[:, core], left.at[:, 1 - core]) if cut_left else (left, left)
            rights = (right.at[:, core], right.at[:, 1 - core]) if cut_right else (right, right)
            self.sources.append((*lefts, *rights))
            self.buffers.append(pop(scratch, 2))
        if self.extra:
            self.extra_refs = (operands[0].at[:, core], operands[0].at[:, 1 - core])
            self.extra_buffer = scratch.pop(0)
        self.grads = scratch.pop(0)
        self.parts = [pop(scratch, 5) for _ in self.sizes]
        xs = [(d, at, device(me, x=at)) for d, at in around(me, "x")]
        zs = [(d, at, device(me, z=at)) for d, at in around(me, "z")]
        x, z = me["x"], me["z"]
        self.plans = (
            (0, self.sizes[0], xs, zs, x, z),
            (16 * self.sizes[0], self.sizes[1], zs, xs, z, x),
        )
        self.first, self.second, self.third = {}, {}, {}

    def trade(self):
        mate = device(self.me, c=1 - self.me["c"])
        push = self.sems.push
        self.mine, self.traded = [], []

        def keep(src, dst):
            copy = pltpu.make_async_copy(src, dst, self.local.at[len(self.mine)])
            copy.start()
            self.mine.append(copy)

        here_, there = pl.ds(0, 128), pl.ds(128, 128)
        for (lm, lt, rm, rt), (lb, rb) in zip(self.sources, self.buffers):
            self.traded.append(push(lt, lb.at[:, :, there], mate))
            self.traded.append(push(rt, rb.at[:, there], mate))
            keep(lm, lb.at[:, :, here_])
            keep(rm, rb.at[:, here_])
        if self.extra:
            self.traded.append(push(self.extra_refs[1], self.extra_buffer.at[1], mate))
            keep(self.extra_refs[0], self.extra_buffer.at[0])

    def multiply(self):
        for copy in self.mine:
            copy.wait()
        for copy in self.traded:
            copy.wait_recv()
        base, grads = 0, self.grads
        for (_, m, _, n), (lb, rb) in zip(self.jobs, self.buffers):
            width = 256 if n % 256 == 0 else 128
            for s in range(2):
                left = lb[min(s, lb.shape[0] - 1)]

                def block(i, _, left=left, rb=rb, s=s, m=m, width=width, base=base):
                    at = pl.multiple_of(i * width, 128)
                    right = rb[min(s, rb.shape[0] - 1), :, pl.ds(at, width)]
                    result = dot_nn(left, right).astype(BF16)
                    for w in range(width // 128):
                        to = pl.multiple_of(base + (i * (width // 128) + w) * m, 16)
                        grads[s, pl.ds(to, m), :] = result[:, w * 128 : (w + 1) * 128]
                    return 0

                lax.fori_loop(0, n // width, block, 0)
            base += m * (n // 128)
        if self.extra:
            for s in range(2):
                both = self.extra_buffer[0, s].astype(F32) + self.extra_buffer[1, s].astype(F32)
                grads[s, pl.ds(base, 16), :] = both.astype(BF16)
            base += 16
        if base < self.used:
            for s in range(2):
                grads[s, pl.ds(base, self.used - base), :] = jnp.zeros(
                    (self.used - base, 128), BF16
                )
        for k in (1, 3, 2, 0):
            for n, (lo, size, ring, _, _, j_me) in enumerate(self.plans):
                r1 = self.parts[n][0]
                j = lax.rem(j_me + k, 4)
                for d, at, dev in ring:
                    src = grads.at[:, pl.ds(pl.multiple_of(lo + (at * 4 + j) * size, 16), size)]
                    self.first[n, k, d] = self.sems.push(src, r1.at[d - 1, k], dev)

    def fold_first(self, k):
        for n, (lo, size, _, cross, i_me, j_me) in enumerate(self.plans):
            r1, s1, r2, _, _ = self.parts[n]
            j = lax.rem(j_me + k, 4)
            for d in (1, 2, 3):
                self.first[n, k, d].wait_recv()
            for s in range(2):
                own = self.grads[s, pl.ds(pl.multiple_of(lo + (i_me * 4 + j) * size, 16), size)]
                total = own.astype(F32)
                for d in (0, 1, 2):
                    total = total + r1[d, k, s].astype(F32)
                s1[k, s] = total.astype(BF16)
            if k:
                dev = [dev for d, _, dev in cross if d == k][0]
                self.second[n, k] = self.sems.push(s1.at[k], r2.at[k - 1], dev)

    def fold_second(self):
        me, push = self.me, self.sems.push
        yh, yl = me["yh"], me["yl"]
        for n in (0, 1):
            _, s1, r2, s2, r3 = self.parts[n]
            for k in (1, 2, 3):
                self.second[n, k].wait_recv()
            for s in range(2):
                total = s1[0, s].astype(F32)
                for d in (0, 1, 2):
                    total = total + r2[d, s].astype(F32)
                s2[s] = total.astype(BF16)
            slot = r3.at[yl * 2 + yh]
            self.third[n, 0] = push(s2.at[1 - yl], slot, device(me, yl=1 - yl))
            self.third[n, 1] = push(s2.at[1 - yl], slot, device(me, yl=1 - yl, yh=1 - yh))
            self.third[n, 2] = push(s2.at[yl], slot, device(me, yh=1 - yh))

    def fold_third(self):
        yh, yl = self.me["yh"], self.me["yl"]
        at = 0
        for n, size in enumerate(self.sizes):
            _, _, _, s2, r3 = self.parts[n]
            r3[yl * 2 + yh] = s2[yl]
            for i in (0, 1, 2):
                self.third[n, i].wait_recv()
            total = r3[0].astype(F32)
            for i in (1, 2, 3):
                total = total + r3[i].astype(F32)
            self.fin[pl.ds(at, size), :] = total.astype(BF16)
            at += size

    def end(self):
        for group in (self.traded, self.first.values(), self.second.values(), self.third.values()):
            for copy in group:
                copy.wait_send()


class Spread:
    COPIES = 30

    def __init__(self, me, sems, local, fin, out, sizes):
        self.sems = sems
        xs = [(d, at, device(me, x=at)) for d, at in around(me, "x")]
        zs = [(d, at, device(me, z=at)) for d, at in around(me, "z")]
        x, z = me["x"], me["z"]
        self.plans = ((0, sizes[0], xs, zs, x, z), (16 * sizes[0], sizes[1], zs, xs, z, x))
        self.out, self.kept, self.cross, self.ring = out, [], {}, {}
        at = 0
        for n, (lo, size, ring, cross, _, j_me) in enumerate(self.plans):
            src = fin.at[pl.ds(at, size)]
            span = self.span(n, j_me)
            copy = pltpu.make_async_copy(src, span, local.at[n])
            copy.start()
            self.kept.append(copy)
            for d, _, dev in cross:
                self.cross[n, d] = sems.push(src, span, dev)
            for d, _, dev in ring:
                self.ring[n, 0, d] = sems.push(src, span, dev)
            at += size

    def span(self, n, j):
        lo, size, _, _, i_me, _ = self.plans[n]
        return self.out.at[pl.ds(pl.multiple_of(lo + (i_me * 4 + j) * size, 16), size)]

    def relay(self):
        for back in (3, 1, 2):
            for n, (_, _, ring, _, _, j_me) in enumerate(self.plans):
                self.cross[n, back].wait_recv()
                span = self.span(n, lax.rem(j_me + 4 - back, 4))
                for d, _, dev in ring:
                    self.ring[n, back, d] = self.sems.push(span, span, dev)

    def end(self):
        for copy in self.ring.values():
            copy.wait_recv()
        for copy in self.kept:
            copy.wait()
        for copy in list(self.cross.values()) + list(self.ring.values()):
            copy.wait_send()


def greet_axes(me):
    flip = 1 - me["yl"]
    greet(
        [device(me, yl=flip), device(me, yl=flip, yh=1 - me["yh"]), device(me, c=1 - me["c"])]
        + [device(me, yh=1 - me["yh"])]
        + [device(me, x=at) for _, at in around(me, "x")]
        + [device(me, z=at) for _, at in around(me, "z")]
    )


def backward_kernel(reduction, *refs):
    refs = list(refs)
    q, do, o, logs, kv, own, flag, left, right, limit = pop(refs, 10)
    operands = pop(refs, len(reduction.operands))
    dq_ref, dkv_own, fin = pop(refs, 3)
    dkv, kk, vv = pop(refs, 3)
    scatter_scratch = pop(refs, len(Scatter.SCRATCH))
    reduce_scratch = pop(refs, len(reduction.scratch))
    send, recv, local = refs
    me = here()
    greet_axes(me)
    sems = Sems(send, recv)
    reduction.bind(me, sems, local, operands, reduce_scratch, fin)
    scatter = Scatter(me, sems, dkv, dkv_own, scatter_scratch)
    flat = dkv.reshape(CTX, 640, 128)

    def one(head, _):
        dq_ref[head] = attend_back_head(
            head, q[head], do[head], o[head], logs[head], kv, own, flag,
            left, right, limit, flat, kk, vv,
        )
        return 0

    reduction.trade()
    reduction.multiply()
    lax.fori_loop(0, KV_HEADS, one, 0)
    scatter.start()
    for k in (1, 3, 2, 0):
        reduction.fold_first(k)
    scatter.middle(0)
    scatter.middle(1)
    reduction.fold_second()
    scatter.last(0)
    scatter.last(1)
    reduction.fold_third()
    scatter.end()
    reduction.end()


def backward(q, do, o, logs, kv, own, plan, reduction, collective_id):
    flags, left, right, limits = plan
    copies = reduction.copies + Scatter.COPIES
    return pl.pallas_call(
        functools.partial(backward_kernel, reduction),
        out_shape=[
            jax.ShapeDtypeStruct((KV_HEADS, ROWS, 128), F32),
            jax.ShapeDtypeStruct((640, 128), F32),
            jax.ShapeDtypeStruct(reduction.fin_shape, BF16),
        ],
        in_specs=[VM] * 10 + [ANY] * len(reduction.operands),
        out_specs=[VM, VM, VM],
        scratch_shapes=[
            pltpu.VMEM((4, 2, 4, 640, 128), BF16),
            pltpu.VMEM((KEYS, 128), BF16),
            pltpu.VMEM((KEYS, 128), BF16),
            *Scatter.SCRATCH,
            *reduction.scratch,
            pltpu.SemaphoreType.DMA((copies,)),
            pltpu.SemaphoreType.DMA((copies,)),
            pltpu.SemaphoreType.DMA((reduction.locals,)),
        ],
        compiler_params=pltpu.CompilerParams(
            collective_id=collective_id, has_side_effects=True, vmem_limit_bytes=BIG
        ),
        name="backward",
    )(
        q, do, o, logs, kv, own, flags, left, right, limits, *reduction.operands,
    )


def finish_kernel(reduction, sizes, *refs):
    refs = list(refs)
    done = refs.pop(0)
    operands = pop(refs, len(reduction.operands))
    out_done, out = pop(refs, 2)
    fin = refs.pop(0)
    reduce_scratch = pop(refs, len(reduction.scratch))
    send, recv, local = refs
    me = here()
    greet_axes(me)
    sems = Sems(send, recv)
    reduction.bind(me, sems, local, operands, reduce_scratch, fin)
    reduction.trade()
    spread = Spread(me, sems, local.at[pl.ds(reduction.locals, 2)], done, out_done, sizes)
    reduction.multiply()
    spread.relay()
    for k in (1, 3, 2, 0):
        reduction.fold_first(k)
    reduction.fold_second()
    reduction.fold_third()
    last = Spread(me, sems, local.at[pl.ds(reduction.locals + 2, 2)], fin, out, reduction.sizes)
    last.relay()
    spread.end()
    last.end()
    reduction.end()


def finish(done, sizes, used, reduction, collective_id):
    copies = reduction.copies + 2 * Spread.COPIES
    return pl.pallas_call(
        functools.partial(finish_kernel, reduction, sizes),
        out_shape=[
            jax.ShapeDtypeStruct((used, 128), BF16),
            jax.ShapeDtypeStruct((reduction.used, 128), BF16),
        ],
        in_specs=[VM] + [ANY] * len(reduction.operands),
        out_specs=[ANY, ANY],
        scratch_shapes=[
            pltpu.VMEM(reduction.fin_shape, BF16),
            *reduction.scratch,
            pltpu.SemaphoreType.DMA((copies,)),
            pltpu.SemaphoreType.DMA((copies,)),
            pltpu.SemaphoreType.DMA((reduction.locals + 4,)),
        ],
        compiler_params=pltpu.CompilerParams(
            collective_id=collective_id, has_side_effects=True, vmem_limit_bytes=BIG
        ),
        name="finish",
    )(done, *reduction.operands)


def low_lanes(rows):
    return lax.broadcasted_iota(jnp.int32, (rows, 128), 1) < HALF


def turn(tile):
    return pltpu.roll(tile, HALF, 1)


def heads_of_tile(tile):
    early, late = tile[:HALF], tile[HALF:]
    low = low_lanes(HALF)
    return jnp.where(low, late, turn(early)), jnp.where(low, turn(late), early)


def tile_of_heads(first, second):
    low = low_lanes(HALF)
    early = jnp.where(low, turn(first), second)
    late = jnp.where(low, first, turn(second))
    return jnp.concatenate([early, late], axis=0)


def put_heads(ref, values):
    for t in range(8):
        if t < 7:
            tile = values[:, t * 128 : (t + 1) * 128]
        else:
            last = values[:, 896:960]
            tile = jnp.concatenate([last, jnp.zeros_like(last)], axis=1)
        for i, block in enumerate(heads_of_tile(tile)):
            head = 2 * t + i
            if head < HEADS:
                at = head % GROUP * HALF
                ref[head // GROUP, at : at + HALF, :] = block.astype(ref.dtype)


def get_heads(ref):
    def block(head):
        if head == HEADS:
            return jnp.zeros((HALF, 128), F32)
        at = head % GROUP * HALF
        return ref[head // GROUP, at : at + HALF, :].astype(F32)

    return [tile_of_heads(block(2 * t), block(2 * t + 1)) for t in range(8)]


def partner(tile):
    lane = lax.broadcasted_iota(jnp.int32, tile.shape, 1)
    return jnp.where(lane % HEAD < 32, pltpu.roll(tile, 96, 1), pltpu.roll(tile, 32, 1))


def inverse_rms(values):
    return lax.rsqrt(jnp.sum(values * values, axis=1, keepdims=True) * (1.0 / D) + EPSILON)


def norm_back(values, inv, gain, grad):
    scaled = grad * gain
    mean = jnp.sum(scaled * values, axis=1, keepdims=True) * (1.0 / D)
    grad_values = inv * scaled - values * (inv * inv * inv) * mean
    return grad_values, jnp.sum(grad * values * inv, axis=0, keepdims=True)


def project_kernel(
    table, tok, gain, w, cosine, sine, q_ref, own_ref, nt_ref, flag, left, right, limit
):
    values = tok[...].astype(F32)
    normed = values * inverse_rms(values) * gain[...]
    low = normed.astype(BF16)
    nt_ref[...] = normed.T.astype(BF16)
    lanes = low_lanes(HALF)
    blocks = []
    for t in range(13):
        u = dot_nn(low, w[:, t * 128 : (t + 1) * 128])
        if t < 10:
            u = u * cosine[...] + partner(u) * sine[...]
        blocks += heads_of_tile(u)
    for head in range(HEADS):
        at = head % GROUP * HALF
        q_ref[head // GROUP, at : at + HALF, :] = blocks[head].astype(BF16)
    for i in range(2 * KV_HEADS):
        own_ref[i * HALF : (i + 1) * HALF, :] = turn(blocks[HEADS + i]).astype(BF16)

    ctx = lax.axis_index("ctx")
    mine = jnp.minimum(table[2 * ctx], table[2 * ctx + 1])
    lane = lax.broadcasted_iota(jnp.int32, (1, 128), 1)
    first = lane < HALF
    offset = lax.rem(lane, HALF)

    def one(i, _):
        early = jnp.minimum(table[2 * i], table[2 * i + 1])
        turn_late = early >= mine
        m = jnp.where(turn_late, 1.0, 0.0)
        row = pl.ds(i, 1)
        flag[row, :] = jnp.where(first, 1.0, m)
        left[row, :] = jnp.where(first, m, 1.0 - m)
        right[row, :] = jnp.where(first, 1.0 - m, 0.0)
        gap = jnp.where(turn_late, mine - early, early - mine)
        blocks_back = jnp.where(first, early - (63 - mine), gap)
        limit[row, :] = (blocks_back * HALF + offset).astype(F32)
        return 0

    lax.fori_loop(0, CTX, one, 0)
    zero = jnp.zeros((1, 128), F32)
    for ref in (flag, left, right):
        ref[CTX:TILES, :] = zero
    limit[CTX:TILES, :] = jnp.where(first, offset, 10**6).astype(F32)


def project(table, tok, gain, w, cosine, sine):
    return pl.pallas_call(
        project_kernel,
        out_shape=[
            jax.ShapeDtypeStruct((KV_HEADS, ROWS, 128), BF16),
            jax.ShapeDtypeStruct((640, 128), BF16),
            jax.ShapeDtypeStruct((D, 128), BF16),
        ]
        + [jax.ShapeDtypeStruct((TILES, 128), F32)] * 4,
        in_specs=[pl.BlockSpec(memory_space=pltpu.SMEM)] + [VM] * 5,
        out_specs=[VM] * 7,
        compiler_params=pltpu.CompilerParams(vmem_limit_bytes=BIG),
        name="project",
    )(table, tok, gain, w, cosine, sine)


def middle_kernel(
    o, tok, cot, gain, out_hbm, gate_hbm, up_hbm, down_hbm,
    layer_out, grad_mid, do_rows, gain_grad, nt, dgu, gt, hid, at_t, gb,
    out_w, gate_w, up_w, down_w, sem,
):
    loads = []
    pairs = ((out_hbm, out_w), (gate_hbm, gate_w), (up_hbm, up_w), (down_hbm, down_w))
    for i, (src, dst) in enumerate(pairs):
        copy = pltpu.make_async_copy(src, dst, sem.at[i])
        copy.start()
        loads.append(copy)
    attended = jnp.concatenate(get_heads(o), axis=1)
    at_t[...] = attended.T[:D].astype(BF16)
    cot_low = cot[...]
    gt[0] = cot_low.astype(F32).T.astype(BF16)
    loads[0].wait()
    middle = tok[...].astype(F32) + dot_nn(attended.astype(BF16)[:, :D], out_w[...])
    inv = inverse_rms(middle)
    normed = middle * inv * gain[...]
    low = normed.astype(BF16)
    nt[...] = normed.T.astype(BF16)
    loads[1].wait()
    gate = dot_nn(low, gate_w[...])
    sigmoid = jax.nn.sigmoid(gate)
    silu = gate * sigmoid
    loads[2].wait()
    up = dot_nn(low, up_w[...])
    hidden = (silu * up).astype(BF16)
    for f in range(4):
        hid[f] = hidden[:, f * 640 : (f + 1) * 640]
    loads[3].wait()
    layer_out[...] = (middle + dot_nn(hidden, down_w[...])).astype(BF16)
    grad_hidden = dot_nt(cot_low, down_w[...])
    grad_gate = (grad_hidden * up * sigmoid * (1.0 + gate * (1.0 - sigmoid))).astype(BF16)
    grad_up = (grad_hidden * silu).astype(BF16)
    dgu[0, :, 0:FF] = grad_gate
    dgu[0, :, FF : 2 * FF] = grad_up
    grad_norm = dot_nt(grad_gate, gate_w[...]) + dot_nt(grad_up, up_w[...])
    grad_values, gain_grad[...] = norm_back(middle, inv, gain[...], grad_norm)
    grad_middle = cot_low.astype(F32) + grad_values
    grad_mid[...] = grad_middle
    branch = grad_middle.astype(BF16)
    gb[0] = jnp.concatenate([branch, jnp.zeros((TOK, 64), BF16)], axis=1)
    put_heads(do_rows, dot_nt(branch, out_w[...]))


def middle(o, tok, cot, gain, out_w, gate_w, up_w, down_w):
    weights = (out_w, gate_w, up_w, down_w)
    return pl.pallas_call(
        middle_kernel,
        out_shape=[
            jax.ShapeDtypeStruct((TOK, D), BF16),
            jax.ShapeDtypeStruct((TOK, D), F32),
            jax.ShapeDtypeStruct((KV_HEADS, ROWS, 128), BF16),
            jax.ShapeDtypeStruct((1, D), F32),
            jax.ShapeDtypeStruct((D, 128), BF16),
            jax.ShapeDtypeStruct((1, TOK, 2 * FF), BF16),
            jax.ShapeDtypeStruct((1, D, 128), BF16),
            jax.ShapeDtypeStruct((4, TOK, 640), BF16),
            jax.ShapeDtypeStruct((D, 128), BF16),
            jax.ShapeDtypeStruct((1, TOK, 1024), BF16),
        ],
        in_specs=[VM] * 4 + [ANY] * 4,
        out_specs=[VM] * 10,
        scratch_shapes=[pltpu.VMEM(w.shape, BF16) for w in weights]
        + [pltpu.SemaphoreType.DMA((4,))],
        compiler_params=pltpu.CompilerParams(vmem_limit_bytes=BIG),
        name="middle",
    )(o, tok, cot, gain, *weights)


def unproject_kernel(dq, dkv, cosine, sine, w, tok, gain, grad_mid, grad_tok, dqkv, gain_grad):
    tiles = get_heads(dq)
    low = low_lanes(TOK)
    turned = [turn(dkv[i * 128 : (i + 1) * 128, :].T) for i in range(5)]
    tiles[7] = jnp.where(low, tiles[7], turned[0])
    for i in range(4):
        tiles.append(jnp.where(low, turned[i], turned[i + 1]))
    tiles.append(jnp.where(low, turned[4], 0.0))
    for t in range(13):
        u = tiles[t]
        if t < 10:
            u = u * cosine[...] - partner(u) * sine[...]
        dqkv[0, :, t * 128 : (t + 1) * 128] = u.astype(BF16)
    grad_norm = dot_nt(dqkv[0], w[...])
    values = tok[...].astype(F32)
    grad_values, gain_grad[...] = norm_back(values, inverse_rms(values), gain[...], grad_norm)
    grad_tok[...] = grad_mid[...] + grad_values


def unproject(dq, dkv, cosine, sine, w, tok, gain, grad_mid):
    return pl.pallas_call(
        unproject_kernel,
        out_shape=[
            jax.ShapeDtypeStruct((TOK, D), F32),
            jax.ShapeDtypeStruct((1, TOK, 1664), BF16),
            jax.ShapeDtypeStruct((1, D), F32),
        ],
        in_specs=[VM] * 8,
        out_specs=[VM] * 3,
        compiler_params=pltpu.CompilerParams(vmem_limit_bytes=BIG),
        name="unproject",
    )(dq, dkv, cosine, sine, w, tok, gain, grad_mid)


def unpack_kernel(g_in, u_in, d_in, o_in, qkv, g, u, d, o, q, k, v):
    step = pl.program_id(0)
    g[...] = g_in[...].astype(F32)
    u[...] = u_in[...].astype(F32)

    @pl.when(step < 5)
    def _():
        d[...] = d_in[...].astype(F32).T

    @pl.when(step < 8)
    def _():
        o[...] = o_in[...].astype(F32)

    @pl.when(step == 0)
    def _():
        tiles = [qkv[t * 240 : (t + 1) * 240, :].astype(F32) for t in range(13)]
        low = low_lanes(240)
        for t in range(7):
            q[:, t * 128 : (t + 1) * 128] = tiles[t]
        q[:, 896:960] = tiles[7][:, :64]
        turned = [turn(t) for t in tiles[7:10]]
        k[:, 0:128] = jnp.where(low, turned[0], turned[1])
        k[:, 128:256] = jnp.where(low, turned[1], turned[2])
        k[:, 256:320] = turned[2][:, :64]
        v[:, 0:128] = tiles[10]
        v[:, 128:256] = tiles[11]
        v[:, 256:320] = tiles[12][:, :64]


def unpack(done, qkv):
    def cut(rows, first, last):
        return pl.BlockSpec((rows, 128), lambda i: (first + jnp.minimum(i, last), 0))

    def out(rows, last):
        return pl.BlockSpec((rows, 128), lambda i: (0, jnp.minimum(i, last)))

    def whole(*shape):
        return pl.BlockSpec(shape, lambda i: (0, 0))

    return pl.pallas_call(
        unpack_kernel,
        grid=(20,),
        out_shape=[
            jax.ShapeDtypeStruct(shape, F32)
            for shape in (
                (240, FF), (240, FF), (640, D), (240, D), (240, D), (240, 320), (240, 320),
            )
        ],
        in_specs=[
            cut(240, 0, 19),
            cut(240, 20, 19),
            cut(960, 10, 4),
            cut(240, 60, 7),
            whole(*qkv.shape),
        ],
        out_specs=[
            out(240, 19),
            out(240, 19),
            pl.BlockSpec((128, D), lambda i: (jnp.minimum(i, 4), 0)),
            out(240, 7),
            whole(240, D),
            whole(240, 320),
            whole(240, 320),
        ],
        compiler_params=pltpu.CompilerParams(vmem_limit_bytes=BIG),
        name="unpack",
    )(done, done, done, done, qkv)


def rope_tables(early):
    row = lax.broadcasted_iota(jnp.int32, (TOK, 128), 0)
    lane = lax.broadcasted_iota(jnp.int32, (TOK, 128), 1)
    block = jnp.where(row < HALF, early, 63 - early)
    position = (block * HALF + row % HALF).astype(F32)
    frequency = BASE ** (-(lane % 32).astype(F32) / 32)
    angles = position * frequency
    return jnp.cos(angles), jnp.where(lane % HEAD < 32, -1.0, 1.0) * jnp.sin(angles)


def swap_rows(a, swap):
    return jnp.where(swap, jnp.concatenate([a[HALF:], a[:HALF]], axis=0), a)


def on_device(
    tokens, cotangent, block_table, attn_gain, w_query, w_key, w_value, w_out, mlp_gain,
    w_gate, w_up, w_down,
):
    ctx = lax.axis_index("ctx")
    gains = jnp.pad(jnp.stack([attn_gain, mlp_gain]), ((0, 14), (0, 16)))
    blank = jnp.zeros((240, 64), BF16)
    qkv_shard = jnp.concatenate([w_query, w_key, w_value, blank], axis=1)
    gains_all, qkv_w = gather_weights((gains, qkv_shard), 0)
    gains_all = gains_all.reshape(4, 16, 256)[:, :2, :240].astype(F32)
    gain_a = gains_all[:, 0].reshape(1, D)
    gain_b = gains_all[:, 1].reshape(1, D)

    own_blocks = lax.dynamic_slice_in_dim(block_table, 2 * ctx, 2)
    swap = own_blocks[0] > own_blocks[1]
    cosine, sine = rope_tables(jnp.min(own_blocks))
    tok = swap_rows(tokens[0], swap)
    cot = swap_rows(cotangent[0], swap)

    q_rows, own_kv, na_t, *plan = project(block_table, tok, gain_a, qkv_w, cosine, sine)
    o_rows, logs, kv, out_w, gate_w, up_w, down_w = forward(
        q_rows, own_kv, plan, (w_out, w_gate, w_up, w_down), 1
    )
    kv = kv.reshape(CTX, 640, 128)
    layer_out, grad_mid, do_rows, grad_gain_b, nb_t, dgu, cot_t, hidden, at_t, branch = middle(
        o_rows, tok, cot, gain_b, out_w, gate_w, up_w, down_w
    )
    ready = Reduction(
        (
            (nb_t.reshape(2, 2, 240, 128), dgu),
            (cot_t, hidden.reshape(2, 2, TOK, 640)),
            (at_t.reshape(2, 2, 240, 128), branch),
        ),
        None,
    )
    dq_rows, dkv, done = backward(q_rows, do_rows, o_rows, logs, kv, own_kv, plan, ready, 2)
    grad_tokens, grad_qkv, grad_gain_a = unproject(
        dq_rows, dkv, cosine, sine, qkv_w, tok, gain_a, grad_mid
    )
    gain_rows = jnp.stack([grad_gain_a, grad_gain_b]).reshape(2, 4, 240).transpose(1, 0, 2)
    gain_rows = jnp.pad(gain_rows, ((0, 0), (0, 0), (0, 16))).reshape(2, 2, 4, 128).astype(BF16)
    gain_rows = jnp.pad(gain_rows, ((0, 0), (0, 0), (0, 12), (0, 0)))
    late = Reduction(((na_t.reshape(2, 2, 240, 128), grad_qkv),), gain_rows)
    flat_done, flat = finish(done, ready.sizes, ready.used, late, 3)
    shard_g, shard_u, shard_d, shard_o, shard_q, shard_k, shard_v = unpack(flat_done, flat)
    shard_gains = flat[3120:3124].reshape(2, 256)[:, :240].astype(F32)
    return (
        swap_rows(layer_out, swap)[None],
        swap_rows(grad_tokens, swap)[None],
        shard_gains[0],
        shard_q,
        shard_k,
        shard_v,
        shard_o,
        shard_gains[1],
        shard_g,
        shard_u,
        shard_d,
    )


def solution(mesh):
    rows, cut = P("fsdp", "ctx", None), P("fsdp", None)
    return jax.shard_map(
        on_device,
        mesh=mesh,
        in_specs=(rows, rows, P(), P("fsdp"), cut, cut, cut, cut, P("fsdp"), cut, cut, cut),
        out_specs=(rows, rows, P("fsdp"), cut, cut, cut, cut, P("fsdp"), cut, cut, cut),
        check_vma=False,
    )
```

```python
import functools
import math

import jax
import jax.numpy as jnp
from jax import lax
from jax.experimental import pallas as pl
from jax.experimental.pallas import tpu as pltpu
from jax.sharding import PartitionSpec as P

D = 960
HEADS = 15
KV_HEADS = 5
GROUP = 3
HEAD = 64
FF = 2560
TOK = 128
HALF = 64
CTX = 32
TILES = 33
KEYS = TILES * 128
SCALE = HEAD ** (-0.5)
EPSILON = 1e-05
BASE = 10000.0
LOG2E = math.log2(math.e)
NEG = -1e30
MESH = pl.DeviceIdType.MESH
ANY = pl.BlockSpec(memory_space=pl.ANY)
VM = pl.BlockSpec(memory_space=pltpu.VMEM)
BIG = 56 * 2**20
F32 = jnp.float32
BF16 = jnp.bfloat16


def here():
    ctx = lax.axis_index("ctx")
    shard = lax.axis_index("fsdp")
    return {
        "z": ctx // 8,
        "yh": (ctx // 4) % 2,
        "x": ctx % 4,
        "yl": shard // 2,
        "c": shard % 2,
    }


def device(place, **moved):
    p = {**place, **moved}
    return (p["z"] * 8 + p["yh"] * 4 + p["x"], p["yl"] * 2 + p["c"])


def greet(devices):
    sem = pltpu.get_barrier_semaphore()
    for d in devices:
        pl.semaphore_signal(sem, inc=1, device_id=d, device_id_type=MESH)
    pl.semaphore_wait(sem, len(devices))


class Sems:
    def __init__(self, send, recv):
        self.send, self.recv, self.at = send, recv, 0

    def push(self, src, dst, dev):
        copy = pltpu.make_async_remote_copy(
            src_ref=src,
            dst_ref=dst,
            send_sem=self.send.at[self.at],
            recv_sem=self.recv.at[self.at],
            device_id=dev,
            device_id_type=MESH,
        )
        self.at += 1
        copy.start()
        return copy


def start_gather(me, sems, local, arrays, stages=None):
    f = me["yl"] * 2 + me["c"]
    near = device(me, yl=1 - me["yl"])
    far = device(me, yl=1 - me["yl"], yh=1 - me["yh"])
    mate = device(me, c=1 - me["c"])
    parts, kept, own = [], [], []
    for i, (a, b) in enumerate(arrays):
        rows = a.shape[0]
        first = rows // 32 * 16 if i % 2 else (rows + 31) // 32 * 16
        for lo, size, dev in ((0, first, near), (first, rows - first, far)):
            if size:
                src = a.at[pl.ds(lo, size)]
                dst = b.at[pl.ds(pl.multiple_of(f * rows + lo, 16), size)]
                parts.append((sems.push(src, dst, dev), b, rows, lo, size))
    for i, (a, b) in enumerate(arrays):
        rows = a.shape[0]
        dst = b.at[pl.ds(pl.multiple_of(f * rows, 16), rows)]
        kept.append(sems.push(a, dst, mate))
        stage = a if stages is None else stages[i]
        if stages is not None:
            load = pltpu.make_async_copy(a, stage, local.at[i])
            load.start()
        own.append((stage, dst, local.at[i]))
    if stages is not None:
        for (a, _), (stage, _, sem) in zip(arrays, own):
            pltpu.make_async_copy(a, stage, sem).wait()
    own = [pltpu.make_async_copy(*copy) for copy in own]
    for copy in own:
        copy.start()
    return parts, kept, own


def relay_gather(me, sems, started):
    parts, kept, _ = started
    across = (1 - me["yl"]) * 2 + me["c"]
    mate = device(me, c=1 - me["c"])
    for copy, b, rows, lo, size in parts:
        copy.wait_recv()
        span = b.at[pl.ds(pl.multiple_of(across * rows + lo, 16), size)]
        kept.append(sems.push(span, span, mate))


def end_gather(started):
    parts, kept, own = started
    for copy in own:
        copy.wait()
    for copy in kept:
        copy.wait()
    for copy, *_ in parts:
        copy.wait_send()


def gather_kernel(count, *refs):
    arrays = list(zip(refs[:count], refs[count : 2 * count]))
    send, recv, local = refs[2 * count :]
    me = here()
    flip = 1 - me["yl"]
    greet((device(me, yl=flip), device(me, yl=flip, yh=1 - me["yh"]), device(me, c=1 - me["c"])))
    sems = Sems(send, recv)
    started = start_gather(me, sems, local, arrays)
    relay_gather(me, sems, started)
    end_gather(started)


def gathered(arrays):
    return [jax.ShapeDtypeStruct((4 * a.shape[0], *a.shape[1:]), a.dtype) for a in arrays]


def gather_weights(arrays, collective_id):
    n = len(arrays)
    return pl.pallas_call(
        functools.partial(gather_kernel, n),
        out_shape=gathered(arrays),
        in_specs=[VM] * n,
        out_specs=[ANY] * n,
        scratch_shapes=[
            pltpu.SemaphoreType.DMA((5 * n,)),
            pltpu.SemaphoreType.DMA((5 * n,)),
            pltpu.SemaphoreType.DMA((n,)),
        ],
        compiler_params=pltpu.CompilerParams(
            collective_id=collective_id, has_side_effects=True, vmem_limit_bytes=BIG
        ),
        name="gather_weights",
    )(*arrays)


class Ring:
    def __init__(self, me, axis):
        at = me[axis]
        self.me = at
        self.right_at, self.opposite_at, self.left_at = (lax.rem(at + d, 4) for d in (1, 2, 3))
        self.right = device(me, **{axis: self.right_at})
        self.left = device(me, **{axis: self.left_at})
        self.opposite = device(me, **{axis: self.opposite_at})


class Share:
    def __init__(self, sems, ring, src, place, halves):
        self.sems, self.ring, self.place, self.halves = sems, ring, place, halves
        dst = place(ring.me)
        self.copies = [sems.push(src, dst, ring.right), sems.push(src, dst, ring.left)]
        self.passed, self.here = [], False
        if halves is None:
            self.passed.append(sems.push(src, dst, ring.opposite))

    def near(self):
        if not self.here:
            for copy in self.copies:
                copy.wait_recv()
            self.here = True

    def relay(self):
        self.near()
        if self.halves is not None:
            ring, push = self.ring, self.sems.push
            half = self.halves(self.place(ring.left_at))[0]
            self.passed.append(push(half, half, ring.right))
            half = self.halves(self.place(ring.right_at))[1]
            self.passed.append(push(half, half, ring.left))

    def arrive(self):
        for copy in self.passed:
            copy.wait_recv()

    def end(self):
        for copy in self.copies + self.passed:
            copy.wait_send()


def gather_kv(me, sems, kv, out, once_across):
    x, yh, z = me["x"], me["yh"], me["z"]
    other = device(me, yh=1 - yh)
    rings = Ring(me, "x"), Ring(me, "z")
    spans = pl.ds(0, 320), pl.ds(320, 320)
    across = [sems.push(kv.at[p], out.at[z, yh, x, p], other) for p in spans]

    def near(axis, row, src):
        lo = 320 * axis

        def place(at):
            ref = out.at[z, row, at] if axis == 0 else out.at[at, row, x]
            return ref.at[spans[axis]]

        def halves(ref):
            return ref.at[pl.ds(0, 160)], ref.at[pl.ds(160, 160)]

        return Share(sems, rings[axis], src, place, halves)

    def far(axis, row):
        def place(at):
            return out.at[at, row, :, spans[0]] if axis == 0 else out.at[:, row, at, spans[1]]

        def halves(ref):
            return ref.at[pl.ds(0, 2)], ref.at[pl.ds(2, 2)]

        src = place(rings[1 - axis].me)
        return Share(sems, rings[1 - axis], src, place, halves)

    first = [near(axis, yh, kv.at[spans[axis]]) for axis in (0, 1)]
    out[z, yh, x] = kv[...]
    for share in first:
        share.relay()
    second = []
    for axis in (0, 1):
        across[axis].wait_recv()
        row = 1 - yh
        src = out.at[z, row, x, spans[axis]]
        second.append(near(axis, row, src))
    once_across()
    last = []
    for axis in (0, 1):
        first[axis].arrive()
        last.append(far(axis, yh))
    for share in second:
        share.relay()
    for axis in (0, 1):
        second[axis].arrive()
        last.append(far(axis, 1 - yh))
    for share in last:
        share.relay()
    for share in last:
        share.arrive()
    return across, first + second + last


def add_low(a, b):
    return (a.astype(F32) + b.astype(F32)).astype(BF16)


class Fold:
    def __init__(self, sems, ring, block, landing, passing, direct=False):
        self.sems, self.ring, self.block, self.direct = sems, ring, block, direct
        self.landing, self.passing = landing, passing
        self.copies, self.passed, self.sent = {}, {}, []

    def start_opposite(self, half):
        ring = self.ring
        src = self.block(ring.opposite_at, half)
        dev = ring.opposite if self.direct else (ring.right, ring.left)[half]
        self.passed[half] = self.sems.push(src, self.passing(half), dev)

    def start_direct(self, half):
        ring = self.ring
        at, dev = ((ring.left_at, ring.left), (ring.right_at, ring.right))[half]
        side = 1 - half
        self.copies[side, half] = self.sems.push(
            self.block(at, half), self.landing(side, half), dev
        )

    def relay(self, half):
        ring = self.ring
        at, dev = ((ring.right_at, ring.right), (ring.left_at, ring.left))[half]
        src = self.block(at, half)
        if not self.direct:
            self.passed[half].wait_recv()
            src[...] = add_low(src[...], self.passing(half)[...])
        self.copies[half, half] = self.sems.push(src, self.landing(half, half), dev)

    def total(self, half):
        for side in (0, 1):
            self.copies[side, half].wait_recv()
        total = self.block(self.ring.me, half)[...].astype(F32)
        for side in (0, 1):
            total = total + self.landing(side, half)[...].astype(F32)
        if self.direct:
            self.passed[half].wait_recv()
            total = total + self.passing(half)[...].astype(F32)
        return total

    def end(self):
        for copy in list(self.copies.values()) + list(self.passed.values()):
            copy.wait_send()


class Scatter:
    COPIES = 26
    SCRATCH = [
        pltpu.VMEM((2, 3, 2, 4, 320, 128), BF16),
        pltpu.VMEM((2, 2, 4, 320, 128), BF16),
        pltpu.VMEM((2, 3, 2, 320, 128), BF16),
        pltpu.VMEM((2, 320, 128), BF16),
        pltpu.VMEM((2, 320, 128), BF16),
    ]

    def __init__(self, me, sems, part, out, scratch):
        self.me, self.sems, self.part, self.out = me, sems, part, out
        self.r1, self.s1, self.r2, self.s2, self.r3 = scratch
        self.rings = Ring(me, "x"), Ring(me, "z")
        self.first, self.second, self.third = [], [], []
        rows = (1 - me["yh"], me["yh"])
        key, value = pl.ds(0, 320), pl.ds(320, 320)

        def block0(at, half):
            return part.at[at, rows[half], :, key]

        def block1(at, half):
            return part.at[:, rows[half], at, value]

        for axis, block in enumerate((block0, block1)):
            r1, s1, r2 = self.r1, self.s1, self.r2
            self.first.append(
                Fold(
                    sems,
                    self.rings[1 - axis],
                    block,
                    lambda side, half, axis=axis: r1.at[axis, side, half],
                    lambda half, axis=axis: r1.at[axis, 2, half],
                )
            )
            self.second.append(
                Fold(
                    sems,
                    self.rings[axis],
                    lambda at, half, axis=axis: s1.at[axis, half, at],
                    lambda side, half, axis=axis: r2.at[axis, side, half],
                    lambda half, axis=axis: r2.at[axis, 2, half],
                )
            )

    def start(self):
        for half in (0, 1):
            for fold in self.first:
                fold.start_opposite(half)
        for half in (0, 1):
            for fold in self.first:
                fold.start_direct(half)

    def relay(self):
        for half in (0, 1):
            for fold in self.first:
                fold.relay(half)

    def middle(self):
        for half in (0, 1):
            for axis in (0, 1):
                self.s1[axis, half] = self.first[axis].total(half).astype(BF16)
                self.second[axis].start_opposite(half)
                self.second[axis].start_direct(half)
        for half in (0, 1):
            for fold in self.second:
                fold.relay(half)

    def last(self):
        other = device(self.me, yh=1 - self.me["yh"])
        for axis in (0, 1):
            self.s2[axis] = self.second[axis].total(0).astype(BF16)
            self.third.append(self.sems.push(self.s2.at[axis], self.r3.at[axis], other))
        for axis in (0, 1):
            self.out[pl.ds(axis * 320, 320), :] = self.second[axis].total(1)

    def end(self):
        for axis in (0, 1):
            self.third[axis].wait_recv()
            span = pl.ds(axis * 320, 320)
            self.out[span, :] = self.out[span, :] + self.r3[axis].astype(F32)
        for fold in self.first + self.second:
            fold.end()
        for c in self.third:
            c.wait_send()


def build_tiles(head, kv_ref, own_ref, left_ref, tiles_ref, base):
    lane = lax.broadcasted_iota(jnp.int32, (HALF, 128), 1)
    start = pl.multiple_of(base + head * HALF, HALF)

    def one(i, _):
        block = kv_ref[i, pl.ds(start, HALF), :].astype(F32)
        top = jnp.where(lane < HALF, block, 0.0)
        low = pltpu.roll(block, HALF, 1) * left_ref[pl.ds(i, 1), :]
        at = pl.multiple_of(i * 128, 128)
        tiles_ref[pl.ds(at, 128), :] = jnp.concatenate([top, low], axis=0).astype(BF16)
        return 0

    lax.fori_loop(0, CTX, one, 0, unroll=32)
    block = own_ref[pl.ds(start, HALF), :].astype(F32)
    top = jnp.where(lane < HALF, 0.0, pltpu.roll(block, HALF, 1))
    tiles_ref[pl.ds(CTX * 128, 128), :] = jnp.concatenate(
        [top, jnp.zeros_like(top)], axis=0
    ).astype(BF16)


def dot_nt(a, b):
    return lax.dot_general(a, b, (((1,), (1,)), ((), ())), preferred_element_type=F32)


def dot_nn(a, b):
    return lax.dot_general(a, b, (((1,), (0,)), ((), ())), preferred_element_type=F32)


ROWS = GROUP * HALF


def row_offset():
    return lax.rem(lax.broadcasted_iota(jnp.int32, (ROWS, 128), 0), HALF).astype(F32)


def attend_head(head, q, kv_ref, own_ref, flag_ref, left_ref, limit_ref, kk, vv):
    build_tiles(head, kv_ref, own_ref, left_ref, kk, 0)
    build_tiles(head, kv_ref, own_ref, left_ref, vv, 320)
    offset = row_offset()
    low = jnp.full((ROWS, 128), NEG, F32)
    s = dot_nt(q, kk[...]) * (SCALE * LOG2E)
    tiles = []
    top_l, top_e = low, low
    for i in range(TILES):
        tile = s[:, i * 128 : (i + 1) * 128]
        tile = jnp.where(limit_ref[i : i + 1, :] <= offset, tile, NEG)
        tiles.append(tile)
        late = flag_ref[i : i + 1, :] > 0.5
        top_l = jnp.maximum(top_l, jnp.where(late, tile, NEG))
        top_e = jnp.maximum(top_e, jnp.where(late, NEG, tile))
    max_l = jnp.broadcast_to(jnp.max(top_l, axis=1, keepdims=True), (ROWS, 128))
    max_e = jnp.broadcast_to(jnp.max(top_e, axis=1, keepdims=True), (ROWS, 128))
    sum_l = jnp.zeros((ROWS, 128), F32)
    sum_e = jnp.zeros((ROWS, 128), F32)
    probs = []
    for i in range(TILES):
        late = flag_ref[i : i + 1, :] > 0.5
        p = jnp.exp2(tiles[i] - jnp.where(late, max_l, max_e))
        p_l = jnp.where(late, p, 0.0)
        sum_l = sum_l + p_l
        sum_e = sum_e + (p - p_l)
        probs.append(p.astype(BF16))
    total = dot_nn(jnp.concatenate(probs, axis=1), vv[...])
    late = lax.broadcasted_iota(jnp.int32, (ROWS, 128), 1) < HALF
    row_sum = jnp.where(
        late, jnp.sum(sum_l, axis=1, keepdims=True), jnp.sum(sum_e, axis=1, keepdims=True)
    )
    return total / row_sum, jnp.where(late, max_l, max_e) + jnp.log2(row_sum)


def forward_kernel(count, q_ref, own_ref, flag_ref, left_ref, limit_ref, *refs):
    shards, refs = refs[:count], refs[count:]
    o_ref, l_ref, kv_out, *full = refs[: 3 + count]
    kv, kk, vv, *stages, send, recv, local = refs[3 + count :]
    me = here()
    greet_axes(me)
    sems = Sems(send, recv)
    started = []

    def start_weights():
        started.extend(start_gather(me, sems, local, list(zip(shards, full)), stages))

    across, shares = gather_kv(me, sems, own_ref, kv, start_weights)
    keep = pltpu.make_async_copy(kv, kv_out, local.at[count])
    keep.start()
    flat = kv.reshape(CTX, 640, 128)

    def one(head, _):
        o, logs = attend_head(
            head, q_ref[head], flat, own_ref, flag_ref, left_ref, limit_ref, kk, vv
        )
        o_ref[head] = o
        l_ref[head] = logs
        return 0

    lax.fori_loop(0, 3, one, 0)
    relay_gather(me, sems, started)
    lax.fori_loop(3, KV_HEADS, one, 0)
    end_gather(started)
    for copy in across:
        copy.wait_send()
    for share in shares:
        share.end()
    keep.wait()


def forward(q, own, plan, shards, collective_id):
    flags, left, _, limits = plan
    n = len(shards)
    copies = 5 * n + 2 + 8 * 4
    return pl.pallas_call(
        functools.partial(forward_kernel, n),
        out_shape=[jax.ShapeDtypeStruct((KV_HEADS, ROWS, 128), F32)] * 2
        + [jax.ShapeDtypeStruct((4, 2, 4, 640, 128), BF16)]
        + gathered(shards),
        in_specs=[VM] * 5 + [ANY] * n,
        out_specs=[VM, VM, ANY] + [ANY] * n,
        scratch_shapes=[
            pltpu.VMEM((4, 2, 4, 640, 128), BF16),
            pltpu.VMEM((KEYS, 128), BF16),
            pltpu.VMEM((KEYS, 128), BF16),
            *[pltpu.VMEM(a.shape, BF16) for a in shards],
            pltpu.SemaphoreType.DMA((copies,)),
            pltpu.SemaphoreType.DMA((copies,)),
            pltpu.SemaphoreType.DMA((n + 1,)),
        ],
        compiler_params=pltpu.CompilerParams(
            collective_id=collective_id, has_side_effects=True, vmem_limit_bytes=BIG
        ),
        name="forward",
    )(q, own, flags, left, limits, *shards)


def attend_back_head(
    head, q, do, o, logs, kv_ref, own_ref, flag_ref, left_ref, right_ref, limit_ref,
    dkv_ref, kk, vv,
):
    build_tiles(head, kv_ref, own_ref, left_ref, kk, 0)
    build_tiles(head, kv_ref, own_ref, left_ref, vv, 320)
    offset = row_offset()
    lane = lax.broadcasted_iota(jnp.int32, (ROWS, 128), 1)
    product = do.astype(F32) * o
    shape = (ROWS, 128)
    delta_l = jnp.broadcast_to(
        jnp.sum(jnp.where(lane < HALF, product, 0.0), axis=1, keepdims=True), shape
    )
    delta_e = jnp.broadcast_to(
        jnp.sum(jnp.where(lane < HALF, 0.0, product), axis=1, keepdims=True), shape
    )
    log_l = jnp.broadcast_to(logs[:, 0:1], shape)
    log_e = jnp.broadcast_to(logs[:, HALF : HALF + 1], shape)
    k_rows = pl.ds(pl.multiple_of(head * HALF, HALF), HALF)
    v_rows = pl.ds(pl.multiple_of(320 + head * HALF, HALF), HALF)
    small = lax.broadcasted_iota(jnp.int32, (HALF, 128), 1)
    keys = kk[...]
    s = dot_nt(q, keys) * (SCALE * LOG2E)
    dp = dot_nt(do, vv[...])
    probs, scores = [], []
    for i in range(TILES):
        cut = slice(i * 128, (i + 1) * 128)
        late = flag_ref[i : i + 1, :] > 0.5
        tile = jnp.where(limit_ref[i : i + 1, :] <= offset, s[:, cut], NEG)
        p = jnp.exp2(tile - jnp.where(late, log_l, log_e))
        probs.append(p.astype(BF16))
        scores.append((p * (dp[:, cut] - jnp.where(late, delta_l, delta_e))).astype(BF16))
    ds = jnp.concatenate(scores, axis=1)
    dq = dot_nn(ds, keys) * SCALE
    dk = dot_nn(q.astype(F32).T.astype(BF16), ds) * SCALE
    dv = dot_nn(do.astype(F32).T.astype(BF16), jnp.concatenate(probs, axis=1))
    mine = lax.axis_index("ctx")
    for rows, both in ((k_rows, dk), (v_rows, dv)):
        for i in range(CTX):
            cut = slice(i * 128, (i + 1) * 128)
            top, bottom = both[0:HALF, cut], both[HALF:128, cut]
            total = (
                top * flag_ref[i : i + 1, :]
                + pltpu.roll(bottom, HALF, 1) * right_ref[i : i + 1, :]
            )
            dkv_ref[i, rows, :] = total.astype(BF16)
        bottom = both[HALF:128, CTX * 128 :]
        before = dkv_ref[mine, rows, :].astype(F32)
        dkv_ref[mine, rows, :] = (before + jnp.where(small < HALF, bottom, 0.0)).astype(BF16)
    return dq


def pop(refs, count):
    taken = refs[:count]
    del refs[:count]
    return taken


class Reduction:
    def __init__(self, jobs, extra, direct=False):
        self.operands, self.jobs, self.scratch, rows = [], [], [], 0
        self.direct = direct
        for left, right in jobs:
            self.operands += [left, right]
            m, n = left.shape[-2], right.shape[-1]
            self.jobs.append((left.ndim == 4, m, right.ndim == 4, n))
            self.scratch.append(pltpu.VMEM((left.shape[0], m, 256), BF16))
            self.scratch.append(pltpu.VMEM((right.shape[0], 256, n), BF16))
            rows += m * (n // 128)
        self.extra = extra is not None
        if self.extra:
            self.operands.append(extra)
            self.scratch.append(pltpu.VMEM((2, 2, 16, 128), BF16))
            rows += 16
        pieces = -(-rows // 256)
        self.sizes = ((pieces + 1) // 2 * 16, pieces // 2 * 16)
        self.used = 16 * sum(self.sizes)
        self.scratch.append(pltpu.VMEM((2, self.used, 128), BF16))
        for size in self.sizes:
            self.scratch += [
                pltpu.VMEM((3, 4, 2, size, 128), BF16),
                pltpu.VMEM((4, 2, size, 128), BF16),
                pltpu.VMEM((3, 2, size, 128), BF16),
                pltpu.VMEM((2, size, 128), BF16),
                pltpu.VMEM((4, size, 128), BF16),
            ]
        self.locals = 2 * len(jobs) + 1
        self.copies = 2 * len(jobs) + 1 + 48 + 12 + 6
        self.fin_shape = (sum(self.sizes), 128)

    def bind(self, me, sems, local, operands, scratch, fin):
        operands, scratch = list(operands), list(scratch)
        self.me, self.sems, self.local, self.fin = me, sems, local, fin
        self.sources, self.buffers = [], []
        core = me["c"]
        for cut_left, _, cut_right, _ in self.jobs:
            left, right = pop(operands, 2)
            lefts = (left.at[:, core], left.at[:, 1 - core]) if cut_left else (left, left)
            rights = (right.at[:, core], right.at[:, 1 - core]) if cut_right else (right, right)
            self.sources.append((*lefts, *rights))
            self.buffers.append(pop(scratch, 2))
        if self.extra:
            self.extra_refs = (operands[0].at[:, core], operands[0].at[:, 1 - core])
            self.extra_buffer = scratch.pop(0)
        self.grads = scratch.pop(0)
        self.parts = [pop(scratch, 5) for _ in self.sizes]
        xs, zs = Ring(me, "x"), Ring(me, "z")
        self.plans = (
            (0, self.sizes[0], xs, zs),
            (16 * self.sizes[0], self.sizes[1], zs, xs),
        )
        self.first, self.second, self.third = {}, {}, {}
        for n, (lo, size, ring, cross) in enumerate(self.plans):
            r1, s1, r2, _, _ = self.parts[n]
            for k in range(4):
                j = lax.rem(cross.me + k, 4)

                def block(at, half, lo=lo, size=size, j=j):
                    start = pl.multiple_of(lo + (at * 4 + j) * size, 16)
                    return self.grads.at[half, pl.ds(start, size)]

                self.first[n, k] = Fold(
                    sems,
                    ring,
                    block,
                    lambda side, half, r1=r1, k=k: r1.at[side, k, half],
                    lambda half, r1=r1, k=k: r1.at[2, k, half],
                    self.direct,
                )

            def turned(at, half, s1=s1, cross=cross):
                return s1.at[lax.rem(at + 4 - cross.me, 4), half]

            self.second[n] = Fold(
                sems,
                cross,
                turned,
                lambda side, half, r2=r2: r2.at[side, half],
                lambda half, r2=r2: r2.at[2, half],
                self.direct,
            )

    def trade(self):
        mate = device(self.me, c=1 - self.me["c"])
        push = self.sems.push
        self.mine, self.traded = [], []

        def keep(src, dst):
            copy = pltpu.make_async_copy(src, dst, self.local.at[len(self.mine)])
            copy.start()
            self.mine.append(copy)

        here_, there = pl.ds(0, 128), pl.ds(128, 128)
        for (lm, lt, rm, rt), (lb, rb) in zip(self.sources, self.buffers):
            self.traded.append(push(lt, lb.at[:, :, there], mate))
            self.traded.append(push(rt, rb.at[:, there], mate))
            keep(lm, lb.at[:, :, here_])
            keep(rm, rb.at[:, here_])
        if self.extra:
            self.traded.append(push(self.extra_refs[1], self.extra_buffer.at[1], mate))
            keep(self.extra_refs[0], self.extra_buffer.at[0])

    def multiply(self, job):
        base = sum(m * (n // 128) for _, m, _, n in self.jobs[:job])
        for copy in self.mine[2 * job : 2 * job + 2]:
            copy.wait()
        for copy in self.traded[2 * job : 2 * job + 2]:
            copy.wait_recv()
        grads, (_, m, _, n), (lb, rb) = self.grads, self.jobs[job], self.buffers[job]
        strip = min(n, 1280) if n % 1280 == 0 else n
        for s in range(2):
            left = lb[min(s, lb.shape[0] - 1)]

            def block(i, _, left=left, s=s):
                at = pl.multiple_of(i * strip, 128)
                right = rb[min(s, rb.shape[0] - 1), :, pl.ds(at, strip)]
                result = dot_nn(left, right).astype(BF16)
                for w in range(strip // 128):
                    to = pl.multiple_of(base + (i * (strip // 128) + w) * m, 16)
                    grads[s, pl.ds(to, m), :] = result[:, w * 128 : (w + 1) * 128]
                return 0

            if n == strip:
                block(0, 0)
            else:
                lax.fori_loop(0, n // strip, block, 0)

    def pad(self):
        base, grads = sum(m * (n // 128) for _, m, _, n in self.jobs), self.grads
        if self.extra:
            self.mine[-1].wait()
            self.traded[-1].wait_recv()
            for s in range(2):
                both = self.extra_buffer[0, s].astype(F32) + self.extra_buffer[1, s].astype(F32)
                grads[s, pl.ds(base, 16), :] = both.astype(BF16)
            base += 16
        if base < self.used:
            for s in range(2):
                grads[s, pl.ds(base, self.used - base), :] = jnp.zeros(
                    (self.used - base, 128), BF16
                )

    def start(self, n):
        for k in (2, 1, 3, 0):
            for half in (0, 1):
                self.first[n, k].start_opposite(half)
        for k in (2, 1, 3, 0):
            for half in (0, 1):
                self.first[n, k].start_direct(half)

    def relay(self, k):
        for half in (0, 1):
            for n in (0, 1):
                self.first[n, k].relay(half)

    def fold_first(self, k):
        for n in (0, 1):
            s1, second = self.parts[n][1], self.second[n]
            for half in (0, 1):
                s1[k, half] = self.first[n, k].total(half).astype(BF16)
            if k == 2:
                second.start_opposite(0)
                second.start_opposite(1)
            elif k == 1:
                second.start_direct(1)
            elif k == 3:
                second.start_direct(0)

    def fold_second(self):
        me, push = self.me, self.sems.push
        yh, yl = me["yh"], me["yl"]
        for half in (0, 1):
            for n in (0, 1):
                self.second[n].relay(half)
        for n in (0, 1):
            s2, r3 = self.parts[n][3:]
            for half in (0, 1):
                s2[half] = self.second[n].total(half).astype(BF16)
            slot = r3.at[yl * 2 + yh]
            self.third[n, 0] = push(s2.at[1 - yl], slot, device(me, yl=1 - yl))
            self.third[n, 1] = push(s2.at[1 - yl], slot, device(me, yl=1 - yl, yh=1 - yh))
            self.third[n, 2] = push(s2.at[yl], slot, device(me, yh=1 - yh))

    def fold_third(self):
        yh, yl = self.me["yh"], self.me["yl"]
        at = 0
        for n, size in enumerate(self.sizes):
            _, _, _, s2, r3 = self.parts[n]
            r3[yl * 2 + yh] = s2[yl]
            for i in (0, 1, 2):
                self.third[n, i].wait_recv()
            total = r3[0].astype(F32)
            for i in (1, 2, 3):
                total = total + r3[i].astype(F32)
            self.fin[pl.ds(at, size), :] = total.astype(BF16)
            at += size

    def end(self):
        for fold in list(self.first.values()) + list(self.second.values()):
            fold.end()
        for copy in self.traded + list(self.third.values()):
            copy.wait_send()


class Spread:
    COPIES = 40

    def __init__(self, me, sems, local, fin, out, sizes, direct=False):
        self.direct = direct
        self.sems, self.out, self.kept, self.cross, self.ring = sems, out, [], [], []
        xs, zs = Ring(me, "x"), Ring(me, "z")
        self.plans = ((0, sizes[0], xs, zs), (16 * sizes[0], sizes[1], zs, xs))
        at = 0
        for n, (_, size, ring, cross) in enumerate(self.plans):
            src = fin.at[pl.ds(at, size)]
            copy = pltpu.make_async_copy(src, self.span(n, ring.me, cross.me), local.at[n])
            copy.start()
            self.kept.append(copy)
            at += size
            self.cross.append(
                Share(sems, cross, src, functools.partial(self.span, n, ring.me), self.halves(n))
            )
            self.share(n, cross.me, src)

    def span(self, n, i, j):
        lo, size, _, _ = self.plans[n]
        return self.out.at[pl.ds(pl.multiple_of(lo + (i * 4 + j) * size, 16), size)]

    def halves(self, n):
        if self.direct:
            return None
        size = self.plans[n][1]
        first = size // 32 * 16
        return lambda ref: (ref.at[pl.ds(0, first)], ref.at[pl.ds(first, size - first)])

    def share(self, n, j, src=None):
        ring = self.plans[n][2]

        def place(i):
            return self.span(n, i, j)

        src = place(ring.me) if src is None else src
        self.ring.append(Share(self.sems, ring, src, place, self.halves(n)))

    def relay(self):
        for n in (0, 1):
            self.cross[n].relay()
        for n in (0, 1):
            cross = self.plans[n][3]
            self.share(n, cross.left_at)
            self.share(n, cross.right_at)

    def pass_on(self):
        self.ring[0].relay()
        self.ring[1].relay()
        for n in (0, 1):
            self.cross[n].arrive()
            self.share(n, self.plans[n][3].opposite_at)

    def end(self):
        for share in self.ring[2:]:
            share.relay()
        for share in self.ring:
            share.arrive()
        for copy in self.kept:
            copy.wait()
        for share in self.cross + self.ring:
            share.end()


def greet_axes(me, reach=2):
    flip = 1 - me["yl"]
    rings = Ring(me, "x"), Ring(me, "z")
    greet(
        [device(me, yl=flip), device(me, yl=flip, yh=1 - me["yh"]), device(me, c=1 - me["c"])]
        + [device(me, yh=1 - me["yh"])]
        + [dev for ring in rings for dev in (ring.left, ring.right, ring.opposite)[:reach]]
    )


def backward_kernel(reduction, *refs):
    refs = list(refs)
    q, do, o, logs, kv, own, flag, left, right, limit = pop(refs, 10)
    operands = pop(refs, len(reduction.operands))
    dq_ref, dkv_own, fin = pop(refs, 3)
    kv_here, dkv, kk, vv = pop(refs, 4)
    scatter_scratch = pop(refs, len(Scatter.SCRATCH))
    reduce_scratch = pop(refs, len(reduction.scratch))
    send, recv, local = refs
    me = here()
    greet_axes(me)
    sems = Sems(send, recv)
    reduction.bind(me, sems, local, operands, reduce_scratch, fin)
    reduction.trade()
    load = pltpu.make_async_copy(kv, kv_here, local.at[reduction.locals])
    load.start()
    scatter = Scatter(me, sems, dkv, dkv_own, scatter_scratch)
    flat = dkv.reshape(CTX, 640, 128)

    def one(head, _):
        dq_ref[head] = attend_back_head(
            head, q[head], do[head], o[head], logs[head], kv_here, own, flag,
            left, right, limit, flat, kk, vv,
        )
        return 0

    reduction.multiply(0)
    reduction.start(0)
    reduction.multiply(1)
    reduction.multiply(2)
    reduction.pad()
    reduction.start(1)
    load.wait()
    lax.fori_loop(0, KV_HEADS, one, 0)
    for k in (2, 1):
        reduction.relay(k)
    scatter.start()
    for k in (3, 0):
        reduction.relay(k)
    scatter.relay()
    for k in (2, 1, 3, 0):
        reduction.fold_first(k)
    scatter.middle()
    reduction.fold_second()
    scatter.last()
    reduction.fold_third()
    scatter.end()
    reduction.end()


def backward(q, do, o, logs, kv, own, plan, reduction, collective_id):
    flags, left, right, limits = plan
    copies = reduction.copies + Scatter.COPIES
    return pl.pallas_call(
        functools.partial(backward_kernel, reduction),
        out_shape=[
            jax.ShapeDtypeStruct((KV_HEADS, ROWS, 128), F32),
            jax.ShapeDtypeStruct((640, 128), F32),
            jax.ShapeDtypeStruct(reduction.fin_shape, BF16),
        ],
        in_specs=[VM] * 4 + [ANY] + [VM] * 5 + [ANY] * len(reduction.operands),
        out_specs=[VM, VM, VM],
        scratch_shapes=[
            pltpu.VMEM((CTX, 640, 128), BF16),
            pltpu.VMEM((4, 2, 4, 640, 128), BF16),
            pltpu.VMEM((KEYS, 128), BF16),
            pltpu.VMEM((KEYS, 128), BF16),
            *Scatter.SCRATCH,
            *reduction.scratch,
            pltpu.SemaphoreType.DMA((copies,)),
            pltpu.SemaphoreType.DMA((copies,)),
            pltpu.SemaphoreType.DMA((reduction.locals + 1,)),
        ],
        compiler_params=pltpu.CompilerParams(
            collective_id=collective_id, has_side_effects=True, vmem_limit_bytes=BIG
        ),
        name="backward",
    )(
        q, do, o, logs, kv, own, flags, left, right, limits, *reduction.operands,
    )


def finish_kernel(reduction, sizes, *refs):
    refs = list(refs)
    done = refs.pop(0)
    operands = pop(refs, len(reduction.operands))
    out_done, out = pop(refs, 2)
    fin = refs.pop(0)
    reduce_scratch = pop(refs, len(reduction.scratch))
    send, recv, local = refs
    me = here()
    greet_axes(me, 3)
    sems = Sems(send, recv)
    reduction.bind(me, sems, local, operands, reduce_scratch, fin)
    reduction.trade()
    spread = Spread(me, sems, local.at[pl.ds(reduction.locals, 2)], done, out_done, sizes)
    reduction.multiply(0)
    reduction.pad()
    for n in (0, 1):
        reduction.start(n)
    for k in (2, 1, 3, 0):
        reduction.relay(k)
    spread.relay()
    for k in (2, 1, 3, 0):
        reduction.fold_first(k)
    reduction.fold_second()
    spread.pass_on()
    reduction.fold_third()
    last = Spread(
        me, sems, local.at[pl.ds(reduction.locals + 2, 2)], fin, out, reduction.sizes, True
    )
    last.relay()
    last.pass_on()
    spread.end()
    last.end()
    reduction.end()


def finish(done, sizes, used, reduction, collective_id):
    copies = reduction.copies + 2 * Spread.COPIES
    return pl.pallas_call(
        functools.partial(finish_kernel, reduction, sizes),
        out_shape=[
            jax.ShapeDtypeStruct((used, 128), BF16),
            jax.ShapeDtypeStruct((reduction.used, 128), BF16),
        ],
        in_specs=[VM] + [ANY] * len(reduction.operands),
        out_specs=[ANY, ANY],
        scratch_shapes=[
            pltpu.VMEM(reduction.fin_shape, BF16),
            *reduction.scratch,
            pltpu.SemaphoreType.DMA((copies,)),
            pltpu.SemaphoreType.DMA((copies,)),
            pltpu.SemaphoreType.DMA((reduction.locals + 4,)),
        ],
        compiler_params=pltpu.CompilerParams(
            collective_id=collective_id, has_side_effects=True, vmem_limit_bytes=BIG
        ),
        name="finish",
    )(done, *reduction.operands)


def low_lanes(rows):
    return lax.broadcasted_iota(jnp.int32, (rows, 128), 1) < HALF


def turn(tile):
    return pltpu.roll(tile, HALF, 1)


def heads_of_tile(tile):
    early, late = tile[:HALF], tile[HALF:]
    low = low_lanes(HALF)
    return jnp.where(low, late, turn(early)), jnp.where(low, turn(late), early)


def tile_of_heads(first, second):
    low = low_lanes(HALF)
    early = jnp.where(low, turn(first), second)
    late = jnp.where(low, first, turn(second))
    return jnp.concatenate([early, late], axis=0)


def put_heads(ref, values):
    for t in range(8):
        if t < 7:
            tile = values[:, t * 128 : (t + 1) * 128]
        else:
            last = values[:, 896:960]
            tile = jnp.concatenate([last, jnp.zeros_like(last)], axis=1)
        for i, block in enumerate(heads_of_tile(tile)):
            head = 2 * t + i
            if head < HEADS:
                at = head % GROUP * HALF
                ref[head // GROUP, at : at + HALF, :] = block.astype(ref.dtype)


def get_heads(ref):
    def block(head):
        if head == HEADS:
            return jnp.zeros((HALF, 128), F32)
        at = head % GROUP * HALF
        return ref[head // GROUP, at : at + HALF, :].astype(F32)

    return [tile_of_heads(block(2 * t), block(2 * t + 1)) for t in range(8)]


def partner(tile):
    lane = lax.broadcasted_iota(jnp.int32, tile.shape, 1)
    return jnp.where(lane % HEAD < 32, pltpu.roll(tile, 96, 1), pltpu.roll(tile, 32, 1))


def inverse_rms(values):
    return lax.rsqrt(jnp.sum(values * values, axis=1, keepdims=True) * (1.0 / D) + EPSILON)


def norm_back(values, inv, gain, grad):
    scaled = grad * gain
    mean = jnp.sum(scaled * values, axis=1, keepdims=True) * (1.0 / D)
    grad_values = inv * scaled - values * (inv * inv * inv) * mean
    return grad_values, jnp.sum(grad * values * inv, axis=0, keepdims=True)


def project_kernel(
    table, tok, gain, w, cosine, sine, q_ref, own_ref, nt_ref, flag, left, right, limit
):
    values = tok[...].astype(F32)
    normed = values * inverse_rms(values) * gain[...]
    low = normed.astype(BF16)
    nt_ref[...] = normed.T.astype(BF16)
    lanes = low_lanes(HALF)
    blocks = []
    for t in range(13):
        u = dot_nn(low, w[:, t * 128 : (t + 1) * 128])
        if t < 10:
            u = u * cosine[...] + partner(u) * sine[...]
        blocks += heads_of_tile(u)
    for head in range(HEADS):
        at = head % GROUP * HALF
        q_ref[head // GROUP, at : at + HALF, :] = blocks[head].astype(BF16)
    for i in range(2 * KV_HEADS):
        own_ref[i * HALF : (i + 1) * HALF, :] = turn(blocks[HEADS + i]).astype(BF16)

    ctx = lax.axis_index("ctx")
    mine = jnp.minimum(table[2 * ctx], table[2 * ctx + 1])
    lane = lax.broadcasted_iota(jnp.int32, (1, 128), 1)
    first = lane < HALF
    offset = lax.rem(lane, HALF)

    def one(i, _):
        early = jnp.minimum(table[2 * i], table[2 * i + 1])
        turn_late = early >= mine
        m = jnp.where(turn_late, 1.0, 0.0)
        row = pl.ds(i, 1)
        flag[row, :] = jnp.where(first, 1.0, m)
        left[row, :] = jnp.where(first, m, 1.0 - m)
        right[row, :] = jnp.where(first, 1.0 - m, 0.0)
        gap = jnp.where(turn_late, mine - early, early - mine)
        blocks_back = jnp.where(first, early - (63 - mine), gap)
        limit[row, :] = (blocks_back * HALF + offset).astype(F32)
        return 0

    lax.fori_loop(0, CTX, one, 0)
    zero = jnp.zeros((1, 128), F32)
    for ref in (flag, left, right):
        ref[CTX:TILES, :] = zero
    limit[CTX:TILES, :] = jnp.where(first, offset, 10**6).astype(F32)


def project(table, tok, gain, w, cosine, sine):
    return pl.pallas_call(
        project_kernel,
        out_shape=[
            jax.ShapeDtypeStruct((KV_HEADS, ROWS, 128), BF16),
            jax.ShapeDtypeStruct((640, 128), BF16),
            jax.ShapeDtypeStruct((D, 128), BF16),
        ]
        + [jax.ShapeDtypeStruct((TILES, 128), F32)] * 4,
        in_specs=[pl.BlockSpec(memory_space=pltpu.SMEM)] + [VM] * 5,
        out_specs=[VM] * 7,
        compiler_params=pltpu.CompilerParams(vmem_limit_bytes=BIG),
        name="project",
    )(table, tok, gain, w, cosine, sine)


def middle_kernel(
    o, tok, cot, gain, out_hbm, gate_hbm, up_hbm, down_hbm,
    layer_out, grad_mid, do_rows, gain_grad, nt, dgu, gt, hid, at_t, gb,
    out_w, gate_w, up_w, down_w, sem,
):
    loads = []
    pairs = ((out_hbm, out_w), (gate_hbm, gate_w), (up_hbm, up_w), (down_hbm, down_w))
    for i, (src, dst) in enumerate(pairs):
        copy = pltpu.make_async_copy(src, dst, sem.at[i])
        copy.start()
        loads.append(copy)
    attended = jnp.concatenate(get_heads(o), axis=1)
    at_t[...] = attended.T[:D].astype(BF16)
    cot_low = cot[...]
    gt[0] = cot_low.astype(F32).T.astype(BF16)
    loads[0].wait()
    middle = tok[...].astype(F32) + dot_nn(attended.astype(BF16)[:, :D], out_w[...])
    inv = inverse_rms(middle)
    normed = middle * inv * gain[...]
    low = normed.astype(BF16)
    nt[...] = normed.T.astype(BF16)
    loads[1].wait()
    gate = dot_nn(low, gate_w[...])
    sigmoid = jax.nn.sigmoid(gate)
    silu = gate * sigmoid
    loads[2].wait()
    up = dot_nn(low, up_w[...])
    hidden = (silu * up).astype(BF16)
    for f in range(4):
        hid[f] = hidden[:, f * 640 : (f + 1) * 640]
    loads[3].wait()
    total = middle
    for f in range(4):
        total = total + dot_nt(hidden[:, f * 640 : (f + 1) * 640], down_w[f * D : (f + 1) * D, :])
    layer_out[...] = total.astype(BF16)
    grad_hidden = jnp.concatenate(
        [dot_nn(cot_low, down_w[f * D : (f + 1) * D, :]) for f in range(4)], axis=1
    )
    grad_gate = (grad_hidden * up * sigmoid * (1.0 + gate * (1.0 - sigmoid))).astype(BF16)
    grad_up = (grad_hidden * silu).astype(BF16)
    dgu[0, :, 0:FF] = grad_gate
    dgu[0, :, FF : 2 * FF] = grad_up
    grad_norm = dot_nt(grad_gate, gate_w[...]) + dot_nt(grad_up, up_w[...])
    grad_values, gain_grad[...] = norm_back(middle, inv, gain[...], grad_norm)
    grad_middle = cot_low.astype(F32) + grad_values
    grad_mid[...] = grad_middle
    branch = grad_middle.astype(BF16)
    gb[0] = jnp.concatenate([branch, jnp.zeros((TOK, 64), BF16)], axis=1)
    put_heads(do_rows, dot_nt(branch, out_w[...]))


def middle(o, tok, cot, gain, out_w, gate_w, up_w, down_w):
    weights = (out_w, gate_w, up_w, down_w)
    return pl.pallas_call(
        middle_kernel,
        out_shape=[
            jax.ShapeDtypeStruct((TOK, D), BF16),
            jax.ShapeDtypeStruct((TOK, D), F32),
            jax.ShapeDtypeStruct((KV_HEADS, ROWS, 128), BF16),
            jax.ShapeDtypeStruct((1, D), F32),
            jax.ShapeDtypeStruct((D, 128), BF16),
            jax.ShapeDtypeStruct((1, TOK, 2 * FF), BF16),
            jax.ShapeDtypeStruct((1, D, 128), BF16),
            jax.ShapeDtypeStruct((4, TOK, 640), BF16),
            jax.ShapeDtypeStruct((D, 128), BF16),
            jax.ShapeDtypeStruct((1, TOK, 1024), BF16),
        ],
        in_specs=[VM] * 4 + [ANY] * 4,
        out_specs=[VM] * 10,
        scratch_shapes=[pltpu.VMEM(w.shape, BF16) for w in weights]
        + [pltpu.SemaphoreType.DMA((4,))],
        compiler_params=pltpu.CompilerParams(vmem_limit_bytes=BIG),
        name="middle",
    )(o, tok, cot, gain, *weights)


def unproject_kernel(dq, dkv, cosine, sine, w, tok, gain, grad_mid, grad_tok, dqkv, gain_grad):
    tiles = get_heads(dq)
    low = low_lanes(TOK)
    turned = [turn(dkv[i * 128 : (i + 1) * 128, :].T) for i in range(5)]
    tiles[7] = jnp.where(low, tiles[7], turned[0])
    for i in range(4):
        tiles.append(jnp.where(low, turned[i], turned[i + 1]))
    tiles.append(jnp.where(low, turned[4], 0.0))
    for t in range(13):
        u = tiles[t]
        if t < 10:
            u = u * cosine[...] - partner(u) * sine[...]
        dqkv[0, :, t * 128 : (t + 1) * 128] = u.astype(BF16)
    grad_norm = dot_nt(dqkv[0], w[...])
    values = tok[...].astype(F32)
    grad_values, gain_grad[...] = norm_back(values, inverse_rms(values), gain[...], grad_norm)
    grad_tok[...] = grad_mid[...] + grad_values


def unproject(dq, dkv, cosine, sine, w, tok, gain, grad_mid):
    return pl.pallas_call(
        unproject_kernel,
        out_shape=[
            jax.ShapeDtypeStruct((TOK, D), F32),
            jax.ShapeDtypeStruct((1, TOK, 1664), BF16),
            jax.ShapeDtypeStruct((1, D), F32),
        ],
        in_specs=[VM] * 8,
        out_specs=[VM] * 3,
        compiler_params=pltpu.CompilerParams(vmem_limit_bytes=BIG),
        name="unproject",
    )(dq, dkv, cosine, sine, w, tok, gain, grad_mid)


def unpack_kernel(g_in, u_in, d_in, o_in, qkv, g, u, d, o, q, k, v):
    for t in range(4):
        rows, lanes = slice(t * 240, (t + 1) * 240), slice(t * 128, (t + 1) * 128)
        g[:, lanes] = g_in[rows, :].astype(F32)
        u[:, lanes] = u_in[rows, :].astype(F32)
    d[...] = d_in[...].astype(F32)
    step = pl.program_id(0)

    @pl.when(step < 4)
    def _():
        o[:, 0:128] = o_in[0:240, :].astype(F32)
        o[:, 128:256] = o_in[240:480, :].astype(F32)

    @pl.when(step == 0)
    def _():
        tiles = [qkv[t * 240 : (t + 1) * 240, :].astype(F32) for t in range(13)]
        low = low_lanes(240)
        for t in range(7):
            q[:, t * 128 : (t + 1) * 128] = tiles[t]
        q[:, 896:960] = tiles[7][:, :64]
        turned = [turn(t) for t in tiles[7:10]]
        k[:, 0:128] = jnp.where(low, turned[0], turned[1])
        k[:, 128:256] = jnp.where(low, turned[1], turned[2])
        k[:, 256:320] = turned[2][:, :64]
        v[:, 0:128] = tiles[10]
        v[:, 128:256] = tiles[11]
        v[:, 256:320] = tiles[12][:, :64]


def unpack(done, qkv):
    def whole(*shape):
        return pl.BlockSpec(shape, lambda i: (0, 0))

    return pl.pallas_call(
        unpack_kernel,
        grid=(5,),
        out_shape=[
            jax.ShapeDtypeStruct(shape, F32)
            for shape in (
                (240, FF), (240, FF), (D, 640), (240, D), (240, D), (240, 320), (240, 320),
            )
        ],
        in_specs=[
            pl.BlockSpec((960, 128), lambda i: (i, 0)),
            pl.BlockSpec((960, 128), lambda i: (5 + i, 0)),
            pl.BlockSpec((960, 128), lambda i: (10 + i, 0)),
            pl.BlockSpec((480, 128), lambda i: (30 + jnp.minimum(i, 3), 0)),
            whole(*qkv.shape),
        ],
        out_specs=[
            pl.BlockSpec((240, 512), lambda i: (0, i)),
            pl.BlockSpec((240, 512), lambda i: (0, i)),
            pl.BlockSpec((D, 128), lambda i: (0, i)),
            pl.BlockSpec((240, 256), lambda i: (0, jnp.minimum(i, 3))),
            whole(240, D),
            whole(240, 320),
            whole(240, 320),
        ],
        compiler_params=pltpu.CompilerParams(vmem_limit_bytes=BIG),
        name="unpack",
    )(done, done, done, done, qkv)


def rope_tables(early):
    row = lax.broadcasted_iota(jnp.int32, (TOK, 128), 0)
    lane = lax.broadcasted_iota(jnp.int32, (TOK, 128), 1)
    block = jnp.where(row < HALF, early, 63 - early)
    position = (block * HALF + row % HALF).astype(F32)
    frequency = BASE ** (-(lane % 32).astype(F32) / 32)
    angles = position * frequency
    return jnp.cos(angles), jnp.where(lane % HEAD < 32, -1.0, 1.0) * jnp.sin(angles)


def swap_rows(a, swap):
    return jnp.where(swap, jnp.concatenate([a[HALF:], a[:HALF]], axis=0), a)


def on_device(
    tokens, cotangent, block_table, attn_gain, w_query, w_key, w_value, w_out, mlp_gain,
    w_gate, w_up, w_down,
):
    ctx = lax.axis_index("ctx")
    gains = jnp.pad(jnp.stack([attn_gain, mlp_gain]), ((0, 14), (0, 16)))
    blank = jnp.zeros((240, 64), BF16)
    qkv_shard = jnp.concatenate([w_query, w_key, w_value, blank], axis=1)
    gains_all, qkv_w = gather_weights((gains, qkv_shard), 0)
    gains_all = gains_all.reshape(4, 16, 256)[:, :2, :240].astype(F32)
    gain_a = gains_all[:, 0].reshape(1, D)
    gain_b = gains_all[:, 1].reshape(1, D)

    own_blocks = lax.dynamic_slice_in_dim(block_table, 2 * ctx, 2)
    swap = own_blocks[0] > own_blocks[1]
    cosine, sine = rope_tables(jnp.min(own_blocks))
    tok = swap_rows(tokens[0], swap)
    cot = swap_rows(cotangent[0], swap)

    q_rows, own_kv, na_t, *plan = project(block_table, tok, gain_a, qkv_w, cosine, sine)
    o_rows, logs, kv, out_w, gate_w, up_w, down_w = forward(
        q_rows, own_kv, plan, (w_out, w_gate, w_up, w_down.T), 1
    )
    kv = kv.reshape(CTX, 640, 128)
    layer_out, grad_mid, do_rows, grad_gain_b, nb_t, dgu, cot_t, hidden, at_t, branch = middle(
        o_rows, tok, cot, gain_b, out_w, gate_w, up_w, down_w
    )
    ready = Reduction(
        (
            (nb_t.reshape(2, 2, 240, 128), dgu),
            (cot_t, hidden.reshape(2, 2, TOK, 640)),
            (at_t.reshape(2, 2, 240, 128), branch),
        ),
        None,
    )
    dq_rows, dkv, done = backward(q_rows, do_rows, o_rows, logs, kv, own_kv, plan, ready, 2)
    grad_tokens, grad_qkv, grad_gain_a = unproject(
        dq_rows, dkv, cosine, sine, qkv_w, tok, gain_a, grad_mid
    )
    gain_rows = jnp.stack([grad_gain_a, grad_gain_b]).reshape(2, 4, 240).transpose(1, 0, 2)
    gain_rows = jnp.pad(gain_rows, ((0, 0), (0, 0), (0, 16))).reshape(2, 2, 4, 128).astype(BF16)
    gain_rows = jnp.pad(gain_rows, ((0, 0), (0, 0), (0, 12), (0, 0)))
    late = Reduction(((na_t.reshape(2, 2, 240, 128), grad_qkv),), gain_rows, True)
    flat_done, flat = finish(done, ready.sizes, ready.used, late, 3)
    shard_g, shard_u, shard_d, shard_o, shard_q, shard_k, shard_v = unpack(flat_done, flat)
    shard_gains = flat[3120:3124].reshape(2, 256)[:, :240].astype(F32)
    return (
        swap_rows(layer_out, swap)[None],
        swap_rows(grad_tokens, swap)[None],
        shard_gains[0],
        shard_q,
        shard_k,
        shard_v,
        shard_o,
        shard_gains[1],
        shard_g,
        shard_u,
        shard_d.T,
    )


def solution(mesh):
    rows, cut = P("fsdp", "ctx", None), P("fsdp", None)
    return jax.shard_map(
        on_device,
        mesh=mesh,
        in_specs=(rows, rows, P(), P("fsdp"), cut, cut, cut, cut, P("fsdp"), cut, cut, cut),
        out_specs=(rows, rows, P("fsdp"), cut, cut, cut, cut, P("fsdp"), cut, cut, cut),
        check_vma=False,
    )
```

```python
import functools
import math

import jax
import jax.numpy as jnp
from jax import lax
from jax.experimental import pallas as pl
from jax.experimental.pallas import tpu as pltpu
from jax.sharding import PartitionSpec as P

D = 960
HEADS = 15
KV_HEADS = 5
GROUP = 3
HEAD = 64
FF = 2560
TOK = 128
HALF = 64
CTX = 32
TILES = 33
KEYS = TILES * 128
SCALE = HEAD ** (-0.5)
EPSILON = 1e-05
BASE = 10000.0
LOG2E = math.log2(math.e)
NEG = -1e30
MESH = pl.DeviceIdType.MESH
ANY = pl.BlockSpec(memory_space=pl.ANY)
VM = pl.BlockSpec(memory_space=pltpu.VMEM)
BIG = 56 * 2**20
F32 = jnp.float32
BF16 = jnp.bfloat16


def here():
    ctx = lax.axis_index("ctx")
    shard = lax.axis_index("fsdp")
    return {
        "z": ctx // 8,
        "yh": (ctx // 4) % 2,
        "x": ctx % 4,
        "yl": shard // 2,
        "c": shard % 2,
    }


def device(place, **moved):
    p = {**place, **moved}
    return (p["z"] * 8 + p["yh"] * 4 + p["x"], p["yl"] * 2 + p["c"])


def greet(devices):
    sem = pltpu.get_barrier_semaphore()
    for d in devices:
        pl.semaphore_signal(sem, inc=1, device_id=d, device_id_type=MESH)
    pl.semaphore_wait(sem, len(devices))


class Sems:
    def __init__(self, send, recv):
        self.send, self.recv, self.at = send, recv, 0

    def push(self, src, dst, dev):
        copy = pltpu.make_async_remote_copy(
            src_ref=src,
            dst_ref=dst,
            send_sem=self.send.at[self.at],
            recv_sem=self.recv.at[self.at],
            device_id=dev,
            device_id_type=MESH,
        )
        self.at += 1
        copy.start()
        return copy


def start_gather(me, sems, local, arrays, stages=None):
    f = me["yl"] * 2 + me["c"]
    near = device(me, yl=1 - me["yl"])
    far = device(me, yl=1 - me["yl"], yh=1 - me["yh"])
    mate = device(me, c=1 - me["c"])
    parts, kept, own = [], [], []
    for i, (a, b) in enumerate(arrays):
        rows = a.shape[0]
        first = rows // 32 * 16 if i % 2 else (rows + 31) // 32 * 16
        for lo, size, dev in ((0, first, near), (first, rows - first, far)):
            if size:
                src = a.at[pl.ds(lo, size)]
                dst = b.at[pl.ds(pl.multiple_of(f * rows + lo, 16), size)]
                parts.append((sems.push(src, dst, dev), b, rows, lo, size))
    for i, (a, b) in enumerate(arrays):
        rows = a.shape[0]
        dst = b.at[pl.ds(pl.multiple_of(f * rows, 16), rows)]
        kept.append(sems.push(a, dst, mate))
        stage = a if stages is None else stages[i]
        if stages is not None:
            load = pltpu.make_async_copy(a, stage, local.at[i])
            load.start()
        own.append((stage, dst, local.at[i]))
    if stages is not None:
        for (a, _), (stage, _, sem) in zip(arrays, own):
            pltpu.make_async_copy(a, stage, sem).wait()
    own = [pltpu.make_async_copy(*copy) for copy in own]
    for copy in own:
        copy.start()
    return parts, kept, own


def relay_gather(me, sems, started):
    parts, kept, _ = started
    across = (1 - me["yl"]) * 2 + me["c"]
    mate = device(me, c=1 - me["c"])
    for copy, b, rows, lo, size in parts:
        copy.wait_recv()
        span = b.at[pl.ds(pl.multiple_of(across * rows + lo, 16), size)]
        kept.append(sems.push(span, span, mate))


def end_gather(started):
    parts, kept, own = started
    for copy in own:
        copy.wait()
    for copy in kept:
        copy.wait()
    for copy, *_ in parts:
        copy.wait_send()


def gather_kernel(count, *refs):
    arrays = list(zip(refs[:count], refs[count : 2 * count]))
    send, recv, local = refs[2 * count :]
    me = here()
    flip = 1 - me["yl"]
    greet((device(me, yl=flip), device(me, yl=flip, yh=1 - me["yh"]), device(me, c=1 - me["c"])))
    sems = Sems(send, recv)
    started = start_gather(me, sems, local, arrays)
    relay_gather(me, sems, started)
    end_gather(started)


def gathered(arrays):
    return [jax.ShapeDtypeStruct((4 * a.shape[0], *a.shape[1:]), a.dtype) for a in arrays]


def gather_weights(arrays, collective_id):
    n = len(arrays)
    return pl.pallas_call(
        functools.partial(gather_kernel, n),
        out_shape=gathered(arrays),
        in_specs=[VM] * n,
        out_specs=[ANY] * n,
        scratch_shapes=[
            pltpu.SemaphoreType.DMA((5 * n,)),
            pltpu.SemaphoreType.DMA((5 * n,)),
            pltpu.SemaphoreType.DMA((n,)),
        ],
        compiler_params=pltpu.CompilerParams(
            collective_id=collective_id, has_side_effects=True, vmem_limit_bytes=BIG
        ),
        name="gather_weights",
    )(*arrays)


class Ring:
    def __init__(self, me, axis):
        at = me[axis]
        self.me = at
        self.right_at, self.opposite_at, self.left_at = (lax.rem(at + d, 4) for d in (1, 2, 3))
        self.right = device(me, **{axis: self.right_at})
        self.left = device(me, **{axis: self.left_at})
        self.opposite = device(me, **{axis: self.opposite_at})


class Share:
    def __init__(self, sems, ring, src, place, halves):
        self.sems, self.ring, self.place, self.halves = sems, ring, place, halves
        dst = place(ring.me)
        self.copies = [sems.push(src, dst, ring.right), sems.push(src, dst, ring.left)]
        self.passed, self.here = [], False
        if halves is None:
            self.passed.append(sems.push(src, dst, ring.opposite))

    def near(self):
        if not self.here:
            for copy in self.copies:
                copy.wait_recv()
            self.here = True

    def relay(self):
        self.near()
        if self.halves is not None:
            ring, push = self.ring, self.sems.push
            half = self.halves(self.place(ring.left_at))[0]
            self.passed.append(push(half, half, ring.right))
            half = self.halves(self.place(ring.right_at))[1]
            self.passed.append(push(half, half, ring.left))

    def arrive(self):
        for copy in self.passed:
            copy.wait_recv()

    def end(self):
        for copy in self.copies + self.passed:
            copy.wait_send()


def gather_kv(me, sems, kv, out, once_across):
    x, yh, z = me["x"], me["yh"], me["z"]
    other = device(me, yh=1 - yh)
    rings = Ring(me, "x"), Ring(me, "z")
    spans = pl.ds(0, 320), pl.ds(320, 320)
    across = [sems.push(kv.at[p], out.at[z, yh, x, p], other) for p in spans]

    def near(axis, row, src):
        lo = 320 * axis

        def place(at):
            ref = out.at[z, row, at] if axis == 0 else out.at[at, row, x]
            return ref.at[spans[axis]]

        def halves(ref):
            return ref.at[pl.ds(0, 160)], ref.at[pl.ds(160, 160)]

        return Share(sems, rings[axis], src, place, halves)

    def far(axis, row):
        def place(at):
            return out.at[at, row, :, spans[0]] if axis == 0 else out.at[:, row, at, spans[1]]

        def halves(ref):
            return ref.at[pl.ds(0, 2)], ref.at[pl.ds(2, 2)]

        src = place(rings[1 - axis].me)
        return Share(sems, rings[1 - axis], src, place, halves)

    first = [near(axis, yh, kv.at[spans[axis]]) for axis in (0, 1)]
    once_across()
    out[z, yh, x] = kv[...]
    for share in first:
        share.relay()
    second = []
    for axis in (0, 1):
        across[axis].wait_recv()
        row = 1 - yh
        src = out.at[z, row, x, spans[axis]]
        second.append(near(axis, row, src))
    last = []
    for axis in (0, 1):
        first[axis].arrive()
        last.append(far(axis, yh))
    for share in second:
        share.relay()
    for axis in (0, 1):
        second[axis].arrive()
        last.append(far(axis, 1 - yh))
    for share in last:
        share.relay()
    for share in last:
        share.arrive()
    return across, first + second + last


def add_low(a, b):
    return (a.astype(F32) + b.astype(F32)).astype(BF16)


class Fold:
    def __init__(self, sems, ring, block, landing, passing, direct=False):
        self.sems, self.ring, self.block, self.direct = sems, ring, block, direct
        self.landing, self.passing = landing, passing
        self.copies, self.passed, self.sent = {}, {}, []

    def start_opposite(self, half):
        ring = self.ring
        src = self.block(ring.opposite_at, half)
        dev = ring.opposite if self.direct else (ring.right, ring.left)[half]
        self.passed[half] = self.sems.push(src, self.passing(half), dev)

    def start_direct(self, half):
        ring = self.ring
        at, dev = ((ring.left_at, ring.left), (ring.right_at, ring.right))[half]
        side = 1 - half
        self.copies[side, half] = self.sems.push(
            self.block(at, half), self.landing(side, half), dev
        )

    def relay(self, half):
        ring = self.ring
        at, dev = ((ring.right_at, ring.right), (ring.left_at, ring.left))[half]
        src = self.block(at, half)
        if not self.direct:
            self.passed[half].wait_recv()
            src[...] = add_low(src[...], self.passing(half)[...])
        self.copies[half, half] = self.sems.push(src, self.landing(half, half), dev)

    def total(self, half):
        for side in (0, 1):
            self.copies[side, half].wait_recv()
        total = self.block(self.ring.me, half)[...].astype(F32)
        for side in (0, 1):
            total = total + self.landing(side, half)[...].astype(F32)
        if self.direct:
            self.passed[half].wait_recv()
            total = total + self.passing(half)[...].astype(F32)
        return total

    def end(self):
        for copy in list(self.copies.values()) + list(self.passed.values()):
            copy.wait_send()


class Scatter:
    COPIES = 26
    SCRATCH = [
        pltpu.VMEM((2, 3, 2, 4, 320, 128), BF16),
        pltpu.VMEM((2, 2, 4, 320, 128), BF16),
        pltpu.VMEM((2, 3, 2, 320, 128), BF16),
        pltpu.VMEM((2, 320, 128), BF16),
        pltpu.VMEM((2, 320, 128), BF16),
    ]

    def __init__(self, me, sems, part, out, scratch):
        self.me, self.sems, self.part, self.out = me, sems, part, out
        self.r1, self.s1, self.r2, self.s2, self.r3 = scratch
        self.rings = Ring(me, "x"), Ring(me, "z")
        self.first, self.second, self.third = [], [], []
        rows = (1 - me["yh"], me["yh"])
        key, value = pl.ds(0, 320), pl.ds(320, 320)

        def block0(at, half):
            return part.at[at, rows[half], :, key]

        def block1(at, half):
            return part.at[:, rows[half], at, value]

        for axis, block in enumerate((block0, block1)):
            r1, s1, r2 = self.r1, self.s1, self.r2
            self.first.append(
                Fold(
                    sems,
                    self.rings[1 - axis],
                    block,
                    lambda side, half, axis=axis: r1.at[axis, side, half],
                    lambda half, axis=axis: r1.at[axis, 2, half],
                )
            )
            self.second.append(
                Fold(
                    sems,
                    self.rings[axis],
                    lambda at, half, axis=axis: s1.at[axis, half, at],
                    lambda side, half, axis=axis: r2.at[axis, side, half],
                    lambda half, axis=axis: r2.at[axis, 2, half],
                )
            )

    def start(self):
        for half in (0, 1):
            for fold in self.first:
                fold.start_opposite(half)
        for half in (0, 1):
            for fold in self.first:
                fold.start_direct(half)

    def relay(self):
        for half in (0, 1):
            for fold in self.first:
                fold.relay(half)

    def middle(self):
        for half in (0, 1):
            for axis in (0, 1):
                self.s1[axis, half] = self.first[axis].total(half).astype(BF16)
                self.second[axis].start_opposite(half)
                self.second[axis].start_direct(half)
        for half in (0, 1):
            for fold in self.second:
                fold.relay(half)

    def last(self):
        other = device(self.me, yh=1 - self.me["yh"])
        for axis in (0, 1):
            self.s2[axis] = self.second[axis].total(0).astype(BF16)
            self.third.append(self.sems.push(self.s2.at[axis], self.r3.at[axis], other))
        for axis in (0, 1):
            self.out[pl.ds(axis * 320, 320), :] = self.second[axis].total(1)

    def end(self):
        for axis in (0, 1):
            self.third[axis].wait_recv()
            span = pl.ds(axis * 320, 320)
            self.out[span, :] = self.out[span, :] + self.r3[axis].astype(F32)
        for fold in self.first + self.second:
            fold.end()
        for c in self.third:
            c.wait_send()


def build_tiles(head, kv_ref, own_ref, left_ref, tiles_ref, base):
    lane = lax.broadcasted_iota(jnp.int32, (HALF, 128), 1)
    start = pl.multiple_of(base + head * HALF, HALF)

    def one(i, _):
        block = kv_ref[i, pl.ds(start, HALF), :].astype(F32)
        top = jnp.where(lane < HALF, block, 0.0)
        low = pltpu.roll(block, HALF, 1) * left_ref[pl.ds(i, 1), :]
        at = pl.multiple_of(i * 128, 128)
        tiles_ref[pl.ds(at, 128), :] = jnp.concatenate([top, low], axis=0).astype(BF16)
        return 0

    lax.fori_loop(0, CTX, one, 0, unroll=32)
    block = own_ref[pl.ds(start, HALF), :].astype(F32)
    top = jnp.where(lane < HALF, 0.0, pltpu.roll(block, HALF, 1))
    tiles_ref[pl.ds(CTX * 128, 128), :] = jnp.concatenate(
        [top, jnp.zeros_like(top)], axis=0
    ).astype(BF16)


def dot_nt(a, b):
    return lax.dot_general(a, b, (((1,), (1,)), ((), ())), preferred_element_type=F32)


def dot_nn(a, b):
    return lax.dot_general(a, b, (((1,), (0,)), ((), ())), preferred_element_type=F32)


ROWS = GROUP * HALF


def row_offset():
    return lax.rem(lax.broadcasted_iota(jnp.int32, (ROWS, 128), 0), HALF).astype(F32)


def attend_head(head, q, kv_ref, own_ref, flag_ref, left_ref, limit_ref, kk, vv):
    build_tiles(head, kv_ref, own_ref, left_ref, kk, 0)
    build_tiles(head, kv_ref, own_ref, left_ref, vv, 320)
    offset = row_offset()
    low = jnp.full((ROWS, 128), NEG, F32)
    s = dot_nt(q, kk[...]) * (SCALE * LOG2E)
    tiles = []
    top_l, top_e = low, low
    for i in range(TILES):
        tile = s[:, i * 128 : (i + 1) * 128]
        tile = jnp.where(limit_ref[i : i + 1, :] <= offset, tile, NEG)
        tiles.append(tile)
        late = flag_ref[i : i + 1, :] > 0.5
        top_l = jnp.maximum(top_l, jnp.where(late, tile, NEG))
        top_e = jnp.maximum(top_e, jnp.where(late, NEG, tile))
    max_l = jnp.broadcast_to(jnp.max(top_l, axis=1, keepdims=True), (ROWS, 128))
    max_e = jnp.broadcast_to(jnp.max(top_e, axis=1, keepdims=True), (ROWS, 128))
    sum_l = jnp.zeros((ROWS, 128), F32)
    sum_e = jnp.zeros((ROWS, 128), F32)
    probs = []
    for i in range(TILES):
        late = flag_ref[i : i + 1, :] > 0.5
        p = jnp.exp2(tiles[i] - jnp.where(late, max_l, max_e))
        p_l = jnp.where(late, p, 0.0)
        sum_l = sum_l + p_l
        sum_e = sum_e + (p - p_l)
        probs.append(p.astype(BF16))
    total = dot_nn(jnp.concatenate(probs, axis=1), vv[...])
    late = lax.broadcasted_iota(jnp.int32, (ROWS, 128), 1) < HALF
    row_sum = jnp.where(
        late, jnp.sum(sum_l, axis=1, keepdims=True), jnp.sum(sum_e, axis=1, keepdims=True)
    )
    return total / row_sum, jnp.where(late, max_l, max_e) + jnp.log2(row_sum)


def forward_kernel(count, q_ref, own_ref, flag_ref, left_ref, limit_ref, *refs):
    shards, refs = refs[:count], refs[count:]
    o_ref, l_ref, kv_out, *full = refs[: 3 + count]
    kv, kk, vv, *stages, send, recv, local = refs[3 + count :]
    me = here()
    greet_axes(me)
    sems = Sems(send, recv)
    started = []

    def start_weights():
        started.extend(start_gather(me, sems, local, list(zip(shards, full)), stages))

    across, shares = gather_kv(me, sems, own_ref, kv, start_weights)
    keep = pltpu.make_async_copy(kv, kv_out, local.at[count])
    keep.start()
    flat = kv.reshape(CTX, 640, 128)

    def one(head, _):
        o, logs = attend_head(
            head, q_ref[head], flat, own_ref, flag_ref, left_ref, limit_ref, kk, vv
        )
        o_ref[head] = o
        l_ref[head] = logs
        return 0

    lax.fori_loop(0, 3, one, 0)
    relay_gather(me, sems, started)
    lax.fori_loop(3, KV_HEADS, one, 0)
    end_gather(started)
    for copy in across:
        copy.wait_send()
    for share in shares:
        share.end()
    keep.wait()


def forward(q, own, plan, shards, collective_id):
    flags, left, _, limits = plan
    n = len(shards)
    copies = 5 * n + 2 + 8 * 4
    return pl.pallas_call(
        functools.partial(forward_kernel, n),
        out_shape=[jax.ShapeDtypeStruct((KV_HEADS, ROWS, 128), F32)] * 2
        + [jax.ShapeDtypeStruct((4, 2, 4, 640, 128), BF16)]
        + gathered(shards),
        in_specs=[VM] * 5 + [ANY] * n,
        out_specs=[VM, VM, ANY] + [ANY] * n,
        scratch_shapes=[
            pltpu.VMEM((4, 2, 4, 640, 128), BF16),
            pltpu.VMEM((KEYS, 128), BF16),
            pltpu.VMEM((KEYS, 128), BF16),
            *[pltpu.VMEM(a.shape, BF16) for a in shards],
            pltpu.SemaphoreType.DMA((copies,)),
            pltpu.SemaphoreType.DMA((copies,)),
            pltpu.SemaphoreType.DMA((n + 1,)),
        ],
        compiler_params=pltpu.CompilerParams(
            collective_id=collective_id, has_side_effects=True, vmem_limit_bytes=BIG
        ),
        name="forward",
    )(q, own, flags, left, limits, *shards)


def attend_back_head(
    head, q, do, o, logs, kv_ref, own_ref, flag_ref, left_ref, right_ref, limit_ref,
    dkv_ref, kk, vv,
):
    build_tiles(head, kv_ref, own_ref, left_ref, kk, 0)
    build_tiles(head, kv_ref, own_ref, left_ref, vv, 320)
    offset = row_offset()
    lane = lax.broadcasted_iota(jnp.int32, (ROWS, 128), 1)
    product = do.astype(F32) * o
    shape = (ROWS, 128)
    delta_l = jnp.broadcast_to(
        jnp.sum(jnp.where(lane < HALF, product, 0.0), axis=1, keepdims=True), shape
    )
    delta_e = jnp.broadcast_to(
        jnp.sum(jnp.where(lane < HALF, 0.0, product), axis=1, keepdims=True), shape
    )
    log_l = jnp.broadcast_to(logs[:, 0:1], shape)
    log_e = jnp.broadcast_to(logs[:, HALF : HALF + 1], shape)
    k_rows = pl.ds(pl.multiple_of(head * HALF, HALF), HALF)
    v_rows = pl.ds(pl.multiple_of(320 + head * HALF, HALF), HALF)
    small = lax.broadcasted_iota(jnp.int32, (HALF, 128), 1)
    keys = kk[...]
    s = dot_nt(q, keys) * (SCALE * LOG2E)
    dp = dot_nt(do, vv[...])
    probs, scores = [], []
    for i in range(TILES):
        cut = slice(i * 128, (i + 1) * 128)
        late = flag_ref[i : i + 1, :] > 0.5
        tile = jnp.where(limit_ref[i : i + 1, :] <= offset, s[:, cut], NEG)
        p = jnp.exp2(tile - jnp.where(late, log_l, log_e))
        probs.append(p.astype(BF16))
        scores.append((p * (dp[:, cut] - jnp.where(late, delta_l, delta_e))).astype(BF16))
    ds = jnp.concatenate(scores, axis=1)
    dq = dot_nn(ds, keys) * SCALE
    dk = dot_nn(q.astype(F32).T.astype(BF16), ds) * SCALE
    dv = dot_nn(do.astype(F32).T.astype(BF16), jnp.concatenate(probs, axis=1))
    mine = lax.axis_index("ctx")
    for rows, both in ((k_rows, dk), (v_rows, dv)):
        for i in range(CTX):
            cut = slice(i * 128, (i + 1) * 128)
            top, bottom = both[0:HALF, cut], both[HALF:128, cut]
            total = (
                top * flag_ref[i : i + 1, :]
                + pltpu.roll(bottom, HALF, 1) * right_ref[i : i + 1, :]
            )
            dkv_ref[i, rows, :] = total.astype(BF16)
        bottom = both[HALF:128, CTX * 128 :]
        before = dkv_ref[mine, rows, :].astype(F32)
        dkv_ref[mine, rows, :] = (before + jnp.where(small < HALF, bottom, 0.0)).astype(BF16)
    return dq


def pop(refs, count):
    taken = refs[:count]
    del refs[:count]
    return taken


class Column:
    COPIES = 24

    @staticmethod
    def scratch(pc):
        return [
            pltpu.VMEM((3, 4, 4 * pc, 128), BF16),
            pltpu.VMEM((4, 4 * pc, 128), BF16),
            pltpu.VMEM((3, 2, 2 * pc, 128), BF16),
            pltpu.VMEM((4 * pc, 128), BF16),
            pltpu.VMEM((3, 2, pc // 2, 128), BF16),
        ]

    def __init__(self, me, sems, grads, lo, pc, scratch, fin):
        self.me, self.sems, self.grads, self.lo, self.pc, self.fin = me, sems, grads, lo, pc, fin
        self.ry, self.sy, rx, self.sx, rz = scratch
        self.first = {}
        sy, sx, x = self.sy, self.sx, me["x"]

        def strip(at, half):
            return sy.at[lax.rem(at + 4 - x, 4), pl.ds(half * 2 * pc, 2 * pc)]

        def piece(at, half):
            return sx.at[pl.ds(pl.multiple_of(at * pc + half * (pc // 2), 16), pc // 2)]

        self.over_x = Fold(
            sems,
            Ring(me, "x"),
            strip,
            lambda side, half: rx.at[side, half],
            lambda half: rx.at[2, half],
        )
        self.over_z = Fold(
            sems,
            Ring(me, "z"),
            piece,
            lambda side, half: rz.at[side, half],
            lambda half: rz.at[2, half],
        )

    def rows(self, half, k):
        i = lax.rem(self.me["x"] + k, 4)
        start = pl.multiple_of(self.lo + (half * 16 + i * 4) * self.pc, 16)
        return pl.ds(start, 4 * self.pc)

    def start(self):
        me = self.me
        yl, yh = me["yl"], me["yh"]
        ways = (
            (1 - yl, yh, device(me, yl=1 - yl)),
            (1 - yl, 1 - yh, device(me, yl=1 - yl, yh=1 - yh)),
            (yl, 1 - yh, device(me, yh=1 - yh)),
        )
        for k in (2, 1, 3, 0):
            for slot, (shard, half, dev) in enumerate(ways):
                src = self.grads.at[shard, self.rows(half, k)]
                self.first[k, slot] = self.sems.push(src, self.ry.at[slot, k], dev)

    def fold_first(self, k):
        for slot in (0, 1, 2):
            self.first[k, slot].wait_recv()
        total = self.grads[self.me["yl"], self.rows(self.me["yh"], k)].astype(F32)
        for slot in (0, 1, 2):
            total = total + self.ry[slot, k].astype(F32)
        self.sy[k] = total.astype(BF16)
        if k == 2:
            self.over_x.start_opposite(0)
            self.over_x.start_opposite(1)
        elif k == 1:
            self.over_x.start_direct(1)
        elif k == 3:
            self.over_x.start_direct(0)

    def relay(self):
        self.over_x.relay(0)
        self.over_x.relay(1)

    def fold_second(self):
        for half in (0, 1):
            span = pl.ds(half * 2 * self.pc, 2 * self.pc)
            self.sx[span] = self.over_x.total(half).astype(BF16)
        for half in (0, 1):
            self.over_z.start_opposite(half)
            self.over_z.start_direct(half)

    def fold_third(self):
        self.over_z.relay(0)
        self.over_z.relay(1)

    def end(self):
        base = self.fin.shape[0] - self.pc
        for half in (0, 1):
            span = pl.ds(base + half * (self.pc // 2), self.pc // 2)
            self.fin[span, :] = self.over_z.total(half).astype(BF16)
        self.over_x.end()
        self.over_z.end()
        for copy in self.first.values():
            copy.wait_send()


class Reduction:
    def __init__(self, jobs, extra, direct=False, pc=0):
        self.operands, self.jobs, self.scratch, rows = [], [], [], 0
        self.direct = direct
        for left, right in jobs:
            self.operands += [left, right]
            m, n = left.shape[-2], right.shape[-1]
            self.jobs.append((left.ndim == 4, m, right.ndim == 4, n))
            self.scratch.append(pltpu.VMEM((left.shape[0], m, 256), BF16))
            self.scratch.append(pltpu.VMEM((right.shape[0], 256, n), BF16))
            rows += m * (n // 128)
        self.extra = extra is not None
        if self.extra:
            self.operands.append(extra)
            self.scratch.append(pltpu.VMEM((2, 2, 16, 128), BF16))
            rows += 16
        pieces = -(-rows // 256) - pc // 8
        self.sizes = ((pieces + 1) // 2 * 16, pieces // 2 * 16)
        self.pc = pc
        self.used = 16 * (sum(self.sizes) + 2 * pc)
        self.scratch.append(pltpu.VMEM((2, self.used, 128), BF16))
        for size in self.sizes:
            self.scratch += [
                pltpu.VMEM((3, 4, 2, size, 128), BF16),
                pltpu.VMEM((4, 2, size, 128), BF16),
                pltpu.VMEM((3, 2, size, 128), BF16),
                pltpu.VMEM((2, size, 128), BF16),
                pltpu.VMEM((4, size, 128), BF16),
            ]
        self.locals = 2 * len(jobs) + 1
        self.copies = 2 * len(jobs) + 1 + 48 + 12 + 6
        self.fin_shape = (sum(self.sizes) + pc, 128)
        if pc:
            self.scratch += Column.scratch(pc)
            self.copies += Column.COPIES

    def bind(self, me, sems, local, operands, scratch, fin):
        operands, scratch = list(operands), list(scratch)
        self.me, self.sems, self.local, self.fin = me, sems, local, fin
        self.sources, self.buffers = [], []
        core = me["c"]
        for cut_left, _, cut_right, _ in self.jobs:
            left, right = pop(operands, 2)
            lefts = (left.at[:, core], left.at[:, 1 - core]) if cut_left else (left, left)
            rights = (right.at[:, core], right.at[:, 1 - core]) if cut_right else (right, right)
            self.sources.append((*lefts, *rights))
            self.buffers.append(pop(scratch, 2))
        if self.extra:
            self.extra_refs = (operands[0].at[:, core], operands[0].at[:, 1 - core])
            self.extra_buffer = scratch.pop(0)
        self.grads = scratch.pop(0)
        self.parts = [pop(scratch, 5) for _ in self.sizes]
        if self.pc:
            lo = 16 * sum(self.sizes)
            self.column = Column(me, sems, self.grads, lo, self.pc, scratch, fin)
        xs, zs = Ring(me, "x"), Ring(me, "z")
        self.plans = (
            (0, self.sizes[0], xs, zs),
            (16 * self.sizes[0], self.sizes[1], zs, xs),
        )
        self.first, self.second, self.third = {}, {}, {}
        for n, (lo, size, ring, cross) in enumerate(self.plans):
            r1, s1, r2, _, _ = self.parts[n]
            for k in range(4):
                j = lax.rem(cross.me + k, 4)

                def block(at, half, lo=lo, size=size, j=j):
                    start = pl.multiple_of(lo + (at * 4 + j) * size, 16)
                    return self.grads.at[half, pl.ds(start, size)]

                self.first[n, k] = Fold(
                    sems,
                    ring,
                    block,
                    lambda side, half, r1=r1, k=k: r1.at[side, k, half],
                    lambda half, r1=r1, k=k: r1.at[2, k, half],
                    self.direct,
                )

            def turned(at, half, s1=s1, cross=cross):
                return s1.at[lax.rem(at + 4 - cross.me, 4), half]

            self.second[n] = Fold(
                sems,
                cross,
                turned,
                lambda side, half, r2=r2: r2.at[side, half],
                lambda half, r2=r2: r2.at[2, half],
                self.direct,
            )

    def trade(self):
        mate = device(self.me, c=1 - self.me["c"])
        push = self.sems.push
        self.mine, self.traded = [], []

        def keep(src, dst):
            copy = pltpu.make_async_copy(src, dst, self.local.at[len(self.mine)])
            copy.start()
            self.mine.append(copy)

        here_, there = pl.ds(0, 128), pl.ds(128, 128)
        for (lm, lt, rm, rt), (lb, rb) in zip(self.sources, self.buffers):
            self.traded.append(push(lt, lb.at[:, :, there], mate))
            self.traded.append(push(rt, rb.at[:, there], mate))
            keep(lm, lb.at[:, :, here_])
            keep(rm, rb.at[:, here_])
        if self.extra:
            self.traded.append(push(self.extra_refs[1], self.extra_buffer.at[1], mate))
            keep(self.extra_refs[0], self.extra_buffer.at[0])

    def multiply(self, job):
        base = sum(m * (n // 128) for _, m, _, n in self.jobs[:job])
        for copy in self.mine[2 * job : 2 * job + 2]:
            copy.wait()
        for copy in self.traded[2 * job : 2 * job + 2]:
            copy.wait_recv()
        grads, (_, m, _, n), (lb, rb) = self.grads, self.jobs[job], self.buffers[job]
        strip = min(n, 1280) if n % 1280 == 0 else n
        for s in range(2):
            left = lb[min(s, lb.shape[0] - 1)]

            def block(i, _, left=left, s=s):
                at = pl.multiple_of(i * strip, 128)
                right = rb[min(s, rb.shape[0] - 1), :, pl.ds(at, strip)]
                result = dot_nn(left, right).astype(BF16)
                for w in range(strip // 128):
                    to = pl.multiple_of(base + (i * (strip // 128) + w) * m, 16)
                    grads[s, pl.ds(to, m), :] = result[:, w * 128 : (w + 1) * 128]
                return 0

            if n == strip:
                block(0, 0)
            else:
                lax.fori_loop(0, n // strip, block, 0)

    def pad(self):
        base, grads = sum(m * (n // 128) for _, m, _, n in self.jobs), self.grads
        if self.extra:
            self.mine[-1].wait()
            self.traded[-1].wait_recv()
            for s in range(2):
                both = self.extra_buffer[0, s].astype(F32) + self.extra_buffer[1, s].astype(F32)
                grads[s, pl.ds(base, 16), :] = both.astype(BF16)
            base += 16
        if base < self.used:
            for s in range(2):
                grads[s, pl.ds(base, self.used - base), :] = jnp.zeros(
                    (self.used - base, 128), BF16
                )

    def start(self, n):
        for k in (2, 1, 3, 0):
            for half in (0, 1):
                self.first[n, k].start_opposite(half)
        for k in (2, 1, 3, 0):
            for half in (0, 1):
                self.first[n, k].start_direct(half)

    def relay(self, k):
        for half in (0, 1):
            for n in (0, 1):
                self.first[n, k].relay(half)

    def fold_first(self, k):
        for n in (0, 1):
            s1, second = self.parts[n][1], self.second[n]
            for half in (0, 1):
                s1[k, half] = self.first[n, k].total(half).astype(BF16)
            if k == 2:
                second.start_opposite(0)
                second.start_opposite(1)
            elif k == 1:
                second.start_direct(1)
            elif k == 3:
                second.start_direct(0)

    def fold_second(self):
        me, push = self.me, self.sems.push
        yh, yl = me["yh"], me["yl"]
        for half in (0, 1):
            for n in (0, 1):
                self.second[n].relay(half)
        for n in (0, 1):
            s2, r3 = self.parts[n][3:]
            for half in (0, 1):
                s2[half] = self.second[n].total(half).astype(BF16)
            slot = r3.at[yl * 2 + yh]
            self.third[n, 0] = push(s2.at[1 - yl], slot, device(me, yl=1 - yl))
            self.third[n, 1] = push(s2.at[1 - yl], slot, device(me, yl=1 - yl, yh=1 - yh))
            self.third[n, 2] = push(s2.at[yl], slot, device(me, yh=1 - yh))

    def fold_third(self):
        yh, yl = self.me["yh"], self.me["yl"]
        at = 0
        for n, size in enumerate(self.sizes):
            _, _, _, s2, r3 = self.parts[n]
            r3[yl * 2 + yh] = s2[yl]
            for i in (0, 1, 2):
                self.third[n, i].wait_recv()
            total = r3[0].astype(F32)
            for i in (1, 2, 3):
                total = total + r3[i].astype(F32)
            self.fin[pl.ds(at, size), :] = total.astype(BF16)
            at += size

    def end(self):
        for fold in list(self.first.values()) + list(self.second.values()):
            fold.end()
        for copy in self.traded + list(self.third.values()):
            copy.wait_send()


class Spread:
    COPIES = 81

    def __init__(self, me, sems, local, fin, out, sizes, direct=False, pc=0, other=None):
        self.direct, self.fin, self.pc, self.other = direct, fin, pc, other
        self.sems, self.local, self.out = sems, local, out
        self.kept, self.cross, self.own, self.near, self.far = [], [], [], [], []
        xs, zs = Ring(me, "x"), Ring(me, "z")
        base, yh = 16 * sum(sizes), me["yh"]
        self.plans = [(0, sizes[0], xs, zs), (16 * sizes[0], sizes[1], zs, xs)]
        self.swap = None
        if pc:
            self.plans.append((base + yh * (16 * pc), pc, xs, zs))
            self.plans.append((base + (1 - yh) * (16 * pc), pc, zs, xs))
            src = fin.at[pl.ds(sum(sizes), pc)]
            self.swap = sems.push(src, other, device(me, yh=1 - yh))
        at = 0
        for n in range(3 if pc else 2):
            size = self.plans[n][1]
            self.begin(n, fin.at[pl.ds(at, size)])
            at += size

    def begin(self, n, src):
        _, _, ring, cross = self.plans[n]
        copy = pltpu.make_async_copy(src, self.span(n, ring.me, cross.me), self.local.at[n])
        copy.start()
        self.kept.append(copy)
        place = functools.partial(self.span, n, ring.me)
        self.cross.append(Share(self.sems, cross, src, place, self.halves(n)))
        self.own.append(self.share(n, cross.me, src))

    def across(self):
        if self.pc:
            self.swap.wait_recv()
            self.begin(3, self.other)

    def span(self, n, i, j):
        lo, size, _, _ = self.plans[n]
        at = j * 4 + i if n == 3 else i * 4 + j
        return self.out.at[pl.ds(pl.multiple_of(lo + at * size, 16), size)]

    def halves(self, n):
        if self.direct:
            return None
        size = self.plans[n][1]
        first = size // 32 * 16
        return lambda ref: (ref.at[pl.ds(0, first)], ref.at[pl.ds(first, size - first)])

    def share(self, n, j, src=None):
        ring = self.plans[n][2]

        def place(i):
            return self.span(n, i, j)

        src = place(ring.me) if src is None else src
        return Share(self.sems, ring, src, place, self.halves(n))

    def relay(self):
        for share in self.cross:
            share.relay()
        for n, plan in enumerate(self.plans):
            self.near.append(self.share(n, plan[3].left_at))
            self.near.append(self.share(n, plan[3].right_at))

    def pass_on(self):
        for share in self.own:
            share.relay()
        for n, plan in enumerate(self.plans):
            self.cross[n].arrive()
            self.far.append(self.share(n, plan[3].opposite_at))

    def end(self):
        for share in self.near + self.far:
            share.relay()
        for share in self.own + self.near + self.far:
            share.arrive()
        for copy in self.kept:
            copy.wait()
        for share in self.cross + self.own + self.near + self.far:
            share.end()
        if self.pc:
            self.swap.wait_send()


def greet_axes(me, reach=2):
    flip = 1 - me["yl"]
    rings = Ring(me, "x"), Ring(me, "z")
    greet(
        [device(me, yl=flip), device(me, yl=flip, yh=1 - me["yh"]), device(me, c=1 - me["c"])]
        + [device(me, yh=1 - me["yh"])]
        + [dev for ring in rings for dev in (ring.left, ring.right, ring.opposite)[:reach]]
    )


def backward_kernel(reduction, *refs):
    refs = list(refs)
    q, do, o, logs, kv, own, flag, left, right, limit = pop(refs, 10)
    operands = pop(refs, len(reduction.operands))
    dq_ref, dkv_own, fin = pop(refs, 3)
    kv_here, dkv, kk, vv = pop(refs, 4)
    scatter_scratch = pop(refs, len(Scatter.SCRATCH))
    reduce_scratch = pop(refs, len(reduction.scratch))
    send, recv, local = refs
    me = here()
    greet_axes(me)
    sems = Sems(send, recv)
    reduction.bind(me, sems, local, operands, reduce_scratch, fin)
    reduction.trade()
    load = pltpu.make_async_copy(kv, kv_here, local.at[reduction.locals])
    load.start()
    scatter = Scatter(me, sems, dkv, dkv_own, scatter_scratch)
    flat = dkv.reshape(CTX, 640, 128)

    def one(head, _):
        dq_ref[head] = attend_back_head(
            head, q[head], do[head], o[head], logs[head], kv_here, own, flag,
            left, right, limit, flat, kk, vv,
        )
        return 0

    column = reduction.column
    reduction.multiply(0)
    reduction.start(0)
    reduction.multiply(1)
    reduction.start(1)
    reduction.multiply(2)
    reduction.pad()
    column.start()
    load.wait()
    lax.fori_loop(0, KV_HEADS, one, 0)
    for k in (2, 1):
        reduction.relay(k)
    scatter.start()
    for k in (3, 0):
        reduction.relay(k)
    for k in (2, 1, 3, 0):
        column.fold_first(k)
    scatter.relay()
    for k in (2, 1, 3, 0):
        reduction.fold_first(k)
    column.relay()
    scatter.middle()
    reduction.fold_second()
    column.fold_second()
    scatter.last()
    reduction.fold_third()
    column.fold_third()
    scatter.end()
    column.end()
    reduction.end()


def backward(q, do, o, logs, kv, own, plan, reduction, collective_id):
    flags, left, right, limits = plan
    copies = reduction.copies + Scatter.COPIES
    return pl.pallas_call(
        functools.partial(backward_kernel, reduction),
        out_shape=[
            jax.ShapeDtypeStruct((KV_HEADS, ROWS, 128), F32),
            jax.ShapeDtypeStruct((640, 128), F32),
            jax.ShapeDtypeStruct(reduction.fin_shape, BF16),
        ],
        in_specs=[VM] * 4 + [ANY] + [VM] * 5 + [ANY] * len(reduction.operands),
        out_specs=[VM, VM, VM],
        scratch_shapes=[
            pltpu.VMEM((CTX, 640, 128), BF16),
            pltpu.VMEM((4, 2, 4, 640, 128), BF16),
            pltpu.VMEM((KEYS, 128), BF16),
            pltpu.VMEM((KEYS, 128), BF16),
            *Scatter.SCRATCH,
            *reduction.scratch,
            pltpu.SemaphoreType.DMA((copies,)),
            pltpu.SemaphoreType.DMA((copies,)),
            pltpu.SemaphoreType.DMA((reduction.locals + 1,)),
        ],
        compiler_params=pltpu.CompilerParams(
            collective_id=collective_id, has_side_effects=True, vmem_limit_bytes=BIG
        ),
        name="backward",
    )(
        q, do, o, logs, kv, own, flags, left, right, limits, *reduction.operands,
    )


def finish_kernel(reduction, sizes, pc, *refs):
    refs = list(refs)
    done = refs.pop(0)
    operands = pop(refs, len(reduction.operands))
    out_done, out = pop(refs, 2)
    fin, other = pop(refs, 2)
    reduce_scratch = pop(refs, len(reduction.scratch))
    send, recv, local = refs
    me = here()
    greet_axes(me, 3)
    sems = Sems(send, recv)
    reduction.bind(me, sems, local, operands, reduce_scratch, fin)
    reduction.trade()
    slots = local.at[pl.ds(reduction.locals, 4)]
    spread = Spread(me, sems, slots, done, out_done, sizes, False, pc, other)
    reduction.multiply(0)
    reduction.pad()
    for n in (0, 1):
        reduction.start(n)
    for k in (2, 1, 3, 0):
        reduction.relay(k)
    spread.across()
    spread.relay()
    for k in (2, 1, 3, 0):
        reduction.fold_first(k)
    reduction.fold_second()
    spread.pass_on()
    reduction.fold_third()
    last = Spread(
        me, sems, local.at[pl.ds(reduction.locals + 4, 2)], fin, out, reduction.sizes, True
    )
    last.relay()
    last.pass_on()
    spread.end()
    last.end()
    reduction.end()


def finish(done, ready, reduction, collective_id):
    copies = reduction.copies + 2 * Spread.COPIES
    return pl.pallas_call(
        functools.partial(finish_kernel, reduction, ready.sizes, ready.pc),
        out_shape=[
            jax.ShapeDtypeStruct((ready.used, 128), BF16),
            jax.ShapeDtypeStruct((reduction.used, 128), BF16),
        ],
        in_specs=[VM] + [ANY] * len(reduction.operands),
        out_specs=[ANY, ANY],
        scratch_shapes=[
            pltpu.VMEM(reduction.fin_shape, BF16),
            pltpu.VMEM((ready.pc, 128), BF16),
            *reduction.scratch,
            pltpu.SemaphoreType.DMA((copies,)),
            pltpu.SemaphoreType.DMA((copies,)),
            pltpu.SemaphoreType.DMA((reduction.locals + 6,)),
        ],
        compiler_params=pltpu.CompilerParams(
            collective_id=collective_id, has_side_effects=True, vmem_limit_bytes=BIG
        ),
        name="finish",
    )(done, *reduction.operands)


def low_lanes(rows):
    return lax.broadcasted_iota(jnp.int32, (rows, 128), 1) < HALF


def turn(tile):
    return pltpu.roll(tile, HALF, 1)


def heads_of_tile(tile):
    early, late = tile[:HALF], tile[HALF:]
    low = low_lanes(HALF)
    return jnp.where(low, late, turn(early)), jnp.where(low, turn(late), early)


def tile_of_heads(first, second):
    low = low_lanes(HALF)
    early = jnp.where(low, turn(first), second)
    late = jnp.where(low, first, turn(second))
    return jnp.concatenate([early, late], axis=0)


def put_heads(ref, values):
    for t in range(8):
        if t < 7:
            tile = values[:, t * 128 : (t + 1) * 128]
        else:
            last = values[:, 896:960]
            tile = jnp.concatenate([last, jnp.zeros_like(last)], axis=1)
        for i, block in enumerate(heads_of_tile(tile)):
            head = 2 * t + i
            if head < HEADS:
                at = head % GROUP * HALF
                ref[head // GROUP, at : at + HALF, :] = block.astype(ref.dtype)


def get_heads(ref):
    def block(head):
        if head == HEADS:
            return jnp.zeros((HALF, 128), F32)
        at = head % GROUP * HALF
        return ref[head // GROUP, at : at + HALF, :].astype(F32)

    return [tile_of_heads(block(2 * t), block(2 * t + 1)) for t in range(8)]


def partner(tile):
    lane = lax.broadcasted_iota(jnp.int32, tile.shape, 1)
    return jnp.where(lane % HEAD < 32, pltpu.roll(tile, 96, 1), pltpu.roll(tile, 32, 1))


def inverse_rms(values):
    return lax.rsqrt(jnp.sum(values * values, axis=1, keepdims=True) * (1.0 / D) + EPSILON)


def norm_back(values, inv, gain, grad):
    scaled = grad * gain
    mean = jnp.sum(scaled * values, axis=1, keepdims=True) * (1.0 / D)
    grad_values = inv * scaled - values * (inv * inv * inv) * mean
    return grad_values, jnp.sum(grad * values * inv, axis=0, keepdims=True)


def project_kernel(
    table, tok, gain, w, cosine, sine, q_ref, own_ref, nt_ref, flag, left, right, limit
):
    values = tok[...].astype(F32)
    normed = values * inverse_rms(values) * gain[...]
    low = normed.astype(BF16)
    nt_ref[...] = normed.T.astype(BF16)
    lanes = low_lanes(HALF)
    blocks = []
    for t in range(13):
        u = dot_nn(low, w[:, t * 128 : (t + 1) * 128])
        if t < 10:
            u = u * cosine[...] + partner(u) * sine[...]
        blocks += heads_of_tile(u)
    for head in range(HEADS):
        at = head % GROUP * HALF
        q_ref[head // GROUP, at : at + HALF, :] = blocks[head].astype(BF16)
    for i in range(2 * KV_HEADS):
        own_ref[i * HALF : (i + 1) * HALF, :] = turn(blocks[HEADS + i]).astype(BF16)

    ctx = lax.axis_index("ctx")
    mine = jnp.minimum(table[2 * ctx], table[2 * ctx + 1])
    lane = lax.broadcasted_iota(jnp.int32, (1, 128), 1)
    first = lane < HALF
    offset = lax.rem(lane, HALF)

    def one(i, _):
        early = jnp.minimum(table[2 * i], table[2 * i + 1])
        turn_late = early >= mine
        m = jnp.where(turn_late, 1.0, 0.0)
        row = pl.ds(i, 1)
        flag[row, :] = jnp.where(first, 1.0, m)
        left[row, :] = jnp.where(first, m, 1.0 - m)
        right[row, :] = jnp.where(first, 1.0 - m, 0.0)
        gap = jnp.where(turn_late, mine - early, early - mine)
        blocks_back = jnp.where(first, early - (63 - mine), gap)
        limit[row, :] = (blocks_back * HALF + offset).astype(F32)
        return 0

    lax.fori_loop(0, CTX, one, 0)
    zero = jnp.zeros((1, 128), F32)
    for ref in (flag, left, right):
        ref[CTX:TILES, :] = zero
    limit[CTX:TILES, :] = jnp.where(first, offset, 10**6).astype(F32)


def project(table, tok, gain, w, cosine, sine):
    return pl.pallas_call(
        project_kernel,
        out_shape=[
            jax.ShapeDtypeStruct((KV_HEADS, ROWS, 128), BF16),
            jax.ShapeDtypeStruct((640, 128), BF16),
            jax.ShapeDtypeStruct((D, 128), BF16),
        ]
        + [jax.ShapeDtypeStruct((TILES, 128), F32)] * 4,
        in_specs=[pl.BlockSpec(memory_space=pltpu.SMEM)] + [VM] * 5,
        out_specs=[VM] * 7,
        compiler_params=pltpu.CompilerParams(vmem_limit_bytes=BIG),
        name="project",
    )(table, tok, gain, w, cosine, sine)


def middle_kernel(
    o, tok, cot, gain, out_hbm, gate_hbm, up_hbm, down_hbm,
    layer_out, grad_mid, do_rows, gain_grad, nt, dgu, gt, hid, at_t, gb,
    out_w, gate_w, up_w, down_w, sem,
):
    loads = []
    pairs = ((out_hbm, out_w), (gate_hbm, gate_w), (up_hbm, up_w), (down_hbm, down_w))
    for i, (src, dst) in enumerate(pairs):
        copy = pltpu.make_async_copy(src, dst, sem.at[i])
        copy.start()
        loads.append(copy)
    attended = jnp.concatenate(get_heads(o), axis=1)
    at_t[...] = attended.T[:D].astype(BF16)
    cot_low = cot[...]
    gt[0] = cot_low.astype(F32).T.astype(BF16)
    loads[0].wait()
    middle = tok[...].astype(F32) + dot_nn(attended.astype(BF16)[:, :D], out_w[...])
    inv = inverse_rms(middle)
    normed = middle * inv * gain[...]
    low = normed.astype(BF16)
    nt[...] = normed.T.astype(BF16)
    loads[1].wait()
    gate = dot_nn(low, gate_w[...])
    sigmoid = jax.nn.sigmoid(gate)
    silu = gate * sigmoid
    loads[2].wait()
    up = dot_nn(low, up_w[...])
    hidden = (silu * up).astype(BF16)
    for f in range(4):
        hid[f] = hidden[:, f * 640 : (f + 1) * 640]
    loads[3].wait()
    total = middle
    for f in range(4):
        total = total + dot_nt(hidden[:, f * 640 : (f + 1) * 640], down_w[f * D : (f + 1) * D, :])
    layer_out[...] = total.astype(BF16)
    grad_hidden = jnp.concatenate(
        [dot_nn(cot_low, down_w[f * D : (f + 1) * D, :]) for f in range(4)], axis=1
    )
    grad_gate = (grad_hidden * up * sigmoid * (1.0 + gate * (1.0 - sigmoid))).astype(BF16)
    grad_up = (grad_hidden * silu).astype(BF16)
    dgu[0, :, 0:FF] = grad_gate
    dgu[0, :, FF : 2 * FF] = grad_up
    grad_norm = dot_nt(grad_gate, gate_w[...]) + dot_nt(grad_up, up_w[...])
    grad_values, gain_grad[...] = norm_back(middle, inv, gain[...], grad_norm)
    grad_middle = cot_low.astype(F32) + grad_values
    grad_mid[...] = grad_middle
    branch = grad_middle.astype(BF16)
    gb[0] = jnp.concatenate([branch, jnp.zeros((TOK, 64), BF16)], axis=1)
    put_heads(do_rows, dot_nt(branch, out_w[...]))


def middle(o, tok, cot, gain, out_w, gate_w, up_w, down_w):
    weights = (out_w, gate_w, up_w, down_w)
    return pl.pallas_call(
        middle_kernel,
        out_shape=[
            jax.ShapeDtypeStruct((TOK, D), BF16),
            jax.ShapeDtypeStruct((TOK, D), F32),
            jax.ShapeDtypeStruct((KV_HEADS, ROWS, 128), BF16),
            jax.ShapeDtypeStruct((1, D), F32),
            jax.ShapeDtypeStruct((D, 128), BF16),
            jax.ShapeDtypeStruct((1, TOK, 2 * FF), BF16),
            jax.ShapeDtypeStruct((1, D, 128), BF16),
            jax.ShapeDtypeStruct((4, TOK, 640), BF16),
            jax.ShapeDtypeStruct((D, 128), BF16),
            jax.ShapeDtypeStruct((1, TOK, 1024), BF16),
        ],
        in_specs=[VM] * 4 + [ANY] * 4,
        out_specs=[VM] * 10,
        scratch_shapes=[pltpu.VMEM(w.shape, BF16) for w in weights]
        + [pltpu.SemaphoreType.DMA((4,))],
        compiler_params=pltpu.CompilerParams(vmem_limit_bytes=BIG),
        name="middle",
    )(o, tok, cot, gain, *weights)


def unproject_kernel(dq, dkv, cosine, sine, w, tok, gain, grad_mid, grad_tok, dqkv, gain_grad):
    tiles = get_heads(dq)
    low = low_lanes(TOK)
    turned = [turn(dkv[i * 128 : (i + 1) * 128, :].T) for i in range(5)]
    tiles[7] = jnp.where(low, tiles[7], turned[0])
    for i in range(4):
        tiles.append(jnp.where(low, turned[i], turned[i + 1]))
    tiles.append(jnp.where(low, turned[4], 0.0))
    for t in range(13):
        u = tiles[t]
        if t < 10:
            u = u * cosine[...] - partner(u) * sine[...]
        dqkv[0, :, t * 128 : (t + 1) * 128] = u.astype(BF16)
    grad_norm = dot_nt(dqkv[0], w[...])
    values = tok[...].astype(F32)
    grad_values, gain_grad[...] = norm_back(values, inverse_rms(values), gain[...], grad_norm)
    grad_tok[...] = grad_mid[...] + grad_values


def unproject(dq, dkv, cosine, sine, w, tok, gain, grad_mid):
    return pl.pallas_call(
        unproject_kernel,
        out_shape=[
            jax.ShapeDtypeStruct((TOK, D), F32),
            jax.ShapeDtypeStruct((1, TOK, 1664), BF16),
            jax.ShapeDtypeStruct((1, D), F32),
        ],
        in_specs=[VM] * 8,
        out_specs=[VM] * 3,
        compiler_params=pltpu.CompilerParams(vmem_limit_bytes=BIG),
        name="unproject",
    )(dq, dkv, cosine, sine, w, tok, gain, grad_mid)


def unpack_kernel(g_in, u_in, d_in, o_in, qkv, g, u, d, o, q, k, v):
    for t in range(4):
        rows, lanes = slice(t * 240, (t + 1) * 240), slice(t * 128, (t + 1) * 128)
        g[:, lanes] = g_in[rows, :].astype(F32)
        u[:, lanes] = u_in[rows, :].astype(F32)
    d[...] = d_in[...].astype(F32)
    step = pl.program_id(0)

    @pl.when(step < 4)
    def _():
        o[:, 0:128] = o_in[0:240, :].astype(F32)
        o[:, 128:256] = o_in[240:480, :].astype(F32)

    @pl.when(step == 0)
    def _():
        tiles = [qkv[t * 240 : (t + 1) * 240, :].astype(F32) for t in range(13)]
        low = low_lanes(240)
        for t in range(7):
            q[:, t * 128 : (t + 1) * 128] = tiles[t]
        q[:, 896:960] = tiles[7][:, :64]
        turned = [turn(t) for t in tiles[7:10]]
        k[:, 0:128] = jnp.where(low, turned[0], turned[1])
        k[:, 128:256] = jnp.where(low, turned[1], turned[2])
        k[:, 256:320] = turned[2][:, :64]
        v[:, 0:128] = tiles[10]
        v[:, 128:256] = tiles[11]
        v[:, 256:320] = tiles[12][:, :64]


def unpack(done, qkv):
    def whole(*shape):
        return pl.BlockSpec(shape, lambda i: (0, 0))

    return pl.pallas_call(
        unpack_kernel,
        grid=(5,),
        out_shape=[
            jax.ShapeDtypeStruct(shape, F32)
            for shape in (
                (240, FF), (240, FF), (D, 640), (240, D), (240, D), (240, 320), (240, 320),
            )
        ],
        in_specs=[
            pl.BlockSpec((960, 128), lambda i: (i, 0)),
            pl.BlockSpec((960, 128), lambda i: (5 + i, 0)),
            pl.BlockSpec((960, 128), lambda i: (12 + i, 0)),
            pl.BlockSpec((480, 128), lambda i: (20 + jnp.minimum(i, 3), 0)),
            whole(*qkv.shape),
        ],
        out_specs=[
            pl.BlockSpec((240, 512), lambda i: (0, i)),
            pl.BlockSpec((240, 512), lambda i: (0, i)),
            pl.BlockSpec((D, 128), lambda i: (0, i)),
            pl.BlockSpec((240, 256), lambda i: (0, jnp.minimum(i, 3))),
            whole(240, D),
            whole(240, 320),
            whole(240, 320),
        ],
        compiler_params=pltpu.CompilerParams(vmem_limit_bytes=BIG),
        name="unpack",
    )(done, done, done, done, qkv)


def rope_tables(early):
    row = lax.broadcasted_iota(jnp.int32, (TOK, 128), 0)
    lane = lax.broadcasted_iota(jnp.int32, (TOK, 128), 1)
    block = jnp.where(row < HALF, early, 63 - early)
    position = (block * HALF + row % HALF).astype(F32)
    frequency = BASE ** (-(lane % 32).astype(F32) / 32)
    angles = position * frequency
    return jnp.cos(angles), jnp.where(lane % HEAD < 32, -1.0, 1.0) * jnp.sin(angles)


def swap_rows(a, swap):
    return jnp.where(swap, jnp.concatenate([a[HALF:], a[:HALF]], axis=0), a)


def on_device(
    tokens, cotangent, block_table, attn_gain, w_query, w_key, w_value, w_out, mlp_gain,
    w_gate, w_up, w_down,
):
    ctx = lax.axis_index("ctx")
    gains = jnp.pad(jnp.stack([attn_gain, mlp_gain]), ((0, 14), (0, 16)))
    blank = jnp.zeros((240, 64), BF16)
    qkv_shard = jnp.concatenate([w_query, w_key, w_value, blank], axis=1)
    gains_all, qkv_w = gather_weights((gains, qkv_shard), 0)
    gains_all = gains_all.reshape(4, 16, 256)[:, :2, :240].astype(F32)
    gain_a = gains_all[:, 0].reshape(1, D)
    gain_b = gains_all[:, 1].reshape(1, D)

    own_blocks = lax.dynamic_slice_in_dim(block_table, 2 * ctx, 2)
    swap = own_blocks[0] > own_blocks[1]
    cosine, sine = rope_tables(jnp.min(own_blocks))
    tok = swap_rows(tokens[0], swap)
    cot = swap_rows(cotangent[0], swap)

    q_rows, own_kv, na_t, *plan = project(block_table, tok, gain_a, qkv_w, cosine, sine)
    o_rows, logs, kv, out_w, gate_w, up_w, down_w = forward(
        q_rows, own_kv, plan, (w_out, w_gate, w_up, w_down.T), 1
    )
    kv = kv.reshape(CTX, 640, 128)
    layer_out, grad_mid, do_rows, grad_gain_b, nb_t, dgu, cot_t, hidden, at_t, branch = middle(
        o_rows, tok, cot, gain_b, out_w, gate_w, up_w, down_w
    )
    ready = Reduction(
        (
            (nb_t.reshape(2, 2, 240, 128), dgu),
            (at_t.reshape(2, 2, 240, 128), branch),
            (cot_t, hidden.reshape(2, 2, TOK, 640)),
        ),
        None,
        False,
        192,
    )
    dq_rows, dkv, done = backward(q_rows, do_rows, o_rows, logs, kv, own_kv, plan, ready, 2)
    grad_tokens, grad_qkv, grad_gain_a = unproject(
        dq_rows, dkv, cosine, sine, qkv_w, tok, gain_a, grad_mid
    )
    gain_rows = jnp.stack([grad_gain_a, grad_gain_b]).reshape(2, 4, 240).transpose(1, 0, 2)
    gain_rows = jnp.pad(gain_rows, ((0, 0), (0, 0), (0, 16))).reshape(2, 2, 4, 128).astype(BF16)
    gain_rows = jnp.pad(gain_rows, ((0, 0), (0, 0), (0, 12), (0, 0)))
    late = Reduction(((na_t.reshape(2, 2, 240, 128), grad_qkv),), gain_rows, True)
    flat_done, flat = finish(done, ready, late, 3)
    shard_g, shard_u, shard_d, shard_o, shard_q, shard_k, shard_v = unpack(flat_done, flat)
    shard_gains = flat[3120:3124].reshape(2, 256)[:, :240].astype(F32)
    return (
        swap_rows(layer_out, swap)[None],
        swap_rows(grad_tokens, swap)[None],
        shard_gains[0],
        shard_q,
        shard_k,
        shard_v,
        shard_o,
        shard_gains[1],
        shard_g,
        shard_u,
        shard_d.T,
    )


def solution(mesh):
    rows, cut = P("fsdp", "ctx", None), P("fsdp", None)
    return jax.shard_map(
        on_device,
        mesh=mesh,
        in_specs=(rows, rows, P(), P("fsdp"), cut, cut, cut, cut, P("fsdp"), cut, cut, cut),
        out_specs=(rows, rows, P("fsdp"), cut, cut, cut, cut, P("fsdp"), cut, cut, cut),
        check_vma=False,
    )
```

```python
import functools
import math

import jax
import jax.numpy as jnp
import numpy as np
from jax import lax
from jax.experimental import pallas as pl
from jax.experimental.pallas import tpu as pltpu
from jax.sharding import PartitionSpec as P

D = 960
HEADS = 15
KV_HEADS = 5
GROUP = 3
HEAD = 64
FF = 2560
TOK = 128
HALF = 64
CTX = 32
TILES = 33
KEYS = TILES * 128
SCALE = HEAD ** (-0.5)
EPSILON = 1e-05
BASE = 10000.0
LOG2E = math.log2(math.e)
NEG = -1e30
MESH = pl.DeviceIdType.MESH
ANY = pl.BlockSpec(memory_space=pl.ANY)
VM = pl.BlockSpec(memory_space=pltpu.VMEM)
BIG = 56 * 2**20
F32 = jnp.float32
BF16 = jnp.bfloat16


def here():
    ctx = lax.axis_index("ctx")
    shard = lax.axis_index("fsdp")
    return {
        "z": ctx // 8,
        "yh": (ctx // 4) % 2,
        "x": ctx % 4,
        "yl": shard // 2,
        "c": shard % 2,
    }


def device(place, **moved):
    p = {**place, **moved}
    return (p["z"] * 8 + p["yh"] * 4 + p["x"], p["yl"] * 2 + p["c"])


def greet(devices):
    sem = pltpu.get_barrier_semaphore()
    for d in devices:
        pl.semaphore_signal(sem, inc=1, device_id=d, device_id_type=MESH)
    pl.semaphore_wait(sem, len(devices))


class Sems:
    def __init__(self, send, recv):
        self.send, self.recv, self.at = send, recv, 0

    def push(self, src, dst, dev):
        copy = pltpu.make_async_remote_copy(
            src_ref=src,
            dst_ref=dst,
            send_sem=self.send.at[self.at],
            recv_sem=self.recv.at[self.at],
            device_id=dev,
            device_id_type=MESH,
        )
        self.at += 1
        copy.start()
        return copy


def start_gather(me, sems, local, arrays, stages=None):
    f = me["yl"] * 2 + me["c"]
    near = device(me, yl=1 - me["yl"])
    far = device(me, yl=1 - me["yl"], yh=1 - me["yh"])
    mate = device(me, c=1 - me["c"])
    parts, kept, own = [], [], []
    for i, (a, b) in enumerate(arrays):
        rows = a.shape[0]
        first = rows // 32 * 16 if i % 2 else (rows + 31) // 32 * 16
        for lo, size, dev in ((0, first, near), (first, rows - first, far)):
            if size:
                src = a.at[pl.ds(lo, size)]
                dst = b.at[pl.ds(pl.multiple_of(f * rows + lo, 16), size)]
                parts.append((sems.push(src, dst, dev), b, rows, lo, size))
    for i, (a, b) in enumerate(arrays):
        rows = a.shape[0]
        dst = b.at[pl.ds(pl.multiple_of(f * rows, 16), rows)]
        kept.append(sems.push(a, dst, mate))
        stage = a if stages is None else stages[i]
        if stages is not None:
            load = pltpu.make_async_copy(a, stage, local.at[i])
            load.start()
        own.append((stage, dst, local.at[i]))
    if stages is not None:
        for (a, _), (stage, _, sem) in zip(arrays, own):
            pltpu.make_async_copy(a, stage, sem).wait()
    own = [pltpu.make_async_copy(*copy) for copy in own]
    for copy in own:
        copy.start()
    return parts, kept, own


def relay_gather(me, sems, started):
    parts, kept, _ = started
    across = (1 - me["yl"]) * 2 + me["c"]
    mate = device(me, c=1 - me["c"])
    for copy, b, rows, lo, size in parts:
        copy.wait_recv()
        span = b.at[pl.ds(pl.multiple_of(across * rows + lo, 16), size)]
        kept.append(sems.push(span, span, mate))


def end_gather(started):
    parts, kept, own = started
    for copy in own:
        copy.wait()
    for copy in kept:
        copy.wait()
    for copy, *_ in parts:
        copy.wait_send()


def gathered(arrays):
    return [jax.ShapeDtypeStruct((4 * a.shape[0], *a.shape[1:]), a.dtype) for a in arrays]


def gather_qkv_kernel(
    gain_a, gain_b, wq, wk_t, wv_t, gains, qkv, gains_own, qkv_own, send, recv, local
):
    blank = jnp.zeros((1, 16), F32)
    lines = [jnp.concatenate([g[...].astype(F32), blank], axis=1) for g in (gain_a, gain_b)]
    gains_own[...] = jnp.concatenate([*lines, jnp.zeros((14, 256), F32)], axis=0).astype(BF16)
    qkv_own[:, 0:896] = wq[:, 0:896]
    rest = [wq[:, 896:960].astype(F32), wk_t[...].astype(F32).T, wv_t[...].astype(F32).T]
    qkv_own[:, 896:1664] = jnp.concatenate([*rest, jnp.zeros((240, 64), F32)], axis=1).astype(BF16)
    me = here()
    flip = 1 - me["yl"]
    greet((device(me, yl=flip), device(me, yl=flip, yh=1 - me["yh"]), device(me, c=1 - me["c"])))
    sems = Sems(send, recv)
    started = start_gather(me, sems, local, [(gains_own, gains), (qkv_own, qkv)])
    relay_gather(me, sems, started)
    end_gather(started)


def gather_qkv(gain_a, gain_b, wq, wk_t, wv_t, collective_id):
    own = [jax.ShapeDtypeStruct((16, 256), BF16), jax.ShapeDtypeStruct((240, 1664), BF16)]
    return pl.pallas_call(
        gather_qkv_kernel,
        out_shape=gathered(own),
        in_specs=[VM] * 5,
        out_specs=[ANY] * 2,
        scratch_shapes=[pltpu.VMEM(a.shape, BF16) for a in own]
        + [
            pltpu.SemaphoreType.DMA((10,)),
            pltpu.SemaphoreType.DMA((10,)),
            pltpu.SemaphoreType.DMA((2,)),
        ],
        compiler_params=pltpu.CompilerParams(
            collective_id=collective_id, has_side_effects=True, vmem_limit_bytes=BIG
        ),
        name="gather_qkv",
    )(gain_a, gain_b, wq, wk_t, wv_t)


class Ring:
    def __init__(self, me, axis):
        at = me[axis]
        self.me = at
        self.right_at, self.opposite_at, self.left_at = (lax.rem(at + d, 4) for d in (1, 2, 3))
        self.right = device(me, **{axis: self.right_at})
        self.left = device(me, **{axis: self.left_at})
        self.opposite = device(me, **{axis: self.opposite_at})


class Share:
    def __init__(self, sems, ring, src, place, halves):
        self.sems, self.ring, self.place, self.halves = sems, ring, place, halves
        dst = place(ring.me)
        self.copies = [sems.push(src, dst, ring.right), sems.push(src, dst, ring.left)]
        self.passed, self.here = [], False
        if halves is None:
            self.passed.append(sems.push(src, dst, ring.opposite))

    def near(self):
        if not self.here:
            for copy in self.copies:
                copy.wait_recv()
            self.here = True

    def relay(self):
        self.near()
        if self.halves is not None:
            ring, push = self.ring, self.sems.push
            half = self.halves(self.place(ring.left_at))[0]
            self.passed.append(push(half, half, ring.right))
            half = self.halves(self.place(ring.right_at))[1]
            self.passed.append(push(half, half, ring.left))

    def arrive(self):
        for copy in self.passed:
            copy.wait_recv()

    def end(self):
        for copy in self.copies + self.passed:
            copy.wait_send()


def gather_kv(me, sems, kv, out, once_across):
    x, yh, z = me["x"], me["yh"], me["z"]
    other = device(me, yh=1 - yh)
    rings = Ring(me, "x"), Ring(me, "z")
    spans = pl.ds(0, 320), pl.ds(320, 320)
    across = [sems.push(kv.at[p], out.at[z, yh, x, p], other) for p in spans]

    def near(axis, row, src):
        lo = 320 * axis

        def place(at):
            ref = out.at[z, row, at] if axis == 0 else out.at[at, row, x]
            return ref.at[spans[axis]]

        def halves(ref):
            return ref.at[pl.ds(0, 160)], ref.at[pl.ds(160, 160)]

        return Share(sems, rings[axis], src, place, halves)

    def far(axis, row):
        def place(at):
            return out.at[at, row, :, spans[0]] if axis == 0 else out.at[:, row, at, spans[1]]

        def halves(ref):
            return ref.at[pl.ds(0, 2)], ref.at[pl.ds(2, 2)]

        src = place(rings[1 - axis].me)
        return Share(sems, rings[1 - axis], src, place, halves)

    first = [near(axis, yh, kv.at[spans[axis]]) for axis in (0, 1)]
    once_across()
    out[z, yh, x] = kv[...]
    for share in first:
        share.relay()
    second = []
    for axis in (0, 1):
        across[axis].wait_recv()
        row = 1 - yh
        src = out.at[z, row, x, spans[axis]]
        second.append(near(axis, row, src))
    last = []
    for axis in (0, 1):
        first[axis].arrive()
        last.append(far(axis, yh))
    for share in second:
        share.relay()
    for axis in (0, 1):
        second[axis].arrive()
        last.append(far(axis, 1 - yh))
    for share in last:
        share.relay()
    for share in last:
        share.arrive()
    return across, first + second + last


def add_low(a, b):
    return (a.astype(F32) + b.astype(F32)).astype(BF16)


class Fold:
    def __init__(self, sems, ring, block, landing, passing, direct=False):
        self.sems, self.ring, self.block, self.direct = sems, ring, block, direct
        self.landing, self.passing = landing, passing
        self.copies, self.passed, self.sent = {}, {}, []

    def start_opposite(self, half):
        ring = self.ring
        src = self.block(ring.opposite_at, half)
        dev = ring.opposite if self.direct else (ring.right, ring.left)[half]
        self.passed[half] = self.sems.push(src, self.passing(half), dev)

    def start_direct(self, half):
        ring = self.ring
        at, dev = ((ring.left_at, ring.left), (ring.right_at, ring.right))[half]
        side = 1 - half
        self.copies[side, half] = self.sems.push(
            self.block(at, half), self.landing(side, half), dev
        )

    def relay(self, half):
        ring = self.ring
        at, dev = ((ring.right_at, ring.right), (ring.left_at, ring.left))[half]
        src = self.block(at, half)
        if not self.direct:
            self.passed[half].wait_recv()
            src[...] = add_low(src[...], self.passing(half)[...])
        self.copies[half, half] = self.sems.push(src, self.landing(half, half), dev)

    def total(self, half):
        for side in (0, 1):
            self.copies[side, half].wait_recv()
        total = self.block(self.ring.me, half)[...].astype(F32)
        for side in (0, 1):
            total = total + self.landing(side, half)[...].astype(F32)
        if self.direct:
            self.passed[half].wait_recv()
            total = total + self.passing(half)[...].astype(F32)
        return total

    def end(self):
        for copy in list(self.copies.values()) + list(self.passed.values()):
            copy.wait_send()


class Scatter:
    COPIES = 26
    SCRATCH = [
        pltpu.VMEM((2, 3, 2, 4, 320, 128), BF16),
        pltpu.VMEM((2, 2, 4, 320, 128), BF16),
        pltpu.VMEM((2, 3, 2, 320, 128), BF16),
        pltpu.VMEM((2, 320, 128), BF16),
        pltpu.VMEM((2, 320, 128), BF16),
    ]

    def __init__(self, me, sems, part, out, scratch):
        self.me, self.sems, self.part, self.out = me, sems, part, out
        self.r1, self.s1, self.r2, self.s2, self.r3 = scratch
        self.rings = Ring(me, "x"), Ring(me, "z")
        self.first, self.second, self.third = [], [], []
        rows = (1 - me["yh"], me["yh"])
        key, value = pl.ds(0, 320), pl.ds(320, 320)

        def block0(at, half):
            return part.at[at, rows[half], :, key]

        def block1(at, half):
            return part.at[:, rows[half], at, value]

        for axis, block in enumerate((block0, block1)):
            r1, s1, r2 = self.r1, self.s1, self.r2
            self.first.append(
                Fold(
                    sems,
                    self.rings[1 - axis],
                    block,
                    lambda side, half, axis=axis: r1.at[axis, side, half],
                    lambda half, axis=axis: r1.at[axis, 2, half],
                )
            )
            self.second.append(
                Fold(
                    sems,
                    self.rings[axis],
                    lambda at, half, axis=axis: s1.at[axis, half, at],
                    lambda side, half, axis=axis: r2.at[axis, side, half],
                    lambda half, axis=axis: r2.at[axis, 2, half],
                )
            )

    def start(self):
        for half in (0, 1):
            for fold in self.first:
                fold.start_opposite(half)
        for half in (0, 1):
            for fold in self.first:
                fold.start_direct(half)

    def relay(self):
        for half in (0, 1):
            for fold in self.first:
                fold.relay(half)

    def middle(self):
        for half in (0, 1):
            for axis in (0, 1):
                self.s1[axis, half] = self.first[axis].total(half).astype(BF16)
                self.second[axis].start_opposite(half)
                self.second[axis].start_direct(half)
        for half in (0, 1):
            for fold in self.second:
                fold.relay(half)

    def last(self):
        other = device(self.me, yh=1 - self.me["yh"])
        for axis in (0, 1):
            self.s2[axis] = self.second[axis].total(0).astype(BF16)
            self.third.append(self.sems.push(self.s2.at[axis], self.r3.at[axis], other))
        for axis in (0, 1):
            self.out[pl.ds(axis * 320, 320), :] = self.second[axis].total(1)

    def end(self):
        for axis in (0, 1):
            self.third[axis].wait_recv()
            span = pl.ds(axis * 320, 320)
            self.out[span, :] = self.out[span, :] + self.r3[axis].astype(F32)
        for fold in self.first + self.second:
            fold.end()
        for c in self.third:
            c.wait_send()


def build_tiles(head, kv_ref, own_ref, left_ref, tiles_ref, base):
    lane = lax.broadcasted_iota(jnp.int32, (HALF, 128), 1)
    start = pl.multiple_of(base + head * HALF, HALF)

    def one(i, _):
        block = kv_ref[i, pl.ds(start, HALF), :].astype(F32)
        top = jnp.where(lane < HALF, block, 0.0)
        low = pltpu.roll(block, HALF, 1) * left_ref[pl.ds(i, 1), :]
        at = pl.multiple_of(i * 128, 128)
        tiles_ref[pl.ds(at, 128), :] = jnp.concatenate([top, low], axis=0).astype(BF16)
        return 0

    lax.fori_loop(0, CTX, one, 0, unroll=32)
    block = own_ref[pl.ds(start, HALF), :].astype(F32)
    top = jnp.where(lane < HALF, 0.0, pltpu.roll(block, HALF, 1))
    tiles_ref[pl.ds(CTX * 128, 128), :] = jnp.concatenate(
        [top, jnp.zeros_like(top)], axis=0
    ).astype(BF16)


def dot_nt(a, b):
    return lax.dot_general(a, b, (((1,), (1,)), ((), ())), preferred_element_type=F32)


def dot_nn(a, b):
    return lax.dot_general(a, b, (((1,), (0,)), ((), ())), preferred_element_type=F32)


ROWS = GROUP * HALF


def row_offset():
    return lax.rem(lax.broadcasted_iota(jnp.int32, (ROWS, 128), 0), HALF).astype(F32)


def attend_head(head, q, kv_ref, own_ref, flag_ref, left_ref, limit_ref, kk, vv):
    build_tiles(head, kv_ref, own_ref, left_ref, kk, 0)
    build_tiles(head, kv_ref, own_ref, left_ref, vv, 320)
    offset = row_offset()
    low = jnp.full((ROWS, 128), NEG, F32)
    s = dot_nt(q, kk[...]) * (SCALE * LOG2E)
    tiles = []
    top_l, top_e = low, low
    for i in range(TILES):
        tile = s[:, i * 128 : (i + 1) * 128]
        tile = jnp.where(limit_ref[i : i + 1, :] <= offset, tile, NEG)
        tiles.append(tile)
        late = flag_ref[i : i + 1, :] > 0.5
        top_l = jnp.maximum(top_l, jnp.where(late, tile, NEG))
        top_e = jnp.maximum(top_e, jnp.where(late, NEG, tile))
    max_l = jnp.broadcast_to(jnp.max(top_l, axis=1, keepdims=True), (ROWS, 128))
    max_e = jnp.broadcast_to(jnp.max(top_e, axis=1, keepdims=True), (ROWS, 128))
    sum_l = jnp.zeros((ROWS, 128), F32)
    sum_e = jnp.zeros((ROWS, 128), F32)
    probs = []
    for i in range(TILES):
        late = flag_ref[i : i + 1, :] > 0.5
        p = jnp.exp2(tiles[i] - jnp.where(late, max_l, max_e))
        p_l = jnp.where(late, p, 0.0)
        sum_l = sum_l + p_l
        sum_e = sum_e + (p - p_l)
        probs.append(p.astype(BF16))
    total = dot_nn(jnp.concatenate(probs, axis=1), vv[...])
    late = lax.broadcasted_iota(jnp.int32, (ROWS, 128), 1) < HALF
    row_sum = jnp.where(
        late, jnp.sum(sum_l, axis=1, keepdims=True), jnp.sum(sum_e, axis=1, keepdims=True)
    )
    return total / row_sum, jnp.where(late, max_l, max_e) + jnp.log2(row_sum)


def forward_kernel(count, q_ref, own_ref, flag_ref, left_ref, limit_ref, *refs):
    shards, refs = refs[:count], refs[count:]
    o_ref, l_ref, kv_out, *full = refs[: 3 + count]
    kv, kk, vv, *stages, send, recv, local = refs[3 + count :]
    me = here()
    greet_axes(me)
    sems = Sems(send, recv)
    started = []

    def start_weights():
        started.extend(start_gather(me, sems, local, list(zip(shards, full)), stages))

    across, shares = gather_kv(me, sems, own_ref, kv, start_weights)
    keep = pltpu.make_async_copy(kv, kv_out, local.at[count])
    keep.start()
    flat = kv.reshape(CTX, 640, 128)

    def one(head, _):
        o, logs = attend_head(
            head, q_ref[head], flat, own_ref, flag_ref, left_ref, limit_ref, kk, vv
        )
        o_ref[head] = o
        l_ref[head] = logs
        return 0

    lax.fori_loop(0, 3, one, 0)
    relay_gather(me, sems, started)
    lax.fori_loop(3, KV_HEADS, one, 0)
    end_gather(started)
    for copy in across:
        copy.wait_send()
    for share in shares:
        share.end()
    keep.wait()


def forward(q, own, plan, shards, collective_id):
    flags, left, _, limits = plan
    n = len(shards)
    copies = 5 * n + 2 + 8 * 4
    return pl.pallas_call(
        functools.partial(forward_kernel, n),
        out_shape=[jax.ShapeDtypeStruct((KV_HEADS, ROWS, 128), F32)] * 2
        + [jax.ShapeDtypeStruct((4, 2, 4, 640, 128), BF16)]
        + gathered(shards),
        in_specs=[VM] * 5 + [ANY] * n,
        out_specs=[VM, VM, ANY] + [ANY] * n,
        scratch_shapes=[
            pltpu.VMEM((4, 2, 4, 640, 128), BF16),
            pltpu.VMEM((KEYS, 128), BF16),
            pltpu.VMEM((KEYS, 128), BF16),
            *[pltpu.VMEM(a.shape, BF16) for a in shards],
            pltpu.SemaphoreType.DMA((copies,)),
            pltpu.SemaphoreType.DMA((copies,)),
            pltpu.SemaphoreType.DMA((n + 1,)),
        ],
        compiler_params=pltpu.CompilerParams(
            collective_id=collective_id, has_side_effects=True, vmem_limit_bytes=BIG
        ),
        name="forward",
    )(q, own, flags, left, limits, *shards)


def attend_back_head(
    head, q, do, o, logs, kv_ref, own_ref, flag_ref, left_ref, right_ref, limit_ref,
    dkv_ref, kk, vv,
):
    build_tiles(head, kv_ref, own_ref, left_ref, kk, 0)
    build_tiles(head, kv_ref, own_ref, left_ref, vv, 320)
    offset = row_offset()
    lane = lax.broadcasted_iota(jnp.int32, (ROWS, 128), 1)
    product = do.astype(F32) * o
    shape = (ROWS, 128)
    delta_l = jnp.broadcast_to(
        jnp.sum(jnp.where(lane < HALF, product, 0.0), axis=1, keepdims=True), shape
    )
    delta_e = jnp.broadcast_to(
        jnp.sum(jnp.where(lane < HALF, 0.0, product), axis=1, keepdims=True), shape
    )
    log_l = jnp.broadcast_to(logs[:, 0:1], shape)
    log_e = jnp.broadcast_to(logs[:, HALF : HALF + 1], shape)
    k_rows = pl.ds(pl.multiple_of(head * HALF, HALF), HALF)
    v_rows = pl.ds(pl.multiple_of(320 + head * HALF, HALF), HALF)
    small = lax.broadcasted_iota(jnp.int32, (HALF, 128), 1)
    keys = kk[...]
    s = dot_nt(q, keys) * (SCALE * LOG2E)
    dp = dot_nt(do, vv[...])
    probs, scores = [], []
    for i in range(TILES):
        cut = slice(i * 128, (i + 1) * 128)
        late = flag_ref[i : i + 1, :] > 0.5
        tile = jnp.where(limit_ref[i : i + 1, :] <= offset, s[:, cut], NEG)
        p = jnp.exp2(tile - jnp.where(late, log_l, log_e))
        probs.append(p.astype(BF16))
        scores.append((p * (dp[:, cut] - jnp.where(late, delta_l, delta_e))).astype(BF16))
    ds = jnp.concatenate(scores, axis=1)
    dq = dot_nn(ds, keys) * SCALE
    dk = dot_nn(q.astype(F32).T.astype(BF16), ds) * SCALE
    dv = dot_nn(do.astype(F32).T.astype(BF16), jnp.concatenate(probs, axis=1))
    mine = lax.axis_index("ctx")
    for rows, both in ((k_rows, dk), (v_rows, dv)):
        for i in range(CTX):
            cut = slice(i * 128, (i + 1) * 128)
            top, bottom = both[0:HALF, cut], both[HALF:128, cut]
            total = (
                top * flag_ref[i : i + 1, :]
                + pltpu.roll(bottom, HALF, 1) * right_ref[i : i + 1, :]
            )
            dkv_ref[i, rows, :] = total.astype(BF16)
        bottom = both[HALF:128, CTX * 128 :]
        before = dkv_ref[mine, rows, :].astype(F32)
        dkv_ref[mine, rows, :] = (before + jnp.where(small < HALF, bottom, 0.0)).astype(BF16)
    return dq


def pop(refs, count):
    taken = refs[:count]
    del refs[:count]
    return taken


class Column:
    COPIES = 24

    @staticmethod
    def scratch(pc):
        return [
            pltpu.VMEM((3, 4, 4 * pc, 128), BF16),
            pltpu.VMEM((4, 4 * pc, 128), BF16),
            pltpu.VMEM((3, 2, 2 * pc, 128), BF16),
            pltpu.VMEM((4 * pc, 128), BF16),
            pltpu.VMEM((3, 2, pc // 2, 128), BF16),
        ]

    def __init__(self, me, sems, grads, lo, pc, scratch, fin):
        self.me, self.sems, self.grads, self.lo, self.pc, self.fin = me, sems, grads, lo, pc, fin
        self.ry, self.sy, rx, self.sx, rz = scratch
        self.first = {}
        sy, sx, x = self.sy, self.sx, me["x"]

        def strip(at, half):
            return sy.at[lax.rem(at + 4 - x, 4), pl.ds(half * 2 * pc, 2 * pc)]

        def piece(at, half):
            return sx.at[pl.ds(pl.multiple_of(at * pc + half * (pc // 2), 16), pc // 2)]

        self.over_x = Fold(
            sems,
            Ring(me, "x"),
            strip,
            lambda side, half: rx.at[side, half],
            lambda half: rx.at[2, half],
        )
        self.over_z = Fold(
            sems,
            Ring(me, "z"),
            piece,
            lambda side, half: rz.at[side, half],
            lambda half: rz.at[2, half],
        )

    def rows(self, half, k):
        i = lax.rem(self.me["x"] + k, 4)
        start = pl.multiple_of(self.lo + (half * 16 + i * 4) * self.pc, 16)
        return pl.ds(start, 4 * self.pc)

    def start(self):
        me = self.me
        yl, yh = me["yl"], me["yh"]
        ways = (
            (1 - yl, yh, device(me, yl=1 - yl)),
            (1 - yl, 1 - yh, device(me, yl=1 - yl, yh=1 - yh)),
            (yl, 1 - yh, device(me, yh=1 - yh)),
        )
        for k in (2, 1, 3, 0):
            for slot, (shard, half, dev) in enumerate(ways):
                src = self.grads.at[shard, self.rows(half, k)]
                self.first[k, slot] = self.sems.push(src, self.ry.at[slot, k], dev)

    def fold_first(self, k):
        for slot in (0, 1, 2):
            self.first[k, slot].wait_recv()
        total = self.grads[self.me["yl"], self.rows(self.me["yh"], k)].astype(F32)
        for slot in (0, 1, 2):
            total = total + self.ry[slot, k].astype(F32)
        self.sy[k] = total.astype(BF16)
        if k == 2:
            self.over_x.start_opposite(0)
            self.over_x.start_opposite(1)
        elif k == 1:
            self.over_x.start_direct(1)
        elif k == 3:
            self.over_x.start_direct(0)

    def relay(self):
        self.over_x.relay(0)
        self.over_x.relay(1)

    def fold_second(self):
        for half in (0, 1):
            span = pl.ds(half * 2 * self.pc, 2 * self.pc)
            self.sx[span] = self.over_x.total(half).astype(BF16)
        for half in (0, 1):
            self.over_z.start_opposite(half)
            self.over_z.start_direct(half)

    def fold_third(self):
        self.over_z.relay(0)
        self.over_z.relay(1)

    def end(self):
        base = self.fin.shape[0] - self.pc
        for half in (0, 1):
            span = pl.ds(base + half * (self.pc // 2), self.pc // 2)
            self.fin[span, :] = self.over_z.total(half).astype(BF16)
        self.over_x.end()
        self.over_z.end()
        for copy in self.first.values():
            copy.wait_send()


class Reduction:
    def __init__(self, jobs, extra, direct=False, pc=0):
        self.operands, self.jobs, self.scratch, rows = [], [], [], 0
        self.direct = direct
        for left, right in jobs:
            self.operands += [left, right]
            m, n = left.shape[-2], right.shape[-1]
            self.jobs.append((left.ndim == 4, m, right.ndim == 4, n))
            self.scratch.append(pltpu.VMEM((left.shape[0], m, 256), BF16))
            self.scratch.append(pltpu.VMEM((right.shape[0], 256, n), BF16))
            rows += m * (n // 128)
        self.extra = extra is not None
        if self.extra:
            self.operands.append(extra)
            self.scratch.append(pltpu.VMEM((2, 2, 16, 128), BF16))
            rows += 16
        pieces = -(-rows // 256) - pc // 8
        self.sizes = ((pieces + 1) // 2 * 16, pieces // 2 * 16)
        self.pc = pc
        self.used = 16 * (sum(self.sizes) + 2 * pc)
        self.scratch.append(pltpu.VMEM((2, self.used, 128), BF16))
        for size in self.sizes:
            self.scratch += [
                pltpu.VMEM((3, 4, 2, size, 128), BF16),
                pltpu.VMEM((4, 2, size, 128), BF16),
                pltpu.VMEM((3, 2, size, 128), BF16),
                pltpu.VMEM((2, size, 128), BF16),
                pltpu.VMEM((4, size, 128), BF16),
            ]
        self.locals = 2 * len(jobs) + 1
        self.copies = 2 * len(jobs) + 1 + 48 + 12 + 6
        self.fin_shape = (sum(self.sizes) + pc, 128)
        if pc:
            self.scratch += Column.scratch(pc)
            self.copies += Column.COPIES

    def bind(self, me, sems, local, operands, scratch, fin):
        operands, scratch = list(operands), list(scratch)
        self.me, self.sems, self.local, self.fin = me, sems, local, fin
        self.sources, self.buffers = [], []
        core = me["c"]
        for cut_left, _, cut_right, _ in self.jobs:
            left, right = pop(operands, 2)
            lefts = (left.at[:, core], left.at[:, 1 - core]) if cut_left else (left, left)
            rights = (right.at[:, core], right.at[:, 1 - core]) if cut_right else (right, right)
            self.sources.append((*lefts, *rights))
            self.buffers.append(pop(scratch, 2))
        if self.extra:
            self.extra_refs = (operands[0].at[:, core], operands[0].at[:, 1 - core])
            self.extra_buffer = scratch.pop(0)
        self.grads = scratch.pop(0)
        self.parts = [pop(scratch, 5) for _ in self.sizes]
        if self.pc:
            lo = 16 * sum(self.sizes)
            self.column = Column(me, sems, self.grads, lo, self.pc, scratch, fin)
        xs, zs = Ring(me, "x"), Ring(me, "z")
        self.plans = (
            (0, self.sizes[0], xs, zs),
            (16 * self.sizes[0], self.sizes[1], zs, xs),
        )
        self.first, self.second, self.third = {}, {}, {}
        for n, (lo, size, ring, cross) in enumerate(self.plans):
            r1, s1, r2, _, _ = self.parts[n]
            for k in range(4):
                j = lax.rem(cross.me + k, 4)

                def block(at, half, lo=lo, size=size, j=j):
                    start = pl.multiple_of(lo + (at * 4 + j) * size, 16)
                    return self.grads.at[half, pl.ds(start, size)]

                self.first[n, k] = Fold(
                    sems,
                    ring,
                    block,
                    lambda side, half, r1=r1, k=k: r1.at[side, k, half],
                    lambda half, r1=r1, k=k: r1.at[2, k, half],
                    self.direct,
                )

            def turned(at, half, s1=s1, cross=cross):
                return s1.at[lax.rem(at + 4 - cross.me, 4), half]

            self.second[n] = Fold(
                sems,
                cross,
                turned,
                lambda side, half, r2=r2: r2.at[side, half],
                lambda half, r2=r2: r2.at[2, half],
                self.direct,
            )

    def trade(self):
        mate = device(self.me, c=1 - self.me["c"])
        push = self.sems.push
        self.mine, self.traded = [], []

        def keep(src, dst):
            copy = pltpu.make_async_copy(src, dst, self.local.at[len(self.mine)])
            copy.start()
            self.mine.append(copy)

        here_, there = pl.ds(0, 128), pl.ds(128, 128)
        for (lm, lt, rm, rt), (lb, rb) in zip(self.sources, self.buffers):
            self.traded.append(push(lt, lb.at[:, :, there], mate))
            self.traded.append(push(rt, rb.at[:, there], mate))
            keep(lm, lb.at[:, :, here_])
            keep(rm, rb.at[:, here_])
        if self.extra:
            self.traded.append(push(self.extra_refs[1], self.extra_buffer.at[1], mate))
            keep(self.extra_refs[0], self.extra_buffer.at[0])

    def multiply(self, job):
        base = sum(m * (n // 128) for _, m, _, n in self.jobs[:job])
        for copy in self.mine[2 * job : 2 * job + 2]:
            copy.wait()
        for copy in self.traded[2 * job : 2 * job + 2]:
            copy.wait_recv()
        grads, (_, m, _, n), (lb, rb) = self.grads, self.jobs[job], self.buffers[job]
        strip = min(n, 1280) if n % 1280 == 0 else n
        for s in range(2):
            left = lb[min(s, lb.shape[0] - 1)]

            def block(i, _, left=left, s=s):
                at = pl.multiple_of(i * strip, 128)
                right = rb[min(s, rb.shape[0] - 1), :, pl.ds(at, strip)]
                result = dot_nn(left, right).astype(BF16)
                for w in range(strip // 128):
                    to = pl.multiple_of(base + (i * (strip // 128) + w) * m, 16)
                    grads[s, pl.ds(to, m), :] = result[:, w * 128 : (w + 1) * 128]
                return 0

            if n == strip:
                block(0, 0)
            else:
                lax.fori_loop(0, n // strip, block, 0)

    def pad(self):
        base, grads = sum(m * (n // 128) for _, m, _, n in self.jobs), self.grads
        if self.extra:
            self.mine[-1].wait()
            self.traded[-1].wait_recv()
            for s in range(2):
                both = self.extra_buffer[0, s].astype(F32) + self.extra_buffer[1, s].astype(F32)
                grads[s, pl.ds(base, 16), :] = both.astype(BF16)
            base += 16
        if base < self.used:
            for s in range(2):
                grads[s, pl.ds(base, self.used - base), :] = jnp.zeros(
                    (self.used - base, 128), BF16
                )

    def start(self, n):
        for k in (2, 1, 3, 0):
            for half in (0, 1):
                self.first[n, k].start_opposite(half)
        for k in (2, 1, 3, 0):
            for half in (0, 1):
                self.first[n, k].start_direct(half)

    def relay(self, k):
        for half in (0, 1):
            for n in (0, 1):
                self.first[n, k].relay(half)

    def fold_first(self, k):
        for n in (0, 1):
            s1, second = self.parts[n][1], self.second[n]
            for half in (0, 1):
                s1[k, half] = self.first[n, k].total(half).astype(BF16)
            if k == 2:
                second.start_opposite(0)
                second.start_opposite(1)
            elif k == 1:
                second.start_direct(1)
            elif k == 3:
                second.start_direct(0)

    def fold_second(self):
        me, push = self.me, self.sems.push
        yh, yl = me["yh"], me["yl"]
        for half in (0, 1):
            for n in (0, 1):
                self.second[n].relay(half)
        for n in (0, 1):
            s2, r3 = self.parts[n][3:]
            for half in (0, 1):
                s2[half] = self.second[n].total(half).astype(BF16)
            slot = r3.at[yl * 2 + yh]
            self.third[n, 0] = push(s2.at[1 - yl], slot, device(me, yl=1 - yl))
            self.third[n, 1] = push(s2.at[1 - yl], slot, device(me, yl=1 - yl, yh=1 - yh))
            self.third[n, 2] = push(s2.at[yl], slot, device(me, yh=1 - yh))

    def fold_third(self):
        yh, yl = self.me["yh"], self.me["yl"]
        at = 0
        for n, size in enumerate(self.sizes):
            _, _, _, s2, r3 = self.parts[n]
            r3[yl * 2 + yh] = s2[yl]
            for i in (0, 1, 2):
                self.third[n, i].wait_recv()
            total = r3[0].astype(F32)
            for i in (1, 2, 3):
                total = total + r3[i].astype(F32)
            self.fin[pl.ds(at, size), :] = total.astype(BF16)
            at += size

    def end(self):
        for fold in list(self.first.values()) + list(self.second.values()):
            fold.end()
        for copy in self.traded + list(self.third.values()):
            copy.wait_send()


class Spread:
    COPIES = 81

    def __init__(self, me, sems, local, fin, out, sizes, direct=False, pc=0, other=None):
        self.direct, self.fin, self.pc, self.other = direct, fin, pc, other
        self.sems, self.local, self.out = sems, local, out
        self.kept, self.cross, self.own, self.near, self.far = [], [], [], [], []
        xs, zs = Ring(me, "x"), Ring(me, "z")
        base, yh = 16 * sum(sizes), me["yh"]
        self.plans = [(0, sizes[0], xs, zs), (16 * sizes[0], sizes[1], zs, xs)]
        self.swap = None
        if pc:
            self.plans.append((base + yh * (16 * pc), pc, xs, zs))
            self.plans.append((base + (1 - yh) * (16 * pc), pc, zs, xs))
            src = fin.at[pl.ds(sum(sizes), pc)]
            self.swap = sems.push(src, other, device(me, yh=1 - yh))
        at = 0
        for n in range(3 if pc else 2):
            size = self.plans[n][1]
            self.begin(n, fin.at[pl.ds(at, size)])
            at += size

    def begin(self, n, src):
        _, _, ring, cross = self.plans[n]
        copy = pltpu.make_async_copy(src, self.span(n, ring.me, cross.me), self.local.at[n])
        copy.start()
        self.kept.append(copy)
        place = functools.partial(self.span, n, ring.me)
        self.cross.append(Share(self.sems, cross, src, place, self.halves(n)))
        self.own.append(self.share(n, cross.me, src))

    def across(self):
        if self.pc:
            self.swap.wait_recv()
            self.begin(3, self.other)

    def span(self, n, i, j):
        lo, size, _, _ = self.plans[n]
        at = j * 4 + i if n == 3 else i * 4 + j
        return self.out.at[pl.ds(pl.multiple_of(lo + at * size, 16), size)]

    def halves(self, n):
        if self.direct:
            return None
        size = self.plans[n][1]
        first = size // 32 * 16
        return lambda ref: (ref.at[pl.ds(0, first)], ref.at[pl.ds(first, size - first)])

    def share(self, n, j, src=None):
        ring = self.plans[n][2]

        def place(i):
            return self.span(n, i, j)

        src = place(ring.me) if src is None else src
        return Share(self.sems, ring, src, place, self.halves(n))

    def relay(self):
        for share in self.cross:
            share.relay()
        for n, plan in enumerate(self.plans):
            self.near.append(self.share(n, plan[3].left_at))
            self.near.append(self.share(n, plan[3].right_at))

    def pass_on(self):
        for share in self.own:
            share.relay()
        for n, plan in enumerate(self.plans):
            self.cross[n].arrive()
            self.far.append(self.share(n, plan[3].opposite_at))

    def end(self):
        for share in self.near + self.far:
            share.relay()
        for share in self.own + self.near + self.far:
            share.arrive()
        for copy in self.kept:
            copy.wait()
        for share in self.cross + self.own + self.near + self.far:
            share.end()
        if self.pc:
            self.swap.wait_send()


def greet_axes(me, reach=2):
    flip = 1 - me["yl"]
    rings = Ring(me, "x"), Ring(me, "z")
    greet(
        [device(me, yl=flip), device(me, yl=flip, yh=1 - me["yh"]), device(me, c=1 - me["c"])]
        + [device(me, yh=1 - me["yh"])]
        + [dev for ring in rings for dev in (ring.left, ring.right, ring.opposite)[:reach]]
    )


def backward_kernel(reduction, *refs):
    refs = list(refs)
    q, do, o, logs, kv, own, flag, left, right, limit = pop(refs, 10)
    operands = pop(refs, len(reduction.operands))
    dq_ref, dkv_own, fin = pop(refs, 3)
    kv_here, dkv, kk, vv = pop(refs, 4)
    scatter_scratch = pop(refs, len(Scatter.SCRATCH))
    reduce_scratch = pop(refs, len(reduction.scratch))
    send, recv, local = refs
    me = here()
    greet_axes(me)
    sems = Sems(send, recv)
    reduction.bind(me, sems, local, operands, reduce_scratch, fin)
    reduction.trade()
    load = pltpu.make_async_copy(kv, kv_here, local.at[reduction.locals])
    load.start()
    scatter = Scatter(me, sems, dkv, dkv_own, scatter_scratch)
    flat = dkv.reshape(CTX, 640, 128)

    def one(head, _):
        dq_ref[head] = attend_back_head(
            head, q[head], do[head], o[head], logs[head], kv_here, own, flag,
            left, right, limit, flat, kk, vv,
        )
        return 0

    column = reduction.column
    reduction.multiply(0)
    reduction.start(0)
    reduction.multiply(1)
    reduction.start(1)
    reduction.multiply(2)
    reduction.pad()
    column.start()
    load.wait()
    lax.fori_loop(0, KV_HEADS, one, 0)
    for k in (2, 1):
        reduction.relay(k)
    scatter.start()
    for k in (3, 0):
        reduction.relay(k)
    for k in (2, 1, 3, 0):
        column.fold_first(k)
    scatter.relay()
    for k in (2, 1, 3, 0):
        reduction.fold_first(k)
    column.relay()
    scatter.middle()
    reduction.fold_second()
    column.fold_second()
    scatter.last()
    reduction.fold_third()
    column.fold_third()
    scatter.end()
    column.end()
    reduction.end()


def backward(q, do, o, logs, kv, own, plan, reduction, collective_id):
    flags, left, right, limits = plan
    copies = reduction.copies + Scatter.COPIES
    return pl.pallas_call(
        functools.partial(backward_kernel, reduction),
        out_shape=[
            jax.ShapeDtypeStruct((KV_HEADS, ROWS, 128), F32),
            jax.ShapeDtypeStruct((640, 128), F32),
            jax.ShapeDtypeStruct(reduction.fin_shape, BF16),
        ],
        in_specs=[VM] * 4 + [ANY] + [VM] * 5 + [ANY] * len(reduction.operands),
        out_specs=[VM, VM, VM],
        scratch_shapes=[
            pltpu.VMEM((CTX, 640, 128), BF16),
            pltpu.VMEM((4, 2, 4, 640, 128), BF16),
            pltpu.VMEM((KEYS, 128), BF16),
            pltpu.VMEM((KEYS, 128), BF16),
            *Scatter.SCRATCH,
            *reduction.scratch,
            pltpu.SemaphoreType.DMA((copies,)),
            pltpu.SemaphoreType.DMA((copies,)),
            pltpu.SemaphoreType.DMA((reduction.locals + 1,)),
        ],
        compiler_params=pltpu.CompilerParams(
            collective_id=collective_id, has_side_effects=True, vmem_limit_bytes=BIG
        ),
        name="backward",
    )(
        q, do, o, logs, kv, own, flags, left, right, limits, *reduction.operands,
    )


def finish_kernel(reduction, sizes, pc, *refs):
    refs = list(refs)
    done = refs.pop(0)
    operands = pop(refs, len(reduction.operands))
    out_done, out = pop(refs, 2)
    fin, other = pop(refs, 2)
    reduce_scratch = pop(refs, len(reduction.scratch))
    send, recv, local = refs
    me = here()
    greet_axes(me, 3)
    sems = Sems(send, recv)
    reduction.bind(me, sems, local, operands, reduce_scratch, fin)
    reduction.trade()
    slots = local.at[pl.ds(reduction.locals, 4)]
    spread = Spread(me, sems, slots, done, out_done, sizes, False, pc, other)
    reduction.multiply(0)
    reduction.pad()
    for n in (0, 1):
        reduction.start(n)
    for k in (2, 1, 3, 0):
        reduction.relay(k)
    spread.across()
    spread.relay()
    for k in (2, 1, 3, 0):
        reduction.fold_first(k)
    reduction.fold_second()
    spread.pass_on()
    reduction.fold_third()
    last = Spread(
        me, sems, local.at[pl.ds(reduction.locals + 4, 2)], fin, out, reduction.sizes, True
    )
    last.relay()
    last.pass_on()
    spread.end()
    last.end()
    reduction.end()


def finish(done, ready, reduction, collective_id):
    copies = reduction.copies + 2 * Spread.COPIES
    return pl.pallas_call(
        functools.partial(finish_kernel, reduction, ready.sizes, ready.pc),
        out_shape=[
            jax.ShapeDtypeStruct((ready.used, 128), BF16),
            jax.ShapeDtypeStruct((reduction.used, 128), BF16),
        ],
        in_specs=[VM] + [ANY] * len(reduction.operands),
        out_specs=[ANY, ANY],
        scratch_shapes=[
            pltpu.VMEM(reduction.fin_shape, BF16),
            pltpu.VMEM((ready.pc, 128), BF16),
            *reduction.scratch,
            pltpu.SemaphoreType.DMA((copies,)),
            pltpu.SemaphoreType.DMA((copies,)),
            pltpu.SemaphoreType.DMA((reduction.locals + 6,)),
        ],
        compiler_params=pltpu.CompilerParams(
            collective_id=collective_id, has_side_effects=True, vmem_limit_bytes=BIG
        ),
        name="finish",
    )(done, *reduction.operands)


def low_lanes(rows):
    return lax.broadcasted_iota(jnp.int32, (rows, 128), 1) < HALF


def turn(tile):
    return pltpu.roll(tile, HALF, 1)


def heads_of_tile(tile):
    early, late = tile[:HALF], tile[HALF:]
    low = low_lanes(HALF)
    return jnp.where(low, late, turn(early)), jnp.where(low, turn(late), early)


def tile_of_heads(first, second):
    low = low_lanes(HALF)
    early = jnp.where(low, turn(first), second)
    late = jnp.where(low, first, turn(second))
    return jnp.concatenate([early, late], axis=0)


def put_heads(ref, values):
    for t in range(8):
        if t < 7:
            tile = values[:, t * 128 : (t + 1) * 128]
        else:
            last = values[:, 896:960]
            tile = jnp.concatenate([last, jnp.zeros_like(last)], axis=1)
        for i, block in enumerate(heads_of_tile(tile)):
            head = 2 * t + i
            if head < HEADS:
                at = head % GROUP * HALF
                ref[head // GROUP, at : at + HALF, :] = block.astype(ref.dtype)


def get_heads(ref):
    def block(head):
        if head == HEADS:
            return jnp.zeros((HALF, 128), F32)
        at = head % GROUP * HALF
        return ref[head // GROUP, at : at + HALF, :].astype(F32)

    return [tile_of_heads(block(2 * t), block(2 * t + 1)) for t in range(8)]


def partner(tile):
    lane = lax.broadcasted_iota(jnp.int32, tile.shape, 1)
    return jnp.where(lane % HEAD < 32, pltpu.roll(tile, 96, 1), pltpu.roll(tile, 32, 1))


def inverse_rms(values):
    return lax.rsqrt(jnp.sum(values * values, axis=1, keepdims=True) * (1.0 / D) + EPSILON)


def norm_back(values, inv, gain, grad):
    scaled = grad * gain
    mean = jnp.sum(scaled * values, axis=1, keepdims=True) * (1.0 / D)
    grad_values = inv * scaled - values * (inv * inv * inv) * mean
    return grad_values, jnp.sum(grad * values * inv, axis=0, keepdims=True)


def swapped(table):
    ctx = lax.axis_index("ctx")
    return jnp.where(table[2 * ctx] > table[2 * ctx + 1], 1.0, 0.0)


def swap_lanes(a, swap):
    return a * (1.0 - swap) + turn(a) * swap


def project_kernel(
    table, tok_t, cot_t, gains, w, frequency,
    q_ref, own_ref, nt_ref, tok_ref, cot_ref, cott_ref, cosine, sine, gain_a, gain_b,
    flag, left, right, limit,
):
    ctx = lax.axis_index("ctx")
    mine = jnp.minimum(table[2 * ctx], table[2 * ctx + 1])
    swap = swapped(table)
    for row, ref in enumerate((gain_a, gain_b)):
        parts = [gains[16 * f : 16 * (f + 1), :].astype(F32)[row : row + 1, :240] for f in range(4)]
        ref[...] = jnp.concatenate(parts, axis=1)
    line = lax.broadcasted_iota(jnp.int32, (TOK, 128), 0)
    column = lax.broadcasted_iota(jnp.int32, (TOK, 128), 1)
    position = jnp.where(line < HALF, mine, 63 - mine) * HALF + lax.rem(line, HALF)
    angles = position.astype(F32) * frequency[...]
    cosine[...] = jnp.cos(angles)
    sine[...] = jnp.where(column % HEAD < 32, -1.0, 1.0) * jnp.sin(angles)
    cot = swap_lanes(cot_t[...].astype(F32), swap)
    cott_ref[0] = cot.astype(BF16)
    cot_ref[...] = cot.T.astype(BF16)
    values = swap_lanes(tok_t[...].astype(F32), swap).T
    tok_ref[...] = values.astype(BF16)
    normed = values * inverse_rms(values) * gain_a[...]
    low = normed.astype(BF16)
    nt_ref[...] = normed.T.astype(BF16)
    blocks = []
    for t in range(13):
        u = dot_nn(low, w[:, t * 128 : (t + 1) * 128])
        if t < 10:
            u = u * cosine[...] + partner(u) * sine[...]
        blocks += heads_of_tile(u)
    for head in range(HEADS):
        at = head % GROUP * HALF
        q_ref[head // GROUP, at : at + HALF, :] = blocks[head].astype(BF16)
    for i in range(2 * KV_HEADS):
        own_ref[i * HALF : (i + 1) * HALF, :] = turn(blocks[HEADS + i]).astype(BF16)

    lane = lax.broadcasted_iota(jnp.int32, (1, 128), 1)
    first = lane < HALF
    offset = lax.rem(lane, HALF)

    def one(i, _):
        early = jnp.minimum(table[2 * i], table[2 * i + 1])
        turn_late = early >= mine
        m = jnp.where(turn_late, 1.0, 0.0)
        row = pl.ds(i, 1)
        flag[row, :] = jnp.where(first, 1.0, m)
        left[row, :] = jnp.where(first, m, 1.0 - m)
        right[row, :] = jnp.where(first, 1.0 - m, 0.0)
        gap = jnp.where(turn_late, mine - early, early - mine)
        blocks_back = jnp.where(first, early - (63 - mine), gap)
        limit[row, :] = (blocks_back * HALF + offset).astype(F32)
        return 0

    lax.fori_loop(0, CTX, one, 0)
    zero = jnp.zeros((1, 128), F32)
    for ref in (flag, left, right):
        ref[CTX:TILES, :] = zero
    limit[CTX:TILES, :] = jnp.where(first, offset, 10**6).astype(F32)


SMEM = pl.BlockSpec(memory_space=pltpu.SMEM)


def project(table, tok_t, cot_t, gains, w):
    exponent = -(np.arange(128) % 32).astype(np.float32) / 32
    frequency = jnp.asarray(np.power(BASE, exponent).astype(np.float32).reshape(1, 128))
    return pl.pallas_call(
        project_kernel,
        out_shape=[
            jax.ShapeDtypeStruct((KV_HEADS, ROWS, 128), BF16),
            jax.ShapeDtypeStruct((640, 128), BF16),
            jax.ShapeDtypeStruct((D, 128), BF16),
            jax.ShapeDtypeStruct((TOK, D), BF16),
            jax.ShapeDtypeStruct((TOK, D), BF16),
            jax.ShapeDtypeStruct((1, D, 128), BF16),
            jax.ShapeDtypeStruct((TOK, 128), F32),
            jax.ShapeDtypeStruct((TOK, 128), F32),
            jax.ShapeDtypeStruct((1, D), F32),
            jax.ShapeDtypeStruct((1, D), F32),
        ]
        + [jax.ShapeDtypeStruct((TILES, 128), F32)] * 4,
        in_specs=[SMEM] + [VM] * 5,
        out_specs=[VM] * 14,
        compiler_params=pltpu.CompilerParams(vmem_limit_bytes=BIG),
        name="project",
    )(table, tok_t, cot_t, gains, w, frequency)


def middle_kernel(
    table, o, tok, cot, gain, out_hbm, gate_hbm, up_hbm, down_hbm,
    layer_out, grad_mid, do_rows, gain_grad, nt, dgu, hid, at_t, gb,
    out_w, gate_w, up_w, down_w, sem,
):
    loads = []
    pairs = ((out_hbm, out_w), (gate_hbm, gate_w), (up_hbm, up_w), (down_hbm, down_w))
    for i, (src, dst) in enumerate(pairs):
        copy = pltpu.make_async_copy(src, dst, sem.at[i])
        copy.start()
        loads.append(copy)
    attended = jnp.concatenate(get_heads(o), axis=1)
    at_t[...] = attended.T[:D].astype(BF16)
    cot_low = cot[...]
    loads[0].wait()
    middle = tok[...].astype(F32) + dot_nn(attended.astype(BF16)[:, :D], out_w[...])
    inv = inverse_rms(middle)
    normed = middle * inv * gain[...]
    low = normed.astype(BF16)
    nt[...] = normed.T.astype(BF16)
    loads[1].wait()
    gate = dot_nn(low, gate_w[...])
    sigmoid = jax.nn.sigmoid(gate)
    silu = gate * sigmoid
    loads[2].wait()
    up = dot_nn(low, up_w[...])
    hidden = (silu * up).astype(BF16)
    for f in range(4):
        hid[f] = hidden[:, f * 640 : (f + 1) * 640]
    loads[3].wait()
    total = middle
    for f in range(4):
        total = total + dot_nt(hidden[:, f * 640 : (f + 1) * 640], down_w[f * D : (f + 1) * D, :])
    layer_out[...] = swap_lanes(total.T, swapped(table)).astype(BF16)
    grad_hidden = jnp.concatenate(
        [dot_nn(cot_low, down_w[f * D : (f + 1) * D, :]) for f in range(4)], axis=1
    )
    grad_gate = (grad_hidden * up * sigmoid * (1.0 + gate * (1.0 - sigmoid))).astype(BF16)
    grad_up = (grad_hidden * silu).astype(BF16)
    dgu[0, :, 0:FF] = grad_gate
    dgu[0, :, FF : 2 * FF] = grad_up
    grad_norm = dot_nt(grad_gate, gate_w[...]) + dot_nt(grad_up, up_w[...])
    grad_values, gain_grad[...] = norm_back(middle, inv, gain[...], grad_norm)
    grad_middle = cot_low.astype(F32) + grad_values
    grad_mid[...] = grad_middle
    branch = grad_middle.astype(BF16)
    gb[0] = jnp.concatenate([branch, jnp.zeros((TOK, 64), BF16)], axis=1)
    put_heads(do_rows, dot_nt(branch, out_w[...]))


def middle(table, o, tok, cot, gain, out_w, gate_w, up_w, down_w):
    weights = (out_w, gate_w, up_w, down_w)
    return pl.pallas_call(
        middle_kernel,
        out_shape=[
            jax.ShapeDtypeStruct((D, TOK), BF16),
            jax.ShapeDtypeStruct((TOK, D), F32),
            jax.ShapeDtypeStruct((KV_HEADS, ROWS, 128), BF16),
            jax.ShapeDtypeStruct((1, D), F32),
            jax.ShapeDtypeStruct((D, 128), BF16),
            jax.ShapeDtypeStruct((1, TOK, 2 * FF), BF16),
            jax.ShapeDtypeStruct((4, TOK, 640), BF16),
            jax.ShapeDtypeStruct((D, 128), BF16),
            jax.ShapeDtypeStruct((1, TOK, 1024), BF16),
        ],
        in_specs=[SMEM] + [VM] * 4 + [ANY] * 4,
        out_specs=[VM] * 9,
        scratch_shapes=[pltpu.VMEM(w.shape, BF16) for w in weights]
        + [pltpu.SemaphoreType.DMA((4,))],
        compiler_params=pltpu.CompilerParams(vmem_limit_bytes=BIG),
        name="middle",
    )(table, o, tok, cot, gain, *weights)


def unproject_kernel(
    table, dq, dkv, cosine, sine, w, tok, gain, grad_mid, gain_grad_b, grad_tok, dqkv, gain_rows
):
    tiles = get_heads(dq)
    low = low_lanes(TOK)
    turned = [turn(dkv[i * 128 : (i + 1) * 128, :].T) for i in range(5)]
    tiles[7] = jnp.where(low, tiles[7], turned[0])
    for i in range(4):
        tiles.append(jnp.where(low, turned[i], turned[i + 1]))
    tiles.append(jnp.where(low, turned[4], 0.0))
    for t in range(13):
        u = tiles[t]
        if t < 10:
            u = u * cosine[...] - partner(u) * sine[...]
        dqkv[0, :, t * 128 : (t + 1) * 128] = u.astype(BF16)
    grad_norm = dot_nt(dqkv[0], w[...])
    values = tok[...].astype(F32)
    grad_values, gain_grad = norm_back(values, inverse_rms(values), gain[...], grad_norm)
    grad_tok[...] = swap_lanes((grad_mid[...] + grad_values).T, swapped(table))
    blank, below = jnp.zeros((1, 16), F32), jnp.zeros((12, 128), F32)
    for f in range(4):
        lines = []
        for grad in (gain_grad, gain_grad_b[...]):
            both = jnp.concatenate([grad[:, f * 240 : (f + 1) * 240], blank], axis=1)
            lines += [both[:, :128], both[:, 128:]]
        gain_rows[f] = jnp.concatenate([*lines, below], axis=0).astype(BF16)


def unproject(table, dq, dkv, cosine, sine, w, tok, gain, grad_mid, gain_grad_b):
    return pl.pallas_call(
        unproject_kernel,
        out_shape=[
            jax.ShapeDtypeStruct((D, TOK), F32),
            jax.ShapeDtypeStruct((1, TOK, 1664), BF16),
            jax.ShapeDtypeStruct((4, 16, 128), BF16),
        ],
        in_specs=[SMEM] + [VM] * 9,
        out_specs=[VM] * 3,
        compiler_params=pltpu.CompilerParams(vmem_limit_bytes=BIG),
        name="unproject",
    )(table, dq, dkv, cosine, sine, w, tok, gain, grad_mid, gain_grad_b)


def unpack_kernel(g_in, u_in, d_in, o_in, qkv, g, u, d, o, q, k, v, gain_a, gain_b):
    for t in range(4):
        rows, lanes = slice(t * 240, (t + 1) * 240), slice(t * 128, (t + 1) * 128)
        g[:, lanes] = g_in[rows, :].astype(F32)
        u[:, lanes] = u_in[rows, :].astype(F32)
    d[...] = d_in[...].astype(F32)
    step = pl.program_id(0)

    @pl.when(step < 4)
    def _():
        o[:, 0:128] = o_in[0:240, :].astype(F32)
        o[:, 128:256] = o_in[240:480, :].astype(F32)

    @pl.when(step == 0)
    def _():
        tiles = [qkv[t * 240 : (t + 1) * 240, :].astype(F32) for t in range(13)]
        low = low_lanes(240)
        for t in range(7):
            q[:, t * 128 : (t + 1) * 128] = tiles[t]
        q[:, 896:960] = tiles[7][:, :64]
        turned = [turn(t) for t in tiles[7:10]]
        k[0:128, :] = jnp.where(low, turned[0], turned[1]).T
        k[128:256, :] = jnp.where(low, turned[1], turned[2]).T
        k[256:320, :] = turned[2].T[:64]
        v[0:128, :] = tiles[10].T
        v[128:256, :] = tiles[11].T
        v[256:320, :] = tiles[12].T[:64]
        lines = qkv[3120:3136, :].astype(F32)
        for n, ref in enumerate((gain_a, gain_b)):
            both = [lines[2 * n : 2 * n + 1], lines[2 * n + 1 : 2 * n + 2, :112]]
            ref[...] = jnp.concatenate(both, axis=1)


def unpack(done, qkv):
    def whole(*shape):
        return pl.BlockSpec(shape, lambda i: (0, 0))

    return pl.pallas_call(
        unpack_kernel,
        grid=(5,),
        out_shape=[
            jax.ShapeDtypeStruct(shape, F32)
            for shape in (
                (240, FF), (240, FF), (D, 640), (240, D), (240, D), (320, 240), (320, 240),
                (1, 240), (1, 240),
            )
        ],
        in_specs=[
            pl.BlockSpec((960, 128), lambda i: (i, 0)),
            pl.BlockSpec((960, 128), lambda i: (5 + i, 0)),
            pl.BlockSpec((960, 128), lambda i: (12 + i, 0)),
            pl.BlockSpec((480, 128), lambda i: (20 + jnp.minimum(i, 3), 0)),
            whole(*qkv.shape),
        ],
        out_specs=[
            pl.BlockSpec((240, 512), lambda i: (0, i)),
            pl.BlockSpec((240, 512), lambda i: (0, i)),
            pl.BlockSpec((D, 128), lambda i: (0, i)),
            pl.BlockSpec((240, 256), lambda i: (0, jnp.minimum(i, 3))),
            whole(240, D),
            whole(320, 240),
            whole(320, 240),
            whole(1, 240),
            whole(1, 240),
        ],
        compiler_params=pltpu.CompilerParams(vmem_limit_bytes=BIG),
        name="unpack",
    )(done, done, done, done, qkv)


def on_device(
    tokens, cotangent, block_table, attn_gain, w_query, w_key, w_value, w_out, mlp_gain,
    w_gate, w_up, w_down,
):
    gains, qkv_w = gather_qkv(
        attn_gain.reshape(1, 240), mlp_gain.reshape(1, 240), w_query, w_key.T, w_value.T, 0
    )
    q_rows, own_kv, na_t, tok, cot, cot_t, cosine, sine, gain_a, gain_b, *plan = project(
        block_table, tokens[0].T, cotangent[0].T, gains, qkv_w
    )
    o_rows, logs, kv, out_w, gate_w, up_w, down_w = forward(
        q_rows, own_kv, plan, (w_out, w_gate, w_up, w_down.T), 1
    )
    kv = kv.reshape(CTX, 640, 128)
    layer_out, grad_mid, do_rows, grad_gain_b, nb_t, dgu, hidden, at_t, branch = middle(
        block_table, o_rows, tok, cot, gain_b, out_w, gate_w, up_w, down_w
    )
    ready = Reduction(
        (
            (nb_t.reshape(2, 2, 240, 128), dgu),
            (at_t.reshape(2, 2, 240, 128), branch),
            (cot_t, hidden.reshape(2, 2, TOK, 640)),
        ),
        None,
        False,
        192,
    )
    dq_rows, dkv, done = backward(q_rows, do_rows, o_rows, logs, kv, own_kv, plan, ready, 2)
    grad_tokens, grad_qkv, gain_rows = unproject(
        block_table, dq_rows, dkv, cosine, sine, qkv_w, tok, gain_a, grad_mid, grad_gain_b
    )
    late = Reduction(
        ((na_t.reshape(2, 2, 240, 128), grad_qkv),), gain_rows.reshape(2, 2, 16, 128), True
    )
    flat_done, flat = finish(done, ready, late, 3)
    shard_g, shard_u, shard_d, shard_o, shard_q, shard_k, shard_v, total_a, total_b = unpack(
        flat_done, flat
    )
    return (
        layer_out.T[None],
        grad_tokens.T[None],
        total_a.reshape(240),
        shard_q,
        shard_k.T,
        shard_v.T,
        shard_o,
        total_b.reshape(240),
        shard_g,
        shard_u,
        shard_d.T,
    )


def solution(mesh):
    rows, cut = P("fsdp", "ctx", None), P("fsdp", None)
    return jax.shard_map(
        on_device,
        mesh=mesh,
        in_specs=(rows, rows, P(), P("fsdp"), cut, cut, cut, cut, P("fsdp"), cut, cut, cut),
        out_specs=(rows, rows, P("fsdp"), cut, cut, cut, cut, P("fsdp"), cut, cut, cut),
        check_vma=False,
    )
```

```python
import functools
import math

import jax
import jax.numpy as jnp
import numpy as np
from jax import lax
from jax.experimental import pallas as pl
from jax.experimental.pallas import tpu as pltpu
from jax.sharding import PartitionSpec as P

D = 960
HEADS = 15
KV_HEADS = 5
GROUP = 3
HEAD = 64
FF = 2560
TOK = 128
HALF = 64
CTX = 32
TILES = 33
KEYS = TILES * 128
SCALE = HEAD ** (-0.5)
EPSILON = 1e-05
BASE = 10000.0
LOG2E = math.log2(math.e)
NEG = -1e30
MESH = pl.DeviceIdType.MESH
ANY = pl.BlockSpec(memory_space=pl.ANY)
VM = pl.BlockSpec(memory_space=pltpu.VMEM)
BIG = 56 * 2**20
F32 = jnp.float32
BF16 = jnp.bfloat16


def here():
    ctx = lax.axis_index("ctx")
    shard = lax.axis_index("fsdp")
    return {
        "z": ctx // 8,
        "yh": (ctx // 4) % 2,
        "x": ctx % 4,
        "yl": shard // 2,
        "c": shard % 2,
    }


def device(place, **moved):
    p = {**place, **moved}
    return (p["z"] * 8 + p["yh"] * 4 + p["x"], p["yl"] * 2 + p["c"])


def greet(devices):
    sem = pltpu.get_barrier_semaphore()
    for d in devices:
        pl.semaphore_signal(sem, inc=1, device_id=d, device_id_type=MESH)
    pl.semaphore_wait(sem, len(devices))


class Sems:
    def __init__(self, send, recv):
        self.send, self.recv, self.at = send, recv, 0

    def push(self, src, dst, dev):
        copy = pltpu.make_async_remote_copy(
            src_ref=src,
            dst_ref=dst,
            send_sem=self.send.at[self.at],
            recv_sem=self.recv.at[self.at],
            device_id=dev,
            device_id_type=MESH,
        )
        self.at += 1
        copy.start()
        return copy


def start_gather(me, sems, local, arrays, stages=None, ringed=None):
    f = me["yl"] * 2 + me["c"]
    near = device(me, yl=1 - me["yl"])
    far = device(me, yl=1 - me["yl"], yh=1 - me["yh"])
    mate = device(me, c=1 - me["c"])
    parts, kept, own = [], [], []
    for i, (a, b) in enumerate(arrays):
        rows = a.shape[0]
        if i == ringed:
            continue
        first = rows // 32 * 16 if i % 2 else (rows + 31) // 32 * 16
        for lo, size, dev in ((0, first, near), (first, rows - first, far)):
            if size:
                src = a.at[pl.ds(lo, size)]
                dst = b.at[pl.ds(pl.multiple_of(f * rows + lo, 16), size)]
                parts.append((sems.push(src, dst, dev), b, rows, lo, size))
    for i, (a, b) in enumerate(arrays):
        rows = a.shape[0]
        dst = b.at[pl.ds(pl.multiple_of(f * rows, 16), rows)]
        kept.append(sems.push(a, dst, mate))
        stage = a if stages is None else stages[i]
        if stages is not None:
            load = pltpu.make_async_copy(a, stage, local.at[i])
            load.start()
        own.append((stage, dst, local.at[i]))
    if stages is not None:
        for (a, _), (stage, _, sem) in zip(arrays, own):
            pltpu.make_async_copy(a, stage, sem).wait()
    own = [pltpu.make_async_copy(*copy) for copy in own]
    for copy in own:
        copy.start()
    return parts, kept, own


class Quartered:
    def __init__(self, me, sems, a, b):
        self.me, self.sems, self.b = me, sems, b
        self.rows = a.shape[0]
        self.quarter = self.rows // 4
        self.first = (self.quarter + 31) // 32 * 16
        f = me["yl"] * 2 + me["c"]
        near = device(me, yl=1 - me["yl"])
        far = device(me, yl=1 - me["yl"], yh=1 - me["yh"])
        base = me["x"] * self.quarter
        self.parts = []
        for lo, size, dev in ((0, self.first, near), (self.first, self.quarter - self.first, far)):
            src = a.at[pl.ds(pl.multiple_of(base + lo, 16), size)]
            dst = b.at[pl.ds(pl.multiple_of(f * self.rows + base + lo, 16), size)]
            self.parts.append(sems.push(src, dst, dev))
        self.across = ((1 - me["yl"]) * 2 + me["c"]) * self.rows

    def place(self, at):
        start = pl.multiple_of(self.across + at * self.quarter, 16)
        return self.b.at[pl.ds(start, self.quarter)]

    def halves(self, ref):
        return ref.at[pl.ds(0, self.first)], ref.at[pl.ds(self.first, self.quarter - self.first)]

    def share(self):
        for copy in self.parts:
            copy.wait_recv()
        ring = Ring(self.me, "x")
        self.shared = Share(self.sems, ring, self.place(ring.me), self.place, self.halves)

    def relay(self):
        self.shared.relay()

    def pass_on(self):
        self.shared.arrive()
        span = self.b.at[pl.ds(pl.multiple_of(self.across, 16), self.rows)]
        self.mate = self.sems.push(span, span, device(self.me, c=1 - self.me["c"]))

    def end(self):
        self.shared.end()
        self.mate.wait()
        for copy in self.parts:
            copy.wait_send()


def relay_gather(me, sems, started):
    parts, kept, _ = started
    across = (1 - me["yl"]) * 2 + me["c"]
    mate = device(me, c=1 - me["c"])
    for copy, b, rows, lo, size in parts:
        copy.wait_recv()
        span = b.at[pl.ds(pl.multiple_of(across * rows + lo, 16), size)]
        kept.append(sems.push(span, span, mate))


def end_gather(started):
    parts, kept, own = started
    for copy in own:
        copy.wait()
    for copy in kept:
        copy.wait()
    for copy, *_ in parts:
        copy.wait_send()


def gathered(arrays):
    return [jax.ShapeDtypeStruct((4 * a.shape[0], *a.shape[1:]), a.dtype) for a in arrays]


def gather_qkv_kernel(
    both, wq, wk_t, wv_t, gains, qkv, gains_own, qkv_own, send, recv, local
):
    lines = jnp.concatenate([both[...].astype(F32), jnp.zeros((2, 16), F32)], axis=1)
    gains_own[...] = jnp.concatenate([lines, jnp.zeros((14, 256), F32)], axis=0).astype(BF16)
    qkv_own[:, 0:896] = wq[:, 0:896]
    rest = [wq[:, 896:960].astype(F32), wk_t[...].astype(F32).T, wv_t[...].astype(F32).T]
    qkv_own[:, 896:1664] = jnp.concatenate([*rest, jnp.zeros((240, 64), F32)], axis=1).astype(BF16)
    me = here()
    flip = 1 - me["yl"]
    greet((device(me, yl=flip), device(me, yl=flip, yh=1 - me["yh"]), device(me, c=1 - me["c"])))
    sems = Sems(send, recv)
    started = start_gather(me, sems, local, [(gains_own, gains), (qkv_own, qkv)])
    relay_gather(me, sems, started)
    end_gather(started)


def gather_qkv(both, wq, wk_t, wv_t, collective_id):
    own = [jax.ShapeDtypeStruct((16, 256), BF16), jax.ShapeDtypeStruct((240, 1664), BF16)]
    return pl.pallas_call(
        gather_qkv_kernel,
        out_shape=gathered(own),
        in_specs=[VM] * 4,
        out_specs=[ANY] * 2,
        scratch_shapes=[pltpu.VMEM(a.shape, BF16) for a in own]
        + [
            pltpu.SemaphoreType.DMA((10,)),
            pltpu.SemaphoreType.DMA((10,)),
            pltpu.SemaphoreType.DMA((2,)),
        ],
        compiler_params=pltpu.CompilerParams(
            collective_id=collective_id, has_side_effects=True, vmem_limit_bytes=BIG
        ),
        name="gather_qkv",
    )(both, wq, wk_t, wv_t)


class Ring:
    def __init__(self, me, axis):
        at = me[axis]
        self.me = at
        self.right_at, self.opposite_at, self.left_at = (lax.rem(at + d, 4) for d in (1, 2, 3))
        self.right = device(me, **{axis: self.right_at})
        self.left = device(me, **{axis: self.left_at})
        self.opposite = device(me, **{axis: self.opposite_at})


class Share:
    def __init__(self, sems, ring, src, place, halves):
        self.sems, self.ring, self.place, self.halves = sems, ring, place, halves
        dst = place(ring.me)
        self.copies = [sems.push(src, dst, ring.right), sems.push(src, dst, ring.left)]
        self.passed, self.here = [], False
        if halves is None:
            self.passed.append(sems.push(src, dst, ring.opposite))

    def near(self):
        if not self.here:
            for copy in self.copies:
                copy.wait_recv()
            self.here = True

    def relay(self):
        self.near()
        if self.halves is not None:
            ring, push = self.ring, self.sems.push
            half = self.halves(self.place(ring.left_at))[0]
            self.passed.append(push(half, half, ring.right))
            half = self.halves(self.place(ring.right_at))[1]
            self.passed.append(push(half, half, ring.left))

    def arrive(self):
        for copy in self.passed:
            copy.wait_recv()

    def end(self):
        for copy in self.copies + self.passed:
            copy.wait_send()


def gather_kv(me, sems, kv, out, once_across):
    x, yh, z = me["x"], me["yh"], me["z"]
    other = device(me, yh=1 - yh)
    rings = Ring(me, "x"), Ring(me, "z")
    spans = pl.ds(0, 320), pl.ds(320, 320)
    across = [sems.push(kv.at[p], out.at[z, yh, x, p], other) for p in spans]

    def near(axis, row, src):
        lo = 320 * axis

        def place(at):
            ref = out.at[z, row, at] if axis == 0 else out.at[at, row, x]
            return ref.at[spans[axis]]

        def halves(ref):
            return ref.at[pl.ds(0, 160)], ref.at[pl.ds(160, 160)]

        return Share(sems, rings[axis], src, place, halves)

    def far(axis, row):
        def place(at):
            return out.at[at, row, :, spans[0]] if axis == 0 else out.at[:, row, at, spans[1]]

        def halves(ref):
            return ref.at[pl.ds(0, 2)], ref.at[pl.ds(2, 2)]

        src = place(rings[1 - axis].me)
        return Share(sems, rings[1 - axis], src, place, halves)

    first = [near(axis, yh, kv.at[spans[axis]]) for axis in (0, 1)]
    out[z, yh, x] = kv[...]
    for share in first:
        share.relay()
    second = []
    for axis in (0, 1):
        across[axis].wait_recv()
        row = 1 - yh
        src = out.at[z, row, x, spans[axis]]
        second.append(near(axis, row, src))
    once_across()
    last = []
    for axis in (0, 1):
        first[axis].arrive()
        last.append(far(axis, yh))
    for share in second:
        share.relay()
    for axis in (0, 1):
        second[axis].arrive()
        last.append(far(axis, 1 - yh))
    for share in last:
        share.relay()
    for share in last:
        share.arrive()
    return across, first + second + last


def add_low(a, b):
    return (a.astype(F32) + b.astype(F32)).astype(BF16)


class Fold:
    def __init__(self, sems, ring, block, landing, passing, direct=False):
        self.sems, self.ring, self.block, self.direct = sems, ring, block, direct
        self.landing, self.passing = landing, passing
        self.copies, self.passed, self.sent = {}, {}, []

    def start_opposite(self, half):
        ring = self.ring
        src = self.block(ring.opposite_at, half)
        dev = ring.opposite if self.direct else (ring.right, ring.left)[half]
        self.passed[half] = self.sems.push(src, self.passing(half), dev)

    def start_direct(self, half):
        ring = self.ring
        at, dev = ((ring.left_at, ring.left), (ring.right_at, ring.right))[half]
        side = 1 - half
        self.copies[side, half] = self.sems.push(
            self.block(at, half), self.landing(side, half), dev
        )

    def relay(self, half):
        ring = self.ring
        at, dev = ((ring.right_at, ring.right), (ring.left_at, ring.left))[half]
        src = self.block(at, half)
        if not self.direct:
            self.passed[half].wait_recv()
            src[...] = add_low(src[...], self.passing(half)[...])
        self.copies[half, half] = self.sems.push(src, self.landing(half, half), dev)

    def total(self, half):
        for side in (0, 1):
            self.copies[side, half].wait_recv()
        total = self.block(self.ring.me, half)[...].astype(F32)
        for side in (0, 1):
            total = total + self.landing(side, half)[...].astype(F32)
        if self.direct:
            self.passed[half].wait_recv()
            total = total + self.passing(half)[...].astype(F32)
        return total

    def end(self):
        for copy in list(self.copies.values()) + list(self.passed.values()):
            copy.wait_send()


class Scatter:
    COPIES = 26
    SCRATCH = [
        pltpu.VMEM((2, 3, 2, 4, 320, 128), BF16),
        pltpu.VMEM((2, 2, 4, 320, 128), BF16),
        pltpu.VMEM((2, 3, 2, 320, 128), BF16),
        pltpu.VMEM((2, 320, 128), BF16),
        pltpu.VMEM((2, 320, 128), BF16),
    ]

    def __init__(self, me, sems, part, out, scratch):
        self.me, self.sems, self.part, self.out = me, sems, part, out
        self.r1, self.s1, self.r2, self.s2, self.r3 = scratch
        self.rings = Ring(me, "x"), Ring(me, "z")
        self.first, self.second, self.third = [], [], []
        rows = (1 - me["yh"], me["yh"])
        key, value = pl.ds(0, 320), pl.ds(320, 320)

        def block0(at, half):
            return part.at[at, rows[half], :, key]

        def block1(at, half):
            return part.at[:, rows[half], at, value]

        for axis, block in enumerate((block0, block1)):
            r1, s1, r2 = self.r1, self.s1, self.r2
            self.first.append(
                Fold(
                    sems,
                    self.rings[1 - axis],
                    block,
                    lambda side, half, axis=axis: r1.at[axis, side, half],
                    lambda half, axis=axis: r1.at[axis, 2, half],
                )
            )
            self.second.append(
                Fold(
                    sems,
                    self.rings[axis],
                    lambda at, half, axis=axis: s1.at[axis, half, at],
                    lambda side, half, axis=axis: r2.at[axis, side, half],
                    lambda half, axis=axis: r2.at[axis, 2, half],
                )
            )

    def start(self):
        for half in (0, 1):
            for fold in self.first:
                fold.start_opposite(half)
        for half in (0, 1):
            for fold in self.first:
                fold.start_direct(half)

    def relay(self):
        for half in (0, 1):
            for fold in self.first:
                fold.relay(half)

    def middle(self):
        for half in (0, 1):
            for axis in (0, 1):
                self.s1[axis, half] = self.first[axis].total(half).astype(BF16)
                self.second[axis].start_opposite(half)
                self.second[axis].start_direct(half)
        for half in (0, 1):
            for fold in self.second:
                fold.relay(half)

    def last(self):
        other = device(self.me, yh=1 - self.me["yh"])
        for axis in (0, 1):
            self.s2[axis] = self.second[axis].total(0).astype(BF16)
            self.third.append(self.sems.push(self.s2.at[axis], self.r3.at[axis], other))
        for axis in (0, 1):
            self.out[pl.ds(axis * 320, 320), :] = self.second[axis].total(1)

    def end(self):
        for axis in (0, 1):
            self.third[axis].wait_recv()
            span = pl.ds(axis * 320, 320)
            self.out[span, :] = self.out[span, :] + self.r3[axis].astype(F32)
        for fold in self.first + self.second:
            fold.end()
        for c in self.third:
            c.wait_send()


def build_tiles(head, kv_ref, own_ref, left_ref, tiles_ref, base):
    lane = lax.broadcasted_iota(jnp.int32, (HALF, 128), 1)
    start = pl.multiple_of(base + head * HALF, HALF)

    def one(i, _):
        block = kv_ref[i, pl.ds(start, HALF), :].astype(F32)
        top = jnp.where(lane < HALF, block, 0.0)
        low = pltpu.roll(block, HALF, 1) * left_ref[pl.ds(i, 1), :]
        at = pl.multiple_of(i * 128, 128)
        tiles_ref[pl.ds(at, 128), :] = jnp.concatenate([top, low], axis=0).astype(BF16)
        return 0

    lax.fori_loop(0, CTX, one, 0, unroll=32)
    block = own_ref[pl.ds(start, HALF), :].astype(F32)
    top = jnp.where(lane < HALF, 0.0, pltpu.roll(block, HALF, 1))
    tiles_ref[pl.ds(CTX * 128, 128), :] = jnp.concatenate(
        [top, jnp.zeros_like(top)], axis=0
    ).astype(BF16)


def dot_nt(a, b):
    return lax.dot_general(a, b, (((1,), (1,)), ((), ())), preferred_element_type=F32)


def dot_nn(a, b):
    return lax.dot_general(a, b, (((1,), (0,)), ((), ())), preferred_element_type=F32)


ROWS = GROUP * HALF


def row_offset():
    return lax.rem(lax.broadcasted_iota(jnp.int32, (ROWS, 128), 0), HALF).astype(F32)


def attend_head(head, q, kv_ref, own_ref, flag_ref, left_ref, limit_ref, kk, vv):
    build_tiles(head, kv_ref, own_ref, left_ref, kk, 0)
    build_tiles(head, kv_ref, own_ref, left_ref, vv, 320)
    offset = row_offset()
    low = jnp.full((ROWS, 128), NEG, F32)
    s = dot_nt(q, kk[...]) * (SCALE * LOG2E)
    tiles = []
    top_l, top_e = low, low
    for i in range(TILES):
        tile = s[:, i * 128 : (i + 1) * 128]
        tile = jnp.where(limit_ref[i : i + 1, :] <= offset, tile, NEG)
        tiles.append(tile)
        late = flag_ref[i : i + 1, :] > 0.5
        top_l = jnp.maximum(top_l, jnp.where(late, tile, NEG))
        top_e = jnp.maximum(top_e, jnp.where(late, NEG, tile))
    max_l = jnp.broadcast_to(jnp.max(top_l, axis=1, keepdims=True), (ROWS, 128))
    max_e = jnp.broadcast_to(jnp.max(top_e, axis=1, keepdims=True), (ROWS, 128))
    sum_l = jnp.zeros((ROWS, 128), F32)
    sum_e = jnp.zeros((ROWS, 128), F32)
    probs = []
    for i in range(TILES):
        late = flag_ref[i : i + 1, :] > 0.5
        p = jnp.exp2(tiles[i] - jnp.where(late, max_l, max_e))
        p_l = jnp.where(late, p, 0.0)
        sum_l = sum_l + p_l
        sum_e = sum_e + (p - p_l)
        probs.append(p.astype(BF16))
    total = dot_nn(jnp.concatenate(probs, axis=1), vv[...])
    late = lax.broadcasted_iota(jnp.int32, (ROWS, 128), 1) < HALF
    row_sum = jnp.where(
        late, jnp.sum(sum_l, axis=1, keepdims=True), jnp.sum(sum_e, axis=1, keepdims=True)
    )
    return total / row_sum, jnp.where(late, max_l, max_e) + jnp.log2(row_sum)


def forward_kernel(count, q_ref, own_ref, flag_ref, left_ref, limit_ref, *refs):
    shards, refs = refs[:count], refs[count:]
    o_ref, l_ref, kv_out, *full = refs[: 3 + count]
    kv, kk, vv, *stages, send, recv, local = refs[3 + count :]
    me = here()
    greet_axes(me)
    sems = Sems(send, recv)
    started, quartered = [], []

    def start_weights():
        quartered.append(Quartered(me, sems, shards[-1], full[-1]))
        pairs = list(zip(shards, full))
        started.extend(start_gather(me, sems, local, pairs, stages, count - 1))

    across, shares = gather_kv(me, sems, own_ref, kv, start_weights)
    keep = pltpu.make_async_copy(kv, kv_out, local.at[count])
    keep.start()
    flat = kv.reshape(CTX, 640, 128)

    def one(head, _):
        o, logs = attend_head(
            head, q_ref[head], flat, own_ref, flag_ref, left_ref, limit_ref, kk, vv
        )
        o_ref[head] = o
        l_ref[head] = logs
        return 0

    down = quartered[0]
    down.share()
    lax.fori_loop(0, 1, one, 0)
    down.relay()
    lax.fori_loop(1, 3, one, 0)
    down.pass_on()
    relay_gather(me, sems, started)
    lax.fori_loop(3, KV_HEADS, one, 0)
    end_gather(started)
    down.end()
    for copy in across:
        copy.wait_send()
    for share in shares:
        share.end()
    keep.wait()


def forward(q, own, plan, shards, collective_id):
    flags, left, _, limits = plan
    n = len(shards)
    copies = 5 * n + 3 + 2 + 8 * 4
    return pl.pallas_call(
        functools.partial(forward_kernel, n),
        out_shape=[jax.ShapeDtypeStruct((KV_HEADS, ROWS, 128), F32)] * 2
        + [jax.ShapeDtypeStruct((4, 2, 4, 640, 128), BF16)]
        + gathered(shards),
        in_specs=[VM] * 5 + [ANY] * n,
        out_specs=[VM, VM, ANY] + [ANY] * n,
        scratch_shapes=[
            pltpu.VMEM((4, 2, 4, 640, 128), BF16),
            pltpu.VMEM((KEYS, 128), BF16),
            pltpu.VMEM((KEYS, 128), BF16),
            *[pltpu.VMEM(a.shape, BF16) for a in shards],
            pltpu.SemaphoreType.DMA((copies,)),
            pltpu.SemaphoreType.DMA((copies,)),
            pltpu.SemaphoreType.DMA((n + 1,)),
        ],
        compiler_params=pltpu.CompilerParams(
            collective_id=collective_id, has_side_effects=True, vmem_limit_bytes=BIG
        ),
        name="forward",
    )(q, own, flags, left, limits, *shards)


def attend_back_head(
    head, q, do, o, logs, kv_ref, own_ref, flag_ref, left_ref, right_ref, limit_ref,
    dkv_ref, kk, vv,
):
    build_tiles(head, kv_ref, own_ref, left_ref, kk, 0)
    build_tiles(head, kv_ref, own_ref, left_ref, vv, 320)
    offset = row_offset()
    lane = lax.broadcasted_iota(jnp.int32, (ROWS, 128), 1)
    product = do.astype(F32) * o
    shape = (ROWS, 128)
    delta_l = jnp.broadcast_to(
        jnp.sum(jnp.where(lane < HALF, product, 0.0), axis=1, keepdims=True), shape
    )
    delta_e = jnp.broadcast_to(
        jnp.sum(jnp.where(lane < HALF, 0.0, product), axis=1, keepdims=True), shape
    )
    log_l = jnp.broadcast_to(logs[:, 0:1], shape)
    log_e = jnp.broadcast_to(logs[:, HALF : HALF + 1], shape)
    k_rows = pl.ds(pl.multiple_of(head * HALF, HALF), HALF)
    v_rows = pl.ds(pl.multiple_of(320 + head * HALF, HALF), HALF)
    small = lax.broadcasted_iota(jnp.int32, (HALF, 128), 1)
    keys = kk[...]
    s = dot_nt(q, keys) * (SCALE * LOG2E)
    dp = dot_nt(do, vv[...])
    probs, scores = [], []
    for i in range(TILES):
        cut = slice(i * 128, (i + 1) * 128)
        late = flag_ref[i : i + 1, :] > 0.5
        tile = jnp.where(limit_ref[i : i + 1, :] <= offset, s[:, cut], NEG)
        p = jnp.exp2(tile - jnp.where(late, log_l, log_e))
        probs.append(p.astype(BF16))
        scores.append((p * (dp[:, cut] - jnp.where(late, delta_l, delta_e))).astype(BF16))
    ds = jnp.concatenate(scores, axis=1)
    dq = dot_nn(ds, keys) * SCALE
    dk = dot_nn(q.astype(F32).T.astype(BF16), ds) * SCALE
    dv = dot_nn(do.astype(F32).T.astype(BF16), jnp.concatenate(probs, axis=1))
    mine = lax.axis_index("ctx")
    for rows, both in ((k_rows, dk), (v_rows, dv)):
        for i in range(CTX):
            cut = slice(i * 128, (i + 1) * 128)
            top, bottom = both[0:HALF, cut], both[HALF:128, cut]
            total = (
                top * flag_ref[i : i + 1, :]
                + pltpu.roll(bottom, HALF, 1) * right_ref[i : i + 1, :]
            )
            dkv_ref[i, rows, :] = total.astype(BF16)
        bottom = both[HALF:128, CTX * 128 :]
        before = dkv_ref[mine, rows, :].astype(F32)
        dkv_ref[mine, rows, :] = (before + jnp.where(small < HALF, bottom, 0.0)).astype(BF16)
    return dq


def pop(refs, count):
    taken = refs[:count]
    del refs[:count]
    return taken


class Column:
    COPIES = 24

    @staticmethod
    def scratch(pc):
        return [
            pltpu.VMEM((3, 4, 4 * pc, 128), BF16),
            pltpu.VMEM((4, 4 * pc, 128), BF16),
            pltpu.VMEM((3, 2, 2 * pc, 128), BF16),
            pltpu.VMEM((4 * pc, 128), BF16),
            pltpu.VMEM((3, 2, pc // 2, 128), BF16),
        ]

    def __init__(self, me, sems, grads, lo, pc, scratch, fin):
        self.me, self.sems, self.grads, self.lo, self.pc, self.fin = me, sems, grads, lo, pc, fin
        self.ry, self.sy, rx, self.sx, rz = scratch
        self.first = {}
        sy, sx, x = self.sy, self.sx, me["x"]

        def strip(at, half):
            return sy.at[lax.rem(at + 4 - x, 4), pl.ds(half * 2 * pc, 2 * pc)]

        def piece(at, half):
            return sx.at[pl.ds(pl.multiple_of(at * pc + half * (pc // 2), 16), pc // 2)]

        self.over_x = Fold(
            sems,
            Ring(me, "x"),
            strip,
            lambda side, half: rx.at[side, half],
            lambda half: rx.at[2, half],
        )
        self.over_z = Fold(
            sems,
            Ring(me, "z"),
            piece,
            lambda side, half: rz.at[side, half],
            lambda half: rz.at[2, half],
        )

    def rows(self, half, k):
        i = lax.rem(self.me["x"] + k, 4)
        start = pl.multiple_of(self.lo + (half * 16 + i * 4) * self.pc, 16)
        return pl.ds(start, 4 * self.pc)

    def start(self):
        me = self.me
        yl, yh = me["yl"], me["yh"]
        ways = (
            (1 - yl, yh, device(me, yl=1 - yl)),
            (1 - yl, 1 - yh, device(me, yl=1 - yl, yh=1 - yh)),
            (yl, 1 - yh, device(me, yh=1 - yh)),
        )
        for k in (2, 1, 3, 0):
            for slot, (shard, half, dev) in enumerate(ways):
                src = self.grads.at[shard, self.rows(half, k)]
                self.first[k, slot] = self.sems.push(src, self.ry.at[slot, k], dev)

    def fold_first(self, k):
        for slot in (0, 1, 2):
            self.first[k, slot].wait_recv()
        total = self.grads[self.me["yl"], self.rows(self.me["yh"], k)].astype(F32)
        for slot in (0, 1, 2):
            total = total + self.ry[slot, k].astype(F32)
        self.sy[k] = total.astype(BF16)
        if k == 2:
            self.over_x.start_opposite(0)
            self.over_x.start_opposite(1)
        elif k == 1:
            self.over_x.start_direct(1)
        elif k == 3:
            self.over_x.start_direct(0)

    def relay(self):
        self.over_x.relay(0)
        self.over_x.relay(1)

    def fold_second(self):
        for half in (0, 1):
            span = pl.ds(half * 2 * self.pc, 2 * self.pc)
            self.sx[span] = self.over_x.total(half).astype(BF16)
        for half in (0, 1):
            self.over_z.start_opposite(half)
            self.over_z.start_direct(half)

    def fold_third(self):
        self.over_z.relay(0)
        self.over_z.relay(1)

    def end(self):
        base = self.fin.shape[0] - self.pc
        for half in (0, 1):
            span = pl.ds(base + half * (self.pc // 2), self.pc // 2)
            self.fin[span, :] = self.over_z.total(half).astype(BF16)
        self.over_x.end()
        self.over_z.end()
        for copy in self.first.values():
            copy.wait_send()


class Reduction:
    def __init__(self, jobs, extra, direct=False, pc=0):
        self.operands, self.jobs, self.scratch, rows = [], [], [], 0
        self.direct = direct
        for left, right in jobs:
            self.operands += [left, right]
            m, n = left.shape[-2], right.shape[-1]
            self.jobs.append((left.ndim == 4, m, right.ndim == 4, n))
            self.scratch.append(pltpu.VMEM((left.shape[0], m, 256), BF16))
            self.scratch.append(pltpu.VMEM((right.shape[0], 256, n), BF16))
            rows += m * (n // 128)
        self.extra = extra is not None
        if self.extra:
            self.operands.append(extra)
            self.scratch.append(pltpu.VMEM((2, 2, 16, 128), BF16))
            rows += 16
        pieces = -(-rows // 256) - pc // 8
        self.sizes = ((pieces + 1) // 2 * 16, pieces // 2 * 16)
        self.pc = pc
        self.used = 16 * (sum(self.sizes) + 2 * pc)
        self.scratch.append(pltpu.VMEM((2, self.used, 128), BF16))
        for size in self.sizes:
            self.scratch += [
                pltpu.VMEM((3, 4, 2, size, 128), BF16),
                pltpu.VMEM((4, 2, size, 128), BF16),
                pltpu.VMEM((3, 2, size, 128), BF16),
                pltpu.VMEM((2, size, 128), BF16),
                pltpu.VMEM((4, size, 128), BF16),
            ]
        self.locals = 2 * len(jobs) + 1
        self.copies = 2 * len(jobs) + 1 + 48 + 12 + 6
        self.fin_shape = (sum(self.sizes) + pc, 128)
        if pc:
            self.scratch += Column.scratch(pc)
            self.copies += Column.COPIES

    def bind(self, me, sems, local, operands, scratch, fin):
        operands, scratch = list(operands), list(scratch)
        self.me, self.sems, self.local, self.fin = me, sems, local, fin
        self.sources, self.buffers = [], []
        core = me["c"]
        for cut_left, _, cut_right, _ in self.jobs:
            left, right = pop(operands, 2)
            lefts = (left.at[:, core], left.at[:, 1 - core]) if cut_left else (left, left)
            rights = (right.at[:, core], right.at[:, 1 - core]) if cut_right else (right, right)
            self.sources.append((*lefts, *rights))
            self.buffers.append(pop(scratch, 2))
        if self.extra:
            self.extra_refs = (operands[0].at[:, core], operands[0].at[:, 1 - core])
            self.extra_buffer = scratch.pop(0)
        self.grads = scratch.pop(0)
        self.parts = [pop(scratch, 5) for _ in self.sizes]
        if self.pc:
            lo = 16 * sum(self.sizes)
            self.column = Column(me, sems, self.grads, lo, self.pc, scratch, fin)
        xs, zs = Ring(me, "x"), Ring(me, "z")
        self.plans = (
            (0, self.sizes[0], xs, zs),
            (16 * self.sizes[0], self.sizes[1], zs, xs),
        )
        self.first, self.second, self.third = {}, {}, {}
        for n, (lo, size, ring, cross) in enumerate(self.plans):
            r1, s1, r2, _, _ = self.parts[n]
            for k in range(4):
                j = lax.rem(cross.me + k, 4)

                def block(at, half, lo=lo, size=size, j=j):
                    start = pl.multiple_of(lo + (at * 4 + j) * size, 16)
                    return self.grads.at[half, pl.ds(start, size)]

                self.first[n, k] = Fold(
                    sems,
                    ring,
                    block,
                    lambda side, half, r1=r1, k=k: r1.at[side, k, half],
                    lambda half, r1=r1, k=k: r1.at[2, k, half],
                    self.direct,
                )

            def turned(at, half, s1=s1, cross=cross):
                return s1.at[lax.rem(at + 4 - cross.me, 4), half]

            self.second[n] = Fold(
                sems,
                cross,
                turned,
                lambda side, half, r2=r2: r2.at[side, half],
                lambda half, r2=r2: r2.at[2, half],
                self.direct,
            )

    def trade(self):
        mate = device(self.me, c=1 - self.me["c"])
        push = self.sems.push
        self.mine, self.traded = [], []

        def keep(src, dst):
            copy = pltpu.make_async_copy(src, dst, self.local.at[len(self.mine)])
            copy.start()
            self.mine.append(copy)

        here_, there = pl.ds(0, 128), pl.ds(128, 128)
        for (lm, lt, rm, rt), (lb, rb) in zip(self.sources, self.buffers):
            self.traded.append(push(lt, lb.at[:, :, there], mate))
            self.traded.append(push(rt, rb.at[:, there], mate))
            keep(lm, lb.at[:, :, here_])
            keep(rm, rb.at[:, here_])
        if self.extra:
            self.traded.append(push(self.extra_refs[1], self.extra_buffer.at[1], mate))
            keep(self.extra_refs[0], self.extra_buffer.at[0])

    def multiply(self, job):
        base = sum(m * (n // 128) for _, m, _, n in self.jobs[:job])
        for copy in self.mine[2 * job : 2 * job + 2]:
            copy.wait()
        for copy in self.traded[2 * job : 2 * job + 2]:
            copy.wait_recv()
        grads, (_, m, _, n), (lb, rb) = self.grads, self.jobs[job], self.buffers[job]
        strip = min(n, 1280) if n % 1280 == 0 else n
        for s in range(2):
            left = lb[min(s, lb.shape[0] - 1)]

            def block(i, _, left=left, s=s):
                at = pl.multiple_of(i * strip, 128)
                right = rb[min(s, rb.shape[0] - 1), :, pl.ds(at, strip)]
                result = dot_nn(left, right).astype(BF16)
                for w in range(strip // 128):
                    to = pl.multiple_of(base + (i * (strip // 128) + w) * m, 16)
                    grads[s, pl.ds(to, m), :] = result[:, w * 128 : (w + 1) * 128]
                return 0

            if n == strip:
                block(0, 0)
            else:
                lax.fori_loop(0, n // strip, block, 0)

    def pad(self):
        base, grads = sum(m * (n // 128) for _, m, _, n in self.jobs), self.grads
        if self.extra:
            self.mine[-1].wait()
            self.traded[-1].wait_recv()
            for s in range(2):
                both = self.extra_buffer[0, s].astype(F32) + self.extra_buffer[1, s].astype(F32)
                grads[s, pl.ds(base, 16), :] = both.astype(BF16)
            base += 16
        if base < self.used:
            for s in range(2):
                grads[s, pl.ds(base, self.used - base), :] = jnp.zeros(
                    (self.used - base, 128), BF16
                )

    def start(self, n):
        for k in (2, 1, 3, 0):
            for half in (0, 1):
                self.first[n, k].start_opposite(half)
        for k in (2, 1, 3, 0):
            for half in (0, 1):
                self.first[n, k].start_direct(half)

    def relay(self, k):
        for half in (0, 1):
            for n in (0, 1):
                self.first[n, k].relay(half)

    def fold_first(self, k):
        for n in (0, 1):
            s1, second = self.parts[n][1], self.second[n]
            for half in (0, 1):
                s1[k, half] = self.first[n, k].total(half).astype(BF16)
            if k == 2:
                second.start_opposite(0)
                second.start_opposite(1)
            elif k == 1:
                second.start_direct(1)
            elif k == 3:
                second.start_direct(0)

    def fold_second(self):
        me, push = self.me, self.sems.push
        yh, yl = me["yh"], me["yl"]
        for half in (0, 1):
            for n in (0, 1):
                self.second[n].relay(half)
        for n in (0, 1):
            s2, r3 = self.parts[n][3:]
            for half in (0, 1):
                s2[half] = self.second[n].total(half).astype(BF16)
            slot = r3.at[yl * 2 + yh]
            self.third[n, 0] = push(s2.at[1 - yl], slot, device(me, yl=1 - yl))
            self.third[n, 1] = push(s2.at[1 - yl], slot, device(me, yl=1 - yl, yh=1 - yh))
            self.third[n, 2] = push(s2.at[yl], slot, device(me, yh=1 - yh))

    def fold_third(self):
        yh, yl = self.me["yh"], self.me["yl"]
        at = 0
        for n, size in enumerate(self.sizes):
            _, _, _, s2, r3 = self.parts[n]
            r3[yl * 2 + yh] = s2[yl]
            for i in (0, 1, 2):
                self.third[n, i].wait_recv()
            total = r3[0].astype(F32)
            for i in (1, 2, 3):
                total = total + r3[i].astype(F32)
            self.fin[pl.ds(at, size), :] = total.astype(BF16)
            at += size

    def end(self):
        for fold in list(self.first.values()) + list(self.second.values()):
            fold.end()
        for copy in self.traded + list(self.third.values()):
            copy.wait_send()


class Spread:
    COPIES = 81

    def __init__(self, me, sems, local, fin, out, sizes, direct=False, pc=0, other=None):
        self.direct, self.fin, self.pc, self.other = direct, fin, pc, other
        self.sems, self.local, self.out = sems, local, out
        self.kept, self.cross, self.own, self.near, self.far = [], [], [], [], []
        xs, zs = Ring(me, "x"), Ring(me, "z")
        base, yh = 16 * sum(sizes), me["yh"]
        self.plans = [(0, sizes[0], xs, zs), (16 * sizes[0], sizes[1], zs, xs)]
        self.swap = None
        if pc:
            self.plans.append((base + yh * (16 * pc), pc, xs, zs))
            self.plans.append((base + (1 - yh) * (16 * pc), pc, zs, xs))
            src = fin.at[pl.ds(sum(sizes), pc)]
            self.swap = sems.push(src, other, device(me, yh=1 - yh))
        at = 0
        for n in range(3 if pc else 2):
            size = self.plans[n][1]
            self.begin(n, fin.at[pl.ds(at, size)])
            at += size

    def begin(self, n, src):
        _, _, ring, cross = self.plans[n]
        copy = pltpu.make_async_copy(src, self.span(n, ring.me, cross.me), self.local.at[n])
        copy.start()
        self.kept.append(copy)
        place = functools.partial(self.span, n, ring.me)
        self.cross.append(Share(self.sems, cross, src, place, self.halves(n)))
        self.own.append(self.share(n, cross.me, src))

    def across(self):
        if self.pc:
            self.swap.wait_recv()
            self.begin(3, self.other)

    def span(self, n, i, j):
        lo, size, _, _ = self.plans[n]
        at = j * 4 + i if n == 3 else i * 4 + j
        return self.out.at[pl.ds(pl.multiple_of(lo + at * size, 16), size)]

    def halves(self, n):
        if self.direct:
            return None
        size = self.plans[n][1]
        first = size // 32 * 16
        return lambda ref: (ref.at[pl.ds(0, first)], ref.at[pl.ds(first, size - first)])

    def share(self, n, j, src=None):
        ring = self.plans[n][2]

        def place(i):
            return self.span(n, i, j)

        src = place(ring.me) if src is None else src
        return Share(self.sems, ring, src, place, self.halves(n))

    def relay(self):
        for share in self.cross:
            share.relay()
        for n, plan in enumerate(self.plans):
            self.near.append(self.share(n, plan[3].left_at))
            self.near.append(self.share(n, plan[3].right_at))

    def pass_on(self):
        for share in self.own:
            share.relay()
        for n, plan in enumerate(self.plans):
            self.cross[n].arrive()
            self.far.append(self.share(n, plan[3].opposite_at))

    def end(self):
        for share in self.near + self.far:
            share.relay()
        for share in self.own + self.near + self.far:
            share.arrive()
        for copy in self.kept:
            copy.wait()
        for share in self.cross + self.own + self.near + self.far:
            share.end()
        if self.pc:
            self.swap.wait_send()


def greet_axes(me, reach=2):
    flip = 1 - me["yl"]
    rings = Ring(me, "x"), Ring(me, "z")
    greet(
        [device(me, yl=flip), device(me, yl=flip, yh=1 - me["yh"]), device(me, c=1 - me["c"])]
        + [device(me, yh=1 - me["yh"])]
        + [dev for ring in rings for dev in (ring.left, ring.right, ring.opposite)[:reach]]
    )


def backward_kernel(reduction, *refs):
    refs = list(refs)
    q, do, o, logs, kv, own, flag, left, right, limit = pop(refs, 10)
    operands = pop(refs, len(reduction.operands))
    dq_ref, dkv_own, fin = pop(refs, 3)
    kv_here, dkv, kk, vv = pop(refs, 4)
    scatter_scratch = pop(refs, len(Scatter.SCRATCH))
    reduce_scratch = pop(refs, len(reduction.scratch))
    send, recv, local = refs
    me = here()
    greet_axes(me)
    sems = Sems(send, recv)
    reduction.bind(me, sems, local, operands, reduce_scratch, fin)
    reduction.trade()
    load = pltpu.make_async_copy(kv, kv_here, local.at[reduction.locals])
    load.start()
    scatter = Scatter(me, sems, dkv, dkv_own, scatter_scratch)
    flat = dkv.reshape(CTX, 640, 128)

    def one(head, _):
        dq_ref[head] = attend_back_head(
            head, q[head], do[head], o[head], logs[head], kv_here, own, flag,
            left, right, limit, flat, kk, vv,
        )
        return 0

    column = reduction.column
    reduction.multiply(0)
    reduction.start(0)
    reduction.multiply(1)
    reduction.start(1)
    reduction.multiply(2)
    reduction.pad()
    column.start()
    load.wait()
    lax.fori_loop(0, KV_HEADS, one, 0)
    for k in (2, 1):
        reduction.relay(k)
    scatter.start()
    for k in (3, 0):
        reduction.relay(k)
    for k in (2, 1, 3, 0):
        column.fold_first(k)
    scatter.relay()
    for k in (2, 1, 3, 0):
        reduction.fold_first(k)
    column.relay()
    scatter.middle()
    reduction.fold_second()
    column.fold_second()
    scatter.last()
    reduction.fold_third()
    column.fold_third()
    scatter.end()
    column.end()
    reduction.end()


def backward(q, do, o, logs, kv, own, plan, reduction, collective_id):
    flags, left, right, limits = plan
    copies = reduction.copies + Scatter.COPIES
    return pl.pallas_call(
        functools.partial(backward_kernel, reduction),
        out_shape=[
            jax.ShapeDtypeStruct((KV_HEADS, ROWS, 128), F32),
            jax.ShapeDtypeStruct((640, 128), F32),
            jax.ShapeDtypeStruct(reduction.fin_shape, BF16),
        ],
        in_specs=[VM] * 4 + [ANY] + [VM] * 5 + [ANY] * len(reduction.operands),
        out_specs=[VM, VM, VM],
        scratch_shapes=[
            pltpu.VMEM((CTX, 640, 128), BF16),
            pltpu.VMEM((4, 2, 4, 640, 128), BF16),
            pltpu.VMEM((KEYS, 128), BF16),
            pltpu.VMEM((KEYS, 128), BF16),
            *Scatter.SCRATCH,
            *reduction.scratch,
            pltpu.SemaphoreType.DMA((copies,)),
            pltpu.SemaphoreType.DMA((copies,)),
            pltpu.SemaphoreType.DMA((reduction.locals + 1,)),
        ],
        compiler_params=pltpu.CompilerParams(
            collective_id=collective_id, has_side_effects=True, vmem_limit_bytes=BIG
        ),
        name="backward",
    )(
        q, do, o, logs, kv, own, flags, left, right, limits, *reduction.operands,
    )


def finish_kernel(reduction, sizes, pc, *refs):
    refs = list(refs)
    done = refs.pop(0)
    operands = pop(refs, len(reduction.operands))
    out_done, out = pop(refs, 2)
    fin, other = pop(refs, 2)
    reduce_scratch = pop(refs, len(reduction.scratch))
    send, recv, local = refs
    me = here()
    greet_axes(me, 3)
    sems = Sems(send, recv)
    reduction.bind(me, sems, local, operands, reduce_scratch, fin)
    reduction.trade()
    slots = local.at[pl.ds(reduction.locals, 4)]
    spread = Spread(me, sems, slots, done, out_done, sizes, False, pc, other)
    reduction.multiply(0)
    reduction.pad()
    for n in (0, 1):
        reduction.start(n)
    for k in (2, 1, 3, 0):
        reduction.relay(k)
    spread.across()
    spread.relay()
    for k in (2, 1, 3, 0):
        reduction.fold_first(k)
    reduction.fold_second()
    spread.pass_on()
    reduction.fold_third()
    last = Spread(
        me, sems, local.at[pl.ds(reduction.locals + 4, 2)], fin, out, reduction.sizes, True
    )
    last.relay()
    last.pass_on()
    spread.end()
    last.end()
    reduction.end()


def finish(done, ready, reduction, collective_id):
    copies = reduction.copies + 2 * Spread.COPIES
    return pl.pallas_call(
        functools.partial(finish_kernel, reduction, ready.sizes, ready.pc),
        out_shape=[
            jax.ShapeDtypeStruct((ready.used, 128), BF16),
            jax.ShapeDtypeStruct((reduction.used, 128), BF16),
        ],
        in_specs=[VM] + [ANY] * len(reduction.operands),
        out_specs=[ANY, ANY],
        scratch_shapes=[
            pltpu.VMEM(reduction.fin_shape, BF16),
            pltpu.VMEM((ready.pc, 128), BF16),
            *reduction.scratch,
            pltpu.SemaphoreType.DMA((copies,)),
            pltpu.SemaphoreType.DMA((copies,)),
            pltpu.SemaphoreType.DMA((reduction.locals + 6,)),
        ],
        compiler_params=pltpu.CompilerParams(
            collective_id=collective_id, has_side_effects=True, vmem_limit_bytes=BIG
        ),
        name="finish",
    )(done, *reduction.operands)


def low_lanes(rows):
    return lax.broadcasted_iota(jnp.int32, (rows, 128), 1) < HALF


def turn(tile):
    return pltpu.roll(tile, HALF, 1)


def heads_of_tile(tile):
    early, late = tile[:HALF], tile[HALF:]
    low = low_lanes(HALF)
    return jnp.where(low, late, turn(early)), jnp.where(low, turn(late), early)


def tile_of_heads(first, second):
    low = low_lanes(HALF)
    early = jnp.where(low, turn(first), second)
    late = jnp.where(low, first, turn(second))
    return jnp.concatenate([early, late], axis=0)


def put_heads(ref, values):
    for t in range(8):
        if t < 7:
            tile = values[:, t * 128 : (t + 1) * 128]
        else:
            last = values[:, 896:960]
            tile = jnp.concatenate([last, jnp.zeros_like(last)], axis=1)
        for i, block in enumerate(heads_of_tile(tile)):
            head = 2 * t + i
            if head < HEADS:
                at = head % GROUP * HALF
                ref[head // GROUP, at : at + HALF, :] = block.astype(ref.dtype)


def get_heads(ref):
    def block(head):
        if head == HEADS:
            return jnp.zeros((HALF, 128), F32)
        at = head % GROUP * HALF
        return ref[head // GROUP, at : at + HALF, :].astype(F32)

    return [tile_of_heads(block(2 * t), block(2 * t + 1)) for t in range(8)]


def partner(tile):
    lane = lax.broadcasted_iota(jnp.int32, tile.shape, 1)
    return jnp.where(lane % HEAD < 32, pltpu.roll(tile, 96, 1), pltpu.roll(tile, 32, 1))


def inverse_rms(values):
    return lax.rsqrt(jnp.sum(values * values, axis=1, keepdims=True) * (1.0 / D) + EPSILON)


def norm_back(values, inv, gain, grad):
    scaled = grad * gain
    mean = jnp.sum(scaled * values, axis=1, keepdims=True) * (1.0 / D)
    grad_values = inv * scaled - values * (inv * inv * inv) * mean
    return grad_values, jnp.sum(grad * values * inv, axis=0, keepdims=True)


def swapped(table):
    ctx = lax.axis_index("ctx")
    return jnp.where(table[2 * ctx] > table[2 * ctx + 1], 1.0, 0.0)


def swap_lanes(a, swap):
    return a * (1.0 - swap) + turn(a) * swap


def project_kernel(
    table, tok_t, cot_t, gains, w, frequency,
    q_ref, own_ref, nt_ref, tok_ref, cot_ref, cott_ref, cosine, sine, gain_a, gain_b,
    flag, left, right, limit,
):
    ctx = lax.axis_index("ctx")
    mine = jnp.minimum(table[2 * ctx], table[2 * ctx + 1])
    swap = swapped(table)
    for row, ref in enumerate((gain_a, gain_b)):
        parts = [gains[16 * f : 16 * (f + 1), :].astype(F32)[row : row + 1, :240] for f in range(4)]
        ref[...] = jnp.concatenate(parts, axis=1)
    line = lax.broadcasted_iota(jnp.int32, (TOK, 128), 0)
    column = lax.broadcasted_iota(jnp.int32, (TOK, 128), 1)
    position = jnp.where(line < HALF, mine, 63 - mine) * HALF + lax.rem(line, HALF)
    angles = position.astype(F32) * frequency[...]
    cosine[...] = jnp.cos(angles)
    sine[...] = jnp.where(column % HEAD < 32, -1.0, 1.0) * jnp.sin(angles)
    cot = swap_lanes(cot_t[...].astype(F32), swap)
    cott_ref[0] = cot.astype(BF16)
    cot_ref[...] = cot.T.astype(BF16)
    values = swap_lanes(tok_t[...].astype(F32), swap).T
    tok_ref[...] = values.astype(BF16)
    normed = values * inverse_rms(values) * gain_a[...]
    low = normed.astype(BF16)
    nt_ref[...] = normed.T.astype(BF16)
    blocks = []
    for t in range(13):
        u = dot_nn(low, w[:, t * 128 : (t + 1) * 128])
        if t < 10:
            u = u * cosine[...] + partner(u) * sine[...]
        blocks += heads_of_tile(u)
    for head in range(HEADS):
        at = head % GROUP * HALF
        q_ref[head // GROUP, at : at + HALF, :] = blocks[head].astype(BF16)
    for i in range(2 * KV_HEADS):
        own_ref[i * HALF : (i + 1) * HALF, :] = turn(blocks[HEADS + i]).astype(BF16)

    lane = lax.broadcasted_iota(jnp.int32, (1, 128), 1)
    first = lane < HALF
    offset = lax.rem(lane, HALF)

    def one(i, _):
        early = jnp.minimum(table[2 * i], table[2 * i + 1])
        turn_late = early >= mine
        m = jnp.where(turn_late, 1.0, 0.0)
        row = pl.ds(i, 1)
        flag[row, :] = jnp.where(first, 1.0, m)
        left[row, :] = jnp.where(first, m, 1.0 - m)
        right[row, :] = jnp.where(first, 1.0 - m, 0.0)
        gap = jnp.where(turn_late, mine - early, early - mine)
        blocks_back = jnp.where(first, early - (63 - mine), gap)
        limit[row, :] = (blocks_back * HALF + offset).astype(F32)
        return 0

    lax.fori_loop(0, CTX, one, 0)
    zero = jnp.zeros((1, 128), F32)
    for ref in (flag, left, right):
        ref[CTX:TILES, :] = zero
    limit[CTX:TILES, :] = jnp.where(first, offset, 10**6).astype(F32)


SMEM = pl.BlockSpec(memory_space=pltpu.SMEM)


def project(table, tok_t, cot_t, gains, w):
    exponent = -(np.arange(128) % 32).astype(np.float32) / 32
    frequency = jnp.asarray(np.power(BASE, exponent).astype(np.float32).reshape(1, 128))
    return pl.pallas_call(
        project_kernel,
        out_shape=[
            jax.ShapeDtypeStruct((KV_HEADS, ROWS, 128), BF16),
            jax.ShapeDtypeStruct((640, 128), BF16),
            jax.ShapeDtypeStruct((D, 128), BF16),
            jax.ShapeDtypeStruct((TOK, D), BF16),
            jax.ShapeDtypeStruct((TOK, D), BF16),
            jax.ShapeDtypeStruct((1, D, 128), BF16),
            jax.ShapeDtypeStruct((TOK, 128), F32),
            jax.ShapeDtypeStruct((TOK, 128), F32),
            jax.ShapeDtypeStruct((1, D), F32),
            jax.ShapeDtypeStruct((1, D), F32),
        ]
        + [jax.ShapeDtypeStruct((TILES, 128), F32)] * 4,
        in_specs=[SMEM] + [VM] * 5,
        out_specs=[VM] * 14,
        compiler_params=pltpu.CompilerParams(vmem_limit_bytes=BIG),
        name="project",
    )(table, tok_t, cot_t, gains, w, frequency)


def middle_kernel(
    table, o, tok, cot, gain, out_hbm, gate_hbm, up_hbm, down_hbm,
    layer_out, grad_mid, do_rows, gain_grad, nt, dgu, hid, at_t, gb,
    out_w, gate_w, up_w, down_w, sem,
):
    loads = []
    pairs = ((out_hbm, out_w), (gate_hbm, gate_w), (up_hbm, up_w), (down_hbm, down_w))
    for i, (src, dst) in enumerate(pairs):
        copy = pltpu.make_async_copy(src, dst, sem.at[i])
        copy.start()
        loads.append(copy)
    attended = jnp.concatenate(get_heads(o), axis=1)
    at_t[...] = attended.T[:D].astype(BF16)
    cot_low = cot[...]
    loads[0].wait()
    middle = tok[...].astype(F32) + dot_nn(attended.astype(BF16)[:, :D], out_w[...])
    inv = inverse_rms(middle)
    normed = middle * inv * gain[...]
    low = normed.astype(BF16)
    nt[...] = normed.T.astype(BF16)
    loads[1].wait()
    gate = dot_nn(low, gate_w[...])
    sigmoid = jax.nn.sigmoid(gate)
    silu = gate * sigmoid
    loads[2].wait()
    up = dot_nn(low, up_w[...])
    hidden = (silu * up).astype(BF16)
    for f in range(4):
        hid[f] = hidden[:, f * 640 : (f + 1) * 640]
    loads[3].wait()
    total = middle
    for f in range(4):
        total = total + dot_nt(hidden[:, f * 640 : (f + 1) * 640], down_w[f * D : (f + 1) * D, :])
    layer_out[...] = swap_lanes(total.T, swapped(table)).astype(BF16)
    grad_hidden = jnp.concatenate(
        [dot_nn(cot_low, down_w[f * D : (f + 1) * D, :]) for f in range(4)], axis=1
    )
    grad_gate = (grad_hidden * up * sigmoid * (1.0 + gate * (1.0 - sigmoid))).astype(BF16)
    grad_up = (grad_hidden * silu).astype(BF16)
    dgu[0, :, 0:FF] = grad_gate
    dgu[0, :, FF : 2 * FF] = grad_up
    grad_norm = dot_nt(grad_gate, gate_w[...]) + dot_nt(grad_up, up_w[...])
    grad_values, gain_grad[...] = norm_back(middle, inv, gain[...], grad_norm)
    grad_middle = cot_low.astype(F32) + grad_values
    grad_mid[...] = grad_middle
    branch = grad_middle.astype(BF16)
    gb[0] = jnp.concatenate([branch, jnp.zeros((TOK, 64), BF16)], axis=1)
    put_heads(do_rows, dot_nt(branch, out_w[...]))


def middle(table, o, tok, cot, gain, out_w, gate_w, up_w, down_w):
    weights = (out_w, gate_w, up_w, down_w)
    return pl.pallas_call(
        middle_kernel,
        out_shape=[
            jax.ShapeDtypeStruct((D, TOK), BF16),
            jax.ShapeDtypeStruct((TOK, D), F32),
            jax.ShapeDtypeStruct((KV_HEADS, ROWS, 128), BF16),
            jax.ShapeDtypeStruct((1, D), F32),
            jax.ShapeDtypeStruct((D, 128), BF16),
            jax.ShapeDtypeStruct((1, TOK, 2 * FF), BF16),
            jax.ShapeDtypeStruct((4, TOK, 640), BF16),
            jax.ShapeDtypeStruct((D, 128), BF16),
            jax.ShapeDtypeStruct((1, TOK, 1024), BF16),
        ],
        in_specs=[SMEM] + [VM] * 4 + [ANY] * 4,
        out_specs=[VM] * 9,
        scratch_shapes=[pltpu.VMEM(w.shape, BF16) for w in weights]
        + [pltpu.SemaphoreType.DMA((4,))],
        compiler_params=pltpu.CompilerParams(vmem_limit_bytes=BIG),
        name="middle",
    )(table, o, tok, cot, gain, *weights)


def unproject_kernel(
    table, dq, dkv, cosine, sine, w, tok, gain, grad_mid, gain_grad_b, grad_tok, dqkv, gain_rows
):
    tiles = get_heads(dq)
    low = low_lanes(TOK)
    turned = [turn(dkv[i * 128 : (i + 1) * 128, :].T) for i in range(5)]
    tiles[7] = jnp.where(low, tiles[7], turned[0])
    for i in range(4):
        tiles.append(jnp.where(low, turned[i], turned[i + 1]))
    tiles.append(jnp.where(low, turned[4], 0.0))
    for t in range(13):
        u = tiles[t]
        if t < 10:
            u = u * cosine[...] - partner(u) * sine[...]
        dqkv[0, :, t * 128 : (t + 1) * 128] = u.astype(BF16)
    grad_norm = dot_nt(dqkv[0], w[...])
    values = tok[...].astype(F32)
    grad_values, gain_grad = norm_back(values, inverse_rms(values), gain[...], grad_norm)
    grad_tok[...] = swap_lanes((grad_mid[...] + grad_values).T, swapped(table))
    blank, below = jnp.zeros((1, 16), F32), jnp.zeros((12, 128), F32)
    for f in range(4):
        lines = []
        for grad in (gain_grad, gain_grad_b[...]):
            both = jnp.concatenate([grad[:, f * 240 : (f + 1) * 240], blank], axis=1)
            lines += [both[:, :128], both[:, 128:]]
        gain_rows[f] = jnp.concatenate([*lines, below], axis=0).astype(BF16)


def unproject(table, dq, dkv, cosine, sine, w, tok, gain, grad_mid, gain_grad_b):
    return pl.pallas_call(
        unproject_kernel,
        out_shape=[
            jax.ShapeDtypeStruct((D, TOK), F32),
            jax.ShapeDtypeStruct((1, TOK, 1664), BF16),
            jax.ShapeDtypeStruct((4, 16, 128), BF16),
        ],
        in_specs=[SMEM] + [VM] * 9,
        out_specs=[VM] * 3,
        compiler_params=pltpu.CompilerParams(vmem_limit_bytes=BIG),
        name="unproject",
    )(table, dq, dkv, cosine, sine, w, tok, gain, grad_mid, gain_grad_b)


def unpack_kernel(g_in, u_in, d_in, o_in, qkv, g, u, d, o, q, k, v, gain_a, gain_b):
    for t in range(4):
        rows, lanes = slice(t * 240, (t + 1) * 240), slice(t * 128, (t + 1) * 128)
        g[:, lanes] = g_in[rows, :].astype(F32)
        u[:, lanes] = u_in[rows, :].astype(F32)
    d[...] = d_in[...].astype(F32)
    step = pl.program_id(0)

    @pl.when(step < 4)
    def _():
        o[:, 0:128] = o_in[0:240, :].astype(F32)
        o[:, 128:256] = o_in[240:480, :].astype(F32)

    @pl.when(step == 0)
    def _():
        tiles = [qkv[t * 240 : (t + 1) * 240, :].astype(F32) for t in range(13)]
        low = low_lanes(240)
        for t in range(7):
            q[:, t * 128 : (t + 1) * 128] = tiles[t]
        q[:, 896:960] = tiles[7][:, :64]
        turned = [turn(t) for t in tiles[7:10]]
        k[0:128, :] = jnp.where(low, turned[0], turned[1]).T
        k[128:256, :] = jnp.where(low, turned[1], turned[2]).T
        k[256:320, :] = turned[2].T[:64]
        v[0:128, :] = tiles[10].T
        v[128:256, :] = tiles[11].T
        v[256:320, :] = tiles[12].T[:64]
        lines = qkv[3120:3136, :].astype(F32)
        for n, ref in enumerate((gain_a, gain_b)):
            both = [lines[2 * n : 2 * n + 1], lines[2 * n + 1 : 2 * n + 2, :112]]
            ref[...] = jnp.concatenate(both, axis=1)


def unpack(done, qkv):
    def whole(*shape):
        return pl.BlockSpec(shape, lambda i: (0, 0))

    return pl.pallas_call(
        unpack_kernel,
        grid=(5,),
        out_shape=[
            jax.ShapeDtypeStruct(shape, F32)
            for shape in (
                (240, FF), (240, FF), (D, 640), (240, D), (240, D), (320, 240), (320, 240),
                (1, 240), (1, 240),
            )
        ],
        in_specs=[
            pl.BlockSpec((960, 128), lambda i: (i, 0)),
            pl.BlockSpec((960, 128), lambda i: (5 + i, 0)),
            pl.BlockSpec((960, 128), lambda i: (12 + i, 0)),
            pl.BlockSpec((480, 128), lambda i: (20 + jnp.minimum(i, 3), 0)),
            whole(*qkv.shape),
        ],
        out_specs=[
            pl.BlockSpec((240, 512), lambda i: (0, i)),
            pl.BlockSpec((240, 512), lambda i: (0, i)),
            pl.BlockSpec((D, 128), lambda i: (0, i)),
            pl.BlockSpec((240, 256), lambda i: (0, jnp.minimum(i, 3))),
            whole(240, D),
            whole(320, 240),
            whole(320, 240),
            whole(1, 240),
            whole(1, 240),
        ],
        compiler_params=pltpu.CompilerParams(vmem_limit_bytes=BIG),
        name="unpack",
    )(done, done, done, done, qkv)


def on_device(
    tokens, cotangent, block_table, attn_gain, w_query, w_key, w_value, w_out, mlp_gain,
    w_gate, w_up, w_down,
):
    gains, qkv_w = gather_qkv(
        jnp.stack([attn_gain, mlp_gain]), w_query, w_key.T, w_value.T, 0
    )
    q_rows, own_kv, na_t, tok, cot, cot_t, cosine, sine, gain_a, gain_b, *plan = project(
        block_table, tokens[0].T, cotangent[0].T, gains, qkv_w
    )
    o_rows, logs, kv, out_w, gate_w, up_w, down_w = forward(
        q_rows, own_kv, plan, (w_out, w_gate, w_up, w_down.T), 1
    )
    kv = kv.reshape(CTX, 640, 128)
    layer_out, grad_mid, do_rows, grad_gain_b, nb_t, dgu, hidden, at_t, branch = middle(
        block_table, o_rows, tok, cot, gain_b, out_w, gate_w, up_w, down_w
    )
    ready = Reduction(
        (
            (nb_t.reshape(2, 2, 240, 128), dgu),
            (at_t.reshape(2, 2, 240, 128), branch),
            (cot_t, hidden.reshape(2, 2, TOK, 640)),
        ),
        None,
        False,
        192,
    )
    dq_rows, dkv, done = backward(q_rows, do_rows, o_rows, logs, kv, own_kv, plan, ready, 2)
    grad_tokens, grad_qkv, gain_rows = unproject(
        block_table, dq_rows, dkv, cosine, sine, qkv_w, tok, gain_a, grad_mid, grad_gain_b
    )
    late = Reduction(
        ((na_t.reshape(2, 2, 240, 128), grad_qkv),), gain_rows.reshape(2, 2, 16, 128), True
    )
    flat_done, flat = finish(done, ready, late, 3)
    shard_g, shard_u, shard_d, shard_o, shard_q, shard_k, shard_v, total_a, total_b = unpack(
        flat_done, flat
    )
    return (
        layer_out.T[None],
        grad_tokens.T[None],
        total_a.reshape(240),
        shard_q,
        shard_k.T,
        shard_v.T,
        shard_o,
        total_b.reshape(240),
        shard_g,
        shard_u,
        shard_d.T,
    )


def solution(mesh):
    rows, cut = P("fsdp", "ctx", None), P("fsdp", None)
    return jax.shard_map(
        on_device,
        mesh=mesh,
        in_specs=(rows, rows, P(), P("fsdp"), cut, cut, cut, cut, P("fsdp"), cut, cut, cut),
        out_specs=(rows, rows, P("fsdp"), cut, cut, cut, cut, P("fsdp"), cut, cut, cut),
        check_vma=False,
    )
```
